32 devices in a mesh: groups: 2 (over y), band: 4 (over z), dom: 2 (over x), lat: 2 (over core).
Axes of the slice: x: 2, y: 2, z: 4, core: 2. Of those that a mesh axis runs over, the one named last changes fastest.
Arguments:
- grid_in: bfloat16 [24, 1440, 227], P(('groups', 'band'), ('dom', 'lat')), parts along dimension 0, may hold values from -6 to 6
- w_grid: bfloat16 [227, 512], replicated, may hold values from -0.375 to 0.375
- w_gs: bfloat16 [512, 512], replicated, may hold values from -0.25 to 0.25
- w_gr: bfloat16 [512, 512], replicated, may hold values from -0.25 to 0.25
- w_gn: bfloat16 [512, 512], replicated, may hold values from -0.03125 to 0.03125
- w_ms: bfloat16 [512, 512], replicated, may hold values from -0.25 to 0.25
- w_mr: bfloat16 [512, 512], replicated, may hold values from -0.25 to 0.25
- w_mn: bfloat16 [512, 512], replicated, may hold values from -0.0625 to 0.0625
- mesh_in: bfloat16 [1024, 512], P(('groups', 'band', 'dom', 'lat')), parts along dimension 0, may hold values from -6 to 6
- d_out: bfloat16 [1024, 512], P(('groups', 'band', 'dom', 'lat')), parts along dimension 0, may hold values from -0.119628906 to 0.119628906
- g2m_send: int32 [8, 4, 1024], P(('groups', 'band'), ('dom', 'lat')), parts along dimension 0, may hold values from 0 to 3239, as said below
- g2m_recv: int32 [8, 4, 1024], P(('groups', 'band'), ('dom', 'lat')), parts along dimension 0, may hold values from 0 to 63, as said below
- g2m_count: int32 [8, 4], P(('groups', 'band'), ('dom', 'lat')), parts along dimension 0, may hold values from 1 to 1024, as said below
- mesh_send: int32 [8, 4, 512], P(('groups', 'band'), ('dom', 'lat')), parts along dimension 0, may hold values from 0 to 191, as said below
- mesh_recv: int32 [8, 4, 512], P(('groups', 'band'), ('dom', 'lat')), parts along dimension 0, may hold values from 0 to 31, as said below
- mesh_count: int32 [8, 4], P(('groups', 'band'), ('dom', 'lat')), parts along dimension 0, may hold values from 1 to 512, as said below
Outputs:
- mesh_out: bfloat16 [1024, 512], P(('groups', 'band', 'dom', 'lat')), parts along dimension 0
- grad_gs: float32 [1024, 512], P(('groups', 'band'), ('dom', 'lat')), parts along dimension 0
- grad_ms: float32 [1024, 512], P(('groups', 'band'), ('dom', 'lat')), parts along dimension 0
The draws below stay inside these ranges and needn't reach their ends.
There are 2 independent parts, one for each index of `groups`. The reference program is written for one: setup_inputs(seed, part) draws one part's arguments, and reference() takes and returns one part's arrays. A program takes and returns all parts, laid end to end along the dimension named above; an argument that names none is the same for every part. Nothing has to cross between parts.
Inputs may be any that keep to these rules, and one draw needn't show every extreme that they name: `g2m_send`: row of the slot's grid_block; on the first band it is 1080 or more, on the last band under (6) * 360. `g2m_recv`: entry of the slot's cycle block. `g2m_count`: slots from this count on are padding. `mesh_send`: row of the slot's mesh_block; on the first band it is 64 or more, on the last band under 4 * 32. `mesh_recv`: one of the 32 nodes of the slot's band and sector. `mesh_count`: slots from this count on are padding.
All inputs are finite; a program needn't handle non-finite values.
Results may differ from the reference program's by a relative error of at most 0.009.
Values may be sent and summed in bfloat16 or wider, within the bound.
No kernel may reach another device: no remote copies, remote signals or barrier semaphores. Data moves between devices by JAX's collectives and lax.ppermute only.
A program may use at most 64 MiB of HBM per device.

```python
import jax
import jax.numpy as jnp
from jax import lax

L = 512
F = 227
LON = 1440
H = 3
GLAT = 3
M_DEV = 128
EG = 1024
EM = 512
SECTORS = 4
LONS = 360
NLAT = 12
NMESH = 512
N_BAND = 4


def skewed_counts(key, most, drop):
    band_ids = jnp.arange(N_BAND, dtype=jnp.int32)[:, None]
    sector_ids = jnp.arange(SECTORS, dtype=jnp.int32)[None, :]
    base = most - drop * band_ids // (N_BAND - 1)
    jitter = jax.random.randint(key, (N_BAND, SECTORS), 0, most // 8 + 1)
    first = (band_ids == 0) & (sector_ids == 0)
    return jnp.where(first, most, base - jitter).astype(jnp.int32)


def bounded_rows(key, slots, rim_span, whole_span):
    band_ids = jnp.arange(N_BAND, dtype=jnp.int32)[:, None, None]
    lower = jnp.where(band_ids == 0, rim_span, 0)
    upper = jnp.where(band_ids == N_BAND - 1, whole_span - rim_span, whole_span)
    return jax.random.randint(key, (N_BAND, SECTORS, slots), lower, upper).astype(jnp.int32)


def draw_g2m_count(key, part):
    key = jax.random.fold_in(key, 11)
    return skewed_counts(key, EG, EG // 2)


def draw_mesh_count(key, part):
    key = jax.random.fold_in(key, 12)
    return skewed_counts(key, EM, 3 * EM // 4)


def draw_g2m_send(key, part):
    key = jax.random.fold_in(key, 13)
    return bounded_rows(key, EG, H * LONS, (GLAT + 2 * H) * LONS)


def draw_mesh_send(key, part):
    key = jax.random.fold_in(key, 14)
    node_count = M_DEV // SECTORS
    return bounded_rows(key, EM, 2 * node_count, 6 * node_count)


def draw_g2m_recv(key, part):
    key = jax.random.fold_in(key, 15)
    node_count = M_DEV // SECTORS
    rim_rows = node_count // 2
    shape = (N_BAND, SECTORS, EG)
    pick_key, own_key, rim_key = jax.random.split(key, 3)
    chooser = jax.random.randint(pick_key, shape, 0, 4)
    own_rows = rim_rows + jax.random.randint(own_key, shape, 0, node_count)
    rim_pick = jax.random.randint(rim_key, shape, 0, 2 * rim_rows)
    rim_pick = jnp.where(rim_pick < rim_rows, rim_pick, rim_pick + node_count)
    return jnp.where(chooser == 0, rim_pick, own_rows).astype(jnp.int32)


def draw_mesh_recv(key, part):
    key = jax.random.fold_in(key, 16)
    return jax.random.randint(key, (N_BAND, SECTORS, EM), 0, M_DEV // SECTORS).astype(jnp.int32)


def levels(stream_key, shape, cuts, smallest, top_value):
    def one(axis_at, parts):
        draws = jax.random.uniform(jax.random.fold_in(jax.random.fold_in(stream_key, 6), axis_at), (parts,), jnp.float32, smallest / len(cuts), top_value / len(cuts))
        return jnp.repeat(jnp.exp(draws), shape[axis_at] // parts).reshape((-1,) + (1,) * (len(shape) - axis_at - 1))

    loudness = one(*cuts[0])
    for cut in cuts[1:]:
        loudness = loudness * one(*cut)
    return loudness


def gaussian(stream_key, shape, scale, reach, cuts=(), held_as=jnp.bfloat16):
    drawn = scale * jax.random.normal(stream_key, shape, jnp.float32)
    if cuts:
        drawn = drawn * levels(stream_key, shape, cuts, -0.22, 0.18)
    return jnp.clip(drawn, -reach, reach).astype(held_as)


def setup_inputs(seed: int = 0, part: int = 0) -> dict:
    arg_keys = jax.random.split(jax.random.key(seed), 17)
    own_keys = jax.random.split(jax.random.fold_in(arg_keys[16], part), 17)
    return {
        "grid_in": gaussian(own_keys[0], (NLAT, LON, F), 1.0, 6.0, ((0, 4), (1, 4))),
        "w_grid": gaussian(arg_keys[1], (F, L), F ** -0.5, 0.375),
        "w_gs": gaussian(arg_keys[2], (L, L), L ** -0.5, 0.25),
        "w_gr": gaussian(arg_keys[3], (L, L), L ** -0.5, 0.25),
        "w_gn": gaussian(arg_keys[4], (L, L), (L * 64) ** -0.5, 0.03125),
        "w_ms": gaussian(arg_keys[5], (L, L), L ** -0.5, 0.25),
        "w_mr": gaussian(arg_keys[6], (L, L), L ** -0.5, 0.25),
        "w_mn": gaussian(arg_keys[7], (L, L), (L * 16) ** -0.5, 0.0625),
        "mesh_in": gaussian(own_keys[8], (NMESH, L), 1.0, 6.0, ((0, 16),)),
        "d_out": gaussian(own_keys[9], (NMESH, L), 0.02, 0.119628906, ((0, 16),)),
        "g2m_send": draw_g2m_send(jax.random.fold_in(jax.random.fold_in(arg_keys[16], part), 71), part),
        "g2m_recv": draw_g2m_recv(jax.random.fold_in(jax.random.fold_in(arg_keys[16], part), 71), part),
        "g2m_count": draw_g2m_count(jax.random.fold_in(jax.random.fold_in(arg_keys[16], part), 71), part),
        "mesh_send": draw_mesh_send(jax.random.fold_in(jax.random.fold_in(arg_keys[16], part), 71), part),
        "mesh_recv": draw_mesh_recv(jax.random.fold_in(jax.random.fold_in(arg_keys[16], part), 71), part),
        "mesh_count": draw_mesh_count(jax.random.fold_in(jax.random.fold_in(arg_keys[16], part), 71), part),
    }


def silu_slope(inputs):
    logistic = jax.nn.sigmoid(inputs)
    return logistic * (1.0 + inputs * (1.0 - logistic))


def matmul(first_op, second_op):
    return jnp.dot(first_op, second_op, preferred_element_type=jnp.float32)


def matmul_back(first_op, second_op):
    return lax.dot_general(first_op, second_op, (((1,), (1,)), ((), ())), preferred_element_type=jnp.float32)


def outer_sum(rows, terms):
    return lax.dot_general(rows, terms, (((0,), (0,)), ((), ())), preferred_element_type=jnp.float32)


def reference(grid_in, w_grid, w_gs, w_gr, w_gn, w_ms, w_mr, w_mn, mesh_in, d_out, g2m_send, g2m_recv, g2m_count, mesh_send, mesh_recv, mesh_count):
    node_count = M_DEV // SECTORS
    rim_rows = node_count // 2
    cycle_rows = 2 * node_count
    devices = jnp.arange(N_BAND * SECTORS, dtype=jnp.int32)
    grid_lat = jax.nn.silu(matmul(grid_in.reshape(-1, F), w_grid)).astype(jnp.bfloat16).reshape(GLAT * N_BAND, LON, L)
    grid_pad = jnp.pad(grid_lat, ((H, H), (0, 0), (0, 0)))
    recv_grid = matmul(mesh_in, w_gr).reshape(N_BAND, M_DEV, L)
    edge_slot = jnp.arange(EG, dtype=jnp.int32)
    mesh_slot = jnp.arange(EM, dtype=jnp.int32)
    cycle_step = jnp.arange(cycle_rows, dtype=jnp.int32)
    block_of_row = jnp.arange(3 * cycle_rows, dtype=jnp.int32) // cycle_rows
    place_of_row = jnp.arange(3 * cycle_rows, dtype=jnp.int32) % cycle_rows

    def cycle_of(sector_index):
        return (sector_index * node_count - rim_rows + cycle_step) % M_DEV

    def grid_edges(device):
        band_index = device // SECTORS
        sector_index = device % SECTORS
        block = lax.dynamic_slice(grid_pad, (band_index * GLAT, sector_index * LONS, jnp.int32(0)), (GLAT + 2 * H, LONS, L)).reshape(-1, L)
        senders = jnp.take(block, g2m_send[band_index, sector_index], axis=0)
        receivers = jnp.take(cycle_of(sector_index), g2m_recv[band_index, sector_index], axis=0)
        live = (edge_slot < g2m_count[band_index, sector_index]).astype(jnp.float32)[:, None]
        pre = matmul(senders, w_gs) + jnp.take(recv_grid[band_index], receivers, axis=0)
        return band_index, senders, receivers, live, pre

    def grid_part(device):
        band_index, senders, receivers, live, pre = grid_edges(device)
        return jax.ops.segment_sum(jax.nn.silu(pre) * live, receivers, num_segments=M_DEV)

    agg_one = lax.map(grid_part, devices).reshape(N_BAND, SECTORS, M_DEV, L).sum(axis=1)
    enc_gate = matmul(agg_one.reshape(-1, L).astype(jnp.bfloat16), w_gn)
    mesh_one = (mesh_in.astype(jnp.float32) + jax.nn.silu(enc_gate)).astype(jnp.bfloat16)
    mesh_pad = jnp.pad(mesh_one.reshape(N_BAND, M_DEV, L), ((1, 1), (0, 0), (0, 0)))
    recv_mesh = matmul(mesh_one, w_mr).reshape(N_BAND, M_DEV, L)

    def mesh_edges(device):
        band_index = device // SECTORS
        sector_index = device % SECTORS
        cycle_ids = cycle_of(sector_index)
        extended = jnp.concatenate([jnp.take(mesh_pad[band_index + offset], cycle_ids, axis=0) for offset in range(3)], axis=0)
        sender_ids = mesh_send[band_index, sector_index]
        receivers = sector_index * node_count + mesh_recv[band_index, sector_index]
        live = (mesh_slot < mesh_count[band_index, sector_index]).astype(jnp.float32)[:, None]
        pre = jnp.take(matmul(extended, w_ms), sender_ids, axis=0) + jnp.take(recv_mesh[band_index], receivers, axis=0)
        return band_index, cycle_ids, extended, sender_ids, receivers, live, pre

    def mesh_part(device):
        band_index, cycle_ids, extended, sender_ids, receivers, live, pre = mesh_edges(device)
        return jax.ops.segment_sum(jax.nn.silu(pre) * live, receivers, num_segments=M_DEV)

    agg_two = lax.map(mesh_part, devices).reshape(N_BAND, SECTORS, M_DEV, L).sum(axis=1)
    proc_gate = matmul(agg_two.reshape(-1, L).astype(jnp.bfloat16), w_mn)
    mesh_out = (mesh_one.astype(jnp.float32) + jax.nn.silu(proc_gate)).astype(jnp.bfloat16)
    cotangent = d_out.astype(jnp.float32)
    gate_two = (cotangent * silu_slope(proc_gate)).astype(jnp.bfloat16)
    back_two = matmul_back(gate_two, w_mn).reshape(N_BAND, M_DEV, L)

    def mesh_step(total, device):
        band_index, cycle_ids, extended, sender_ids, receivers, live, pre = mesh_edges(device)
        slope = (jnp.take(back_two[band_index], receivers, axis=0) * silu_slope(pre) * live).astype(jnp.bfloat16)
        gradient = outer_sum(jnp.take(extended, sender_ids, axis=0), slope)
        slope_wide = slope.astype(jnp.float32)
        row_band = band_index - 1 + block_of_row
        row_node = row_band * M_DEV + jnp.take(cycle_ids, place_of_row, axis=0)
        row_node = jnp.where((row_band >= 0) & (row_band < N_BAND), row_node, NMESH).astype(jnp.int32)
        send_part = jax.ops.segment_sum(slope_wide, jnp.take(row_node, sender_ids, axis=0), num_segments=NMESH + 1)[:NMESH]
        recv_part = jax.ops.segment_sum(slope_wide, band_index * M_DEV + receivers, num_segments=NMESH)
        return (total[0] + gradient, total[1] + send_part, total[2] + recv_part), None

    start = (jnp.zeros((L, L), jnp.float32), jnp.zeros((NMESH, L), jnp.float32), jnp.zeros((NMESH, L), jnp.float32))
    (grad_ms, send_total, recv_total), unused = lax.scan(mesh_step, start, devices)
    cot_one = cotangent + matmul_back(send_total.astype(jnp.bfloat16), w_ms) + matmul_back(recv_total.astype(jnp.bfloat16), w_mr)
    gate_one = (cot_one * silu_slope(enc_gate)).astype(jnp.bfloat16)
    back_one = matmul_back(gate_one, w_gn).reshape(N_BAND, M_DEV, L)

    def grid_step(total, device):
        band_index, senders, receivers, live, pre = grid_edges(device)
        slope = (jnp.take(back_one[band_index], receivers, axis=0) * silu_slope(pre) * live).astype(jnp.bfloat16)
        return total + outer_sum(senders, slope), None

    grad_gs, unused_two = lax.scan(grid_step, jnp.zeros((L, L), jnp.float32), devices)
    return mesh_out, grad_gs, grad_ms
```

```python
import jax
import jax.numpy as jnp
from jax import lax
from jax.sharding import PartitionSpec as P

H = 3


def with_halo(cells, sides, width, closed):
    for axis, dim in sides:
        count = lax.axis_size(axis)
        ends = count if closed else count - 1
        head = lax.slice_in_dim(cells, 0, width, axis=dim)
        tail = lax.slice_in_dim(cells, cells.shape[dim] - width, cells.shape[dim], axis=dim)
        cells = jnp.concatenate(
            [
                lax.ppermute(tail, axis, [(i, (i + 1) % count) for i in range(ends)]),
                cells,
                lax.ppermute(head, axis, [((i + 1) % count, i) for i in range(ends)]),
            ],
            axis=dim,
        )
    return cells


def silu_slope(inputs):
    logistic = jax.nn.sigmoid(inputs)
    return logistic * (1.0 + inputs * (1.0 - logistic))


def matmul(first_op, second_op):
    return jnp.dot(first_op, second_op, preferred_element_type=jnp.float32)


def matmul_back(first_op, second_op):
    return lax.dot_general(
        first_op, second_op, (((1,), (1,)), ((), ())), preferred_element_type=jnp.float32
    )


def outer_sum(rows, terms):
    return lax.dot_general(
        rows, terms, (((0,), (0,)), ((), ())), preferred_element_type=jnp.float32
    )


def exact_sum(table, values):
    return jnp.dot(
        table, values, precision=lax.Precision.HIGHEST, preferred_element_type=jnp.float32
    )


def hit_table(count, targets):
    return lax.iota(jnp.int32, count)[:, None] == targets[None, :]


def on_device(
    grid_in,
    w_grid,
    w_gs,
    w_gr,
    w_gn,
    w_ms,
    w_mr,
    w_mn,
    mesh_in,
    d_out,
    g2m_send,
    g2m_recv,
    g2m_count,
    mesh_send,
    mesh_recv,
    mesh_count,
):
    band_rows, cycle_cols, variables = grid_in.shape
    latent = w_grid.shape[1]
    node_count = mesh_in.shape[0]
    rim_rows = node_count // 2
    cycle_rows = 2 * node_count
    sectors = lax.axis_size(("dom", "lat"))
    band_count = lax.axis_size("band")
    grid_raw = with_halo(grid_in, (("band", 0),), H, False).reshape(-1, variables)
    grid_from = g2m_send.reshape(-1)
    grid_to = g2m_recv.reshape(-1)
    grid_flag = (lax.iota(jnp.int32, grid_from.shape[0]) < g2m_count.reshape(())).astype(
        jnp.float32
    )
    grid_live = grid_flag[:, None]
    senders = jax.nn.silu(matmul(jnp.take(grid_raw, grid_from, axis=0), w_grid)).astype(
        jnp.bfloat16
    )
    cycle_in = with_halo(mesh_in, ((("dom", "lat"), 0),), rim_rows, True)
    enc_pre = matmul(senders, w_gs) + jnp.take(matmul(cycle_in, w_gr), grid_to, axis=0)
    grid_hits = hit_table(cycle_rows, grid_to).astype(jnp.float32) * grid_flag[None, :]
    enc_part = exact_sum(grid_hits, jax.nn.silu(enc_pre))
    rim_parts = jnp.concatenate([enc_part[:rim_rows], enc_part[rim_rows + node_count :]], axis=0)
    returned = with_halo(rim_parts, ((("dom", "lat"), 0),), rim_rows, True)
    agg_one = enc_part[rim_rows : rim_rows + node_count] + jnp.concatenate(
        [returned[:rim_rows], returned[rim_rows + node_count :]], axis=0
    )
    enc_gate = matmul(agg_one.astype(jnp.bfloat16), w_gn)
    mesh_one = (mesh_in.astype(jnp.float32) + jax.nn.silu(enc_gate)).astype(jnp.bfloat16)
    cycle_one = with_halo(mesh_one, ((("dom", "lat"), 0),), rim_rows, True)
    mesh_block = with_halo(cycle_one[None], (("band", 0),), 1, False).reshape(-1, latent)
    mesh_from = mesh_send.reshape(-1)
    mesh_to = mesh_recv.reshape(-1)
    mesh_flag = (lax.iota(jnp.int32, mesh_from.shape[0]) < mesh_count.reshape(())).astype(
        jnp.float32
    )
    mesh_live = mesh_flag[:, None]
    proc_pre = jnp.take(matmul(mesh_block, w_ms), mesh_from, axis=0) + jnp.take(
        matmul(mesh_one, w_mr), mesh_to, axis=0
    )
    recv_hits = hit_table(node_count, mesh_to)
    agg_two = exact_sum(recv_hits.astype(jnp.float32) * mesh_flag[None, :], jax.nn.silu(proc_pre))
    proc_gate = matmul(agg_two.astype(jnp.bfloat16), w_mn)
    mesh_out = (mesh_one.astype(jnp.float32) + jax.nn.silu(proc_gate)).astype(jnp.bfloat16)
    cotangent = d_out.astype(jnp.float32)
    gate_two = (cotangent * silu_slope(proc_gate)).astype(jnp.bfloat16)
    back_two = matmul_back(gate_two, w_mn)
    proc_slope = (jnp.take(back_two, mesh_to, axis=0) * silu_slope(proc_pre) * mesh_live).astype(
        jnp.bfloat16
    )
    grad_proc = outer_sum(jnp.take(mesh_block, mesh_from, axis=0), proc_slope)
    send_sum = matmul(hit_table(3 * cycle_rows, mesh_from).astype(jnp.bfloat16), proc_slope)
    recv_sum = matmul(recv_hits.astype(jnp.bfloat16), proc_slope)
    by_band = send_sum.reshape(3, cycle_rows, latent)
    outward = jnp.concatenate([by_band[0], by_band[2]], axis=0)
    returned_band = with_halo(
        outward.astype(jnp.bfloat16), (("band", 0),), cycle_rows, False
    ).astype(outward.dtype)
    cycle_sum = by_band[1] + returned_band[:cycle_rows] + returned_band[3 * cycle_rows :]
    side_rows = jnp.concatenate([cycle_sum[:rim_rows], cycle_sum[rim_rows + node_count :]], axis=0)
    returned_cycle = with_halo(
        side_rows.astype(jnp.bfloat16), ((("dom", "lat"), 0),), rim_rows, True
    ).astype(side_rows.dtype)
    send_total = cycle_sum[rim_rows : rim_rows + node_count] + jnp.concatenate(
        [returned_cycle[:rim_rows], returned_cycle[rim_rows + node_count :]], axis=0
    )
    cot_one = (
        cotangent
        + matmul_back(send_total.astype(jnp.bfloat16), w_ms)
        + matmul_back(recv_sum.astype(jnp.bfloat16), w_mr)
    )
    gate_one = (cot_one * silu_slope(enc_gate)).astype(jnp.bfloat16)
    back_one = matmul_back(gate_one, w_gn)
    back_cycle = with_halo(back_one, ((("dom", "lat"), 0),), rim_rows, True)
    enc_slope = (jnp.take(back_cycle, grid_to, axis=0) * silu_slope(enc_pre) * grid_live).astype(
        jnp.bfloat16
    )
    grad_enc = outer_sum(senders, enc_slope)

    def as_tiles(gradient):
        split = gradient.reshape(band_count, latent // band_count, sectors, latent // sectors)
        return split.transpose(0, 2, 1, 3).reshape(
            band_count * sectors, latent // band_count, latent // sectors
        )

    def summed_tile(gradient):
        tiles = as_tiles(gradient).astype(jnp.bfloat16)
        shares = lax.all_to_all(tiles, ("band", "dom", "lat"), 0, 0, tiled=True)
        return jnp.sum(shares.astype(jnp.float32), axis=0)

    return (mesh_out, summed_tile(grad_enc), summed_tile(grad_proc))


def solution(mesh):
    placed = (
        P(("groups", "band"), ("dom", "lat"), None),
        P(),
        P(),
        P(),
        P(),
        P(),
        P(),
        P(),
        P(("groups", "band", "dom", "lat"), None),
        P(("groups", "band", "dom", "lat"), None),
        P(("groups", "band"), ("dom", "lat"), None),
        P(("groups", "band"), ("dom", "lat"), None),
        P(("groups", "band"), ("dom", "lat")),
        P(("groups", "band"), ("dom", "lat"), None),
        P(("groups", "band"), ("dom", "lat"), None),
        P(("groups", "band"), ("dom", "lat")),
    )
    return jax.shard_map(
        on_device,
        mesh=mesh,
        in_specs=placed,
        out_specs=(
            P(("groups", "band", "dom", "lat"), None),
            P(("groups", "band"), ("dom", "lat")),
            P(("groups", "band"), ("dom", "lat")),
        ),
        check_vma=False,
    )
```

```python
import functools

import jax
import jax.numpy as jnp
from jax import lax
from jax.experimental import pallas as pl
from jax.experimental.pallas import tpu as pltpu
from jax.sharding import PartitionSpec as P

F32 = jnp.float32
BF16 = jnp.bfloat16
LANES = 128


def mm(a, b):
    return jnp.dot(a, b, preferred_element_type=F32)


def mm_nt(a, b):
    return lax.dot_general(a, b, (((1,), (1,)), ((), ())), preferred_element_type=F32)


def mm_tn(a, b):
    return lax.dot_general(a, b, (((0,), (0,)), ((), ())), preferred_element_type=F32)


def halves(x):
    high = x.astype(BF16)
    return high, (x - high.astype(F32)).astype(BF16)


def silu_parts(x):
    g = 1.0 / (1.0 + jnp.exp(-x))
    return x * g, g * (1.0 + x * (1.0 - g))


def ones_at(mask):
    return jnp.where(mask, 1.0, 0.0).astype(BF16)


def columns(row):
    count = row.shape[1]
    parts = [
        jnp.broadcast_to(row[:, i : i + LANES], (LANES, LANES)).T
        for i in range(0, count, LANES)
    ]
    return parts[0] if len(parts) == 1 else jnp.concatenate(parts, axis=0)


def hits_from(cols, width, period, start=0):
    parts = []
    for i in range(0, width, LANES):
        size = min(LANES, width - i)
        lane = lax.broadcasted_iota(jnp.int32, (cols.shape[0], size), 1) + i
        if period < width:
            lane = lax.rem(lane, period)
        parts.append(ones_at(cols[:, :size] == lane + start))
    return parts[0] if len(parts) == 1 else jnp.concatenate(parts, axis=1)


def hits_to(row, count):
    return ones_at(lax.broadcasted_iota(jnp.int32, (count, row.shape[1]), 0) == row)


def live_only(row, count, first=0):
    slot = lax.broadcasted_iota(jnp.int32, row.shape, 1) + first
    return jnp.where(slot < count, row, -1)


def even_on(axis):
    return lax.rem(lax.axis_index(axis), 2) == 0


def own_gather_kernel(send, grid, near, far, mesh_in, w_gr, rows_out, table_out):
    band_rows, cols, _ = grid.shape
    node_count = mesh_in.shape[0]
    rim = node_count // 2
    even = even_on("lat")
    left = jnp.where(even, far[...], near[...])[rim:]
    right = jnp.where(even, near[...], far[...])[:rim]
    cycle = jnp.concatenate([left, mesh_in[...], right], axis=0)
    high, low = halves(mm(cycle, w_gr[...]))
    table_out[: 2 * node_count] = high
    table_out[2 * node_count :] = low
    block = 256
    for first in range(0, send.shape[2], block):
        index = columns(send[0, :, first : first + block])
        total = None
        for k in range(band_rows):
            hit = hits_from(index, cols, cols, (band_rows + k) * cols)
            part = mm(hit, grid[k])
            total = part if total is None else total + part
        rows_out[first : first + block] = total.astype(BF16)


def encode_kernel(
    send, recv, count, near, far, own, table, w_grid, w_gs,
    senders_out, slope_out, part_out, near_out, far_out,
):
    band_rows, cols, _ = near.shape
    cycle = table.shape[0] // 2
    half = cycle // 2
    even_band = even_on("band")
    near_base = jnp.where(even_band, 2 * band_rows * cols, 0)
    far_base = jnp.where(even_band, 0, 2 * band_rows * cols)
    block = 256
    sums = None
    for first in range(0, send.shape[2], block):
        part_of = slice(first, first + block)
        index = columns(send[0, :, part_of])
        total = own[part_of].astype(F32)
        for base, halo in ((near_base, near), (far_base, far)):
            for k in range(band_rows):
                total = total + mm(hits_from(index, cols, cols, base + k * cols), halo[k])
        latent, _ = silu_parts(mm(total.astype(BF16), w_grid[...]))
        latent = latent.astype(BF16)
        senders_out[part_of] = latent
        target = live_only(recv[0, :, part_of], count[0, 0], first)
        pre = mm(latent, w_gs[...]) + mm(
            hits_from(columns(target), 2 * cycle, cycle), table[...]
        )
        value, slope = silu_parts(pre)
        slope_out[part_of] = slope.astype(BF16)
        part = mm(hits_to(target, cycle), value.astype(BF16))
        sums = part if sums is None else sums + part
    part_out[...] = sums
    even = even_on("lat")
    near_out[...] = jnp.where(even, sums[half:], sums[:half]).astype(BF16)
    far_out[...] = jnp.where(even, sums[:half], sums[half:]).astype(BF16)


def node_kernel(part, near, far, mesh_near, mesh_far, mesh_in, w_gn, mesh_out, slope_out):
    node_count = mesh_in.shape[0]
    rim = node_count // 2
    even = even_on("lat")
    left = jnp.where(even, far[...], near[...]).astype(F32)
    right = jnp.where(even, near[...], far[...]).astype(F32)
    total = part[...] + jnp.concatenate([left, right], axis=0)
    mesh_left = jnp.where(even, mesh_far[...], mesh_near[...])[rim:]
    mesh_right = jnp.where(even, mesh_near[...], mesh_far[...])[:rim]
    cycle = jnp.concatenate([mesh_left, mesh_in[...], mesh_right], axis=0)
    value, slope = silu_parts(mm(total.astype(BF16), w_gn[...]))
    mesh_out[...] = (cycle.astype(F32) + value).astype(BF16)
    slope_out[...] = slope


def process_kernel(
    send, recv, count, near, own, far, d_out, w_ms, w_mr, w_mn,
    mesh_out, sums_out, recv_out, near_out, far_out,
):
    cycle = own.shape[0]
    node_count = cycle // 2
    rim = node_count // 2
    even_band = even_on("band")
    raw = send[0]
    flipped = jnp.where(
        raw < cycle, raw + 2 * cycle, jnp.where(raw < 2 * cycle, raw, raw - 2 * cycle)
    )
    source = jnp.where(even_band, flipped, raw)
    target = live_only(recv[0], count[0, 0])
    home = own[rim : rim + node_count]
    block = jnp.concatenate([near[...], own[...], far[...]], axis=0)
    table = jnp.concatenate(
        [*halves(mm(block, w_ms[...])), *halves(mm(home, w_mr[...]))], axis=0
    )
    from_hits = hits_from(columns(source), 6 * cycle, 3 * cycle)
    to_hits = hits_from(columns(target), 2 * node_count, node_count)
    pre = mm(from_hits, table[: 6 * cycle]) + mm(to_hits, table[6 * cycle :])
    value, slope = silu_parts(pre)
    to_rows = hits_to(target, node_count)
    gate = mm(mm(to_rows, value.astype(BF16)).astype(BF16), w_mn[...])
    gate_value, gate_slope = silu_parts(gate)
    mesh_out[...] = (home.astype(F32) + gate_value).astype(BF16)
    gate_two = (d_out[...].astype(F32) * gate_slope).astype(BF16)
    back = jnp.concatenate(halves(mm_nt(gate_two, w_mn[...])), axis=0)
    edge_slope = (mm(to_hits, back) * slope).astype(BF16)
    sums = mm(hits_to(source, 3 * cycle), edge_slope)
    recv_out[...] = mm(to_rows, edge_slope).astype(BF16)
    sums_out[...] = sums
    near_out[...] = sums[:cycle].astype(BF16)
    far_out[...] = sums[2 * cycle :].astype(BF16)


def store_tiles(out, gradient):
    tiles, rows, cols = out.shape
    across = gradient.shape[1] // cols
    for i in range(tiles):
        r, c = (i // across) * rows, (i % across) * cols
        out[i] = gradient[r : r + rows, c : c + cols].astype(out.dtype)


def process_grad_kernel(near, own, far, sums, recv_sum, d_out, w_mr, tiles_out, home_out):
    block = jnp.concatenate([near[...], own[...], far[...]], axis=0)
    store_tiles(tiles_out, mm_tn(block, sums[...].astype(BF16)))
    home_out[...] = mm_nt(recv_sum[...], w_mr[...]) + d_out[...].astype(F32)


def cotangent_kernel(sums, near, far, home, w_ms, part_out, near_out, far_out):
    cycle = near.shape[0]
    half = cycle // 2
    rim = half // 2
    total = sums[cycle : 2 * cycle] + near[...].astype(F32) + far[...].astype(F32)
    back = mm_nt(total.astype(BF16), w_ms[...])
    back = jnp.concatenate(
        [back[:rim], back[rim : rim + half] + home[...], back[rim + half :]], axis=0
    )
    part_out[...] = back
    even = even_on("lat")
    near_out[...] = jnp.where(even, back[half:], back[:half]).astype(BF16)
    far_out[...] = jnp.where(even, back[:half], back[half:]).astype(BF16)


def encode_grad_kernel(
    recv, count, part, near, far, node_slope, w_gn, senders, edge_slope, tiles_out
):
    cycle = part.shape[0]
    even = even_on("lat")
    left = jnp.where(even, far[...], near[...]).astype(F32)
    right = jnp.where(even, near[...], far[...]).astype(F32)
    cot = part[...] + jnp.concatenate([left, right], axis=0)
    gate_one = (cot * node_slope[...]).astype(BF16)
    back = jnp.concatenate(halves(mm_nt(gate_one, w_gn[...])), axis=0)
    target = live_only(recv[0], count[0, 0])
    hits = hits_from(columns(target), 2 * cycle, cycle)
    slope = (mm(hits, back) * edge_slope[...].astype(F32)).astype(BF16)
    store_tiles(tiles_out, mm_tn(senders[...], slope))


def call(kernel, outs, *args, scalars=()):
    in_specs = [
        pl.BlockSpec(memory_space=pltpu.SMEM if i in scalars else pltpu.VMEM)
        for i in range(len(args))
    ]
    return pl.pallas_call(
        kernel,
        out_shape=[jax.ShapeDtypeStruct(shape, dtype) for shape, dtype in outs],
        in_specs=in_specs,
        out_specs=[pl.BlockSpec(memory_space=pltpu.VMEM)] * len(outs),
        compiler_params=pltpu.CompilerParams(vmem_limit_bytes=48 << 20),
    )(*args)


def pairings(count, closed):
    near = [(i, i ^ 1) for i in range(count)]
    far = []
    for i in range(count):
        j = i + 1 if i % 2 else i - 1
        if closed:
            j %= count
        far.append((i, j if 0 <= j < count else i))
    return near, far


def on_device(
    grid_in, w_grid, w_gs, w_gr, w_gn, w_ms, w_mr, w_mn, mesh_in, d_out,
    g2m_send, g2m_recv, g2m_count, mesh_send, mesh_recv, mesh_count,
):
    latent = w_grid.shape[1]
    variables = w_grid.shape[0]
    node_count = mesh_in.shape[0]
    cycle = 2 * node_count
    bands = lax.axis_size("band")
    sectors = lax.axis_size(("dom", "lat"))
    edges = g2m_send.shape[2]
    around = ("dom", "lat")
    band_near, band_far = pairings(bands, False)
    ring_near, ring_far = pairings(sectors, True)

    raw_near = lax.ppermute(grid_in, "band", band_near)
    raw_far = lax.ppermute(grid_in, "band", band_far)
    mesh_near = lax.ppermute(mesh_in, around, ring_near)
    mesh_far = lax.ppermute(mesh_in, around, ring_far)
    own_rows, table = call(
        own_gather_kernel,
        [((edges, variables), BF16), ((2 * cycle, latent), BF16)],
        g2m_send, grid_in, mesh_near, mesh_far, mesh_in, w_gr,
    )
    senders, edge_slope, part, to_near, to_far = call(
        encode_kernel,
        [
            ((edges, latent), BF16),
            ((edges, latent), BF16),
            ((cycle, latent), F32),
            ((node_count, latent), BF16),
            ((node_count, latent), BF16),
        ],
        g2m_send, g2m_recv, g2m_count, raw_near, raw_far, own_rows, table, w_grid, w_gs,
        scalars=(2,),
    )
    from_near = lax.ppermute(to_near, around, ring_near)
    from_far = lax.ppermute(to_far, around, ring_far)
    mesh_one, node_slope = call(
        node_kernel,
        [((cycle, latent), BF16), ((cycle, latent), F32)],
        part, from_near, from_far, mesh_near, mesh_far, mesh_in, w_gn,
    )
    one_near = lax.ppermute(mesh_one, "band", band_near)
    one_far = lax.ppermute(mesh_one, "band", band_far)
    mesh_out, sums, recv_sum, to_near, to_far = call(
        process_kernel,
        [
            ((node_count, latent), BF16),
            ((3 * cycle, latent), F32),
            ((node_count, latent), BF16),
            ((cycle, latent), BF16),
            ((cycle, latent), BF16),
        ],
        mesh_send, mesh_recv, mesh_count, one_near, mesh_one, one_far, d_out, w_ms, w_mr, w_mn,
        scalars=(2,),
    )
    from_near = lax.ppermute(to_near, "band", band_near)
    from_far = lax.ppermute(to_far, "band", band_far)
    tile_shape = (bands * sectors, latent // bands, latent // sectors)
    tiles_ms, home = call(
        process_grad_kernel,
        [(tile_shape, BF16), ((node_count, latent), F32)],
        one_near, mesh_one, one_far, sums, recv_sum, d_out, w_mr,
    )
    part, to_near, to_far = call(
        cotangent_kernel,
        [
            ((cycle, latent), F32),
            ((node_count, latent), BF16),
            ((node_count, latent), BF16),
        ],
        sums, from_near, from_far, home, w_ms,
    )
    from_near = lax.ppermute(to_near, around, ring_near)
    from_far = lax.ppermute(to_far, around, ring_far)
    (tiles_gs,) = call(
        encode_grad_kernel,
        [(tile_shape, BF16)],
        g2m_recv, g2m_count, part, from_near, from_far, node_slope, w_gn, senders, edge_slope,
        scalars=(1,),
    )

    def summed(tiles):
        shares = lax.all_to_all(tiles, ("band", "dom", "lat"), 0, 0, tiled=True)
        return jnp.sum(shares.astype(F32), axis=0)

    return mesh_out, summed(tiles_gs), summed(tiles_ms)


def solution(mesh):
    flat = P(("groups", "band", "dom", "lat"), None)
    grid = P(("groups", "band"), ("dom", "lat"), None)
    count = P(("groups", "band"), ("dom", "lat"))
    placed = (grid,) + (P(),) * 7 + (flat, flat) + (grid, grid, count) * 2
    return jax.shard_map(
        on_device,
        mesh=mesh,
        in_specs=placed,
        out_specs=(flat, count, count),
        check_vma=False,
    )
```

```python
import jax
import jax.numpy as jnp
from jax import lax
from jax.experimental import pallas as pl
from jax.experimental.pallas import tpu as pltpu
from jax.sharding import PartitionSpec as P

F32 = jnp.float32
BF16 = jnp.bfloat16
LANES = 128


def mm(a, b):
    return jnp.dot(a, b, preferred_element_type=F32)


def mm_nt(a, b):
    return lax.dot_general(a, b, (((1,), (1,)), ((), ())), preferred_element_type=F32)


def mm_tn(a, b):
    return lax.dot_general(a, b, (((0,), (0,)), ((), ())), preferred_element_type=F32)


def halves(x):
    high = x.astype(BF16)
    return high, (x - high.astype(F32)).astype(BF16)


def silu_parts(x):
    g = 0.5 * jnp.tanh(0.5 * x) + 0.5
    value = x * g
    return value, g + value * (1.0 - g)


def ones_at(mask):
    return jnp.where(mask, 1.0, 0.0).astype(BF16)


def columns(row):
    count = row.shape[1]
    parts = [
        jnp.broadcast_to(row[:, i : i + LANES], (LANES, LANES)).T
        for i in range(0, count, LANES)
    ]
    return parts[0] if len(parts) == 1 else jnp.concatenate(parts, axis=0)


def hits_from(cols, width, period, start=0):
    parts = []
    for i in range(0, width, LANES):
        size = min(LANES, width - i)
        lane = lax.broadcasted_iota(jnp.int32, (cols.shape[0], size), 1) + i
        if period < width:
            lane = lax.rem(lane, period)
        parts.append(ones_at(cols[:, :size] == lane + start))
    return parts[0] if len(parts) == 1 else jnp.concatenate(parts, axis=1)


def hits_to(row, count):
    return ones_at(lax.broadcasted_iota(jnp.int32, (count, row.shape[1]), 0) == row)


def live_only(row, count, first=0):
    slot = lax.broadcasted_iota(jnp.int32, row.shape, 1) + first
    return jnp.where(slot < count, row, -1)


def even_on(axis):
    return lax.rem(lax.axis_index(axis), 2) == 0


def spread(index, cols, pitch):
    extra = jnp.zeros_like(index)
    block = 1
    while block * cols < 9 * cols:
        extra = extra + jnp.where(index >= block * cols, pitch - cols, 0)
        block += 1
    return index + extra


def fill(wide, blocks, pitch, first):
    for k in range(blocks.shape[0]):
        at = first + k * pitch
        cols = blocks.shape[2]
        wide[:, at : at + cols] = blocks[k]
        if cols < pitch:
            wide[:, at + cols : at + pitch] = jnp.zeros(
                (wide.shape[0], pitch - cols), wide.dtype
            )


def own_gather_kernel(send, grid, near, far, mesh_in, w_gr, rows_out, table_out, wide):
    band_rows, _, cols = grid.shape
    pitch = wide.shape[1] // band_rows
    node_count = mesh_in.shape[0]
    rim = node_count // 2
    even = even_on("lat")
    left = jnp.where(even, far[...], near[...])[rim:]
    right = jnp.where(even, near[...], far[...])[:rim]
    cycle = jnp.concatenate([left, mesh_in[...], right], axis=0)
    high, low = halves(mm(cycle, w_gr[...]))
    table_out[: 2 * node_count] = high
    table_out[2 * node_count :] = low
    fill(wide, grid, pitch, 0)
    block = 256
    width = band_rows * pitch
    for first in range(0, send.shape[2], block):
        lane = spread(send[0, :, first : first + block], cols, pitch)
        hit = hits_from(columns(lane), width, width, width)
        rows_out[first : first + block] = mm_nt(hit, wide[...]).astype(BF16)


def encode_kernel(
    send, recv, count, near, far, own, table, w_grid, w_gs,
    senders_out, slope_out, part_out, near_out, far_out, wide,
):
    band_rows, _, cols = near.shape
    pitch = wide.shape[1] // (2 * band_rows)
    cycle = table.shape[0] // 2
    half = cycle // 2
    width = band_rows * pitch
    fill(wide, near, pitch, 0)
    fill(wide, far, pitch, width)
    even_band = even_on("band")
    below = jnp.where(even_band, width, 0)
    above = jnp.where(even_band, -2 * width, -width)
    block = 256
    sums = None
    for first in range(0, send.shape[2], block):
        part_of = slice(first, first + block)
        lane = spread(send[0, :, part_of], cols, pitch)
        lane = jnp.where(
            lane < width, lane + below, jnp.where(lane < 2 * width, -1, lane + above)
        )
        hit = hits_from(columns(lane), 2 * width, 2 * width)
        raw = own[part_of] + mm_nt(hit, wide[...]).astype(BF16)
        latent, _ = silu_parts(mm(raw, w_grid[...]))
        latent = latent.astype(BF16)
        senders_out[part_of] = latent
        target = live_only(recv[0, :, part_of], count[0, 0], first)
        pre = mm(latent, w_gs[...]) + mm(
            hits_from(columns(target), 2 * cycle, cycle), table[...]
        )
        value, slope = silu_parts(pre)
        slope_out[part_of] = slope.astype(BF16)
        part = mm(hits_to(target, cycle), value.astype(BF16))
        sums = part if sums is None else sums + part
    part_out[...] = sums
    even = even_on("lat")
    near_out[...] = jnp.where(even, sums[half:], sums[:half]).astype(BF16)
    far_out[...] = jnp.where(even, sums[:half], sums[half:]).astype(BF16)


def node_kernel(part, near, far, mesh_near, mesh_far, mesh_in, w_gn, mesh_out, slope_out):
    node_count = mesh_in.shape[0]
    rim = node_count // 2
    even = even_on("lat")
    left = jnp.where(even, far[...], near[...]).astype(F32)
    right = jnp.where(even, near[...], far[...]).astype(F32)
    total = part[...] + jnp.concatenate([left, right], axis=0)
    mesh_left = jnp.where(even, mesh_far[...], mesh_near[...])[rim:]
    mesh_right = jnp.where(even, mesh_near[...], mesh_far[...])[:rim]
    cycle = jnp.concatenate([mesh_left, mesh_in[...], mesh_right], axis=0)
    value, slope = silu_parts(mm(total.astype(BF16), w_gn[...]))
    mesh_out[...] = (cycle.astype(F32) + value).astype(BF16)
    slope_out[...] = slope


def process_kernel(
    send, recv, count, near, own, far, d_out, w_ms, w_mr, w_mn,
    mesh_out, sums_out, recv_out, near_out, far_out,
):
    cycle = own.shape[0]
    node_count = cycle // 2
    rim = node_count // 2
    even_band = even_on("band")
    raw = send[0]
    flipped = jnp.where(
        raw < cycle, raw + 2 * cycle, jnp.where(raw < 2 * cycle, raw, raw - 2 * cycle)
    )
    source = jnp.where(even_band, flipped, raw)
    target = live_only(recv[0], count[0, 0])
    home = own[rim : rim + node_count]
    block = jnp.concatenate([near[...], own[...], far[...]], axis=0)
    table = jnp.concatenate(
        [*halves(mm(block, w_ms[...])), *halves(mm(home, w_mr[...]))], axis=0
    )
    from_hits = hits_from(columns(source), 6 * cycle, 3 * cycle)
    to_hits = hits_from(columns(target), 2 * node_count, node_count)
    pre = mm(from_hits, table[: 6 * cycle]) + mm(to_hits, table[6 * cycle :])
    value, slope = silu_parts(pre)
    to_rows = hits_to(target, node_count)
    gate = mm(mm(to_rows, value.astype(BF16)).astype(BF16), w_mn[...])
    gate_value, gate_slope = silu_parts(gate)
    mesh_out[...] = (home.astype(F32) + gate_value).astype(BF16)
    gate_two = (d_out[...].astype(F32) * gate_slope).astype(BF16)
    back = jnp.concatenate(halves(mm_nt(gate_two, w_mn[...])), axis=0)
    edge_slope = (mm(to_hits, back) * slope).astype(BF16)
    sums = mm(hits_to(source, 3 * cycle), edge_slope)
    recv_out[...] = mm(to_rows, edge_slope).astype(BF16)
    sums_out[...] = sums
    near_out[...] = sums[:cycle].astype(BF16)
    far_out[...] = sums[2 * cycle :].astype(BF16)


def split_store(gradient, keep, sends):
    doms, _, cols = keep.shape
    lats = sends.shape[0] // doms + 1
    me = lax.axis_index("lat")
    for dom in range(doms):
        block = [
            gradient[:, (dom * lats + i) * cols : (dom * lats + i + 1) * cols]
            for i in range(lats)
        ]
        for shift in range(lats):
            pick = block[shift]
            for i in range(1, lats):
                pick = jnp.where(me == i, block[(shift + i) % lats], pick)
            if shift == 0:
                keep[dom] = pick
            else:
                sends[(shift - 1) * doms + dom] = pick.astype(BF16)


def home_kernel(recv_sum, d_out, w_mr, home_out):
    home_out[...] = mm_nt(recv_sum[...], w_mr[...]) + d_out[...].astype(F32)


def process_grad_kernel(own, total, keep, sends):
    split_store(mm_tn(own[...], total[...]), keep, sends)


def cotangent_kernel(sums, near, far, home, w_ms, total_out, part_out, near_out, far_out):
    cycle = near.shape[0]
    half = cycle // 2
    rim = half // 2
    total = sums[cycle : 2 * cycle] + near[...].astype(F32) + far[...].astype(F32)
    total = total.astype(BF16)
    total_out[...] = total
    back = mm_nt(total, w_ms[...])
    back = jnp.concatenate(
        [back[:rim], back[rim : rim + half] + home[...], back[rim + half :]], axis=0
    )
    part_out[...] = back
    even = even_on("lat")
    near_out[...] = jnp.where(even, back[half:], back[:half]).astype(BF16)
    far_out[...] = jnp.where(even, back[:half], back[half:]).astype(BF16)


def encode_grad_kernel(
    recv, count, part, near, far, node_slope, w_gn, senders, edge_slope, keep, sends
):
    cycle = part.shape[0]
    even = even_on("lat")
    left = jnp.where(even, far[...], near[...]).astype(F32)
    right = jnp.where(even, near[...], far[...]).astype(F32)
    cot = part[...] + jnp.concatenate([left, right], axis=0)
    gate_one = (cot * node_slope[...]).astype(BF16)
    back = jnp.concatenate(halves(mm_nt(gate_one, w_gn[...])), axis=0)
    target = live_only(recv[0], count[0, 0])
    hits = hits_from(columns(target), 2 * cycle, cycle)
    slope = (mm(hits, back) * edge_slope[...].astype(F32)).astype(BF16)
    split_store(mm_tn(senders[...], slope), keep, sends)


def over_lat_kernel(*refs):
    keep, *came, keep_out, sends_out = refs
    doms = keep.shape[0]
    me = lax.axis_index("dom")
    for shift in range(doms):
        at = lax.rem(me + shift, doms)
        total = keep[at]
        for part in came:
            total = total + part[at].astype(F32)
        if shift == 0:
            keep_out[...] = total
        else:
            sends_out[shift - 1] = total.astype(BF16)


def over_dom_kernel(*refs):
    *ins, out = refs
    half = len(ins) // 2
    bands, _, rows, _ = out.shape
    for k in range(2):
        keep, *came = ins[k * half : (k + 1) * half]
        total = keep[...]
        for part in came:
            total = total + part[...].astype(F32)
        for band in range(bands):
            out[band, k] = total[band * rows : (band + 1) * rows].astype(BF16)


def over_band_kernel(shares, first_out, second_out):
    for k, out in enumerate((first_out, second_out)):
        total = shares[0, k].astype(F32)
        for band in range(1, shares.shape[0]):
            total = total + shares[band, k].astype(F32)
        out[...] = total


def call(kernel, outs, *args, scalars=(), scratch=()):
    in_specs = [
        pl.BlockSpec(memory_space=pltpu.SMEM if i in scalars else pltpu.VMEM)
        for i in range(len(args))
    ]
    return pl.pallas_call(
        kernel,
        out_shape=[jax.ShapeDtypeStruct(shape, dtype) for shape, dtype in outs],
        in_specs=in_specs,
        out_specs=[pl.BlockSpec(memory_space=pltpu.VMEM)] * len(outs),
        scratch_shapes=[pltpu.VMEM(shape, dtype) for shape, dtype in scratch],
        compiler_params=pltpu.CompilerParams(vmem_limit_bytes=16 << 20),
    )(*args)


def pairings(count, closed):
    near = [(i, i ^ 1) for i in range(count)]
    far = []
    for i in range(count):
        j = i + 1 if i % 2 else i - 1
        if closed:
            j %= count
        far.append((i, j if 0 <= j < count else i))
    return near, far


def shifted(x, axis, shift):
    count = lax.axis_size(axis)
    return lax.ppermute(x, axis, [(i, (i + shift) % count) for i in range(count)])


def on_device(
    grid_in, w_grid, w_gs, w_gr, w_gn, w_ms, w_mr, w_mn, mesh_in, d_out,
    g2m_send, g2m_recv, g2m_count, mesh_send, mesh_recv, mesh_count,
):
    latent = w_grid.shape[1]
    variables = w_grid.shape[0]
    node_count = mesh_in.shape[0]
    cycle = 2 * node_count
    bands = lax.axis_size("band")
    sectors = lax.axis_size(("dom", "lat"))
    edges = g2m_send.shape[2]
    around = ("dom", "lat")
    band_near, band_far = pairings(bands, False)
    ring_near, ring_far = pairings(sectors, True)

    grid = jnp.transpose(grid_in, (0, 2, 1))
    pitch = -(-grid.shape[2] // LANES) * LANES
    wide = (variables, grid.shape[0] * pitch)
    raw_near = lax.ppermute(grid, "band", band_near)
    raw_far = lax.ppermute(grid, "band", band_far)
    mesh_near = lax.ppermute(mesh_in, around, ring_near)
    mesh_far = lax.ppermute(mesh_in, around, ring_far)
    own_rows, table = call(
        own_gather_kernel,
        [((edges, variables), BF16), ((2 * cycle, latent), BF16)],
        g2m_send, grid, mesh_near, mesh_far, mesh_in, w_gr,
        scratch=[(wide, BF16)],
    )
    senders, edge_slope, part, to_near, to_far = call(
        encode_kernel,
        [
            ((edges, latent), BF16),
            ((edges, latent), BF16),
            ((cycle, latent), F32),
            ((node_count, latent), BF16),
            ((node_count, latent), BF16),
        ],
        g2m_send, g2m_recv, g2m_count, raw_near, raw_far, own_rows, table, w_grid, w_gs,
        scalars=(2,),
        scratch=[((variables, 2 * wide[1]), BF16)],
    )
    from_near = lax.ppermute(to_near, around, ring_near)
    from_far = lax.ppermute(to_far, around, ring_far)
    mesh_one, node_slope = call(
        node_kernel,
        [((cycle, latent), BF16), ((cycle, latent), F32)],
        part, from_near, from_far, mesh_near, mesh_far, mesh_in, w_gn,
    )
    one_near = lax.ppermute(mesh_one, "band", band_near)
    one_far = lax.ppermute(mesh_one, "band", band_far)
    mesh_out, sums, recv_sum, to_near, to_far = call(
        process_kernel,
        [
            ((node_count, latent), BF16),
            ((3 * cycle, latent), F32),
            ((node_count, latent), BF16),
            ((cycle, latent), BF16),
            ((cycle, latent), BF16),
        ],
        mesh_send, mesh_recv, mesh_count, one_near, mesh_one, one_far, d_out, w_ms, w_mr, w_mn,
        scalars=(2,),
    )
    from_near = lax.ppermute(to_near, "band", band_near)
    from_far = lax.ppermute(to_far, "band", band_far)
    (home,) = call(home_kernel, [((node_count, latent), F32)], recv_sum, d_out, w_mr)
    total, part, to_near, to_far = call(
        cotangent_kernel,
        [
            ((cycle, latent), BF16),
            ((cycle, latent), F32),
            ((node_count, latent), BF16),
            ((node_count, latent), BF16),
        ],
        sums, from_near, from_far, home, w_ms,
    )
    from_near = lax.ppermute(to_near, around, ring_near)
    from_far = lax.ppermute(to_far, around, ring_far)

    doms = lax.axis_size("dom")
    lats = lax.axis_size("lat")
    cols = latent // sectors
    halves_shape = [
        ((doms, latent, cols), F32),
        (((lats - 1) * doms, latent, cols), BF16),
    ]

    def over_lat(keep, sends):
        came = [
            shifted(sends[i * doms : (i + 1) * doms], "lat", i + 1) for i in range(lats - 1)
        ]
        keep, sends = call(
            over_lat_kernel,
            [((latent, cols), F32), ((doms - 1, latent, cols), BF16)],
            keep, *came,
        )
        return [keep] + [shifted(sends[i], "dom", i + 1) for i in range(doms - 1)]

    ms_parts = over_lat(*call(process_grad_kernel, halves_shape, mesh_one, total))
    gs_parts = over_lat(
        *call(
            encode_grad_kernel,
            halves_shape,
            g2m_recv, g2m_count, part, from_near, from_far, node_slope, w_gn, senders,
            edge_slope,
            scalars=(1,),
        )
    )
    (shares,) = call(
        over_dom_kernel,
        [((bands, 2, latent // bands, cols), BF16)],
        *gs_parts, *ms_parts,
    )
    shares = lax.all_to_all(shares, "band", 0, 0, tiled=True)
    tile = ((latent // bands, cols), F32)
    grad_gs, grad_ms = call(over_band_kernel, [tile, tile], shares)
    return mesh_out, grad_gs, grad_ms


def solution(mesh):
    flat = P(("groups", "band", "dom", "lat"), None)
    grid = P(("groups", "band"), ("dom", "lat"), None)
    count = P(("groups", "band"), ("dom", "lat"))
    placed = (grid,) + (P(),) * 7 + (flat, flat) + (grid, grid, count) * 2
    return jax.shard_map(
        on_device,
        mesh=mesh,
        in_specs=placed,
        out_specs=(flat, count, count),
        check_vma=False,
    )
```

```python
import jax
import jax.numpy as jnp
from jax import lax
from jax.experimental import pallas as pl
from jax.experimental.pallas import tpu as pltpu
from jax.sharding import PartitionSpec as P

F32 = jnp.float32
BF16 = jnp.bfloat16
LANES = 128


def mm(a, b):
    return jnp.dot(a, b, preferred_element_type=F32)


def mm_nt(a, b):
    return lax.dot_general(a, b, (((1,), (1,)), ((), ())), preferred_element_type=F32)


def mm_tn(a, b):
    return lax.dot_general(a, b, (((0,), (0,)), ((), ())), preferred_element_type=F32)


def halves(x):
    high = x.astype(BF16)
    return high, (x - high.astype(F32)).astype(BF16)


def silu_parts(x):
    g = 0.5 * jnp.tanh(0.5 * x) + 0.5
    value = x * g
    return value, g + value * (1.0 - g)


def ones_at(mask):
    return jnp.where(mask, 1.0, 0.0).astype(BF16)


def columns(row):
    count = row.shape[1]
    parts = [
        jnp.broadcast_to(row[:, i : i + LANES], (LANES, LANES)).T
        for i in range(0, count, LANES)
    ]
    return parts[0] if len(parts) == 1 else jnp.concatenate(parts, axis=0)


def hits_from(cols, width, period, start=0):
    parts = []
    for i in range(0, width, LANES):
        size = min(LANES, width - i)
        lane = lax.broadcasted_iota(jnp.int32, (cols.shape[0], size), 1) + i
        if period < width:
            lane = lax.rem(lane, period)
        parts.append(ones_at(cols[:, :size] == lane + start))
    return parts[0] if len(parts) == 1 else jnp.concatenate(parts, axis=1)


def hits_to(row, count):
    return ones_at(lax.broadcasted_iota(jnp.int32, (count, row.shape[1]), 0) == row)


def live_only(row, count, first=0):
    slot = lax.broadcasted_iota(jnp.int32, row.shape, 1) + first
    return jnp.where(slot < count, row, -1)


def even_on(axis):
    return lax.rem(lax.axis_index(axis), 2) == 0


def spread(index, blocks, cols, pitch):
    extra = jnp.zeros_like(index)
    for block in range(1, blocks):
        extra = extra + jnp.where(index >= block * cols, pitch - cols, 0)
    return index + extra


def fill(wide, blocks, pitch, first):
    cols = blocks.shape[2]
    for k in range(blocks.shape[0]):
        at = first + k * pitch
        wide[:, at : at + cols] = blocks[k]
        if cols < pitch:
            wide[:, at + cols : at + pitch] = jnp.zeros(
                (wide.shape[0], pitch - cols), wide.dtype
            )


def index_kernel(
    send, recv, count, mesh_send, mesh_recv, mesh_count, grid,
    own_out, halo_hits, recv_hits, recv_rows, from_hits, to_hits, from_rows, to_rows, wide,
):
    band_rows, _, cols = grid.shape
    pitch = wide.shape[1] // band_rows
    width = band_rows * pitch
    cycle = recv_rows.shape[0]
    node_count = to_rows.shape[0]
    even_band = even_on("band")
    fill(wide, grid, pitch, 0)
    below = jnp.where(even_band, width, 0)
    above = jnp.where(even_band, -2 * width, -width)
    block = 256
    for first in range(0, send.shape[2], block):
        part_of = slice(first, first + block)
        lane = spread(send[0, :, part_of], 3 * band_rows, cols, pitch)
        inner = (lane >= width) & (lane < 2 * width)
        index = columns(lane)
        own_hit = hits_from(index, width, width, width)
        own_out[part_of] = mm_nt(own_hit, wide[...]).astype(BF16)
        lane = jnp.where(lane < width, lane + below, jnp.where(inner, -1, lane + above))
        halo_hits[part_of] = hits_from(columns(lane), 2 * width, 2 * width)
        target = live_only(recv[0, :, part_of], count[0, 0], first)
        recv_hits[part_of] = hits_from(columns(target), 2 * cycle, cycle)
        recv_rows[:, part_of] = hits_to(target, cycle)
    raw = mesh_send[0]
    flipped = jnp.where(
        raw < cycle, raw + 2 * cycle, jnp.where(raw < 2 * cycle, raw, raw - 2 * cycle)
    )
    source = jnp.where(even_band, flipped, raw)
    target = live_only(mesh_recv[0], mesh_count[0, 0])
    from_hits[...] = hits_from(columns(source), 6 * cycle, 3 * cycle)
    to_hits[...] = hits_from(columns(target), 2 * node_count, node_count)
    from_rows[...] = hits_to(source, 3 * cycle)
    to_rows[...] = hits_to(target, node_count)


def table_kernel(near, far, mesh_in, w_gr, table_out):
    node_count = mesh_in.shape[0]
    rim = node_count // 2
    even = even_on("lat")
    left = jnp.where(even, far[...], near[...])[rim:]
    right = jnp.where(even, near[...], far[...])[:rim]
    cycle = jnp.concatenate([left, mesh_in[...], right], axis=0)
    high, low = halves(mm(cycle, w_gr[...]))
    table_out[: 2 * node_count] = high
    table_out[2 * node_count :] = low


def encode_kernel(
    near, far, halo_hits, recv_hits, recv_rows, own, table, w_grid, w_gs,
    senders_out, slope_out, part_out, near_out, far_out, wide,
):
    band_rows = near.shape[0]
    pitch = wide.shape[1] // (2 * band_rows)
    half = recv_rows.shape[0] // 2
    fill(wide, near, pitch, 0)
    fill(wide, far, pitch, band_rows * pitch)
    block = 256
    sums = None
    for first in range(0, own.shape[0], block):
        part_of = slice(first, first + block)
        raw = own[part_of] + mm_nt(halo_hits[part_of], wide[...]).astype(BF16)
        latent, _ = silu_parts(mm(raw, w_grid[...]))
        latent = latent.astype(BF16)
        senders_out[part_of] = latent
        pre = mm(latent, w_gs[...]) + mm(recv_hits[part_of], table[...])
        value, slope = silu_parts(pre)
        slope_out[part_of] = slope.astype(BF16)
        part = mm(recv_rows[:, part_of], value.astype(BF16))
        sums = part if sums is None else sums + part
    part_out[...] = sums
    even = even_on("lat")
    near_out[...] = jnp.where(even, sums[half:], sums[:half]).astype(BF16)
    far_out[...] = jnp.where(even, sums[:half], sums[half:]).astype(BF16)


def node_kernel(part, near, far, mesh_near, mesh_far, mesh_in, w_gn, mesh_out, slope_out):
    node_count = mesh_in.shape[0]
    rim = node_count // 2
    even = even_on("lat")
    left = jnp.where(even, far[...], near[...]).astype(F32)
    right = jnp.where(even, near[...], far[...]).astype(F32)
    total = part[...] + jnp.concatenate([left, right], axis=0)
    mesh_left = jnp.where(even, mesh_far[...], mesh_near[...])[rim:]
    mesh_right = jnp.where(even, mesh_near[...], mesh_far[...])[:rim]
    cycle = jnp.concatenate([mesh_left, mesh_in[...], mesh_right], axis=0)
    value, slope = silu_parts(mm(total.astype(BF16), w_gn[...]))
    mesh_out[...] = (cycle.astype(F32) + value).astype(BF16)
    slope_out[...] = slope


def process_kernel(
    from_hits, to_hits, from_rows, to_rows, near, own, far, d_out, w_ms, w_mr, w_mn,
    mesh_out, sums_out, recv_out, near_out, far_out,
):
    cycle = own.shape[0]
    node_count = cycle // 2
    rim = node_count // 2
    home = own[rim : rim + node_count]
    block = jnp.concatenate([near[...], own[...], far[...]], axis=0)
    table = jnp.concatenate(halves(mm(block, w_ms[...])), axis=0)
    recv_table = jnp.concatenate(halves(mm(home, w_mr[...])), axis=0)
    pre = mm(from_hits[...], table) + mm(to_hits[...], recv_table)
    value, slope = silu_parts(pre)
    gate = mm(mm(to_rows[...], value.astype(BF16)).astype(BF16), w_mn[...])
    gate_value, gate_slope = silu_parts(gate)
    mesh_out[...] = (home.astype(F32) + gate_value).astype(BF16)
    gate_two = (d_out[...].astype(F32) * gate_slope).astype(BF16)
    back = jnp.concatenate(halves(mm_nt(gate_two, w_mn[...])), axis=0)
    edge_slope = (mm(to_hits[...], back) * slope).astype(BF16)
    sums = mm(from_rows[...], edge_slope)
    recv_out[...] = mm(to_rows[...], edge_slope).astype(BF16)
    sums_out[...] = sums
    near_out[...] = sums[:cycle].astype(BF16)
    far_out[...] = sums[2 * cycle :].astype(BF16)


def split_store(gradient, keep, sends):
    doms, _, cols = keep.shape
    lats = sends.shape[0] // doms + 1
    me = lax.axis_index("lat")
    for dom in range(doms):
        block = [
            gradient[:, (dom * lats + i) * cols : (dom * lats + i + 1) * cols]
            for i in range(lats)
        ]
        for shift in range(lats):
            pick = block[shift]
            for i in range(1, lats):
                pick = jnp.where(me == i, block[(shift + i) % lats], pick)
            if shift == 0:
                keep[dom] = pick
            else:
                sends[(shift - 1) * doms + dom] = pick.astype(BF16)


def home_kernel(recv_sum, d_out, w_mr, home_out):
    home_out[...] = mm_nt(recv_sum[...], w_mr[...]) + d_out[...].astype(F32)


def process_grad_kernel(near, own, far, sums, after, keep, sends):
    block = jnp.concatenate([near[...], own[...], far[...]], axis=0)
    split_store(mm_tn(block, sums[...].astype(BF16)), keep, sends)


def cotangent_kernel(sums, near, far, home, w_ms, part_out, near_out, far_out):
    cycle = near.shape[0]
    half = cycle // 2
    rim = half // 2
    total = sums[cycle : 2 * cycle] + near[...].astype(F32) + far[...].astype(F32)
    back = mm_nt(total.astype(BF16), w_ms[...])
    back = jnp.concatenate(
        [back[:rim], back[rim : rim + half] + home[...], back[rim + half :]], axis=0
    )
    part_out[...] = back
    even = even_on("lat")
    near_out[...] = jnp.where(even, back[half:], back[:half]).astype(BF16)
    far_out[...] = jnp.where(even, back[:half], back[half:]).astype(BF16)


def encode_grad_kernel(
    recv_hits, part, near, far, node_slope, w_gn, senders, edge_slope, keep, sends
):
    even = even_on("lat")
    left = jnp.where(even, far[...], near[...]).astype(F32)
    right = jnp.where(even, near[...], far[...]).astype(F32)
    cot = part[...] + jnp.concatenate([left, right], axis=0)
    gate_one = (cot * node_slope[...]).astype(BF16)
    back = jnp.concatenate(halves(mm_nt(gate_one, w_gn[...])), axis=0)
    slope = (mm(recv_hits[...], back) * edge_slope[...].astype(F32)).astype(BF16)
    split_store(mm_tn(senders[...], slope), keep, sends)


def over_lat_kernel(*refs):
    keep, *came, keep_out, sends_out = refs
    doms = keep.shape[0]
    me = lax.axis_index("dom")
    for shift in range(doms):
        at = lax.rem(me + shift, doms)
        total = keep[at]
        for part in came:
            total = total + part[at].astype(F32)
        if shift == 0:
            keep_out[...] = total
        else:
            sends_out[shift - 1] = total.astype(BF16)


def over_dom_kernel(*refs):
    *ins, out = refs
    half = len(ins) // 2
    bands, _, rows, _ = out.shape
    for k in range(2):
        keep, *came = ins[k * half : (k + 1) * half]
        total = keep[...]
        for part in came:
            total = total + part[...].astype(F32)
        for band in range(bands):
            out[band, k] = total[band * rows : (band + 1) * rows].astype(BF16)


def over_band_kernel(shares, first_out, second_out):
    for k, out in enumerate((first_out, second_out)):
        total = shares[0, k].astype(F32)
        for band in range(1, shares.shape[0]):
            total = total + shares[band, k].astype(F32)
        out[...] = total


def call(kernel, outs, *args, scalars=(), scratch=()):
    in_specs = [
        pl.BlockSpec(memory_space=pltpu.SMEM if i in scalars else pltpu.VMEM)
        for i in range(len(args))
    ]
    return pl.pallas_call(
        kernel,
        out_shape=[jax.ShapeDtypeStruct(shape, dtype) for shape, dtype in outs],
        in_specs=in_specs,
        out_specs=[pl.BlockSpec(memory_space=pltpu.VMEM)] * len(outs),
        scratch_shapes=[pltpu.VMEM(shape, dtype) for shape, dtype in scratch],
        compiler_params=pltpu.CompilerParams(vmem_limit_bytes=16 << 20),
    )(*args)


def pairings(count, closed):
    near = [(i, i ^ 1) for i in range(count)]
    far = []
    for i in range(count):
        j = i + 1 if i % 2 else i - 1
        if closed:
            j %= count
        far.append((i, j if 0 <= j < count else i))
    return near, far


def shifted(x, axis, shift):
    count = lax.axis_size(axis)
    return lax.ppermute(x, axis, [(i, (i + shift) % count) for i in range(count)])


def on_device(
    grid_in, w_grid, w_gs, w_gr, w_gn, w_ms, w_mr, w_mn, mesh_in, d_out,
    g2m_send, g2m_recv, g2m_count, mesh_send, mesh_recv, mesh_count,
):
    latent = w_grid.shape[1]
    variables = w_grid.shape[0]
    node_count = mesh_in.shape[0]
    cycle = 2 * node_count
    bands = lax.axis_size("band")
    sectors = lax.axis_size(("dom", "lat"))
    edges = g2m_send.shape[2]
    around = ("dom", "lat")
    band_near, band_far = pairings(bands, False)
    ring_near, ring_far = pairings(sectors, True)

    grid = jnp.transpose(grid_in, (0, 2, 1))
    pitch = -(-grid.shape[2] // LANES) * LANES
    wide = (variables, grid.shape[0] * pitch)
    raw_far = lax.ppermute(grid, "band", band_far)
    raw_near = lax.ppermute(grid, "band", band_near)
    mesh_far = lax.ppermute(mesh_in, around, ring_far)
    mesh_near = lax.ppermute(mesh_in, around, ring_near)
    mesh_edges = mesh_send.shape[2]
    own_rows, halo_hits, recv_hits, recv_rows, from_hits, to_hits, from_rows, to_rows = call(
        index_kernel,
        [
            ((edges, variables), BF16),
            ((edges, 2 * wide[1]), BF16),
            ((edges, 2 * cycle), BF16),
            ((cycle, edges), BF16),
            ((mesh_edges, 6 * cycle), BF16),
            ((mesh_edges, 2 * node_count), BF16),
            ((3 * cycle, mesh_edges), BF16),
            ((node_count, mesh_edges), BF16),
        ],
        g2m_send, g2m_recv, g2m_count, mesh_send, mesh_recv, mesh_count, grid,
        scalars=(2, 5),
        scratch=[(wide, BF16)],
    )
    (table,) = call(
        table_kernel, [((2 * cycle, latent), BF16)], mesh_near, mesh_far, mesh_in, w_gr
    )
    senders, edge_slope, part, to_near, to_far = call(
        encode_kernel,
        [
            ((edges, latent), BF16),
            ((edges, latent), BF16),
            ((cycle, latent), F32),
            ((node_count, latent), BF16),
            ((node_count, latent), BF16),
        ],
        raw_near, raw_far, halo_hits, recv_hits, recv_rows, own_rows, table, w_grid, w_gs,
        scratch=[((variables, 2 * wide[1]), BF16)],
    )
    from_far = lax.ppermute(to_far, around, ring_far)
    from_near = lax.ppermute(to_near, around, ring_near)
    mesh_one, node_slope = call(
        node_kernel,
        [((cycle, latent), BF16), ((cycle, latent), F32)],
        part, from_near, from_far, mesh_near, mesh_far, mesh_in, w_gn,
    )
    one_far = lax.ppermute(mesh_one, "band", band_far)
    one_near = lax.ppermute(mesh_one, "band", band_near)
    mesh_out, sums, recv_sum, to_near, to_far = call(
        process_kernel,
        [
            ((node_count, latent), BF16),
            ((3 * cycle, latent), F32),
            ((node_count, latent), BF16),
            ((cycle, latent), BF16),
            ((cycle, latent), BF16),
        ],
        from_hits, to_hits, from_rows, to_rows, one_near, mesh_one, one_far, d_out,
        w_ms, w_mr, w_mn,
    )
    from_far = lax.ppermute(to_far, "band", band_far)
    from_near = lax.ppermute(to_near, "band", band_near)
    doms = lax.axis_size("dom")
    lats = lax.axis_size("lat")
    cols = latent // sectors
    halves_shape = [
        ((doms, latent, cols), F32),
        (((lats - 1) * doms, latent, cols), BF16),
    ]
    ms_halves = call(
        process_grad_kernel, halves_shape, one_near, mesh_one, one_far, sums, from_near
    )
    *ms_halves, from_far = lax.optimization_barrier((*ms_halves, from_far))
    (home,) = call(home_kernel, [((node_count, latent), F32)], recv_sum, d_out, w_mr)
    part, to_near, to_far = call(
        cotangent_kernel,
        [
            ((cycle, latent), F32),
            ((node_count, latent), BF16),
            ((node_count, latent), BF16),
        ],
        sums, from_near, from_far, home, w_ms,
    )
    from_far = lax.ppermute(to_far, around, ring_far)
    from_near = lax.ppermute(to_near, around, ring_near)

    def over_lat(keep, sends):
        came = [
            shifted(sends[i * doms : (i + 1) * doms], "lat", i + 1) for i in range(lats - 1)
        ]
        keep, sends = call(
            over_lat_kernel,
            [((latent, cols), F32), ((doms - 1, latent, cols), BF16)],
            keep, *came,
        )
        return [keep] + [shifted(sends[i], "dom", i + 1) for i in range(doms - 1)]

    ms_parts = over_lat(*ms_halves)
    gs_parts = over_lat(
        *call(
            encode_grad_kernel,
            halves_shape,
            recv_hits, part, from_near, from_far, node_slope, w_gn, senders, edge_slope,
        )
    )
    (shares,) = call(
        over_dom_kernel,
        [((bands, 2, latent // bands, cols), BF16)],
        *gs_parts, *ms_parts,
    )
    shares = lax.all_to_all(shares, "band", 0, 0, tiled=True)
    tile = ((latent // bands, cols), F32)
    grad_gs, grad_ms = call(over_band_kernel, [tile, tile], shares)
    return mesh_out, grad_gs, grad_ms


def solution(mesh):
    flat = P(("groups", "band", "dom", "lat"), None)
    grid = P(("groups", "band"), ("dom", "lat"), None)
    count = P(("groups", "band"), ("dom", "lat"))
    placed = (grid,) + (P(),) * 7 + (flat, flat) + (grid, grid, count) * 2
    return jax.shard_map(
        on_device,
        mesh=mesh,
        in_specs=placed,
        out_specs=(flat, count, count),
        check_vma=False,
    )
```

```python
import jax
import jax.numpy as jnp
from jax import lax
from jax.experimental import pallas as pl
from jax.experimental.pallas import tpu as pltpu
from jax.sharding import PartitionSpec as P

F32 = jnp.float32
BF16 = jnp.bfloat16
LANES = 128
FETCHED = 14


def mm(a, b):
    return jnp.dot(a, b, preferred_element_type=F32)


def mm_nt(a, b):
    return lax.dot_general(a, b, (((1,), (1,)), ((), ())), preferred_element_type=F32)


def mm_tn(a, b):
    return lax.dot_general(a, b, (((0,), (0,)), ((), ())), preferred_element_type=F32)


def halves(x):
    high = x.astype(BF16)
    return high, (x - high.astype(F32)).astype(BF16)


def silu_parts(x):
    g = 0.5 * jnp.tanh(0.5 * x) + 0.5
    value = x * g
    return value, g + value * (1.0 - g)


def ones_at(mask):
    return jnp.where(mask, 1.0, 0.0).astype(BF16)


def columns(row):
    count = row.shape[1]
    parts = [
        jnp.broadcast_to(row[:, i : i + LANES], (LANES, LANES)).T
        for i in range(0, count, LANES)
    ]
    return parts[0] if len(parts) == 1 else jnp.concatenate(parts, axis=0)


def hits_from(cols, width, period, start=0):
    parts = []
    for i in range(0, width, LANES):
        size = min(LANES, width - i)
        lane = lax.broadcasted_iota(jnp.int32, (cols.shape[0], size), 1) + i
        if period < width:
            lane = lax.rem(lane, period)
        parts.append(ones_at(cols[:, :size] == lane + start))
    return parts[0] if len(parts) == 1 else jnp.concatenate(parts, axis=1)


def hits_to(row, count):
    return ones_at(lax.broadcasted_iota(jnp.int32, (count, row.shape[1]), 0) == row)


def live_only(row, count, first=0):
    slot = lax.broadcasted_iota(jnp.int32, row.shape, 1) + first
    return jnp.where(slot < count, row, -1)


def even_on(axis):
    return lax.rem(lax.axis_index(axis), 2) == 0


def spread(index, blocks, cols, pitch):
    extra = jnp.zeros_like(index)
    for block in range(1, blocks):
        extra = extra + jnp.where(index >= block * cols, pitch - cols, 0)
    return index + extra


def fill(wide, blocks, pitch, first):
    cols = blocks.shape[2]
    for k in range(blocks.shape[0]):
        at = first + k * pitch
        wide[:, at : at + cols] = blocks[k]
        if cols < pitch:
            wide[:, at + cols : at + pitch] = jnp.zeros(
                (wide.shape[0], pitch - cols), wide.dtype
            )


def index_kernel(count, mesh_count, *refs):
    fetched, refs = refs[:FETCHED], refs[FETCHED:]
    kept = refs[: FETCHED - 5]
    (
        own_out, recv_hits, recv_rows, from_hits, to_hits, from_rows, to_rows
    ) = refs[FETCHED - 5 : FETCHED + 2]
    halo_hits, wide, send, recv, mesh_send, mesh_recv, grid, sems = refs[FETCHED + 2 :]
    copies = [
        pltpu.make_async_copy(source, target, sems.at[i])
        for i, (source, target) in enumerate(
            zip(fetched, (send, recv, mesh_send, mesh_recv, grid) + tuple(kept))
        )
    ]
    for copy in copies:
        copy.start()
    for copy in copies[:5]:
        copy.wait()
    band_rows, _, cols = grid.shape
    pitch = wide.shape[1] // band_rows
    width = band_rows * pitch
    cycle = recv_rows.shape[0]
    node_count = to_rows.shape[0]
    even_band = even_on("band")
    fill(wide, grid, pitch, 0)
    near_base = jnp.where(even_band, 2 * width, 0)
    far_base = jnp.where(even_band, 0, 2 * width)
    block = 256
    for first in range(0, send.shape[2], block):
        part_of = slice(first, first + block)
        index = columns(spread(send[0, :, part_of], 3 * band_rows, cols, pitch))
        own_hit = hits_from(index, width, width, width)
        own_out[part_of] = mm_nt(own_hit, wide[...]).astype(BF16)
        halo_hits[part_of, :width] = hits_from(index, width, width, near_base)
        halo_hits[part_of, width:] = hits_from(index, width, width, far_base)
        target = live_only(recv[0, :, part_of], count[0, 0], first)
        recv_hits[part_of] = hits_from(columns(target), 2 * cycle, cycle)
        recv_rows[:, part_of] = hits_to(target, cycle)
    raw = mesh_send[0]
    flipped = jnp.where(
        raw < cycle, raw + 2 * cycle, jnp.where(raw < 2 * cycle, raw, raw - 2 * cycle)
    )
    source = jnp.where(even_band, flipped, raw)
    target = live_only(mesh_recv[0], mesh_count[0, 0])
    from_hits[...] = hits_from(columns(source), 6 * cycle, 3 * cycle)
    to_hits[...] = hits_from(columns(target), 2 * node_count, node_count)
    from_rows[...] = hits_to(source, 3 * cycle)
    to_rows[...] = hits_to(target, node_count)
    for copy in copies[5:]:
        copy.wait()


def table_kernel(near, far, mesh_in, w_gr, table_out):
    node_count = mesh_in.shape[0]
    rim = node_count // 2
    even = even_on("lat")
    left = jnp.where(even, far[...], near[...])[rim:]
    right = jnp.where(even, near[...], far[...])[:rim]
    cycle = jnp.concatenate([left, mesh_in[...], right], axis=0)
    high, low = halves(mm(cycle, w_gr[...]))
    table_out[: 2 * node_count] = high
    table_out[2 * node_count :] = low


def encode_kernel(
    near, far, halo_hits, recv_hits, recv_rows, own, table, w_grid, w_gs,
    senders_out, slope_out, part_out, near_out, far_out, wide,
):
    half = recv_rows.shape[0] // 2
    width = wide.shape[1] // 2
    pitch = width // near.shape[0]
    fill(wide, near, pitch, 0)
    fill(wide, far, pitch, width)
    raw = own[...] + mm_nt(halo_hits[...], wide[...]).astype(BF16)
    latent, _ = silu_parts(mm(raw, w_grid[...]))
    latent = latent.astype(BF16)
    senders_out[...] = latent
    pre = mm(latent, w_gs[...]) + mm(recv_hits[...], table[...])
    value, slope = silu_parts(pre)
    slope_out[...] = slope.astype(BF16)
    sums = mm(recv_rows[...], value.astype(BF16))
    part_out[...] = sums
    even = even_on("lat")
    near_out[...] = jnp.where(even, sums[half:], sums[:half]).astype(BF16)
    far_out[...] = jnp.where(even, sums[:half], sums[half:]).astype(BF16)


def node_kernel(part, near, far, mesh_near, mesh_far, mesh_in, w_gn, mesh_out, slope_out):
    node_count = mesh_in.shape[0]
    rim = node_count // 2
    even = even_on("lat")
    left = jnp.where(even, far[...], near[...]).astype(F32)
    right = jnp.where(even, near[...], far[...]).astype(F32)
    total = part[...] + jnp.concatenate([left, right], axis=0)
    mesh_left = jnp.where(even, mesh_far[...], mesh_near[...])[rim:]
    mesh_right = jnp.where(even, mesh_near[...], mesh_far[...])[:rim]
    cycle = jnp.concatenate([mesh_left, mesh_in[...], mesh_right], axis=0)
    value, slope = silu_parts(mm(total.astype(BF16), w_gn[...]))
    mesh_out[...] = (cycle.astype(F32) + value).astype(BF16)
    slope_out[...] = slope


def process_kernel(
    from_hits, to_hits, from_rows, to_rows, near, own, far, d_out, w_ms, w_mr, w_mn,
    mesh_out, sums_out, recv_out, near_out, far_out,
):
    cycle = own.shape[0]
    node_count = cycle // 2
    rim = node_count // 2
    home = own[rim : rim + node_count]
    block = jnp.concatenate([near[...], own[...], far[...]], axis=0)
    table = jnp.concatenate(halves(mm(block, w_ms[...])), axis=0)
    recv_table = jnp.concatenate(halves(mm(home, w_mr[...])), axis=0)
    pre = mm(from_hits[...], table) + mm(to_hits[...], recv_table)
    value, slope = silu_parts(pre)
    gate = mm(mm(to_rows[...], value.astype(BF16)).astype(BF16), w_mn[...])
    gate_value, gate_slope = silu_parts(gate)
    mesh_out[...] = (home.astype(F32) + gate_value).astype(BF16)
    gate_two = (d_out[...].astype(F32) * gate_slope).astype(BF16)
    back = jnp.concatenate(halves(mm_nt(gate_two, w_mn[...])), axis=0)
    edge_slope = (mm(to_hits[...], back) * slope).astype(BF16)
    sums = mm(from_rows[...], edge_slope)
    recv_out[...] = mm(to_rows[...], edge_slope).astype(BF16)
    sums_out[...] = sums
    near_out[...] = sums[:cycle].astype(BF16)
    far_out[...] = sums[2 * cycle :].astype(BF16)


def split_store(gradient, keep, sends):
    doms, _, cols = keep.shape
    lats = sends.shape[0] // doms + 1
    me = lax.axis_index("lat")
    for dom in range(doms):
        block = [
            gradient[:, (dom * lats + i) * cols : (dom * lats + i + 1) * cols]
            for i in range(lats)
        ]
        for shift in range(lats):
            pick = block[shift]
            for i in range(1, lats):
                pick = jnp.where(me == i, block[(shift + i) % lats], pick)
            if shift == 0:
                keep[dom] = pick
            else:
                sends[(shift - 1) * doms + dom] = pick.astype(BF16)


def home_kernel(recv_sum, d_out, w_mr, home_out):
    home_out[...] = mm_nt(recv_sum[...], w_mr[...]) + d_out[...].astype(F32)


def process_grad_kernel(near, own, far, sums, after, keep, sends):
    block = jnp.concatenate([near[...], own[...], far[...]], axis=0)
    split_store(mm_tn(block, sums[...].astype(BF16)), keep, sends)


def cotangent_kernel(sums, near, far, home, w_ms, part_out, near_out, far_out):
    cycle = near.shape[0]
    half = cycle // 2
    rim = half // 2
    total = sums[cycle : 2 * cycle] + near[...].astype(F32) + far[...].astype(F32)
    back = mm_nt(total.astype(BF16), w_ms[...])
    back = jnp.concatenate(
        [back[:rim], back[rim : rim + half] + home[...], back[rim + half :]], axis=0
    )
    part_out[...] = back
    even = even_on("lat")
    near_out[...] = jnp.where(even, back[half:], back[:half]).astype(BF16)
    far_out[...] = jnp.where(even, back[:half], back[half:]).astype(BF16)


def encode_grad_kernel(
    recv_hits, part, near, far, node_slope, w_gn, senders, edge_slope, keep, sends
):
    even = even_on("lat")
    left = jnp.where(even, far[...], near[...]).astype(F32)
    right = jnp.where(even, near[...], far[...]).astype(F32)
    cot = part[...] + jnp.concatenate([left, right], axis=0)
    gate_one = (cot * node_slope[...]).astype(BF16)
    back = jnp.concatenate(halves(mm_nt(gate_one, w_gn[...])), axis=0)
    slope = (mm(recv_hits[...], back) * edge_slope[...].astype(F32)).astype(BF16)
    split_store(mm_tn(senders[...], slope), keep, sends)


def over_lat_kernel(*refs):
    keep, *came, keep_out, sends_out = refs
    doms = keep.shape[0]
    me = lax.axis_index("dom")
    for shift in range(doms):
        at = lax.rem(me + shift, doms)
        total = keep[at]
        for part in came:
            total = total + part[at].astype(F32)
        if shift == 0:
            keep_out[...] = total
        else:
            sends_out[shift - 1] = total.astype(BF16)


def over_dom_kernel(keep, *refs):
    *came, out = refs
    total = keep[...]
    for part in came:
        total = total + part[...].astype(F32)
    rows = out.shape[1]
    for band in range(out.shape[0]):
        out[band] = total[band * rows : (band + 1) * rows].astype(BF16)


def over_band_kernel(shares, out):
    total = shares[0].astype(F32)
    for band in range(1, shares.shape[0]):
        total = total + shares[band].astype(F32)
    out[...] = total


def tiles_kernel(keep, *refs):
    *came, out = refs
    doms, _, _ = keep.shape
    rows = out.shape[1]
    for dom in range(doms):
        total = keep[dom]
        for part in came:
            total = total + part[dom].astype(F32)
        for band in range(out.shape[0] // doms):
            out[band * doms + dom] = total[band * rows : (band + 1) * rows].astype(BF16)


def call(kernel, outs, *args, scalars=(), fetched=(), scratch=()):
    in_specs = [
        pl.BlockSpec(
            memory_space=pltpu.SMEM if i in scalars else pltpu.HBM if i in fetched else pltpu.VMEM
        )
        for i in range(len(args))
    ]
    return pl.pallas_call(
        kernel,
        out_shape=[jax.ShapeDtypeStruct(shape, dtype) for shape, dtype in outs],
        in_specs=in_specs,
        out_specs=[pl.BlockSpec(memory_space=pltpu.VMEM)] * len(outs),
        scratch_shapes=scratch,
        compiler_params=pltpu.CompilerParams(vmem_limit_bytes=16 << 20),
    )(*args)


def pairings(count, closed):
    near = [(i, i ^ 1) for i in range(count)]
    far = []
    for i in range(count):
        j = i + 1 if i % 2 else i - 1
        if closed:
            j %= count
        far.append((i, j if 0 <= j < count else i))
    return near, far


def shifted(x, axis, shift):
    count = lax.axis_size(axis)
    return lax.ppermute(x, axis, [(i, (i + shift) % count) for i in range(count)])


def on_device(
    grid_in, w_grid, w_gs, w_gr, w_gn, w_ms, w_mr, w_mn, mesh_in, d_out,
    g2m_send, g2m_recv, g2m_count, mesh_send, mesh_recv, mesh_count,
):
    latent = w_grid.shape[1]
    variables = w_grid.shape[0]
    node_count = mesh_in.shape[0]
    cycle = 2 * node_count
    bands = lax.axis_size("band")
    sectors = lax.axis_size(("dom", "lat"))
    edges = g2m_send.shape[2]
    around = ("dom", "lat")
    band_near, band_far = pairings(bands, False)
    ring_near, ring_far = pairings(sectors, True)

    grid = jnp.transpose(grid_in, (0, 2, 1))
    pitch = -(-grid.shape[2] // LANES) * LANES
    band_rows = grid.shape[0]
    width = band_rows * pitch
    raw_near = lax.ppermute(grid, "band", band_near)
    raw_far = lax.ppermute(grid, "band", band_far)
    mesh_edges = mesh_send.shape[2]
    weights = (w_grid, w_gs, w_gr, w_gn, w_ms, w_mr, w_mn, mesh_in, d_out)
    inputs = (g2m_send, g2m_recv, mesh_send, mesh_recv, grid)
    staged = call(
        index_kernel,
        [(x.shape, x.dtype) for x in weights]
        + [
            ((edges, variables), BF16),
            ((edges, 2 * cycle), BF16),
            ((cycle, edges), BF16),
            ((mesh_edges, 6 * cycle), BF16),
            ((mesh_edges, 2 * node_count), BF16),
            ((3 * cycle, mesh_edges), BF16),
            ((node_count, mesh_edges), BF16),
        ]
        + [((edges, 2 * width), BF16)],
        g2m_count, mesh_count, *inputs, *weights,
        scalars=(0, 1),
        fetched=range(2, 2 + FETCHED),
        scratch=[pltpu.VMEM((variables, width), BF16)]
        + [pltpu.VMEM(x.shape, x.dtype) for x in inputs]
        + [pltpu.SemaphoreType.DMA((FETCHED,))],
    )
    w_grid, w_gs, w_gr, w_gn, w_ms, w_mr, w_mn, mesh_in, d_out = staged[:9]
    rows, recv_hits, recv_rows, from_hits, to_hits, from_rows, to_rows = staged[9:16]
    halo_hits = staged[16]
    mesh_near = lax.ppermute(mesh_in, around, ring_near)
    mesh_far = lax.ppermute(mesh_in, around, ring_far)
    (table,) = call(
        table_kernel, [((2 * cycle, latent), BF16)], mesh_near, mesh_far, mesh_in, w_gr
    )
    senders, edge_slope, part, to_near, to_far = call(
        encode_kernel,
        [
            ((edges, latent), BF16),
            ((edges, latent), BF16),
            ((cycle, latent), F32),
            ((node_count, latent), BF16),
            ((node_count, latent), BF16),
        ],
        raw_near, raw_far, halo_hits, recv_hits, recv_rows, rows, table, w_grid, w_gs,
        scratch=[pltpu.VMEM((variables, 2 * width), BF16)],
    )
    from_near = lax.ppermute(to_near, around, ring_near)
    from_far = lax.ppermute(to_far, around, ring_far)
    mesh_one, node_slope = call(
        node_kernel,
        [((cycle, latent), BF16), ((cycle, latent), F32)],
        part, from_near, from_far, mesh_near, mesh_far, mesh_in, w_gn,
    )
    one_near = lax.ppermute(mesh_one, "band", band_near)
    one_far = lax.ppermute(mesh_one, "band", pairings(bands, True)[1])
    mesh_out, sums, recv_sum, to_near, to_far = call(
        process_kernel,
        [
            ((node_count, latent), BF16),
            ((3 * cycle, latent), F32),
            ((node_count, latent), BF16),
            ((cycle, latent), BF16),
            ((cycle, latent), BF16),
        ],
        from_hits, to_hits, from_rows, to_rows, one_near, mesh_one, one_far, d_out,
        w_ms, w_mr, w_mn,
    )
    from_near = lax.ppermute(to_near, "band", band_near)
    from_far = lax.ppermute(to_far, "band", band_far)
    doms = lax.axis_size("dom")
    lats = lax.axis_size("lat")
    cols = latent // sectors
    halves_shape = [
        ((doms, latent, cols), F32),
        (((lats - 1) * doms, latent, cols), BF16),
    ]
    ms_halves = call(
        process_grad_kernel, halves_shape, one_near, mesh_one, one_far, sums, from_near
    )
    *ms_halves, from_far = lax.optimization_barrier((*ms_halves, from_far))
    (home,) = call(home_kernel, [((node_count, latent), F32)], recv_sum, d_out, w_mr)
    part, to_near, to_far = call(
        cotangent_kernel,
        [
            ((cycle, latent), F32),
            ((node_count, latent), BF16),
            ((node_count, latent), BF16),
        ],
        sums, from_near, from_far, home, w_ms,
    )
    from_near = lax.ppermute(to_near, around, ring_near)
    from_far = lax.ppermute(to_far, around, ring_far)

    def over_lat(sends):
        return [
            shifted(sends[i * doms : (i + 1) * doms], "lat", i + 1) for i in range(lats - 1)
        ]

    rows = latent // bands
    ms_keep, ms_sends = ms_halves
    (ms_tiles,) = call(
        tiles_kernel, [((bands * doms, rows, cols), BF16)], ms_keep, *over_lat(ms_sends)
    )
    ms_tiles, from_near = lax.optimization_barrier((ms_tiles, from_near))
    grad_ms = lax.psum_scatter(ms_tiles, ("band", "dom"), scatter_dimension=0, tiled=True)
    gs_keep, gs_sends = call(
        encode_grad_kernel,
        halves_shape,
        recv_hits, part, from_near, from_far, node_slope, w_gn, senders, edge_slope,
    )
    gs_keep, gs_sends = call(
        over_lat_kernel,
        [((latent, cols), F32), ((doms - 1, latent, cols), BF16)],
        gs_keep, *over_lat(gs_sends),
    )
    gs_came = [shifted(gs_sends[i], "dom", i + 1) for i in range(doms - 1)]
    (shares,) = call(over_dom_kernel, [((bands, rows, cols), BF16)], gs_keep, *gs_came)
    shares = lax.all_to_all(shares, "band", 0, 0, tiled=True)
    (grad_gs,) = call(over_band_kernel, [((rows, cols), F32)], shares)
    return mesh_out, grad_gs, grad_ms[0].astype(F32)


def solution(mesh):
    flat = P(("groups", "band", "dom", "lat"), None)
    grid = P(("groups", "band"), ("dom", "lat"), None)
    count = P(("groups", "band"), ("dom", "lat"))
    placed = (grid,) + (P(),) * 7 + (flat, flat) + (grid, grid, count) * 2
    return jax.shard_map(
        on_device,
        mesh=mesh,
        in_specs=placed,
        out_specs=(flat, count, count),
        check_vma=False,
    )
```

```python
import jax
import jax.numpy as jnp
from jax import lax
from jax.experimental import pallas as pl
from jax.experimental.pallas import tpu as pltpu
from jax.sharding import PartitionSpec as P

F32 = jnp.float32
BF16 = jnp.bfloat16
LANES = 128
FETCHED = 14


def mm(a, b):
    return jnp.dot(a, b, preferred_element_type=F32)


def mm_nt(a, b):
    return lax.dot_general(a, b, (((1,), (1,)), ((), ())), preferred_element_type=F32)


def mm_tn(a, b):
    return lax.dot_general(a, b, (((0,), (0,)), ((), ())), preferred_element_type=F32)


def halves(x):
    high = x.astype(BF16)
    return high, (x - high.astype(F32)).astype(BF16)


def silu_parts(x):
    g = 0.5 * jnp.tanh(0.5 * x) + 0.5
    value = x * g
    return value, g + value * (1.0 - g)


def ones_at(mask):
    return jnp.where(mask, 1.0, 0.0).astype(BF16)


def columns(row):
    count = row.shape[1]
    parts = [
        jnp.broadcast_to(row[:, i : i + LANES], (LANES, LANES)).T
        for i in range(0, count, LANES)
    ]
    return parts[0] if len(parts) == 1 else jnp.concatenate(parts, axis=0)


def hits_from(cols, width, period, start=0):
    parts = []
    for i in range(0, width, LANES):
        size = min(LANES, width - i)
        lane = lax.broadcasted_iota(jnp.int32, (cols.shape[0], size), 1) + i
        if period < width:
            lane = lax.rem(lane, period)
        parts.append(ones_at(cols[:, :size] == lane + start))
    return parts[0] if len(parts) == 1 else jnp.concatenate(parts, axis=1)


def hits_to(row, count):
    return ones_at(lax.broadcasted_iota(jnp.int32, (count, row.shape[1]), 0) == row)


def live_only(row, count, first=0):
    slot = lax.broadcasted_iota(jnp.int32, row.shape, 1) + first
    return jnp.where(slot < count, row, -1)


def even_on(axis):
    return lax.rem(lax.axis_index(axis), 2) == 0


def spread(index, blocks, cols, pitch):
    extra = jnp.zeros_like(index)
    for block in range(1, blocks):
        extra = extra + jnp.where(index >= block * cols, pitch - cols, 0)
    return index + extra


def fill(wide, blocks, pitch, first):
    cols = blocks.shape[2]
    for k in range(blocks.shape[0]):
        at = first + k * pitch
        wide[:, at : at + cols] = blocks[k]
        if cols < pitch:
            wide[:, at + cols : at + pitch] = jnp.zeros(
                (wide.shape[0], pitch - cols), wide.dtype
            )


def index_kernel(count, mesh_count, *refs):
    fetched, refs = refs[:FETCHED], refs[FETCHED:]
    kept = refs[: FETCHED - 5]
    (
        own_out, recv_hits, recv_rows, from_hits, to_hits, from_rows, to_rows
    ) = refs[FETCHED - 5 : FETCHED + 2]
    halo_hits, wide, send, recv, mesh_send, mesh_recv, grid, sems = refs[FETCHED + 2 :]
    copies = [
        pltpu.make_async_copy(source, target, sems.at[i])
        for i, (source, target) in enumerate(
            zip(fetched, (send, recv, mesh_send, mesh_recv, grid) + tuple(kept))
        )
    ]
    for copy in copies:
        copy.start()
    for copy in copies[:5]:
        copy.wait()
    band_rows, _, cols = grid.shape
    pitch = wide.shape[1] // band_rows
    width = band_rows * pitch
    cycle = recv_rows.shape[0]
    node_count = to_rows.shape[0]
    even_band = even_on("band")
    fill(wide, grid, pitch, 0)
    near_base = jnp.where(even_band, 2 * width, 0)
    far_base = jnp.where(even_band, 0, 2 * width)
    block = 256
    for first in range(0, send.shape[2], block):
        part_of = slice(first, first + block)
        index = columns(spread(send[0, :, part_of], 3 * band_rows, cols, pitch))
        own_hit = hits_from(index, width, width, width)
        own_out[part_of] = mm_nt(own_hit, wide[...]).astype(BF16)
        halo_hits[part_of, :width] = hits_from(index, width, width, near_base)
        halo_hits[part_of, width:] = hits_from(index, width, width, far_base)
        target = live_only(recv[0, :, part_of], count[0, 0], first)
        recv_hits[part_of] = hits_from(columns(target), 2 * cycle, cycle)
        recv_rows[:, part_of] = hits_to(target, cycle)
    raw = mesh_send[0]
    flipped = jnp.where(
        raw < cycle, raw + 2 * cycle, jnp.where(raw < 2 * cycle, raw, raw - 2 * cycle)
    )
    source = jnp.where(even_band, flipped, raw)
    target = live_only(mesh_recv[0], mesh_count[0, 0])
    from_hits[...] = hits_from(columns(source), 6 * cycle, 3 * cycle)
    to_hits[...] = hits_from(columns(target), 2 * node_count, node_count)
    from_rows[...] = hits_to(source, 3 * cycle)
    to_rows[...] = hits_to(target, node_count)
    for copy in copies[5:]:
        copy.wait()


def table_kernel(near, far, mesh_in, w_gr, table_out):
    node_count = mesh_in.shape[0]
    rim = node_count // 2
    even = even_on("lat")
    left = jnp.where(even, far[...], near[...])[rim:]
    right = jnp.where(even, near[...], far[...])[:rim]
    cycle = jnp.concatenate([left, mesh_in[...], right], axis=0)
    high, low = halves(mm(cycle, w_gr[...]))
    table_out[: 2 * node_count] = high
    table_out[2 * node_count :] = low


def encode_kernel(
    near, far, halo_hits, recv_hits, recv_rows, own, table, w_grid, w_gs,
    senders_out, slope_out, part_out, near_out, far_out, wide,
):
    half = recv_rows.shape[0] // 2
    width = wide.shape[1] // 2
    pitch = width // near.shape[0]
    fill(wide, near, pitch, 0)
    fill(wide, far, pitch, width)
    raw = own[...] + mm_nt(halo_hits[...], wide[...]).astype(BF16)
    latent, _ = silu_parts(mm(raw, w_grid[...]))
    latent = latent.astype(BF16)
    senders_out[...] = latent
    pre = mm(latent, w_gs[...]) + mm(recv_hits[...], table[...])
    value, slope = silu_parts(pre)
    slope_out[...] = slope.astype(BF16)
    sums = mm(recv_rows[...], value.astype(BF16))
    part_out[...] = sums
    even = even_on("lat")
    near_out[...] = jnp.where(even, sums[half:], sums[:half]).astype(BF16)
    far_out[...] = jnp.where(even, sums[:half], sums[half:]).astype(BF16)


def node_kernel(part, near, far, mesh_near, mesh_far, mesh_in, w_gn, mesh_out, slope_out):
    node_count = mesh_in.shape[0]
    rim = node_count // 2
    even = even_on("lat")
    left = jnp.where(even, far[...], near[...]).astype(F32)
    right = jnp.where(even, near[...], far[...]).astype(F32)
    total = part[...] + jnp.concatenate([left, right], axis=0)
    mesh_left = jnp.where(even, mesh_far[...], mesh_near[...])[rim:]
    mesh_right = jnp.where(even, mesh_near[...], mesh_far[...])[:rim]
    cycle = jnp.concatenate([mesh_left, mesh_in[...], mesh_right], axis=0)
    value, slope = silu_parts(mm(total.astype(BF16), w_gn[...]))
    mesh_out[...] = (cycle.astype(F32) + value).astype(BF16)
    slope_out[...] = slope


def process_kernel(
    from_hits, to_hits, from_rows, to_rows, near, own, far, d_out, w_ms, w_mr, w_mn,
    mesh_out, sums_out, recv_out, near_out, far_out,
):
    cycle = own.shape[0]
    node_count = cycle // 2
    rim = node_count // 2
    home = own[rim : rim + node_count]
    block = jnp.concatenate([near[...], own[...], far[...]], axis=0)
    table = jnp.concatenate(halves(mm(block, w_ms[...])), axis=0)
    recv_table = jnp.concatenate(halves(mm(home, w_mr[...])), axis=0)
    pre = mm(from_hits[...], table) + mm(to_hits[...], recv_table)
    value, slope = silu_parts(pre)
    gate = mm(mm(to_rows[...], value.astype(BF16)).astype(BF16), w_mn[...])
    gate_value, gate_slope = silu_parts(gate)
    mesh_out[...] = (home.astype(F32) + gate_value).astype(BF16)
    gate_two = (d_out[...].astype(F32) * gate_slope).astype(BF16)
    back = jnp.concatenate(halves(mm_nt(gate_two, w_mn[...])), axis=0)
    edge_slope = (mm(to_hits[...], back) * slope).astype(BF16)
    sums = mm(from_rows[...], edge_slope)
    recv_out[...] = mm(to_rows[...], edge_slope).astype(BF16)
    sums_out[...] = sums
    near_out[...] = sums[:cycle].astype(BF16)
    far_out[...] = sums[2 * cycle :].astype(BF16)


def split_store(gradient, keep, sends):
    doms, _, cols = keep.shape
    lats = sends.shape[0] // doms + 1
    me = lax.axis_index("lat")
    for dom in range(doms):
        block = [
            gradient[:, (dom * lats + i) * cols : (dom * lats + i + 1) * cols]
            for i in range(lats)
        ]
        for shift in range(lats):
            pick = block[shift]
            for i in range(1, lats):
                pick = jnp.where(me == i, block[(shift + i) % lats], pick)
            if shift == 0:
                keep[dom] = pick
            else:
                sends[(shift - 1) * doms + dom] = pick.astype(BF16)


def home_kernel(recv_sum, d_out, w_mr, home_out):
    home_out[...] = mm_nt(recv_sum[...], w_mr[...]) + d_out[...].astype(F32)


def cotangent_kernel(sums, near, far, home, part_out, near_out, far_out):
    cycle = near.shape[0]
    half = cycle // 2
    rim = half // 2
    total = sums[cycle : 2 * cycle] + near[...].astype(F32) + far[...].astype(F32)
    part_out[...] = total
    even = even_on("lat")
    near_out[:half] = jnp.where(even, total[half:], total[:half]).astype(BF16)
    near_out[half:] = jnp.where(even, home[rim:], home[:rim]).astype(BF16)
    far_out[:half] = jnp.where(even, total[:half], total[half:]).astype(BF16)
    far_out[half:] = jnp.where(even, home[:rim], home[rim:]).astype(BF16)


def encode_grad_kernel(
    recv_hits, part, near, far, home, node_slope, w_ms, w_gn, senders, edge_slope,
    keep, sends, total_out,
):
    half = part.shape[0] // 2
    even = even_on("lat")
    left = jnp.where(even, far[...], near[...]).astype(F32)
    right = jnp.where(even, near[...], far[...]).astype(F32)
    total = part[...] + jnp.concatenate([left[:half], right[:half]], axis=0)
    total = total.astype(BF16)
    rest = jnp.concatenate([left[half:], home[...], right[half:]], axis=0)
    cot = rest + mm_nt(total, w_ms[...])
    gate_one = (cot * node_slope[...]).astype(BF16)
    back = jnp.concatenate(halves(mm_nt(gate_one, w_gn[...])), axis=0)
    slope = (mm(recv_hits[...], back) * edge_slope[...].astype(F32)).astype(BF16)
    split_store(mm_tn(senders[...], slope), keep, sends)
    doms, _, cols = total_out.shape
    lats = total.shape[1] // cols // doms
    me = lax.axis_index("lat")
    for dom in range(doms):
        pick = total[:, dom * lats * cols : (dom * lats + 1) * cols]
        for i in range(1, lats):
            at = (dom * lats + i) * cols
            pick = jnp.where(me == i, total[:, at : at + cols], pick)
        total_out[dom] = pick


def over_lat_kernel(keep, total, *refs):
    *came, keep_out, sends_out = refs
    doms, rows, _ = keep.shape
    me = lax.axis_index("dom")
    for shift in range(doms):
        at = lax.rem(me + shift, doms)
        block = keep[at]
        for part in came:
            block = block + part[at].astype(F32)
        if shift == 0:
            keep_out[...] = block
        else:
            sends_out[shift - 1, :rows] = block.astype(BF16)
            sends_out[shift - 1, rows:] = total[at]


def over_dom_kernel(keep, total, nodes, *refs):
    *came, out = refs
    bands, _, rows, _ = out.shape
    latent = keep.shape[0]
    came, came_nodes = came[: len(came) // 2], came[len(came) // 2 :]
    first = keep[...]
    second = mm_tn(nodes[...], total[lax.axis_index("dom")])
    for part, part_nodes in zip(came, came_nodes):
        first = first + part[:latent].astype(F32)
        second = second + mm_tn(part_nodes[...], part[latent:])
    for k, block in enumerate((first, second)):
        for band in range(bands):
            out[band, k] = block[band * rows : (band + 1) * rows].astype(BF16)


def over_band_kernel(shares, first_out, second_out):
    for k, out in enumerate((first_out, second_out)):
        total = shares[0, k].astype(F32)
        for band in range(1, shares.shape[0]):
            total = total + shares[band, k].astype(F32)
        out[...] = total


def call(kernel, outs, *args, scalars=(), fetched=(), scratch=()):
    in_specs = [
        pl.BlockSpec(
            memory_space=pltpu.SMEM if i in scalars else pl.ANY if i in fetched else pltpu.VMEM
        )
        for i in range(len(args))
    ]
    return pl.pallas_call(
        kernel,
        out_shape=[jax.ShapeDtypeStruct(shape, dtype) for shape, dtype in outs],
        in_specs=in_specs,
        out_specs=[pl.BlockSpec(memory_space=pltpu.VMEM)] * len(outs),
        scratch_shapes=scratch,
        compiler_params=pltpu.CompilerParams(vmem_limit_bytes=16 << 20),
    )(*args)


def ring_pairings(count):
    far = [(i, (i + 1 if i % 2 else i - 1) % count) for i in range(count)]
    return [(i, i ^ 1) for i in range(count)], far


def line_pairings(bands, doms, lats):
    far = []
    for band in range(bands):
        other = band + 1 if band % 2 else band - 1
        for dom in range(doms):
            for lat in range(lats):
                here = (band * doms + dom) * lats + lat
                if 0 <= other < bands:
                    there = (other * doms + dom) * lats + lat
                else:
                    there = (band * doms + dom) * lats + (lat ^ 1)
                far.append((here, there))
    return [(i, i ^ 1) for i in range(bands)], far


def shifted(x, axis, shift):
    count = lax.axis_size(axis)
    return lax.ppermute(x, axis, [(i, (i + shift) % count) for i in range(count)])


def on_device(
    grid_in, w_grid, w_gs, w_gr, w_gn, w_ms, w_mr, w_mn, mesh_in, d_out,
    g2m_send, g2m_recv, g2m_count, mesh_send, mesh_recv, mesh_count,
):
    latent = w_grid.shape[1]
    variables = w_grid.shape[0]
    node_count = mesh_in.shape[0]
    cycle = 2 * node_count
    bands = lax.axis_size("band")
    sectors = lax.axis_size(("dom", "lat"))
    edges = g2m_send.shape[2]
    around = ("dom", "lat")
    whole = ("band", "dom", "lat")
    band_near, band_far = line_pairings(bands, lax.axis_size("dom"), lax.axis_size("lat"))
    ring_near, ring_far = ring_pairings(sectors)

    grid = jnp.transpose(grid_in, (0, 2, 1))
    pitch = -(-grid.shape[2] // LANES) * LANES
    band_rows = grid.shape[0]
    width = band_rows * pitch
    raw_near = lax.ppermute(grid, "band", band_near)
    raw_far = lax.ppermute(grid, whole, band_far)
    mesh_edges = mesh_send.shape[2]
    weights = (w_grid, w_gs, w_gr, w_gn, w_ms, w_mr, w_mn, mesh_in, d_out)
    inputs = (g2m_send, g2m_recv, mesh_send, mesh_recv, grid)
    staged = call(
        index_kernel,
        [(x.shape, x.dtype) for x in weights]
        + [
            ((edges, variables), BF16),
            ((edges, 2 * cycle), BF16),
            ((cycle, edges), BF16),
            ((mesh_edges, 6 * cycle), BF16),
            ((mesh_edges, 2 * node_count), BF16),
            ((3 * cycle, mesh_edges), BF16),
            ((node_count, mesh_edges), BF16),
        ]
        + [((edges, 2 * width), BF16)],
        g2m_count, mesh_count, *inputs, *weights,
        scalars=(0, 1),
        fetched=range(2, 2 + FETCHED),
        scratch=[pltpu.VMEM((variables, width), BF16)]
        + [pltpu.VMEM(x.shape, x.dtype) for x in inputs]
        + [pltpu.SemaphoreType.DMA((FETCHED,))],
    )
    w_grid, w_gs, w_gr, w_gn, w_ms, w_mr, w_mn, mesh_in, d_out = staged[:9]
    rows, recv_hits, recv_rows, from_hits, to_hits, from_rows, to_rows = staged[9:16]
    halo_hits = staged[16]
    mesh_near = lax.ppermute(mesh_in, around, ring_near)
    mesh_far = lax.ppermute(mesh_in, around, ring_far)
    (table,) = call(
        table_kernel, [((2 * cycle, latent), BF16)], mesh_near, mesh_far, mesh_in, w_gr
    )
    senders, edge_slope, part, to_near, to_far = call(
        encode_kernel,
        [
            ((edges, latent), BF16),
            ((edges, latent), BF16),
            ((cycle, latent), F32),
            ((node_count, latent), BF16),
            ((node_count, latent), BF16),
        ],
        raw_near, raw_far, halo_hits, recv_hits, recv_rows, rows, table, w_grid, w_gs,
        scratch=[pltpu.VMEM((variables, 2 * width), BF16)],
    )
    from_near = lax.ppermute(to_near, around, ring_near)
    from_far = lax.ppermute(to_far, around, ring_far)
    mesh_one, node_slope = call(
        node_kernel,
        [((cycle, latent), BF16), ((cycle, latent), F32)],
        part, from_near, from_far, mesh_near, mesh_far, mesh_in, w_gn,
    )
    one_near = lax.ppermute(mesh_one, "band", band_near)
    one_far = lax.ppermute(mesh_one, whole, band_far)
    doms = lax.axis_size("dom")
    lats = lax.axis_size("lat")
    dom_nodes = [shifted(mesh_one, "dom", i + 1) for i in range(doms - 1)]
    mesh_out, sums, recv_sum, to_near, to_far = call(
        process_kernel,
        [
            ((node_count, latent), BF16),
            ((3 * cycle, latent), F32),
            ((node_count, latent), BF16),
            ((cycle, latent), BF16),
            ((cycle, latent), BF16),
        ],
        from_hits, to_hits, from_rows, to_rows, one_near, mesh_one, one_far, d_out,
        w_ms, w_mr, w_mn,
    )
    from_near = lax.ppermute(to_near, "band", band_near)
    from_far = lax.ppermute(to_far, whole, band_far)
    from_near, *dom_nodes = lax.optimization_barrier((from_near, *dom_nodes))
    (home,) = call(home_kernel, [((node_count, latent), F32)], recv_sum, d_out, w_mr)
    message = (node_count + node_count // 2, latent)
    part, to_near, to_far = call(
        cotangent_kernel,
        [((cycle, latent), F32), (message, BF16), (message, BF16)],
        sums, from_near, from_far, home,
    )
    from_near = lax.ppermute(to_near, around, ring_near)
    from_far = lax.ppermute(to_far, around, ring_far)

    cols = latent // sectors
    rows = latent // bands
    keep, sends, total = call(
        encode_grad_kernel,
        [
            ((doms, latent, cols), F32),
            (((lats - 1) * doms, latent, cols), BF16),
            ((doms, cycle, cols), BF16),
        ],
        recv_hits, part, from_near, from_far, home, node_slope, w_ms, w_gn, senders, edge_slope,
    )
    came = [shifted(sends[i * doms : (i + 1) * doms], "lat", i + 1) for i in range(lats - 1)]
    keep, sends = call(
        over_lat_kernel,
        [((latent, cols), F32), ((doms - 1, latent + cycle, cols), BF16)],
        keep, total, *came,
    )
    came = [shifted(sends[i], "dom", i + 1) for i in range(doms - 1)]
    (shares,) = call(
        over_dom_kernel,
        [((bands, 2, rows, cols), BF16)],
        keep, total, mesh_one, *came, *dom_nodes,
    )
    shares = lax.all_to_all(shares, "band", 0, 0, tiled=True)
    tile = ((rows, cols), F32)
    grad_gs, grad_ms = call(over_band_kernel, [tile, tile], shares)
    return mesh_out, grad_gs, grad_ms


def solution(mesh):
    flat = P(("groups", "band", "dom", "lat"), None)
    grid = P(("groups", "band"), ("dom", "lat"), None)
    count = P(("groups", "band"), ("dom", "lat"))
    placed = (grid,) + (P(),) * 7 + (flat, flat) + (grid, grid, count) * 2
    return jax.shard_map(
        on_device,
        mesh=mesh,
        in_specs=placed,
        out_specs=(flat, count, count),
        check_vma=False,
    )
```

```python
import jax
import jax.numpy as jnp
from jax import lax
from jax.experimental import pallas as pl
from jax.experimental.pallas import tpu as pltpu
from jax.sharding import PartitionSpec as P

F32 = jnp.float32
BF16 = jnp.bfloat16
LANES = 128
GS, GR, GN, MS, MR, MN = range(6)


def mm(a, b):
    return jnp.dot(a, b, preferred_element_type=F32)


def mm_nt(a, b):
    return lax.dot_general(a, b, (((1,), (1,)), ((), ())), preferred_element_type=F32)


def mm_tn(a, b):
    return lax.dot_general(a, b, (((0,), (0,)), ((), ())), preferred_element_type=F32)


def halves(x):
    high = x.astype(BF16)
    return high, (x - high.astype(F32)).astype(BF16)


def silu_parts(x):
    g = 0.5 * jnp.tanh(0.5 * x) + 0.5
    value = x * g
    return value, g + value * (1.0 - g)


def ones_at(mask):
    return jnp.where(mask, 1.0, 0.0).astype(BF16)


def columns(row):
    count = row.shape[1]
    parts = [
        jnp.broadcast_to(row[:, i : i + LANES], (LANES, LANES)).T
        for i in range(0, count, LANES)
    ]
    return parts[0] if len(parts) == 1 else jnp.concatenate(parts, axis=0)


def hits_from(cols, width, period, start=0):
    parts = []
    for i in range(0, width, LANES):
        size = min(LANES, width - i)
        lane = lax.broadcasted_iota(jnp.int32, (cols.shape[0], size), 1) + i
        if period < width:
            lane = lax.rem(lane, period)
        parts.append(ones_at(cols[:, :size] == lane + start))
    return parts[0] if len(parts) == 1 else jnp.concatenate(parts, axis=1)


def hits_to(row, count):
    return ones_at(lax.broadcasted_iota(jnp.int32, (count, row.shape[1]), 0) == row)


def live_only(row, count, first=0):
    slot = lax.broadcasted_iota(jnp.int32, row.shape, 1) + first
    return jnp.where(slot < count, row, -1)


def weight(stack, index):
    latent = stack.shape[1]
    return stack[index * latent : (index + 1) * latent]


def even_on(axis):
    return lax.rem(lax.axis_index(axis), 2) == 0


def spread(index, blocks, cols, pitch):
    extra = jnp.zeros_like(index)
    for block in range(1, blocks):
        extra = extra + jnp.where(index >= block * cols, pitch - cols, 0)
    return index + extra


def fill(wide, blocks, pitch, first):
    cols = blocks.shape[2]
    for k in range(blocks.shape[0]):
        at = first + k * pitch
        wide[:, at : at + cols] = blocks[k]
        if cols < pitch:
            wide[:, at + cols : at + pitch] = jnp.zeros(
                (wide.shape[0], pitch - cols), wide.dtype
            )


def index_kernel(
    count, mesh_count, indices, grid,
    own_out, recv_hits, recv_rows, from_hits, to_hits, from_rows, to_rows, halo_hits, wide,
):
    edges = recv_hits.shape[0]
    mesh_edges = to_hits.shape[0]
    send, recv, mesh_send, mesh_recv = (
        indices[0, :, first : first + size]
        for first, size in (
            (0, edges),
            (edges, edges),
            (2 * edges, mesh_edges),
            (2 * edges + mesh_edges, mesh_edges),
        )
    )
    band_rows, _, cols = grid.shape
    pitch = wide.shape[1] // band_rows
    width = band_rows * pitch
    cycle = recv_rows.shape[0]
    node_count = to_rows.shape[0]
    even_band = even_on("band")
    fill(wide, grid, pitch, 0)
    near_base = jnp.where(even_band, 2 * width, 0)
    far_base = jnp.where(even_band, 0, 2 * width)
    block = 256
    for first in range(0, edges, block):
        part_of = slice(first, first + block)
        index = columns(spread(send[:, part_of], 3 * band_rows, cols, pitch))
        own_hit = hits_from(index, width, width, width)
        own_out[part_of] = mm_nt(own_hit, wide[...]).astype(BF16)
        halo_hits[part_of, :width] = hits_from(index, width, width, near_base)
        halo_hits[part_of, width:] = hits_from(index, width, width, far_base)
        target = live_only(recv[:, part_of], count[0, 0], first)
        recv_hits[part_of] = hits_from(columns(target), 2 * cycle, cycle)
        recv_rows[:, part_of] = hits_to(target, cycle)
    raw = mesh_send
    flipped = jnp.where(
        raw < cycle, raw + 2 * cycle, jnp.where(raw < 2 * cycle, raw, raw - 2 * cycle)
    )
    source = jnp.where(even_band, flipped, raw)
    target = live_only(mesh_recv, mesh_count[0, 0])
    from_hits[...] = hits_from(columns(source), 6 * cycle, 3 * cycle)
    to_hits[...] = hits_from(columns(target), 2 * node_count, node_count)
    from_rows[...] = hits_to(source, 3 * cycle)
    to_rows[...] = hits_to(target, node_count)


def table_kernel(near, far, mesh_in, stack, table_out):
    node_count = mesh_in.shape[0]
    rim = node_count // 2
    even = even_on("lat")
    left = jnp.where(even, far[...], near[...])[rim:]
    right = jnp.where(even, near[...], far[...])[:rim]
    cycle = jnp.concatenate([left, mesh_in[...], right], axis=0)
    high, low = halves(mm(cycle, weight(stack, GR)))
    table_out[: 2 * node_count] = high
    table_out[2 * node_count :] = low


def encode_kernel(
    near, far, halo_hits, recv_hits, recv_rows, own, table, stack,
    senders_out, slope_out, part_out, near_out, far_out, wide,
):
    half = recv_rows.shape[0] // 2
    width = wide.shape[1] // 2
    pitch = width // near.shape[0]
    fill(wide, near, pitch, 0)
    fill(wide, far, pitch, width)
    raw = own[...] + mm_nt(halo_hits[...], wide[...]).astype(BF16)
    latent, _ = silu_parts(mm(raw, stack[stack.shape[0] - raw.shape[1] :]))
    latent = latent.astype(BF16)
    senders_out[...] = latent
    pre = mm(latent, weight(stack, GS)) + mm(recv_hits[...], table[...])
    value, slope = silu_parts(pre)
    slope_out[...] = slope.astype(BF16)
    sums = mm(recv_rows[...], value.astype(BF16))
    part_out[...] = sums
    even = even_on("lat")
    near_out[...] = jnp.where(even, sums[half:], sums[:half]).astype(BF16)
    far_out[...] = jnp.where(even, sums[:half], sums[half:]).astype(BF16)


def node_kernel(part, near, far, mesh_near, mesh_far, mesh_in, stack, mesh_out, slope_out):
    node_count = mesh_in.shape[0]
    rim = node_count // 2
    even = even_on("lat")
    left = jnp.where(even, far[...], near[...]).astype(F32)
    right = jnp.where(even, near[...], far[...]).astype(F32)
    total = part[...] + jnp.concatenate([left, right], axis=0)
    mesh_left = jnp.where(even, mesh_far[...], mesh_near[...])[rim:]
    mesh_right = jnp.where(even, mesh_near[...], mesh_far[...])[:rim]
    cycle = jnp.concatenate([mesh_left, mesh_in[...], mesh_right], axis=0)
    value, slope = silu_parts(mm(total.astype(BF16), weight(stack, GN)))
    mesh_out[...] = (cycle.astype(F32) + value).astype(BF16)
    slope_out[...] = slope


def process_kernel(
    from_hits, to_hits, from_rows, to_rows, near, own, far, d_out, stack,
    mesh_out, sums_out, recv_out, near_out, far_out,
):
    cycle = own.shape[0]
    node_count = cycle // 2
    rim = node_count // 2
    home = own[rim : rim + node_count]
    block = jnp.concatenate([near[...], own[...], far[...]], axis=0)
    table = jnp.concatenate(halves(mm(block, weight(stack, MS))), axis=0)
    recv_table = jnp.concatenate(halves(mm(home, weight(stack, MR))), axis=0)
    pre = mm(from_hits[...], table) + mm(to_hits[...], recv_table)
    value, slope = silu_parts(pre)
    gate = mm(mm(to_rows[...], value.astype(BF16)).astype(BF16), weight(stack, MN))
    gate_value, gate_slope = silu_parts(gate)
    mesh_out[...] = (home.astype(F32) + gate_value).astype(BF16)
    gate_two = (d_out[...].astype(F32) * gate_slope).astype(BF16)
    back = jnp.concatenate(halves(mm_nt(gate_two, weight(stack, MN))), axis=0)
    edge_slope = (mm(to_hits[...], back) * slope).astype(BF16)
    sums = mm(from_rows[...], edge_slope)
    recv_out[...] = mm(to_rows[...], edge_slope).astype(BF16)
    sums_out[...] = sums
    near_out[...] = sums[:cycle].astype(BF16)
    far_out[...] = sums[2 * cycle :].astype(BF16)


def split_store(gradient, keep, sends):
    doms, _, cols = keep.shape
    lats = sends.shape[0] // doms + 1
    me = lax.axis_index("lat")
    for dom in range(doms):
        block = [
            gradient[:, (dom * lats + i) * cols : (dom * lats + i + 1) * cols]
            for i in range(lats)
        ]
        for shift in range(lats):
            pick = block[shift]
            for i in range(1, lats):
                pick = jnp.where(me == i, block[(shift + i) % lats], pick)
            if shift == 0:
                keep[dom] = pick
            else:
                sends[(shift - 1) * doms + dom] = pick.astype(BF16)


def home_kernel(recv_sum, d_out, stack, home_out):
    home_out[...] = mm_nt(recv_sum[...], weight(stack, MR)) + d_out[...].astype(F32)


def cotangent_kernel(sums, near, far, home, part_out, near_out, far_out):
    cycle = near.shape[0]
    half = cycle // 2
    rim = half // 2
    total = sums[cycle : 2 * cycle] + near[...].astype(F32) + far[...].astype(F32)
    part_out[...] = total
    even = even_on("lat")
    near_out[:half] = jnp.where(even, total[half:], total[:half]).astype(BF16)
    near_out[half:] = jnp.where(even, home[rim:], home[:rim]).astype(BF16)
    far_out[:half] = jnp.where(even, total[:half], total[half:]).astype(BF16)
    far_out[half:] = jnp.where(even, home[:rim], home[rim:]).astype(BF16)


def encode_grad_kernel(
    recv_hits, part, near, far, home, node_slope, stack, senders, edge_slope,
    keep, sends, total_out,
):
    half = part.shape[0] // 2
    even = even_on("lat")
    left = jnp.where(even, far[...], near[...]).astype(F32)
    right = jnp.where(even, near[...], far[...]).astype(F32)
    total = part[...] + jnp.concatenate([left[:half], right[:half]], axis=0)
    total = total.astype(BF16)
    rest = jnp.concatenate([left[half:], home[...], right[half:]], axis=0)
    cot = rest + mm_nt(total, weight(stack, MS))
    gate_one = (cot * node_slope[...]).astype(BF16)
    back = jnp.concatenate(halves(mm_nt(gate_one, weight(stack, GN))), axis=0)
    slope = (mm(recv_hits[...], back) * edge_slope[...].astype(F32)).astype(BF16)
    split_store(mm_tn(senders[...], slope), keep, sends)
    doms, _, cols = total_out.shape
    lats = total.shape[1] // cols // doms
    me = lax.axis_index("lat")
    for dom in range(doms):
        pick = total[:, dom * lats * cols : (dom * lats + 1) * cols]
        for i in range(1, lats):
            at = (dom * lats + i) * cols
            pick = jnp.where(me == i, total[:, at : at + cols], pick)
        total_out[dom] = pick


def over_lat_kernel(keep, total, *refs):
    *came, keep_out, sends_out = refs
    doms, rows, _ = keep.shape
    me = lax.axis_index("dom")
    for shift in range(doms):
        at = lax.rem(me + shift, doms)
        block = keep[at]
        for part in came:
            block = block + part[at].astype(F32)
        if shift == 0:
            keep_out[...] = block
        else:
            sends_out[shift - 1, :rows] = block.astype(BF16)
            sends_out[shift - 1, rows:] = total[at]


def over_dom_kernel(keep, total, nodes, *refs):
    *came, out = refs
    bands, _, rows, _ = out.shape
    latent = keep.shape[0]
    came, came_nodes = came[: len(came) // 2], came[len(came) // 2 :]
    first = keep[...]
    second = mm_tn(nodes[...], total[lax.axis_index("dom")])
    for part, part_nodes in zip(came, came_nodes):
        first = first + part[:latent].astype(F32)
        second = second + mm_tn(part_nodes[...], part[latent:])
    for k, block in enumerate((first, second)):
        for band in range(bands):
            out[band, k] = block[band * rows : (band + 1) * rows].astype(BF16)


def over_band_kernel(shares, first_out, second_out):
    for k, out in enumerate((first_out, second_out)):
        total = shares[0, k].astype(F32)
        for band in range(1, shares.shape[0]):
            total = total + shares[band, k].astype(F32)
        out[...] = total


def call(kernel, outs, *args, scalars=(), scratch=()):
    in_specs = [
        pl.BlockSpec(memory_space=pltpu.SMEM if i in scalars else pltpu.VMEM)
        for i in range(len(args))
    ]
    return pl.pallas_call(
        kernel,
        out_shape=[jax.ShapeDtypeStruct(shape, dtype) for shape, dtype in outs],
        in_specs=in_specs,
        out_specs=[pl.BlockSpec(memory_space=pltpu.VMEM)] * len(outs),
        scratch_shapes=scratch,
        compiler_params=pltpu.CompilerParams(vmem_limit_bytes=16 << 20),
    )(*args)


def ring_pairings(count):
    far = [(i, (i + 1 if i % 2 else i - 1) % count) for i in range(count)]
    return [(i, i ^ 1) for i in range(count)], far


def line_pairings(bands, doms, lats):
    far = []
    for band in range(bands):
        other = band + 1 if band % 2 else band - 1
        for dom in range(doms):
            for lat in range(lats):
                here = (band * doms + dom) * lats + lat
                if 0 <= other < bands:
                    there = (other * doms + dom) * lats + lat
                else:
                    there = (band * doms + dom) * lats + (lat ^ 1)
                far.append((here, there))
    return [(i, i ^ 1) for i in range(bands)], far


def shifted(x, axis, shift):
    count = lax.axis_size(axis)
    return lax.ppermute(x, axis, [(i, (i + shift) % count) for i in range(count)])


def on_device(
    grid_in, w_grid, w_gs, w_gr, w_gn, w_ms, w_mr, w_mn, mesh_in, d_out,
    g2m_send, g2m_recv, g2m_count, mesh_send, mesh_recv, mesh_count,
):
    latent = w_grid.shape[1]
    variables = w_grid.shape[0]
    node_count = mesh_in.shape[0]
    cycle = 2 * node_count
    bands = lax.axis_size("band")
    sectors = lax.axis_size(("dom", "lat"))
    edges = g2m_send.shape[2]
    around = ("dom", "lat")
    whole = ("band", "dom", "lat")
    band_near, band_far = line_pairings(bands, lax.axis_size("dom"), lax.axis_size("lat"))
    ring_near, ring_far = ring_pairings(sectors)

    grid = jnp.transpose(grid_in, (0, 2, 1))
    pitch = -(-grid.shape[2] // LANES) * LANES
    band_rows = grid.shape[0]
    width = band_rows * pitch
    raw_near = lax.ppermute(grid, "band", band_near)
    raw_far = lax.ppermute(grid, whole, band_far)
    mesh_edges = mesh_send.shape[2]
    stack = jnp.concatenate([w_gs, w_gr, w_gn, w_ms, w_mr, w_mn, w_grid], axis=0)
    indices = jnp.concatenate([g2m_send, g2m_recv, mesh_send, mesh_recv], axis=2)
    rows, recv_hits, recv_rows, from_hits, to_hits, from_rows, to_rows, halo_hits = call(
        index_kernel,
        [
            ((edges, variables), BF16),
            ((edges, 2 * cycle), BF16),
            ((cycle, edges), BF16),
            ((mesh_edges, 6 * cycle), BF16),
            ((mesh_edges, 2 * node_count), BF16),
            ((3 * cycle, mesh_edges), BF16),
            ((node_count, mesh_edges), BF16),
            ((edges, 2 * width), BF16),
        ],
        g2m_count, mesh_count, indices, grid,
        scalars=(0, 1),
        scratch=[pltpu.VMEM((variables, width), BF16)],
    )
    late_mesh, rows = lax.optimization_barrier((mesh_in, rows))
    mesh_near = lax.ppermute(late_mesh, around, ring_near)
    mesh_far = lax.ppermute(late_mesh, around, ring_far)
    (table,) = call(
        table_kernel, [((2 * cycle, latent), BF16)], mesh_near, mesh_far, mesh_in, stack
    )
    senders, edge_slope, part, to_near, to_far = call(
        encode_kernel,
        [
            ((edges, latent), BF16),
            ((edges, latent), BF16),
            ((cycle, latent), F32),
            ((node_count, latent), BF16),
            ((node_count, latent), BF16),
        ],
        raw_near, raw_far, halo_hits, recv_hits, recv_rows, rows, table, stack,
        scratch=[pltpu.VMEM((variables, 2 * width), BF16)],
    )
    from_near = lax.ppermute(to_near, around, ring_near)
    from_far = lax.ppermute(to_far, around, ring_far)
    mesh_one, node_slope = call(
        node_kernel,
        [((cycle, latent), BF16), ((cycle, latent), F32)],
        part, from_near, from_far, mesh_near, mesh_far, mesh_in, stack,
    )
    one_near = lax.ppermute(mesh_one, "band", band_near)
    one_far = lax.ppermute(mesh_one, whole, band_far)
    doms = lax.axis_size("dom")
    lats = lax.axis_size("lat")
    dom_nodes = [shifted(mesh_one, "dom", i + 1) for i in range(doms - 1)]
    mesh_out, sums, recv_sum, to_near, to_far = call(
        process_kernel,
        [
            ((node_count, latent), BF16),
            ((3 * cycle, latent), F32),
            ((node_count, latent), BF16),
            ((cycle, latent), BF16),
            ((cycle, latent), BF16),
        ],
        from_hits, to_hits, from_rows, to_rows, one_near, mesh_one, one_far, d_out,
        stack,
    )
    from_near = lax.ppermute(to_near, "band", band_near)
    from_far = lax.ppermute(to_far, whole, band_far)
    from_near, *dom_nodes = lax.optimization_barrier((from_near, *dom_nodes))
    (home,) = call(home_kernel, [((node_count, latent), F32)], recv_sum, d_out, stack)
    message = (node_count + node_count // 2, latent)
    part, to_near, to_far = call(
        cotangent_kernel,
        [((cycle, latent), F32), (message, BF16), (message, BF16)],
        sums, from_near, from_far, home,
    )
    from_near = lax.ppermute(to_near, around, ring_near)
    from_far = lax.ppermute(to_far, around, ring_far)

    cols = latent // sectors
    rows = latent // bands
    keep, sends, total = call(
        encode_grad_kernel,
        [
            ((doms, latent, cols), F32),
            (((lats - 1) * doms, latent, cols), BF16),
            ((doms, cycle, cols), BF16),
        ],
        recv_hits, part, from_near, from_far, home, node_slope, stack, senders, edge_slope,
    )
    came = [shifted(sends[i * doms : (i + 1) * doms], "lat", i + 1) for i in range(lats - 1)]
    keep, sends = call(
        over_lat_kernel,
        [((latent, cols), F32), ((doms - 1, latent + cycle, cols), BF16)],
        keep, total, *came,
    )
    came = [shifted(sends[i], "dom", i + 1) for i in range(doms - 1)]
    (shares,) = call(
        over_dom_kernel,
        [((bands, 2, rows, cols), BF16)],
        keep, total, mesh_one, *came, *dom_nodes,
    )
    shares = lax.all_to_all(shares, "band", 0, 0, tiled=True)
    tile = ((rows, cols), F32)
    grad_gs, grad_ms = call(over_band_kernel, [tile, tile], shares)
    return mesh_out, grad_gs, grad_ms


def solution(mesh):
    flat = P(("groups", "band", "dom", "lat"), None)
    grid = P(("groups", "band"), ("dom", "lat"), None)
    count = P(("groups", "band"), ("dom", "lat"))
    placed = (grid,) + (P(),) * 7 + (flat, flat) + (grid, grid, count) * 2
    return jax.shard_map(
        on_device,
        mesh=mesh,
        in_specs=placed,
        out_specs=(flat, count, count),
        check_vma=False,
    )
```

```python
import jax
import jax.numpy as jnp
from jax import lax
from jax.experimental import pallas as pl
from jax.experimental.pallas import tpu as pltpu
from jax.sharding import PartitionSpec as P

F32 = jnp.float32
BF16 = jnp.bfloat16
LANES = 128
GS, GR, GN, MS, MR, MN = range(6)


def mm(a, b):
    return jnp.dot(a, b, preferred_element_type=F32)


def mm_nt(a, b):
    return lax.dot_general(a, b, (((1,), (1,)), ((), ())), preferred_element_type=F32)


def mm_tn(a, b):
    return lax.dot_general(a, b, (((0,), (0,)), ((), ())), preferred_element_type=F32)


def halves(x):
    high = x.astype(BF16)
    return high, (x - high.astype(F32)).astype(BF16)


def silu_parts(x):
    g = 0.5 * jnp.tanh(0.5 * x) + 0.5
    value = x * g
    return value, g + value * (1.0 - g)


def ones_at(mask):
    return jnp.where(mask, 1.0, 0.0).astype(BF16)


def columns(row):
    count = row.shape[1]
    parts = [
        jnp.broadcast_to(row[:, i : i + LANES], (LANES, LANES)).T
        for i in range(0, count, LANES)
    ]
    return parts[0] if len(parts) == 1 else jnp.concatenate(parts, axis=0)


def hits_from(cols, width, period, start=0):
    parts = []
    for i in range(0, width, LANES):
        size = min(LANES, width - i)
        lane = lax.broadcasted_iota(jnp.int32, (cols.shape[0], size), 1) + i
        if period < width:
            lane = lax.rem(lane, period)
        parts.append(ones_at(cols[:, :size] == lane + start))
    return parts[0] if len(parts) == 1 else jnp.concatenate(parts, axis=1)


def hits_to(row, count):
    return ones_at(lax.broadcasted_iota(jnp.int32, (count, row.shape[1]), 0) == row)


def live_only(row, count, first=0):
    slot = lax.broadcasted_iota(jnp.int32, row.shape, 1) + first
    return jnp.where(slot < count, row, -1)


def weight(stack, index):
    latent = stack.shape[1]
    return stack[index * latent : (index + 1) * latent]


def even_on(axis):
    return lax.rem(lax.axis_index(axis), 2) == 0


def spread(index, blocks, cols, pitch):
    extra = jnp.zeros_like(index)
    for block in range(1, blocks):
        extra = extra + jnp.where(index >= block * cols, pitch - cols, 0)
    return index + extra


def fill(wide, blocks, pitch, first):
    cols = blocks.shape[2]
    for k in range(blocks.shape[0]):
        at = first + k * pitch
        wide[:, at : at + cols] = blocks[k]
        if cols < pitch:
            wide[:, at + cols : at + pitch] = jnp.zeros(
                (wide.shape[0], pitch - cols), wide.dtype
            )


def index_kernel(
    count, mesh_count, indices, grid,
    own_out, recv_hits, recv_rows, from_hits, to_hits, from_rows, to_rows, halo_hits, wide,
):
    edges = recv_hits.shape[0]
    mesh_edges = to_hits.shape[0]
    send, recv, mesh_send, mesh_recv = (
        indices[0, :, first : first + size]
        for first, size in (
            (0, edges),
            (edges, edges),
            (2 * edges, mesh_edges),
            (2 * edges + mesh_edges, mesh_edges),
        )
    )
    band_rows, _, cols = grid.shape
    pitch = wide.shape[1] // band_rows
    width = band_rows * pitch
    cycle = recv_rows.shape[0]
    node_count = to_rows.shape[0]
    even_band = even_on("band")
    fill(wide, grid, pitch, 0)
    near_base = jnp.where(even_band, 2 * width, 0)
    far_base = jnp.where(even_band, 0, 2 * width)
    block = 256
    for first in range(0, edges, block):
        part_of = slice(first, first + block)
        index = columns(spread(send[:, part_of], 3 * band_rows, cols, pitch))
        own_hit = hits_from(index, width, width, width)
        own_out[part_of] = mm_nt(own_hit, wide[...]).astype(BF16)
        halo_hits[part_of, :width] = hits_from(index, width, width, near_base)
        halo_hits[part_of, width:] = hits_from(index, width, width, far_base)
        target = live_only(recv[:, part_of], count[0, 0], first)
        recv_hits[part_of] = hits_from(columns(target), 2 * cycle, cycle)
        recv_rows[:, part_of] = hits_to(target, cycle)
    raw = mesh_send
    flipped = jnp.where(
        raw < cycle, raw + 2 * cycle, jnp.where(raw < 2 * cycle, raw, raw - 2 * cycle)
    )
    source = jnp.where(even_band, flipped, raw)
    target = live_only(mesh_recv, mesh_count[0, 0])
    from_hits[...] = hits_from(columns(source), 6 * cycle, 3 * cycle)
    to_hits[...] = hits_from(columns(target), 2 * node_count, node_count)
    from_rows[...] = hits_to(source, 3 * cycle)
    to_rows[...] = hits_to(target, node_count)


def table_kernel(near, far, mesh_in, stack, table_out):
    node_count = mesh_in.shape[0]
    rim = node_count // 2
    even = even_on("lat")
    left = jnp.where(even, far[...], near[...])[rim:]
    right = jnp.where(even, near[...], far[...])[:rim]
    cycle = jnp.concatenate([left, mesh_in[...], right], axis=0)
    high, low = halves(mm(cycle, weight(stack, GR)))
    table_out[: 2 * node_count] = high
    table_out[2 * node_count :] = low


def encode_kernel(
    near, far, halo_hits, recv_hits, recv_rows, own, table, stack,
    senders_out, slope_out, part_out, near_out, far_out, wide,
):
    half = recv_rows.shape[0] // 2
    width = wide.shape[1] // 2
    pitch = width // near.shape[0]
    fill(wide, near, pitch, 0)
    fill(wide, far, pitch, width)
    raw = own[...] + mm_nt(halo_hits[...], wide[...]).astype(BF16)
    latent, _ = silu_parts(mm(raw, stack[stack.shape[0] - raw.shape[1] :]))
    latent = latent.astype(BF16)
    senders_out[...] = latent
    pre = mm(latent, weight(stack, GS)) + mm(recv_hits[...], table[...])
    value, slope = silu_parts(pre)
    slope_out[...] = slope.astype(BF16)
    sums = mm(recv_rows[...], value.astype(BF16))
    part_out[...] = sums
    even = even_on("lat")
    near_out[...] = jnp.where(even, sums[half:], sums[:half]).astype(BF16)
    far_out[...] = jnp.where(even, sums[:half], sums[half:]).astype(BF16)


def node_kernel(part, near, far, mesh_near, mesh_far, mesh_in, stack, mesh_out, slope_out):
    node_count = mesh_in.shape[0]
    rim = node_count // 2
    even = even_on("lat")
    left = jnp.where(even, far[...], near[...]).astype(F32)
    right = jnp.where(even, near[...], far[...]).astype(F32)
    total = part[...] + jnp.concatenate([left, right], axis=0)
    mesh_left = jnp.where(even, mesh_far[...], mesh_near[...])[rim:]
    mesh_right = jnp.where(even, mesh_near[...], mesh_far[...])[:rim]
    cycle = jnp.concatenate([mesh_left, mesh_in[...], mesh_right], axis=0)
    value, slope = silu_parts(mm(total.astype(BF16), weight(stack, GN)))
    mesh_out[...] = (cycle.astype(F32) + value).astype(BF16)
    slope_out[...] = slope


def process_kernel(
    from_hits, to_hits, from_rows, to_rows, near, own, far, d_out, stack,
    mesh_out, sums_out, recv_out, near_out, far_out,
):
    cycle = own.shape[0]
    node_count = cycle // 2
    rim = node_count // 2
    home = own[rim : rim + node_count]
    block = jnp.concatenate([near[...], own[...], far[...]], axis=0)
    table = jnp.concatenate(halves(mm(block, weight(stack, MS))), axis=0)
    recv_table = jnp.concatenate(halves(mm(home, weight(stack, MR))), axis=0)
    pre = mm(from_hits[...], table) + mm(to_hits[...], recv_table)
    value, slope = silu_parts(pre)
    gate = mm(mm(to_rows[...], value.astype(BF16)).astype(BF16), weight(stack, MN))
    gate_value, gate_slope = silu_parts(gate)
    mesh_out[...] = (home.astype(F32) + gate_value).astype(BF16)
    gate_two = (d_out[...].astype(F32) * gate_slope).astype(BF16)
    back = jnp.concatenate(halves(mm_nt(gate_two, weight(stack, MN))), axis=0)
    edge_slope = (mm(to_hits[...], back) * slope).astype(BF16)
    sums = mm(from_rows[...], edge_slope)
    recv_out[...] = mm(to_rows[...], edge_slope).astype(BF16)
    sums_out[...] = sums
    near_out[...] = sums[:cycle].astype(BF16)
    far_out[...] = sums[2 * cycle :].astype(BF16)


def columns_of(x, shift, doms, lats):
    cols = x.shape[1] // (doms * lats)
    me = lax.axis_index("lat")
    picked = []
    for dom in range(doms):
        block = [
            x[:, (dom * lats + i) * cols : (dom * lats + i + 1) * cols] for i in range(lats)
        ]
        pick = block[shift]
        for i in range(1, lats):
            pick = jnp.where(me == i, block[(shift + i) % lats], pick)
        picked.append(pick)
    return jnp.concatenate(picked, axis=1)


def home_kernel(recv_sum, d_out, stack, home_out):
    home_out[...] = mm_nt(recv_sum[...], weight(stack, MR)) + d_out[...].astype(F32)


def cotangent_kernel(sums, near, far, home, part_out, near_out, far_out):
    cycle = near.shape[0]
    half = cycle // 2
    rim = half // 2
    total = sums[cycle : 2 * cycle] + near[...].astype(F32) + far[...].astype(F32)
    part_out[...] = total
    even = even_on("lat")
    near_out[:half] = jnp.where(even, total[half:], total[:half]).astype(BF16)
    near_out[half:] = jnp.where(even, home[rim:], home[:rim]).astype(BF16)
    far_out[:half] = jnp.where(even, total[:half], total[half:]).astype(BF16)
    far_out[half:] = jnp.where(even, home[:rim], home[rim:]).astype(BF16)


def encode_grad_kernel(
    recv_hits, part, near, far, home, node_slope, stack, senders, edge_slope,
    sends, kept_slope, total_out,
):
    half = part.shape[0] // 2
    even = even_on("lat")
    left = jnp.where(even, far[...], near[...]).astype(F32)
    right = jnp.where(even, near[...], far[...]).astype(F32)
    total = part[...] + jnp.concatenate([left[:half], right[:half]], axis=0)
    total = total.astype(BF16)
    rest = jnp.concatenate([left[half:], home[...], right[half:]], axis=0)
    cot = rest + mm_nt(total, weight(stack, MS))
    gate_one = (cot * node_slope[...]).astype(BF16)
    back = jnp.concatenate(halves(mm_nt(gate_one, weight(stack, GN))), axis=0)
    slope = (mm(recv_hits[...], back) * edge_slope[...].astype(F32)).astype(BF16)
    doms, _, cols = total_out.shape
    lats = slope.shape[1] // cols // doms
    for shift in range(1, lats):
        gradient = mm_tn(senders[...], columns_of(slope, shift, doms, lats)).astype(BF16)
        for dom in range(doms):
            sends[(shift - 1) * doms + dom] = gradient[:, dom * cols : (dom + 1) * cols]
    kept_slope[...] = columns_of(slope, 0, doms, lats)
    kept_total = columns_of(total, 0, doms, lats)
    for dom in range(doms):
        total_out[dom] = kept_total[:, dom * cols : (dom + 1) * cols]


def kept_grad_kernel(senders, kept_slope, keep):
    gradient = mm_tn(senders[...], kept_slope[...])
    cols = keep.shape[2]
    for dom in range(keep.shape[0]):
        keep[dom] = gradient[:, dom * cols : (dom + 1) * cols]


def over_lat_kernel(keep, total, *refs):
    *came, keep_out, sends_out = refs
    doms, rows, _ = keep.shape
    me = lax.axis_index("dom")
    for shift in range(doms):
        at = lax.rem(me + shift, doms)
        block = keep[at]
        for part in came:
            block = block + part[at].astype(F32)
        if shift == 0:
            keep_out[...] = block
        else:
            sends_out[shift - 1, :rows] = block.astype(BF16)
            sends_out[shift - 1, rows:] = total[at]


def over_dom_kernel(keep, total, nodes, *refs):
    rows = keep.shape[0] // lax.axis_size("band")
    doms = lax.axis_size("dom")
    came, (own_out, *sends_out, sums) = refs[: 2 * (doms - 1)], refs[2 * (doms - 1) :]
    latent = keep.shape[0]
    came, came_nodes = came[: len(came) // 2], came[len(came) // 2 :]
    first = keep[...]
    second = mm_tn(nodes[...], total[lax.axis_index("dom")])
    for part, part_nodes in zip(came, came_nodes):
        first = first + part[:latent].astype(F32)
        second = second + mm_tn(part_nodes[...], part[latent:])
    sums[0] = first
    sums[1] = second
    me = lax.axis_index("band")
    for k in range(2):
        own_out[k] = sums[k, pl.ds(pl.multiple_of(me * rows, rows), rows)]
        for i, out in enumerate(sends_out):
            at = pl.multiple_of(lax.bitwise_xor(me, i + 1) * rows, rows)
            out[k] = sums[k, pl.ds(at, rows)].astype(BF16)


def over_band_kernel(own, *refs):
    *came, first_out, second_out = refs
    for k, out in enumerate((first_out, second_out)):
        total = own[k]
        for part in came:
            total = total + part[k].astype(F32)
        out[...] = total


def call(kernel, outs, *args, scalars=(), scratch=()):
    in_specs = [
        pl.BlockSpec(memory_space=pltpu.SMEM if i in scalars else pltpu.VMEM)
        for i in range(len(args))
    ]
    return pl.pallas_call(
        kernel,
        out_shape=[jax.ShapeDtypeStruct(shape, dtype) for shape, dtype in outs],
        in_specs=in_specs,
        out_specs=[pl.BlockSpec(memory_space=pltpu.VMEM)] * len(outs),
        scratch_shapes=scratch,
        compiler_params=pltpu.CompilerParams(vmem_limit_bytes=16 << 20),
    )(*args)


def ring_pairings(count):
    far = [(i, (i + 1 if i % 2 else i - 1) % count) for i in range(count)]
    return [(i, i ^ 1) for i in range(count)], far


def line_pairings(bands, doms, lats):
    far = []
    for band in range(bands):
        other = band + 1 if band % 2 else band - 1
        for dom in range(doms):
            for lat in range(lats):
                here = (band * doms + dom) * lats + lat
                if 0 <= other < bands:
                    there = (other * doms + dom) * lats + lat
                else:
                    there = (band * doms + dom) * lats + (lat ^ 1)
                far.append((here, there))
    return [(i, i ^ 1) for i in range(bands)], far


def shifted(x, axis, shift):
    count = lax.axis_size(axis)
    return lax.ppermute(x, axis, [(i, (i + shift) % count) for i in range(count)])


def on_device(
    grid_in, w_grid, w_gs, w_gr, w_gn, w_ms, w_mr, w_mn, mesh_in, d_out,
    g2m_send, g2m_recv, g2m_count, mesh_send, mesh_recv, mesh_count,
):
    latent = w_grid.shape[1]
    variables = w_grid.shape[0]
    node_count = mesh_in.shape[0]
    cycle = 2 * node_count
    bands = lax.axis_size("band")
    sectors = lax.axis_size(("dom", "lat"))
    edges = g2m_send.shape[2]
    around = ("dom", "lat")
    whole = ("band", "dom", "lat")
    band_near, band_far = line_pairings(bands, lax.axis_size("dom"), lax.axis_size("lat"))
    ring_near, ring_far = ring_pairings(sectors)

    grid = jnp.transpose(grid_in, (0, 2, 1))
    pitch = -(-grid.shape[2] // LANES) * LANES
    band_rows = grid.shape[0]
    width = band_rows * pitch
    raw_near = lax.ppermute(grid, "band", band_near)
    raw_far = lax.ppermute(grid, whole, band_far)
    mesh_edges = mesh_send.shape[2]
    stack = jnp.concatenate([w_gs, w_gr, w_gn, w_ms, w_mr, w_mn, w_grid], axis=0)
    indices = jnp.concatenate([g2m_send, g2m_recv, mesh_send, mesh_recv], axis=2)
    rows, recv_hits, recv_rows, from_hits, to_hits, from_rows, to_rows, halo_hits = call(
        index_kernel,
        [
            ((edges, variables), BF16),
            ((edges, 2 * cycle), BF16),
            ((cycle, edges), BF16),
            ((mesh_edges, 6 * cycle), BF16),
            ((mesh_edges, 2 * node_count), BF16),
            ((3 * cycle, mesh_edges), BF16),
            ((node_count, mesh_edges), BF16),
            ((edges, 2 * width), BF16),
        ],
        g2m_count, mesh_count, indices, grid,
        scalars=(0, 1),
        scratch=[pltpu.VMEM((variables, width), BF16)],
    )
    late_mesh, rows = lax.optimization_barrier((mesh_in, rows))
    mesh_near = lax.ppermute(late_mesh, around, ring_near)
    mesh_far = lax.ppermute(late_mesh, around, ring_far)
    (table,) = call(
        table_kernel, [((2 * cycle, latent), BF16)], mesh_near, mesh_far, mesh_in, stack
    )
    senders, edge_slope, part, to_near, to_far = call(
        encode_kernel,
        [
            ((edges, latent), BF16),
            ((edges, latent), BF16),
            ((cycle, latent), F32),
            ((node_count, latent), BF16),
            ((node_count, latent), BF16),
        ],
        raw_near, raw_far, halo_hits, recv_hits, recv_rows, rows, table, stack,
        scratch=[pltpu.VMEM((variables, 2 * width), BF16)],
    )
    from_near = lax.ppermute(to_near, around, ring_near)
    from_far = lax.ppermute(to_far, around, ring_far)
    mesh_one, node_slope = call(
        node_kernel,
        [((cycle, latent), BF16), ((cycle, latent), F32)],
        part, from_near, from_far, mesh_near, mesh_far, mesh_in, stack,
    )
    one_near = lax.ppermute(mesh_one, "band", band_near)
    one_far = lax.ppermute(mesh_one, whole, band_far)
    doms = lax.axis_size("dom")
    lats = lax.axis_size("lat")
    dom_nodes = [shifted(mesh_one, "dom", i + 1) for i in range(doms - 1)]
    mesh_out, sums, recv_sum, to_near, to_far = call(
        process_kernel,
        [
            ((node_count, latent), BF16),
            ((3 * cycle, latent), F32),
            ((node_count, latent), BF16),
            ((cycle, latent), BF16),
            ((cycle, latent), BF16),
        ],
        from_hits, to_hits, from_rows, to_rows, one_near, mesh_one, one_far, d_out,
        stack,
    )
    from_near = lax.ppermute(to_near, "band", band_near)
    from_far = lax.ppermute(to_far, whole, band_far)
    from_near, *dom_nodes = lax.optimization_barrier((from_near, *dom_nodes))
    (home,) = call(home_kernel, [((node_count, latent), F32)], recv_sum, d_out, stack)
    message = (node_count + node_count // 2, latent)
    part, to_near, to_far = call(
        cotangent_kernel,
        [((cycle, latent), F32), (message, BF16), (message, BF16)],
        sums, from_near, from_far, home,
    )
    from_near = lax.ppermute(to_near, around, ring_near)
    from_far = lax.ppermute(to_far, around, ring_far)

    cols = latent // sectors
    rows = latent // bands
    sends, kept_slope, total = call(
        encode_grad_kernel,
        [
            (((lats - 1) * doms, latent, cols), BF16),
            ((edges, doms * cols), BF16),
            ((doms, cycle, cols), BF16),
        ],
        recv_hits, part, from_near, from_far, home, node_slope, stack, senders, edge_slope,
    )
    came = [shifted(sends[i * doms : (i + 1) * doms], "lat", i + 1) for i in range(lats - 1)]
    (keep,) = call(kept_grad_kernel, [((doms, latent, cols), F32)], senders, kept_slope)
    keep, sends = call(
        over_lat_kernel,
        [((latent, cols), F32), ((doms - 1, latent + cycle, cols), BF16)],
        keep, total, *came,
    )
    came = [shifted(sends[i], "dom", i + 1) for i in range(doms - 1)]
    own, *sends = call(
        over_dom_kernel,
        [((2, rows, cols), F32)] + [((2, rows, cols), BF16)] * (bands - 1),
        keep, total, mesh_one, *came, *dom_nodes,
        scratch=[pltpu.VMEM((2, latent, cols), F32)],
    )
    came = [
        lax.ppermute(sends[i], "band", [(b, b ^ (i + 1)) for b in range(bands)])
        for i in reversed(range(bands - 1))
    ]
    tile = ((rows, cols), F32)
    grad_gs, grad_ms = call(over_band_kernel, [tile, tile], own, *came)
    return mesh_out, grad_gs, grad_ms


def solution(mesh):
    flat = P(("groups", "band", "dom", "lat"), None)
    grid = P(("groups", "band"), ("dom", "lat"), None)
    count = P(("groups", "band"), ("dom", "lat"))
    placed = (grid,) + (P(),) * 7 + (flat, flat) + (grid, grid, count) * 2
    return jax.shard_map(
        on_device,
        mesh=mesh,
        in_specs=placed,
        out_specs=(flat, count, count),
        check_vma=False,
    )
```

```python
import jax
import jax.numpy as jnp
from jax import lax
from jax.experimental import pallas as pl
from jax.experimental.pallas import tpu as pltpu
from jax.sharding import PartitionSpec as P

F32 = jnp.float32
BF16 = jnp.bfloat16
LANES = 128
GS, GR, GN, MS, MR, MN = range(6)


def mm(a, b):
    return jnp.dot(a, b, preferred_element_type=F32)


def mm_nt(a, b):
    return lax.dot_general(a, b, (((1,), (1,)), ((), ())), preferred_element_type=F32)


def mm_tn(a, b):
    return lax.dot_general(a, b, (((0,), (0,)), ((), ())), preferred_element_type=F32)


def halves(x):
    high = x.astype(BF16)
    return high, (x - high.astype(F32)).astype(BF16)


def silu_parts(x):
    g = 0.5 * jnp.tanh(0.5 * x) + 0.5
    value = x * g
    return value, g + value * (1.0 - g)


def ones_at(mask):
    return jnp.where(mask, 1.0, 0.0).astype(BF16)


def columns(row):
    count = row.shape[1]
    parts = [
        jnp.broadcast_to(row[:, i : i + LANES], (LANES, LANES)).T
        for i in range(0, count, LANES)
    ]
    return parts[0] if len(parts) == 1 else jnp.concatenate(parts, axis=0)


def hits_from(cols, width, period, start=0):
    parts = []
    for i in range(0, width, LANES):
        size = min(LANES, width - i)
        lane = lax.broadcasted_iota(jnp.int32, (cols.shape[0], size), 1) + i
        if period < width:
            lane = lax.rem(lane, period)
        parts.append(ones_at(cols[:, :size] == lane + start))
    return parts[0] if len(parts) == 1 else jnp.concatenate(parts, axis=1)


def hits_to(row, count):
    return ones_at(lax.broadcasted_iota(jnp.int32, (count, row.shape[1]), 0) == row)


def live_only(row, count, first=0):
    slot = lax.broadcasted_iota(jnp.int32, row.shape, 1) + first
    return jnp.where(slot < count, row, -1)


def weight(stack, index):
    latent = stack.shape[1]
    return stack[index * latent : (index + 1) * latent]


def even_on(axis):
    return lax.rem(lax.axis_index(axis), 2) == 0


def spread(index, blocks, cols, pitch):
    extra = jnp.zeros_like(index)
    for block in range(1, blocks):
        extra = extra + jnp.where(index >= block * cols, pitch - cols, 0)
    return index + extra


def fill(wide, blocks, pitch, first):
    cols = blocks.shape[2]
    for k in range(blocks.shape[0]):
        at = first + k * pitch
        wide[:, at : at + cols] = blocks[k]
        if cols < pitch:
            wide[:, at + cols : at + pitch] = jnp.zeros(
                (wide.shape[0], pitch - cols), wide.dtype
            )


def index_kernel(
    count, mesh_count, indices, grid,
    own_out, recv_hits, recv_rows, from_hits, to_hits, from_rows, to_rows, halo_hits, wide,
):
    edges = recv_hits.shape[0]
    mesh_edges = to_hits.shape[0]
    send, recv, mesh_send, mesh_recv = (
        indices[0, :, first : first + size]
        for first, size in (
            (0, edges),
            (edges, edges),
            (2 * edges, mesh_edges),
            (2 * edges + mesh_edges, mesh_edges),
        )
    )
    band_rows, _, cols = grid.shape
    pitch = wide.shape[1] // band_rows
    width = band_rows * pitch
    cycle = recv_rows.shape[0]
    node_count = to_rows.shape[0]
    even_band = even_on("band")
    fill(wide, grid, pitch, 0)
    near_base = jnp.where(even_band, 2 * width, 0)
    far_base = jnp.where(even_band, 0, 2 * width)
    block = 256
    for first in range(0, edges, block):
        part_of = slice(first, first + block)
        index = columns(spread(send[:, part_of], 3 * band_rows, cols, pitch))
        own_hit = hits_from(index, width, width, width)
        own_out[part_of] = mm_nt(own_hit, wide[...]).astype(BF16)
        halo_hits[part_of, :width] = hits_from(index, width, width, near_base)
        halo_hits[part_of, width:] = hits_from(index, width, width, far_base)
        target = live_only(recv[:, part_of], count[0, 0], first)
        recv_hits[part_of] = hits_from(columns(target), 2 * cycle, cycle)
        recv_rows[:, part_of] = hits_to(target, cycle)
    raw = mesh_send
    flipped = jnp.where(
        raw < cycle, raw + 2 * cycle, jnp.where(raw < 2 * cycle, raw, raw - 2 * cycle)
    )
    source = jnp.where(even_band, flipped, raw)
    target = live_only(mesh_recv, mesh_count[0, 0])
    from_hits[...] = hits_from(columns(source), 6 * cycle, 3 * cycle)
    to_hits[...] = hits_from(columns(target), 2 * node_count, node_count)
    from_rows[...] = hits_to(source, 3 * cycle)
    to_rows[...] = hits_to(target, node_count)


def table_kernel(near, far, mesh_in, stack, table_out):
    node_count = mesh_in.shape[0]
    rim = node_count // 2
    even = even_on("lat")
    left = jnp.where(even, far[...], near[...])[rim:]
    right = jnp.where(even, near[...], far[...])[:rim]
    cycle = jnp.concatenate([left, mesh_in[...], right], axis=0)
    high, low = halves(mm(cycle, weight(stack, GR)))
    table_out[: 2 * node_count] = high
    table_out[2 * node_count :] = low


def encode_kernel(
    near, far, halo_hits, recv_hits, recv_rows, own, table, stack,
    senders_out, slope_out, part_out, far_out, near_out, wide,
):
    half = recv_rows.shape[0] // 2
    width = wide.shape[1] // 2
    pitch = width // near.shape[0]
    fill(wide, near, pitch, 0)
    fill(wide, far, pitch, width)
    raw = own[...] + mm_nt(halo_hits[...], wide[...]).astype(BF16)
    latent, _ = silu_parts(mm(raw, stack[stack.shape[0] - raw.shape[1] :]))
    latent = latent.astype(BF16)
    senders_out[...] = latent
    pre = mm(latent, weight(stack, GS)) + mm(recv_hits[...], table[...])
    value, slope = silu_parts(pre)
    slope_out[...] = slope.astype(BF16)
    sums = mm(recv_rows[...], value.astype(BF16))
    part_out[...] = sums
    even = even_on("lat")
    near_out[...] = jnp.where(even, sums[half:], sums[:half]).astype(BF16)
    far_out[...] = jnp.where(even, sums[:half], sums[half:]).astype(BF16)


def node_kernel(part, far, near, mesh_near, mesh_far, mesh_in, stack, mesh_out, slope_out):
    node_count = mesh_in.shape[0]
    rim = node_count // 2
    even = even_on("lat")
    left = jnp.where(even, far[...], near[...]).astype(F32)
    right = jnp.where(even, near[...], far[...]).astype(F32)
    total = part[...] + jnp.concatenate([left, right], axis=0)
    mesh_left = jnp.where(even, mesh_far[...], mesh_near[...])[rim:]
    mesh_right = jnp.where(even, mesh_near[...], mesh_far[...])[:rim]
    cycle = jnp.concatenate([mesh_left, mesh_in[...], mesh_right], axis=0)
    value, slope = silu_parts(mm(total.astype(BF16), weight(stack, GN)))
    mesh_out[...] = (cycle.astype(F32) + value).astype(BF16)
    slope_out[...] = slope


def process_kernel(
    from_hits, to_hits, from_rows, to_rows, near, own, far, d_out, stack,
    mesh_out, sums_out, recv_out, near_out, far_out,
):
    cycle = own.shape[0]
    node_count = cycle // 2
    rim = node_count // 2
    home = own[rim : rim + node_count]
    block = jnp.concatenate([near[...], own[...], far[...]], axis=0)
    table = jnp.concatenate(halves(mm(block, weight(stack, MS))), axis=0)
    recv_table = jnp.concatenate(halves(mm(home, weight(stack, MR))), axis=0)
    pre = mm(from_hits[...], table) + mm(to_hits[...], recv_table)
    value, slope = silu_parts(pre)
    gate = mm(mm(to_rows[...], value.astype(BF16)).astype(BF16), weight(stack, MN))
    gate_value, gate_slope = silu_parts(gate)
    mesh_out[...] = (home.astype(F32) + gate_value).astype(BF16)
    gate_two = (d_out[...].astype(F32) * gate_slope).astype(BF16)
    back = jnp.concatenate(halves(mm_nt(gate_two, weight(stack, MN))), axis=0)
    edge_slope = (mm(to_hits[...], back) * slope).astype(BF16)
    sums = mm(from_rows[...], edge_slope)
    recv_out[...] = mm(to_rows[...], edge_slope).astype(BF16)
    sums_out[...] = sums
    near_out[...] = sums[:cycle].astype(BF16)
    far_out[...] = sums[2 * cycle :].astype(BF16)


def block_of(x, dom_shift, lat_shift, doms, lats):
    cols = x.shape[1] // (doms * lats)
    dom = lax.rem(lax.axis_index("dom") + dom_shift, doms)
    index = dom * lats + lax.rem(lax.axis_index("lat") + lat_shift, lats)
    pick = x[:, :cols]
    for i in range(1, doms * lats):
        pick = jnp.where(index == i, x[:, i * cols : (i + 1) * cols], pick)
    return pick


def home_kernel(recv_sum, d_out, stack, senders, home_out, turned_out):
    home_out[...] = mm_nt(recv_sum[...], weight(stack, MR)) + d_out[...].astype(F32)
    turned_out[...] = senders[...].T


def cotangent_kernel(sums, near, far, home, part_out, far_out, near_out):
    cycle = near.shape[0]
    half = cycle // 2
    rim = half // 2
    total = sums[cycle : 2 * cycle] + near[...].astype(F32) + far[...].astype(F32)
    part_out[...] = total
    even = even_on("lat")
    near_out[:half] = jnp.where(even, total[half:], total[:half]).astype(BF16)
    near_out[half:] = jnp.where(even, home[rim:], home[:rim]).astype(BF16)
    far_out[:half] = jnp.where(even, total[:half], total[half:]).astype(BF16)
    far_out[half:] = jnp.where(even, home[:rim], home[rim:]).astype(BF16)


def encode_grad_kernel(
    recv_hits, part, far, near, home, node_slope, stack, senders, edge_slope,
    sends, slope_out, total_out,
):
    half = part.shape[0] // 2
    even = even_on("lat")
    left = jnp.where(even, far[...], near[...]).astype(F32)
    right = jnp.where(even, near[...], far[...]).astype(F32)
    total = part[...] + jnp.concatenate([left[:half], right[:half]], axis=0)
    total = total.astype(BF16)
    rest = jnp.concatenate([left[half:], home[...], right[half:]], axis=0)
    cot = rest + mm_nt(total, weight(stack, MS))
    gate_one = (cot * node_slope[...]).astype(BF16)
    back = jnp.concatenate(halves(mm_nt(gate_one, weight(stack, GN))), axis=0)
    slope = (mm(recv_hits[...], back) * edge_slope[...].astype(F32)).astype(BF16)
    slope_out[...] = slope
    lats = sends.shape[0] + 1
    doms = sends.shape[1] + 1
    for i in range(1, lats):
        for j in range(1, doms):
            block = mm(senders[...], block_of(slope, j, i, doms, lats))
            sends[i - 1, j - 1] = block.astype(BF16)
    for j in range(doms):
        total_out[j] = block_of(total, j, 0, doms, lats)


def other_doms_kernel(senders, slope, total, *refs):
    *came, sends = refs
    lats = len(came) + 1
    doms = sends.shape[0] + 1
    rows = senders.shape[0]
    for j in range(1, doms):
        block = mm(senders[...], block_of(slope[...], j, 0, doms, lats))
        for part in came:
            block = block + part[j - 1].astype(F32)
        sends[j - 1, :rows] = block.astype(BF16)
        sends[j - 1, rows:] = total[j]


def other_lats_kernel(senders, slope, after, sends):
    lats = sends.shape[0] + 1
    doms = slope.shape[1] // sends.shape[2] // lats
    for i in range(1, lats):
        block = mm(senders[...], block_of(slope[...], 0, i, doms, lats))
        sends[i - 1] = block.astype(BF16)


def own_block_kernel(senders, slope, total, nodes, *refs):
    *came, out = refs
    lats = len(came) + 1
    doms = slope.shape[1] // out.shape[2] // lats
    block = mm(senders[...], block_of(slope[...], 0, 0, doms, lats))
    for part in came:
        block = block + part[...].astype(F32)
    out[0] = block
    out[1] = mm_tn(nodes[...], total[0])


def over_dom_kernel(kept, *refs):
    rows = kept.shape[1] // lax.axis_size("band")
    doms = lax.axis_size("dom")
    came, (own_out, *sends_out, sums) = refs[: 2 * (doms - 1)], refs[2 * (doms - 1) :]
    latent = kept.shape[1]
    came, came_nodes = came[: len(came) // 2], came[len(came) // 2 :]
    first, second = kept[0], kept[1]
    for part, part_nodes in zip(came, came_nodes):
        first = first + part[:latent].astype(F32)
        second = second + mm_tn(part_nodes[...], part[latent:])
    sums[0] = first
    sums[1] = second
    me = lax.axis_index("band")
    for k in range(2):
        own_out[k] = sums[k, pl.ds(pl.multiple_of(me * rows, rows), rows)]
        for i, out in enumerate(sends_out):
            at = pl.multiple_of(lax.bitwise_xor(me, i + 1) * rows, rows)
            out[k] = sums[k, pl.ds(at, rows)].astype(BF16)


def over_band_kernel(own, *refs):
    *came, first_out, second_out = refs
    for k, out in enumerate((first_out, second_out)):
        total = own[k]
        for part in came:
            total = total + part[k].astype(F32)
        out[...] = total


def call(kernel, outs, *args, scalars=(), scratch=()):
    in_specs = [
        pl.BlockSpec(memory_space=pltpu.SMEM if i in scalars else pltpu.VMEM)
        for i in range(len(args))
    ]
    return pl.pallas_call(
        kernel,
        out_shape=[jax.ShapeDtypeStruct(shape, dtype) for shape, dtype in outs],
        in_specs=in_specs,
        out_specs=[pl.BlockSpec(memory_space=pltpu.VMEM)] * len(outs),
        scratch_shapes=scratch,
        compiler_params=pltpu.CompilerParams(vmem_limit_bytes=16 << 20),
    )(*args)


def ring_pairings(count):
    far = [(i, (i + 1 if i % 2 else i - 1) % count) for i in range(count)]
    return [(i, i ^ 1) for i in range(count)], far


def line_pairings(bands, doms, lats):
    far = []
    for band in range(bands):
        other = band + 1 if band % 2 else band - 1
        for dom in range(doms):
            for lat in range(lats):
                here = (band * doms + dom) * lats + lat
                if 0 <= other < bands:
                    there = (other * doms + dom) * lats + lat
                else:
                    there = (band * doms + dom) * lats + (lat ^ 1)
                far.append((here, there))
    return [(i, i ^ 1) for i in range(bands)], far


def shifted(x, axis, shift):
    count = lax.axis_size(axis)
    return lax.ppermute(x, axis, [(i, (i + shift) % count) for i in range(count)])


def on_device(
    grid_in, w_grid, w_gs, w_gr, w_gn, w_ms, w_mr, w_mn, mesh_in, d_out,
    g2m_send, g2m_recv, g2m_count, mesh_send, mesh_recv, mesh_count,
):
    latent = w_grid.shape[1]
    variables = w_grid.shape[0]
    node_count = mesh_in.shape[0]
    cycle = 2 * node_count
    bands = lax.axis_size("band")
    sectors = lax.axis_size(("dom", "lat"))
    edges = g2m_send.shape[2]
    around = ("dom", "lat")
    whole = ("band", "dom", "lat")
    band_near, band_far = line_pairings(bands, lax.axis_size("dom"), lax.axis_size("lat"))
    ring_near, ring_far = ring_pairings(sectors)

    grid = jnp.transpose(grid_in, (0, 2, 1))
    pitch = -(-grid.shape[2] // LANES) * LANES
    band_rows = grid.shape[0]
    width = band_rows * pitch
    raw_near = lax.ppermute(grid, "band", band_near)
    raw_far = lax.ppermute(grid, whole, band_far)
    mesh_edges = mesh_send.shape[2]
    stack = jnp.concatenate([w_gs, w_gr, w_gn, w_ms, w_mr, w_mn, w_grid], axis=0)
    indices = jnp.concatenate([g2m_send, g2m_recv, mesh_send, mesh_recv], axis=2)
    rows, recv_hits, recv_rows, from_hits, to_hits, from_rows, to_rows, halo_hits = call(
        index_kernel,
        [
            ((edges, variables), BF16),
            ((edges, 2 * cycle), BF16),
            ((cycle, edges), BF16),
            ((mesh_edges, 6 * cycle), BF16),
            ((mesh_edges, 2 * node_count), BF16),
            ((3 * cycle, mesh_edges), BF16),
            ((node_count, mesh_edges), BF16),
            ((edges, 2 * width), BF16),
        ],
        g2m_count, mesh_count, indices, grid,
        scalars=(0, 1),
        scratch=[pltpu.VMEM((variables, width), BF16)],
    )
    late_mesh, rows = lax.optimization_barrier((mesh_in, rows))
    mesh_near = lax.ppermute(late_mesh, around, ring_near)
    mesh_far = lax.ppermute(late_mesh, around, ring_far)
    (table,) = call(
        table_kernel, [((2 * cycle, latent), BF16)], mesh_near, mesh_far, mesh_in, stack
    )
    senders, edge_slope, part, to_far, to_near = call(
        encode_kernel,
        [
            ((edges, latent), BF16),
            ((edges, latent), BF16),
            ((cycle, latent), F32),
            ((node_count, latent), BF16),
            ((node_count, latent), BF16),
        ],
        raw_near, raw_far, halo_hits, recv_hits, recv_rows, rows, table, stack,
        scratch=[pltpu.VMEM((variables, 2 * width), BF16)],
    )
    from_far = lax.ppermute(to_far, around, ring_far)
    from_near = lax.ppermute(to_near, around, ring_near)
    mesh_one, node_slope = call(
        node_kernel,
        [((cycle, latent), BF16), ((cycle, latent), F32)],
        part, from_far, from_near, mesh_near, mesh_far, mesh_in, stack,
    )
    one_near = lax.ppermute(mesh_one, "band", band_near)
    one_far = lax.ppermute(mesh_one, whole, band_far)
    doms = lax.axis_size("dom")
    lats = lax.axis_size("lat")
    dom_nodes = [shifted(mesh_one, "dom", i + 1) for i in range(doms - 1)]
    mesh_out, sums, recv_sum, to_near, to_far = call(
        process_kernel,
        [
            ((node_count, latent), BF16),
            ((3 * cycle, latent), F32),
            ((node_count, latent), BF16),
            ((cycle, latent), BF16),
            ((cycle, latent), BF16),
        ],
        from_hits, to_hits, from_rows, to_rows, one_near, mesh_one, one_far, d_out,
        stack,
    )
    from_near = lax.ppermute(to_near, "band", band_near)
    from_far = lax.ppermute(to_far, whole, band_far)
    from_near, *dom_nodes = lax.optimization_barrier((from_near, *dom_nodes))
    home, senders = call(
        home_kernel,
        [((node_count, latent), F32), ((latent, edges), BF16)],
        recv_sum, d_out, stack, senders,
    )
    message = (node_count + node_count // 2, latent)
    part, to_far, to_near = call(
        cotangent_kernel,
        [((cycle, latent), F32), (message, BF16), (message, BF16)],
        sums, from_near, from_far, home,
    )
    from_far = lax.ppermute(to_far, around, ring_far)
    from_near = lax.ppermute(to_near, around, ring_near)

    cols = latent // sectors
    rows = latent // bands
    sends, slope, total = call(
        encode_grad_kernel,
        [
            ((lats - 1, doms - 1, latent, cols), BF16),
            ((edges, latent), BF16),
            ((doms, cycle, cols), BF16),
        ],
        recv_hits, part, from_far, from_near, home, node_slope, stack, senders, edge_slope,
    )
    came = [shifted(sends[i], "lat", i + 1) for i in range(lats - 1)]
    (sends,) = call(
        other_doms_kernel,
        [((doms - 1, latent + cycle, cols), BF16)],
        senders, slope, total, *came,
    )
    other_doms = [shifted(sends[i], "dom", i + 1) for i in range(doms - 1)]
    (sends,) = call(
        other_lats_kernel, [((lats - 1, latent, cols), BF16)], senders, slope, sends
    )
    came = [shifted(sends[i], "lat", i + 1) for i in range(lats - 1)]
    (kept,) = call(
        own_block_kernel,
        [((2, latent, cols), F32)],
        senders, slope, total, mesh_one, *came,
    )
    own, *sends = call(
        over_dom_kernel,
        [((2, rows, cols), F32)] + [((2, rows, cols), BF16)] * (bands - 1),
        kept, *other_doms, *dom_nodes,
        scratch=[pltpu.VMEM((2, latent, cols), F32)],
    )
    came = [
        lax.ppermute(sends[i], "band", [(b, b ^ (i + 1)) for b in range(bands)])
        for i in reversed(range(bands - 1))
    ]
    tile = ((rows, cols), F32)
    grad_gs, grad_ms = call(over_band_kernel, [tile, tile], own, *came)
    return mesh_out, grad_gs, grad_ms


def solution(mesh):
    flat = P(("groups", "band", "dom", "lat"), None)
    grid = P(("groups", "band"), ("dom", "lat"), None)
    count = P(("groups", "band"), ("dom", "lat"))
    placed = (grid,) + (P(),) * 7 + (flat, flat) + (grid, grid, count) * 2
    return jax.shard_map(
        on_device,
        mesh=mesh,
        in_specs=placed,
        out_specs=(flat, count, count),
        check_vma=False,
    )
```

```python
import jax
import jax.numpy as jnp
from jax import lax
from jax.experimental import pallas as pl
from jax.experimental.pallas import tpu as pltpu
from jax.sharding import PartitionSpec as P

F32 = jnp.float32
BF16 = jnp.bfloat16
LANES = 128
GS, GR, GN, MS, MR, MN = range(6)


def mm(a, b):
    return jnp.dot(a, b, preferred_element_type=F32)


def mm_nt(a, b):
    return lax.dot_general(a, b, (((1,), (1,)), ((), ())), preferred_element_type=F32)


def mm_tn(a, b):
    return lax.dot_general(a, b, (((0,), (0,)), ((), ())), preferred_element_type=F32)


def halves(x):
    high = x.astype(BF16)
    return high, (x - high.astype(F32)).astype(BF16)


def silu_parts(x):
    g = 0.5 * jnp.tanh(0.5 * x) + 0.5
    value = x * g
    return value, g + value * (1.0 - g)


def ones_at(mask):
    return jnp.where(mask, 1.0, 0.0).astype(BF16)


def columns(row):
    count = row.shape[1]
    parts = [
        jnp.broadcast_to(row[:, i : i + LANES], (LANES, LANES)).T
        for i in range(0, count, LANES)
    ]
    return parts[0] if len(parts) == 1 else jnp.concatenate(parts, axis=0)


def hits_from(cols, width, period, start=0):
    parts = []
    for i in range(0, width, LANES):
        size = min(LANES, width - i)
        lane = lax.broadcasted_iota(jnp.int32, (cols.shape[0], size), 1) + i
        if period < width:
            lane = lax.rem(lane, period)
        parts.append(ones_at(cols[:, :size] == lane + start))
    return parts[0] if len(parts) == 1 else jnp.concatenate(parts, axis=1)


def hits_to(row, count):
    return ones_at(lax.broadcasted_iota(jnp.int32, (count, row.shape[1]), 0) == row)


def live_only(row, count, first=0):
    slot = lax.broadcasted_iota(jnp.int32, row.shape, 1) + first
    return jnp.where(slot < count, row, -1)


def weight(stack, index):
    latent = stack.shape[1]
    return stack[index * latent : (index + 1) * latent]


def even_on(axis):
    return lax.rem(lax.axis_index(axis), 2) == 0


def spread(index, blocks, cols, pitch):
    extra = jnp.zeros_like(index)
    for block in range(1, blocks):
        extra = extra + jnp.where(index >= block * cols, pitch - cols, 0)
    return index + extra


def fill(wide, blocks, pitch, first):
    cols = blocks.shape[2]
    for k in range(blocks.shape[0]):
        at = first + k * pitch
        wide[:, at : at + cols] = blocks[k]
        if cols < pitch:
            wide[:, at + cols : at + pitch] = jnp.zeros(
                (wide.shape[0], pitch - cols), wide.dtype
            )


def index_kernel(
    count, mesh_count, indices, grid,
    own_out, recv_hits, recv_rows, from_hits, to_hits, from_rows, to_rows, halo_hits, wide,
):
    edges = recv_hits.shape[0]
    mesh_edges = to_hits.shape[0]
    send, recv, mesh_send, mesh_recv = (
        indices[0, :, first : first + size]
        for first, size in (
            (0, edges),
            (edges, edges),
            (2 * edges, mesh_edges),
            (2 * edges + mesh_edges, mesh_edges),
        )
    )
    band_rows, _, cols = grid.shape
    pitch = wide.shape[1] // band_rows
    width = band_rows * pitch
    cycle = recv_rows.shape[0]
    node_count = to_rows.shape[0]
    even_band = even_on("band")
    fill(wide, grid, pitch, 0)
    near_base = jnp.where(even_band, 2 * width, 0)
    far_base = jnp.where(even_band, 0, 2 * width)
    block = 256
    for first in range(0, edges, block):
        part_of = slice(first, first + block)
        index = columns(spread(send[:, part_of], 3 * band_rows, cols, pitch))
        own_hit = hits_from(index, width, width, width)
        own_out[part_of] = mm_nt(own_hit, wide[...]).astype(BF16)
        halo_hits[part_of, :width] = hits_from(index, width, width, near_base)
        halo_hits[part_of, width:] = hits_from(index, width, width, far_base)
        target = live_only(recv[:, part_of], count[0, 0], first)
        recv_hits[part_of] = hits_from(columns(target), 2 * cycle, cycle)
        recv_rows[:, part_of] = hits_to(target, cycle)
    raw = mesh_send
    flipped = jnp.where(
        raw < cycle, raw + 2 * cycle, jnp.where(raw < 2 * cycle, raw, raw - 2 * cycle)
    )
    source = jnp.where(even_band, flipped, raw)
    target = live_only(mesh_recv, mesh_count[0, 0])
    from_hits[...] = hits_from(columns(source), 6 * cycle, 3 * cycle)
    to_hits[...] = hits_from(columns(target), 2 * node_count, node_count)
    from_rows[...] = hits_to(source, 3 * cycle)
    to_rows[...] = hits_to(target, node_count)


def table_kernel(near, far, mesh_in, stack, table_out):
    node_count = mesh_in.shape[0]
    rim = node_count // 2
    even = even_on("lat")
    left = jnp.where(even, far[...], near[...])[rim:]
    right = jnp.where(even, near[...], far[...])[:rim]
    cycle = jnp.concatenate([left, mesh_in[...], right], axis=0)
    high, low = halves(mm(cycle, weight(stack, GR)))
    table_out[: 2 * node_count] = high
    table_out[2 * node_count :] = low


def encode_kernel(
    far, near, halo_hits, recv_hits, recv_rows, own, table, stack,
    senders_out, slope_out, part_out, far_out, near_out, wide,
):
    half = recv_rows.shape[0] // 2
    width = wide.shape[1] // 2
    pitch = width // near.shape[0]
    fill(wide, near, pitch, 0)
    fill(wide, far, pitch, width)
    raw = own[...] + mm_nt(halo_hits[...], wide[...]).astype(BF16)
    latent, _ = silu_parts(mm(raw, stack[stack.shape[0] - raw.shape[1] :]))
    latent = latent.astype(BF16)
    senders_out[...] = latent
    pre = mm(latent, weight(stack, GS)) + mm(recv_hits[...], table[...])
    value, slope = silu_parts(pre)
    slope_out[...] = slope.astype(BF16)
    sums = mm(recv_rows[...], value.astype(BF16))
    part_out[...] = sums
    even = even_on("lat")
    near_out[...] = jnp.where(even, sums[half:], sums[:half]).astype(BF16)
    far_out[...] = jnp.where(even, sums[:half], sums[half:]).astype(BF16)


def node_kernel(part, far, near, mesh_near, mesh_far, mesh_in, stack, mesh_out, slope_out):
    node_count = mesh_in.shape[0]
    rim = node_count // 2
    even = even_on("lat")
    left = jnp.where(even, far[...], near[...]).astype(F32)
    right = jnp.where(even, near[...], far[...]).astype(F32)
    total = part[...] + jnp.concatenate([left, right], axis=0)
    mesh_left = jnp.where(even, mesh_far[...], mesh_near[...])[rim:]
    mesh_right = jnp.where(even, mesh_near[...], mesh_far[...])[:rim]
    cycle = jnp.concatenate([mesh_left, mesh_in[...], mesh_right], axis=0)
    value, slope = silu_parts(mm(total.astype(BF16), weight(stack, GN)))
    mesh_out[...] = (cycle.astype(F32) + value).astype(BF16)
    slope_out[...] = slope


def process_kernel(
    from_hits, to_hits, from_rows, to_rows, near, own, far, d_out, stack,
    mesh_out, sums_out, recv_out, near_out, far_out,
):
    cycle = own.shape[0]
    node_count = cycle // 2
    rim = node_count // 2
    home = own[rim : rim + node_count]
    block = jnp.concatenate([near[...], own[...], far[...]], axis=0)
    table = jnp.concatenate(halves(mm(block, weight(stack, MS))), axis=0)
    recv_table = jnp.concatenate(halves(mm(home, weight(stack, MR))), axis=0)
    pre = mm(from_hits[...], table) + mm(to_hits[...], recv_table)
    value, slope = silu_parts(pre)
    gate = mm(mm(to_rows[...], value.astype(BF16)).astype(BF16), weight(stack, MN))
    gate_value, gate_slope = silu_parts(gate)
    mesh_out[...] = (home.astype(F32) + gate_value).astype(BF16)
    gate_two = (d_out[...].astype(F32) * gate_slope).astype(BF16)
    back = jnp.concatenate(halves(mm_nt(gate_two, weight(stack, MN))), axis=0)
    edge_slope = (mm(to_hits[...], back) * slope).astype(BF16)
    sums = mm(from_rows[...], edge_slope)
    recv_out[...] = mm(to_rows[...], edge_slope).astype(BF16)
    sums_out[...] = sums
    near_out[...] = sums[:cycle].astype(BF16)
    far_out[...] = sums[2 * cycle :].astype(BF16)


def block_of(x, dom_shift, lat_shift, doms, lats):
    cols = x.shape[1] // (doms * lats)
    dom = lax.rem(lax.axis_index("dom") + dom_shift, doms)
    index = dom * lats + lax.rem(lax.axis_index("lat") + lat_shift, lats)
    pick = x[:, :cols]
    for i in range(1, doms * lats):
        pick = jnp.where(index == i, x[:, i * cols : (i + 1) * cols], pick)
    return pick


def home_kernel(recv_sum, d_out, stack, senders, home_out, turned_out):
    home_out[...] = mm_nt(recv_sum[...], weight(stack, MR)) + d_out[...].astype(F32)
    turned_out[...] = senders[...].T


def cotangent_kernel(sums, near, far, home, part_out, far_out, near_out):
    cycle = near.shape[0]
    half = cycle // 2
    rim = half // 2
    total = sums[cycle : 2 * cycle] + near[...].astype(F32) + far[...].astype(F32)
    part_out[...] = total
    even = even_on("lat")
    near_out[:half] = jnp.where(even, total[half:], total[:half]).astype(BF16)
    near_out[half:] = jnp.where(even, home[rim:], home[:rim]).astype(BF16)
    far_out[:half] = jnp.where(even, total[:half], total[half:]).astype(BF16)
    far_out[half:] = jnp.where(even, home[:rim], home[rim:]).astype(BF16)


def gradient_block(recv_hits, back, edge_slope, senders, dom_shift, lat_shift, doms, lats):
    place = (dom_shift, lat_shift, doms, lats)
    slope = mm(recv_hits[...], block_of(back, *place))
    slope = slope * block_of(edge_slope, *place).astype(F32)
    return mm(senders[...], slope.astype(BF16))


def encode_grad_kernel(
    recv_hits, part, far, near, home, node_slope, stack, senders, edge_slope,
    sends, back_out, total_out,
):
    half = part.shape[0] // 2
    even = even_on("lat")
    left = jnp.where(even, far[...], near[...]).astype(F32)
    right = jnp.where(even, near[...], far[...]).astype(F32)
    total = part[...] + jnp.concatenate([left[:half], right[:half]], axis=0)
    total = total.astype(BF16)
    rest = jnp.concatenate([left[half:], home[...], right[half:]], axis=0)
    cot = rest + mm_nt(total, weight(stack, MS))
    gate_one = (cot * node_slope[...]).astype(BF16)
    back = jnp.concatenate(halves(mm_nt(gate_one, weight(stack, GN))), axis=0)
    back_out[...] = back
    lats = sends.shape[0] + 1
    doms = sends.shape[1] + 1
    for i in range(1, lats):
        for j in range(1, doms):
            block = gradient_block(recv_hits, back, edge_slope, senders, j, i, doms, lats)
            sends[i - 1, j - 1] = block.astype(BF16)
    for j in range(doms):
        total_out[j] = block_of(total, j, 0, doms, lats)


def kept_blocks_kernel(recv_hits, back, edge_slope, senders, after, kept):
    doms = kept.shape[0] + 1
    lats = back.shape[1] // kept.shape[2] // doms
    for j in range(1, doms):
        kept[j - 1] = gradient_block(recv_hits, back, edge_slope, senders, j, 0, doms, lats)


def add_kernel(kept, total, *refs):
    *came, out = refs
    rows = kept.shape[1]
    for j in range(kept.shape[0]):
        block = kept[j]
        for part in came:
            block = block + part[j].astype(F32)
        out[j, :rows] = block.astype(BF16)
        out[j, rows:] = total[j + 1]


def other_lats_kernel(recv_hits, back, edge_slope, senders, after, sends):
    lats = sends.shape[0] + 1
    doms = back.shape[1] // sends.shape[2] // lats
    for i in range(1, lats):
        block = gradient_block(recv_hits, back, edge_slope, senders, 0, i, doms, lats)
        sends[i - 1] = block.astype(BF16)


def own_block_kernel(recv_hits, back, edge_slope, senders, *refs):
    *came, out = refs
    lats = len(came) + 1
    doms = back.shape[1] // out.shape[1] // lats
    block = gradient_block(recv_hits, back, edge_slope, senders, 0, 0, doms, lats)
    for part in came:
        block = block + part[...].astype(F32)
    out[...] = block


def over_dom_kernel(kept, total, nodes, *refs):
    latent = kept.shape[0]
    rows = latent // lax.axis_size("band")
    doms = total.shape[0]
    came, (own_out, *sends_out, sums) = refs[: 2 * (doms - 1)], refs[2 * (doms - 1) :]
    first = kept[...]
    second = mm_tn(nodes[...], total[0])
    for part, part_nodes in zip(came[: doms - 1], came[doms - 1 :]):
        first = first + part[:latent].astype(F32)
        second = second + mm_tn(part_nodes[...], part[latent:])
    sums[0] = first
    sums[1] = second
    me = lax.axis_index("band")
    for k in range(2):
        own_out[k] = sums[k, pl.ds(pl.multiple_of(me * rows, rows), rows)]
        for i, out in enumerate(sends_out):
            at = pl.multiple_of(lax.bitwise_xor(me, i + 1) * rows, rows)
            out[k] = sums[k, pl.ds(at, rows)].astype(BF16)


def over_band_kernel(own, *refs):
    *came, first_out, second_out = refs
    for k, out in enumerate((first_out, second_out)):
        total = own[k]
        for part in came:
            total = total + part[k].astype(F32)
        out[...] = total


def call(kernel, outs, *args, scalars=(), scratch=()):
    in_specs = [
        pl.BlockSpec(memory_space=pltpu.SMEM if i in scalars else pltpu.VMEM)
        for i in range(len(args))
    ]
    return pl.pallas_call(
        kernel,
        out_shape=[jax.ShapeDtypeStruct(shape, dtype) for shape, dtype in outs],
        in_specs=in_specs,
        out_specs=[pl.BlockSpec(memory_space=pltpu.VMEM)] * len(outs),
        scratch_shapes=scratch,
        compiler_params=pltpu.CompilerParams(vmem_limit_bytes=16 << 20),
    )(*args)


def ring_pairings(count):
    far = [(i, (i + 1 if i % 2 else i - 1) % count) for i in range(count)]
    return [(i, i ^ 1) for i in range(count)], far


def line_pairings(bands, doms, lats):
    far = []
    for band in range(bands):
        other = band + 1 if band % 2 else band - 1
        for dom in range(doms):
            for lat in range(lats):
                here = (band * doms + dom) * lats + lat
                if 0 <= other < bands:
                    there = (other * doms + dom) * lats + lat
                else:
                    there = (band * doms + dom) * lats + (lat ^ 1)
                far.append((here, there))
    return [(i, i ^ 1) for i in range(bands)], far


def shifted(x, axis, shift):
    count = lax.axis_size(axis)
    return lax.ppermute(x, axis, [(i, (i + shift) % count) for i in range(count)])


def on_device(
    grid_in, w_grid, w_gs, w_gr, w_gn, w_ms, w_mr, w_mn, mesh_in, d_out,
    g2m_send, g2m_recv, g2m_count, mesh_send, mesh_recv, mesh_count,
):
    latent = w_grid.shape[1]
    variables = w_grid.shape[0]
    node_count = mesh_in.shape[0]
    cycle = 2 * node_count
    bands = lax.axis_size("band")
    sectors = lax.axis_size(("dom", "lat"))
    edges = g2m_send.shape[2]
    around = ("dom", "lat")
    whole = ("band", "dom", "lat")
    band_near, band_far = line_pairings(bands, lax.axis_size("dom"), lax.axis_size("lat"))
    ring_near, ring_far = ring_pairings(sectors)

    grid = jnp.transpose(grid_in, (0, 2, 1))
    pitch = -(-grid.shape[2] // LANES) * LANES
    band_rows = grid.shape[0]
    width = band_rows * pitch
    raw_near = lax.ppermute(grid, "band", band_near)
    raw_far = lax.ppermute(grid, whole, band_far)
    mesh_edges = mesh_send.shape[2]
    stack = jnp.concatenate([w_gs, w_gr, w_gn, w_ms, w_mr, w_mn, w_grid], axis=0)
    indices = jnp.concatenate([g2m_send, g2m_recv, mesh_send, mesh_recv], axis=2)
    rows, recv_hits, recv_rows, from_hits, to_hits, from_rows, to_rows, halo_hits = call(
        index_kernel,
        [
            ((edges, variables), BF16),
            ((edges, 2 * cycle), BF16),
            ((cycle, edges), BF16),
            ((mesh_edges, 6 * cycle), BF16),
            ((mesh_edges, 2 * node_count), BF16),
            ((3 * cycle, mesh_edges), BF16),
            ((node_count, mesh_edges), BF16),
            ((edges, 2 * width), BF16),
        ],
        g2m_count, mesh_count, indices, grid,
        scalars=(0, 1),
        scratch=[pltpu.VMEM((variables, width), BF16)],
    )
    late_mesh, rows = lax.optimization_barrier((mesh_in, rows))
    mesh_near = lax.ppermute(late_mesh, around, ring_near)
    mesh_far = lax.ppermute(late_mesh, around, ring_far)
    (table,) = call(
        table_kernel, [((2 * cycle, latent), BF16)], mesh_near, mesh_far, mesh_in, stack
    )
    senders, edge_slope, part, to_far, to_near = call(
        encode_kernel,
        [
            ((edges, latent), BF16),
            ((edges, latent), BF16),
            ((cycle, latent), F32),
            ((node_count, latent), BF16),
            ((node_count, latent), BF16),
        ],
        raw_far, raw_near, halo_hits, recv_hits, recv_rows, rows, table, stack,
        scratch=[pltpu.VMEM((variables, 2 * width), BF16)],
    )
    from_far = lax.ppermute(to_far, around, ring_far)
    from_near = lax.ppermute(to_near, around, ring_near)
    mesh_one, node_slope = call(
        node_kernel,
        [((cycle, latent), BF16), ((cycle, latent), F32)],
        part, from_far, from_near, mesh_near, mesh_far, mesh_in, stack,
    )
    one_near = lax.ppermute(mesh_one, "band", band_near)
    one_far = lax.ppermute(mesh_one, whole, band_far)
    doms = lax.axis_size("dom")
    lats = lax.axis_size("lat")
    dom_nodes = [shifted(mesh_one, "dom", i + 1) for i in range(doms - 1)]
    mesh_out, sums, recv_sum, to_near, to_far = call(
        process_kernel,
        [
            ((node_count, latent), BF16),
            ((3 * cycle, latent), F32),
            ((node_count, latent), BF16),
            ((cycle, latent), BF16),
            ((cycle, latent), BF16),
        ],
        from_hits, to_hits, from_rows, to_rows, one_near, mesh_one, one_far, d_out,
        stack,
    )
    from_near = lax.ppermute(to_near, "band", band_near)
    from_far = lax.ppermute(to_far, whole, band_far)
    from_near, *dom_nodes = lax.optimization_barrier((from_near, *dom_nodes))
    home, senders = call(
        home_kernel,
        [((node_count, latent), F32), ((latent, edges), BF16)],
        recv_sum, d_out, stack, senders,
    )
    message = (node_count + node_count // 2, latent)
    part, to_far, to_near = call(
        cotangent_kernel,
        [((cycle, latent), F32), (message, BF16), (message, BF16)],
        sums, from_near, from_far, home,
    )
    from_far = lax.ppermute(to_far, around, ring_far)
    from_near = lax.ppermute(to_near, around, ring_near)

    cols = latent // sectors
    rows = latent // bands
    sends, back, total = call(
        encode_grad_kernel,
        [
            ((lats - 1, doms - 1, latent, cols), BF16),
            ((2 * cycle, latent), BF16),
            ((doms, cycle, cols), BF16),
        ],
        recv_hits, part, from_far, from_near, home, node_slope, stack, senders, edge_slope,
    )
    edge = (recv_hits, back, edge_slope, senders)
    came = [shifted(sends[i], "lat", i + 1) for i in range(lats - 1)]
    block = (latent, cols)
    (kept,) = call(kept_blocks_kernel, [((doms - 1,) + block, F32)], *edge, sends)
    (own_sends,) = call(other_lats_kernel, [((lats - 1,) + block, BF16)], *edge, sends)
    own_came = [shifted(own_sends[i], "lat", i + 1) for i in range(lats - 1)]
    kept, own_sends = lax.optimization_barrier((kept, own_sends))
    (sends,) = call(
        add_kernel, [((doms - 1, latent + cycle, cols), BF16)], kept, total, *came
    )
    other_doms = [shifted(sends[i], "dom", i + 1) for i in range(doms - 1)]
    (kept,) = call(own_block_kernel, [(block, F32)], *edge, *own_came)
    own, *sends = call(
        over_dom_kernel,
        [((2, rows, cols), F32)] + [((2, rows, cols), BF16)] * (bands - 1),
        kept, total, mesh_one, *other_doms, *dom_nodes,
        scratch=[pltpu.VMEM((2,) + block, F32)],
    )
    count = lax.axis_size("band")
    came = [
        lax.ppermute(x, "band", [(b, b ^ (i + 1)) for b in range(count)])
        for i, x in enumerate(sends)
    ]
    tile = ((rows, cols), F32)
    grad_gs, grad_ms = call(over_band_kernel, [tile, tile], own, *came)
    return mesh_out, grad_gs, grad_ms


def solution(mesh):
    flat = P(("groups", "band", "dom", "lat"), None)
    grid = P(("groups", "band"), ("dom", "lat"), None)
    count = P(("groups", "band"), ("dom", "lat"))
    placed = (grid,) + (P(),) * 7 + (flat, flat) + (grid, grid, count) * 2
    return jax.shard_map(
        on_device,
        mesh=mesh,
        in_specs=placed,
        out_specs=(flat, count, count),
        check_vma=False,
    )
```

```python
import jax
import jax.numpy as jnp
from jax import lax
from jax.experimental import pallas as pl
from jax.experimental.pallas import tpu as pltpu
from jax.sharding import PartitionSpec as P

F32 = jnp.float32
BF16 = jnp.bfloat16
LANES = 128
GS, GR, GN, MS, MR, MN = range(6)


def mm(a, b):
    return jnp.dot(a, b, preferred_element_type=F32)


def mm_nt(a, b):
    return lax.dot_general(a, b, (((1,), (1,)), ((), ())), preferred_element_type=F32)


def mm_tn(a, b):
    return lax.dot_general(a, b, (((0,), (0,)), ((), ())), preferred_element_type=F32)


def halves(x):
    high = x.astype(BF16)
    return high, (x - high.astype(F32)).astype(BF16)


def silu_parts(x):
    g = 0.5 * jnp.tanh(0.5 * x) + 0.5
    value = x * g
    return value, g + value * (1.0 - g)


def ones_at(mask):
    return jnp.where(mask, 1.0, 0.0).astype(BF16)


def columns(row):
    count = row.shape[1]
    parts = [
        jnp.broadcast_to(row[:, i : i + LANES], (LANES, LANES)).T
        for i in range(0, count, LANES)
    ]
    return parts[0] if len(parts) == 1 else jnp.concatenate(parts, axis=0)


def hits_from(cols, width, period, start=0):
    parts = []
    for i in range(0, width, LANES):
        size = min(LANES, width - i)
        lane = lax.broadcasted_iota(jnp.int32, (cols.shape[0], size), 1) + i
        if period < width:
            lane = lax.rem(lane, period)
        parts.append(ones_at(cols[:, :size] == lane + start))
    return parts[0] if len(parts) == 1 else jnp.concatenate(parts, axis=1)


def hits_to(row, count):
    return ones_at(lax.broadcasted_iota(jnp.int32, (count, row.shape[1]), 0) == row)


def live_only(row, count, first=0):
    slot = lax.broadcasted_iota(jnp.int32, row.shape, 1) + first
    return jnp.where(slot < count, row, -1)


def weight(stack, index):
    latent = stack.shape[1]
    return stack[index * latent : (index + 1) * latent]


def even_on(axis):
    return lax.rem(lax.axis_index(axis), 2) == 0


def spread(index, blocks, cols, pitch):
    extra = jnp.zeros_like(index)
    for block in range(1, blocks):
        extra = extra + jnp.where(index >= block * cols, pitch - cols, 0)
    return index + extra


def fill(wide, blocks, pitch, first):
    cols = blocks.shape[2]
    for k in range(blocks.shape[0]):
        at = first + k * pitch
        wide[:, at : at + cols] = blocks[k]
        if cols < pitch:
            wide[:, at + cols : at + pitch] = jnp.zeros(
                (wide.shape[0], pitch - cols), wide.dtype
            )


def index_kernel(
    count, mesh_count, indices, grid,
    own_out, recv_hits, recv_rows, own_hits, outer_hits, to_hits, from_rows, to_rows, halo_hits, wide,
):
    edges = recv_hits.shape[0]
    mesh_edges = to_hits.shape[0]
    send, recv, mesh_send, mesh_recv = (
        indices[0, :, first : first + size]
        for first, size in (
            (0, edges),
            (edges, edges),
            (2 * edges, mesh_edges),
            (2 * edges + mesh_edges, mesh_edges),
        )
    )
    band_rows, _, cols = grid.shape
    pitch = wide.shape[1] // band_rows
    width = band_rows * pitch
    cycle = recv_rows.shape[0]
    node_count = to_rows.shape[0]
    even_band = even_on("band")
    fill(wide, grid, pitch, 0)
    near_base = jnp.where(even_band, 2 * width, 0)
    far_base = jnp.where(even_band, 0, 2 * width)
    block = 256
    for first in range(0, edges, block):
        part_of = slice(first, first + block)
        index = columns(spread(send[:, part_of], 3 * band_rows, cols, pitch))
        own_hit = hits_from(index, width, width, width)
        own_out[part_of] = mm_nt(own_hit, wide[...]).astype(BF16)
        halo_hits[part_of, :width] = hits_from(index, width, width, near_base)
        halo_hits[part_of, width:] = hits_from(index, width, width, far_base)
        target = live_only(recv[:, part_of], count[0, 0], first)
        recv_hits[part_of] = hits_from(columns(target), 2 * cycle, cycle)
        recv_rows[:, part_of] = hits_to(target, cycle)
    raw = mesh_send
    inner = (raw >= cycle) & (raw < 2 * cycle)
    above_near = jnp.where(raw < cycle, raw + cycle, raw - 2 * cycle)
    below_near = jnp.where(raw < cycle, raw, raw - cycle)
    outer = jnp.where(inner, -1, jnp.where(even_band, above_near, below_near))
    target = live_only(mesh_recv, mesh_count[0, 0])
    own_hits[...] = hits_from(columns(jnp.where(inner, raw - cycle, -1)), 2 * cycle, cycle)
    outer_hits[...] = hits_from(columns(outer), 4 * cycle, 2 * cycle)
    to_hits[...] = hits_from(columns(target), 2 * node_count, node_count)
    source = jnp.where(inner, raw, jnp.where(outer < cycle, outer, outer + cycle))
    from_rows[...] = hits_to(source, 3 * cycle)
    to_rows[...] = hits_to(target, node_count)


def receiver_kernel(near, far, mesh_in, recv_hits, stack, pre_out):
    node_count = mesh_in.shape[0]
    rim = node_count // 2
    even = even_on("lat")
    left = jnp.where(even, far[...], near[...])[rim:]
    right = jnp.where(even, near[...], far[...])[:rim]
    cycle = jnp.concatenate([left, mesh_in[...], right], axis=0)
    table = jnp.concatenate(halves(mm(cycle, weight(stack, GR))), axis=0)
    pre_out[...] = mm(recv_hits[...], table)


def encode_kernel(
    near, far, halo_hits, recv_rows, own, recv_pre, stack,
    senders_out, slope_out, part_out, near_out, far_out, wide,
):
    half = recv_rows.shape[0] // 2
    width = wide.shape[1] // 2
    pitch = width // near.shape[0]
    fill(wide, near, pitch, 0)
    fill(wide, far, pitch, width)
    raw = own[...] + mm_nt(halo_hits[...], wide[...]).astype(BF16)
    latent, _ = silu_parts(mm(raw, stack[stack.shape[0] - raw.shape[1] :]))
    latent = latent.astype(BF16)
    senders_out[...] = latent
    pre = mm(latent, weight(stack, GS)) + recv_pre[...]
    value, slope = silu_parts(pre)
    slope_out[...] = slope.astype(BF16)
    sums = mm(recv_rows[...], value.astype(BF16))
    part_out[...] = sums
    even = even_on("lat")
    near_out[...] = jnp.where(even, sums[half:], sums[:half]).astype(BF16)
    far_out[...] = jnp.where(even, sums[:half], sums[half:]).astype(BF16)


def node_kernel(part, near, far, mesh_near, mesh_far, mesh_in, stack, mesh_out, slope_out):
    node_count = mesh_in.shape[0]
    rim = node_count // 2
    even = even_on("lat")
    left = jnp.where(even, far[...], near[...]).astype(F32)
    right = jnp.where(even, near[...], far[...]).astype(F32)
    total = part[...] + jnp.concatenate([left, right], axis=0)
    mesh_left = jnp.where(even, mesh_far[...], mesh_near[...])[rim:]
    mesh_right = jnp.where(even, mesh_near[...], mesh_far[...])[:rim]
    cycle = jnp.concatenate([mesh_left, mesh_in[...], mesh_right], axis=0)
    value, slope = silu_parts(mm(total.astype(BF16), weight(stack, GN)))
    mesh_out[...] = (cycle.astype(F32) + value).astype(BF16)
    slope_out[...] = slope


def process_own_kernel(own_hits, to_hits, own, stack, pre_out):
    rim = own.shape[0] // 4
    home = own[rim : own.shape[0] - rim]
    table = jnp.concatenate(halves(mm(own[...], weight(stack, MS))), axis=0)
    recv_table = jnp.concatenate(halves(mm(home, weight(stack, MR))), axis=0)
    pre_out[...] = mm(own_hits[...], table) + mm(to_hits[...], recv_table)


def process_kernel(
    own_pre, outer_hits, to_hits, from_rows, to_rows, near, own, far, d_out, stack,
    mesh_out, sums_out, recv_out, near_out, far_out,
):
    cycle = own.shape[0]
    node_count = cycle // 2
    rim = node_count // 2
    home = own[rim : rim + node_count]
    block = jnp.concatenate([near[...], far[...]], axis=0)
    table = jnp.concatenate(halves(mm(block, weight(stack, MS))), axis=0)
    pre = own_pre[...] + mm(outer_hits[...], table)
    value, slope = silu_parts(pre)
    gate = mm(mm(to_rows[...], value.astype(BF16)).astype(BF16), weight(stack, MN))
    gate_value, gate_slope = silu_parts(gate)
    mesh_out[...] = (home.astype(F32) + gate_value).astype(BF16)
    gate_two = (d_out[...].astype(F32) * gate_slope).astype(BF16)
    back = jnp.concatenate(halves(mm_nt(gate_two, weight(stack, MN))), axis=0)
    edge_slope = (mm(to_hits[...], back) * slope).astype(BF16)
    sums = mm(from_rows[...], edge_slope)
    recv_out[...] = mm(to_rows[...], edge_slope).astype(BF16)
    sums_out[...] = sums
    near_out[...] = sums[:cycle].astype(BF16)
    far_out[...] = sums[2 * cycle :].astype(BF16)


def block_of(x, dom_shift, lat_shift, doms, lats):
    cols = x.shape[1] // (doms * lats)
    dom = lax.rem(lax.axis_index("dom") + dom_shift, doms)
    index = dom * lats + lax.rem(lax.axis_index("lat") + lat_shift, lats)
    pick = x[:, :cols]
    for i in range(1, doms * lats):
        pick = jnp.where(index == i, x[:, i * cols : (i + 1) * cols], pick)
    return pick


def home_kernel(recv_sum, d_out, stack, senders, home_out, turned_out):
    home_out[...] = mm_nt(recv_sum[...], weight(stack, MR)) + d_out[...].astype(F32)
    turned_out[...] = senders[...].T


def cotangent_kernel(sums, near, far, home, part_out, near_out, far_out):
    cycle = near.shape[0]
    half = cycle // 2
    rim = half // 2
    total = sums[cycle : 2 * cycle] + near[...].astype(F32) + far[...].astype(F32)
    part_out[...] = total
    even = even_on("lat")
    near_out[:half] = jnp.where(even, total[half:], total[:half]).astype(BF16)
    near_out[half:] = jnp.where(even, home[rim:], home[:rim]).astype(BF16)
    far_out[:half] = jnp.where(even, total[:half], total[half:]).astype(BF16)
    far_out[half:] = jnp.where(even, home[:rim], home[rim:]).astype(BF16)


def gradient_block(recv_hits, back, edge_slope, senders, dom_shift, lat_shift, doms, lats):
    place = (dom_shift, lat_shift, doms, lats)
    slope = mm(recv_hits[...], block_of(back, *place))
    slope = slope * block_of(edge_slope, *place).astype(F32)
    return mm(senders[...], slope.astype(BF16))


def encode_grad_kernel(
    recv_hits, part, near, far, home, node_slope, stack, senders, edge_slope,
    sends, back_out, total_out,
):
    half = part.shape[0] // 2
    even = even_on("lat")
    left = jnp.where(even, far[...], near[...]).astype(F32)
    right = jnp.where(even, near[...], far[...]).astype(F32)
    total = part[...] + jnp.concatenate([left[:half], right[:half]], axis=0)
    total = total.astype(BF16)
    rest = jnp.concatenate([left[half:], home[...], right[half:]], axis=0)
    cot = rest + mm_nt(total, weight(stack, MS))
    gate_one = (cot * node_slope[...]).astype(BF16)
    back = jnp.concatenate(halves(mm_nt(gate_one, weight(stack, GN))), axis=0)
    back_out[...] = back
    lats = sends.shape[0] + 1
    doms = sends.shape[1] + 1
    for i in range(1, lats):
        for j in range(1, doms):
            block = gradient_block(recv_hits, back, edge_slope, senders, j, i, doms, lats)
            sends[i - 1, j - 1] = block.astype(BF16)
    for j in range(doms):
        total_out[j] = block_of(total, j, 0, doms, lats)


def kept_blocks_kernel(recv_hits, back, edge_slope, senders, after, kept):
    doms = kept.shape[0] + 1
    lats = back.shape[1] // kept.shape[2] // doms
    for j in range(1, doms):
        kept[j - 1] = gradient_block(recv_hits, back, edge_slope, senders, j, 0, doms, lats)


def rows_at(ref, place, partner):
    bands = lax.axis_size("band")
    rows = ref.shape[-2] // bands
    at = pl.multiple_of(lax.bitwise_xor(lax.axis_index("band"), partner) * rows, rows)
    return ref[(*place, pl.ds(at, rows))]


def add_kernel(kept, total, *refs):
    *came, first_out, second_out = refs
    bands = lax.axis_size("band")
    half = bands // 2
    rows = kept.shape[1] // bands
    for j in range(kept.shape[0]):
        for k in range(bands):
            block = rows_at(kept, (j,), k)
            for part in came:
                block = block + rows_at(part, (j,), k).astype(F32)
            out = first_out if k >= half else second_out
            at = (k % half) * rows
            out[j, at : at + rows] = block.astype(BF16)
        first_out[j, half * rows :] = total[j + 1]


def other_lats_kernel(recv_hits, back, edge_slope, senders, after, sends):
    lats = sends.shape[0] + 1
    doms = back.shape[1] // sends.shape[2] // lats
    for i in range(1, lats):
        block = gradient_block(recv_hits, back, edge_slope, senders, 0, i, doms, lats)
        sends[i - 1] = block.astype(BF16)


def own_block_kernel(recv_hits, back, edge_slope, senders, *refs):
    *came, out = refs
    lats = len(came) + 1
    doms = back.shape[1] // out.shape[1] // lats
    block = gradient_block(recv_hits, back, edge_slope, senders, 0, 0, doms, lats)
    for part in came:
        block = block + part[...].astype(F32)
    out[...] = block


def first_kernel(kept, total, nodes, *refs):
    doms = total.shape[0]
    came, (*sends_out, sums) = refs[: 2 * (doms - 1)], refs[2 * (doms - 1) :]
    came, came_nodes = came[: doms - 1], came[doms - 1 :]
    half = len(sends_out)
    rows = sends_out[0].shape[1]
    second = mm_tn(nodes[...], total[0])
    for part, part_nodes in zip(came, came_nodes):
        second = second + mm_tn(part_nodes[...], part[half * rows :])
    sums[...] = second
    for i, out in enumerate(sends_out):
        block = rows_at(kept, (), half + i)
        for part in came:
            block = block + part[i * rows : (i + 1) * rows].astype(F32)
        out[0] = block.astype(BF16)
        out[1] = rows_at(sums, (), half + i).astype(BF16)


def second_kernel(kept, sums, *refs):
    half = lax.axis_size("band") // 2
    came, outs = refs[:-half], refs[-half:]
    rows = outs[0].shape[1]
    for i, out in enumerate(outs):
        block = rows_at(kept, (), i)
        for part in came:
            block = block + part[i * rows : (i + 1) * rows].astype(F32)
        out[0] = block.astype(out.dtype)
        out[1] = rows_at(sums, (), i).astype(out.dtype)


def over_band_kernel(*refs):
    *came, own, first_out, second_out = refs
    for k, out in enumerate((first_out, second_out)):
        total = own[k]
        for part in came:
            total = total + part[k].astype(F32)
        out[...] = total


def call(kernel, outs, *args, scalars=(), scratch=()):
    in_specs = [
        pl.BlockSpec(memory_space=pltpu.SMEM if i in scalars else pltpu.VMEM)
        for i in range(len(args))
    ]
    return pl.pallas_call(
        kernel,
        out_shape=[jax.ShapeDtypeStruct(shape, dtype) for shape, dtype in outs],
        in_specs=in_specs,
        out_specs=[pl.BlockSpec(memory_space=pltpu.VMEM)] * len(outs),
        scratch_shapes=scratch,
        compiler_params=pltpu.CompilerParams(vmem_limit_bytes=16 << 20),
    )(*args)


def ring_pairings(count):
    far = [(i, (i + 1 if i % 2 else i - 1) % count) for i in range(count)]
    return [(i, i ^ 1) for i in range(count)], far


def line_pairings(bands, doms, lats):
    far = []
    for band in range(bands):
        other = band + 1 if band % 2 else band - 1
        for dom in range(doms):
            for lat in range(lats):
                here = (band * doms + dom) * lats + lat
                if 0 <= other < bands:
                    there = (other * doms + dom) * lats + lat
                else:
                    there = (band * doms + dom) * lats + (lat ^ 1)
                far.append((here, there))
    return [(i, i ^ 1) for i in range(bands)], far


def shifted(x, axis, shift):
    count = lax.axis_size(axis)
    return lax.ppermute(x, axis, [(i, (i + shift) % count) for i in range(count)])


def over_band(x, partner):
    count = lax.axis_size("band")
    return lax.ppermute(x, "band", [(b, b ^ partner) for b in range(count)])


def on_device(
    grid_in, w_grid, w_gs, w_gr, w_gn, w_ms, w_mr, w_mn, mesh_in, d_out,
    g2m_send, g2m_recv, g2m_count, mesh_send, mesh_recv, mesh_count,
):
    latent = w_grid.shape[1]
    variables = w_grid.shape[0]
    node_count = mesh_in.shape[0]
    cycle = 2 * node_count
    bands = lax.axis_size("band")
    sectors = lax.axis_size(("dom", "lat"))
    edges = g2m_send.shape[2]
    around = ("dom", "lat")
    whole = ("band", "dom", "lat")
    band_near, band_far = line_pairings(bands, lax.axis_size("dom"), lax.axis_size("lat"))
    ring_near, ring_far = ring_pairings(sectors)

    grid = jnp.transpose(grid_in, (0, 2, 1))
    pitch = -(-grid.shape[2] // LANES) * LANES
    band_rows = grid.shape[0]
    width = band_rows * pitch
    raw_near = lax.ppermute(grid, "band", band_near)
    raw_far = lax.ppermute(grid, whole, band_far)
    mesh_edges = mesh_send.shape[2]
    stack = jnp.concatenate([w_gs, w_gr, w_gn, w_ms, w_mr, w_mn, w_grid], axis=0)
    indices = jnp.concatenate([g2m_send, g2m_recv, mesh_send, mesh_recv], axis=2)
    (
        rows, recv_hits, recv_rows, own_hits, outer_hits, to_hits, from_rows, to_rows, halo_hits
    ) = call(
        index_kernel,
        [
            ((edges, variables), BF16),
            ((edges, 2 * cycle), BF16),
            ((cycle, edges), BF16),
            ((mesh_edges, 2 * cycle), BF16),
            ((mesh_edges, 4 * cycle), BF16),
            ((mesh_edges, 2 * node_count), BF16),
            ((3 * cycle, mesh_edges), BF16),
            ((node_count, mesh_edges), BF16),
            ((edges, 2 * width), BF16),
        ],
        g2m_count, mesh_count, indices, grid,
        scalars=(0, 1),
        scratch=[pltpu.VMEM((variables, width), BF16)],
    )
    late_mesh, rows = lax.optimization_barrier((mesh_in, rows))
    mesh_near = lax.ppermute(late_mesh, around, ring_near)
    mesh_far = lax.ppermute(late_mesh, around, ring_far)
    (recv_pre,) = call(
        receiver_kernel,
        [((edges, latent), F32)],
        mesh_near, mesh_far, mesh_in, recv_hits, stack,
    )
    senders, edge_slope, part, to_near, to_far = call(
        encode_kernel,
        [
            ((edges, latent), BF16),
            ((edges, latent), BF16),
            ((cycle, latent), F32),
            ((node_count, latent), BF16),
            ((node_count, latent), BF16),
        ],
        raw_near, raw_far, halo_hits, recv_rows, rows, recv_pre, stack,
        scratch=[pltpu.VMEM((variables, 2 * width), BF16)],
    )
    from_far = lax.ppermute(to_far, around, ring_far)
    from_near = lax.ppermute(to_near, around, ring_near)
    mesh_one, node_slope = call(
        node_kernel,
        [((cycle, latent), BF16), ((cycle, latent), F32)],
        part, from_near, from_far, mesh_near, mesh_far, mesh_in, stack,
    )
    one_near = lax.ppermute(mesh_one, "band", band_near)
    one_far = lax.ppermute(mesh_one, whole, band_far)
    doms = lax.axis_size("dom")
    lats = lax.axis_size("lat")
    dom_nodes = [shifted(mesh_one, "dom", i + 1) for i in range(doms - 1)]
    (own_pre,) = call(
        process_own_kernel, [((mesh_edges, latent), F32)], own_hits, to_hits, mesh_one, stack
    )
    mesh_out, sums, recv_sum, to_near, to_far = call(
        process_kernel,
        [
            ((node_count, latent), BF16),
            ((3 * cycle, latent), F32),
            ((node_count, latent), BF16),
            ((cycle, latent), BF16),
            ((cycle, latent), BF16),
        ],
        own_pre, outer_hits, to_hits, from_rows, to_rows, one_near, mesh_one, one_far, d_out,
        stack,
    )
    from_near = lax.ppermute(to_near, "band", band_near)
    from_far = lax.ppermute(to_far, whole, band_far)
    from_near, *dom_nodes = lax.optimization_barrier((from_near, *dom_nodes))
    home, senders = call(
        home_kernel,
        [((node_count, latent), F32), ((latent, edges), BF16)],
        recv_sum, d_out, stack, senders,
    )
    message = (node_count + node_count // 2, latent)
    part, to_near, to_far = call(
        cotangent_kernel,
        [((cycle, latent), F32), (message, BF16), (message, BF16)],
        sums, from_near, from_far, home,
    )
    from_far = lax.ppermute(to_far, around, ring_far)
    from_near = lax.ppermute(to_near, around, ring_near)

    cols = latent // sectors
    rows = latent // bands
    sends, back, total = call(
        encode_grad_kernel,
        [
            ((lats - 1, doms - 1, latent, cols), BF16),
            ((2 * cycle, latent), BF16),
            ((doms, cycle, cols), BF16),
        ],
        recv_hits, part, from_near, from_far, home, node_slope, stack, senders, edge_slope,
    )
    edge = (recv_hits, back, edge_slope, senders)
    came = [shifted(sends[i], "lat", i + 1) for i in range(lats - 1)]
    block = (latent, cols)
    (kept,) = call(kept_blocks_kernel, [((doms - 1,) + block, F32)], *edge, sends)
    (own_sends,) = call(other_lats_kernel, [((lats - 1,) + block, BF16)], *edge, sends)
    own_came = [shifted(own_sends[i], "lat", i + 1) for i in range(lats - 1)]
    kept, own_sends = lax.optimization_barrier((kept, own_sends))
    half = bands // 2
    first, second = call(
        add_kernel,
        [
            ((doms - 1, half * rows + cycle, cols), BF16),
            ((doms - 1, half * rows, cols), BF16),
        ],
        kept, total, *came,
    )
    first = [shifted(first[i], "dom", i + 1) for i in range(doms - 1)]
    second = [shifted(second[i], "dom", i + 1) for i in range(doms - 1)]
    (kept,) = call(own_block_kernel, [(block, F32)], *edge, *own_came)
    pair = (2, rows, cols)
    *far_sends, sums = call(
        first_kernel,
        [(pair, BF16)] * half + [(block, F32)],
        kept, total, mesh_one, *first, *dom_nodes,
    )
    came = [over_band(x, half + i) for i, x in reversed(list(enumerate(far_sends)))]
    own, *near_sends = call(
        second_kernel,
        [(pair, F32)] + [(pair, BF16)] * (half - 1),
        kept, sums, *second,
    )
    came += [over_band(x, i + 1) for i, x in reversed(list(enumerate(near_sends)))]
    tile = ((rows, cols), F32)
    grad_gs, grad_ms = call(over_band_kernel, [tile, tile], *came, own)
    return mesh_out, grad_gs, grad_ms


def solution(mesh):
    flat = P(("groups", "band", "dom", "lat"), None)
    grid = P(("groups", "band"), ("dom", "lat"), None)
    count = P(("groups", "band"), ("dom", "lat"))
    placed = (grid,) + (P(),) * 7 + (flat, flat) + (grid, grid, count) * 2
    return jax.shard_map(
        on_device,
        mesh=mesh,
        in_specs=placed,
        out_specs=(flat, count, count),
        check_vma=False,
    )
```

```python
import jax
import jax.numpy as jnp
from jax import lax
from jax.experimental import pallas as pl
from jax.experimental.pallas import tpu as pltpu
from jax.sharding import PartitionSpec as P

F32 = jnp.float32
BF16 = jnp.bfloat16
LANES = 128
GS, GR, GN, MS, MR, MN = range(6)


def mm(a, b):
    return jnp.dot(a, b, preferred_element_type=F32)


def mm_nt(a, b):
    return lax.dot_general(a, b, (((1,), (1,)), ((), ())), preferred_element_type=F32)


def mm_tn(a, b):
    return lax.dot_general(a, b, (((0,), (0,)), ((), ())), preferred_element_type=F32)


def halves(x):
    high = x.astype(BF16)
    return high, (x - high.astype(F32)).astype(BF16)


def silu_parts(x):
    g = 0.5 * jnp.tanh(0.5 * x) + 0.5
    value = x * g
    return value, g + value * (1.0 - g)


def ones_at(mask):
    return jnp.where(mask, 1.0, 0.0).astype(BF16)


def columns(row):
    count = row.shape[1]
    parts = [
        jnp.broadcast_to(row[:, i : i + LANES], (LANES, LANES)).T
        for i in range(0, count, LANES)
    ]
    return parts[0] if len(parts) == 1 else jnp.concatenate(parts, axis=0)


def hits_from(cols, width, period, start=0):
    parts = []
    for i in range(0, width, LANES):
        size = min(LANES, width - i)
        lane = lax.broadcasted_iota(jnp.int32, (cols.shape[0], size), 1) + i
        if period < width:
            lane = lax.rem(lane, period)
        parts.append(ones_at(cols[:, :size] == lane + start))
    return parts[0] if len(parts) == 1 else jnp.concatenate(parts, axis=1)


def hits_to(row, count):
    return ones_at(lax.broadcasted_iota(jnp.int32, (count, row.shape[1]), 0) == row)


def live_only(row, count, first=0):
    slot = lax.broadcasted_iota(jnp.int32, row.shape, 1) + first
    return jnp.where(slot < count, row, -1)


def weight(stack, index):
    latent = stack.shape[1]
    return stack[index * latent : (index + 1) * latent]


def even_on(axis):
    return lax.rem(lax.axis_index(axis), 2) == 0


def spread(index, blocks, cols, pitch):
    extra = jnp.zeros_like(index)
    for block in range(1, blocks):
        extra = extra + jnp.where(index >= block * cols, pitch - cols, 0)
    return index + extra


def fill(wide, blocks, pitch, first):
    cols = blocks.shape[2]
    for k in range(blocks.shape[0]):
        at = first + k * pitch
        wide[:, at : at + cols] = blocks[k]
        if cols < pitch:
            wide[:, at + cols : at + pitch] = jnp.zeros(
                (wide.shape[0], pitch - cols), wide.dtype
            )


def index_kernel(
    count, mesh_count, indices, grid,
    own_out, recv_hits, recv_rows, own_hits, outer_hits, to_hits, from_rows, to_rows, near_hits, far_hits, wide,
):
    edges = recv_hits.shape[0]
    mesh_edges = to_hits.shape[0]
    send, recv, mesh_send, mesh_recv = (
        indices[0, :, first : first + size]
        for first, size in (
            (0, edges),
            (edges, edges),
            (2 * edges, mesh_edges),
            (2 * edges + mesh_edges, mesh_edges),
        )
    )
    band_rows, _, cols = grid.shape
    pitch = wide.shape[1] // band_rows
    width = band_rows * pitch
    cycle = recv_rows.shape[0]
    node_count = to_rows.shape[0]
    even_band = even_on("band")
    fill(wide, grid, pitch, 0)
    near_base = jnp.where(even_band, 2 * width, 0)
    far_base = jnp.where(even_band, 0, 2 * width)
    block = 256
    for first in range(0, edges, block):
        part_of = slice(first, first + block)
        index = columns(spread(send[:, part_of], 3 * band_rows, cols, pitch))
        own_hit = hits_from(index, width, width, width)
        own_out[part_of] = mm_nt(own_hit, wide[...]).astype(BF16)
        near_hits[part_of] = hits_from(index, width, width, near_base)
        far_hits[part_of] = hits_from(index, width, width, far_base)
        target = live_only(recv[:, part_of], count[0, 0], first)
        recv_hits[part_of] = hits_from(columns(target), 2 * cycle, cycle)
        recv_rows[:, part_of] = hits_to(target, cycle)
    raw = mesh_send
    inner = (raw >= cycle) & (raw < 2 * cycle)
    above_near = jnp.where(raw < cycle, raw + cycle, raw - 2 * cycle)
    below_near = jnp.where(raw < cycle, raw, raw - cycle)
    outer = jnp.where(inner, -1, jnp.where(even_band, above_near, below_near))
    target = live_only(mesh_recv, mesh_count[0, 0])
    own_hits[...] = hits_from(columns(jnp.where(inner, raw - cycle, -1)), 2 * cycle, cycle)
    outer_hits[...] = hits_from(columns(outer), 4 * cycle, 2 * cycle)
    to_hits[...] = hits_from(columns(target), 2 * node_count, node_count)
    source = jnp.where(inner, raw, jnp.where(outer < cycle, outer, outer + cycle))
    from_rows[...] = hits_to(source, 3 * cycle)
    to_rows[...] = hits_to(target, node_count)


def receiver_kernel(near, far, mesh_in, recv_hits, stack, pre_out):
    node_count = mesh_in.shape[0]
    rim = node_count // 2
    even = even_on("lat")
    left = jnp.where(even, far[...], near[...])[rim:]
    right = jnp.where(even, near[...], far[...])[:rim]
    cycle = jnp.concatenate([left, mesh_in[...], right], axis=0)
    table = jnp.concatenate(halves(mm(cycle, weight(stack, GR))), axis=0)
    pre_out[...] = mm(recv_hits[...], table)


def gather_kernel(halo, hits, rows, rows_out, wide):
    fill(wide, halo, wide.shape[1] // halo.shape[0], 0)
    rows_out[...] = rows[...] + mm_nt(hits[...], wide[...]).astype(BF16)


def encode_kernel(
    near, near_hits, recv_rows, rows, recv_pre, stack,
    senders_out, slope_out, part_out, near_out, far_out, wide,
):
    half = recv_rows.shape[0] // 2
    fill(wide, near, wide.shape[1] // near.shape[0], 0)
    raw = rows[...] + mm_nt(near_hits[...], wide[...]).astype(BF16)
    latent, _ = silu_parts(mm(raw, stack[stack.shape[0] - raw.shape[1] :]))
    latent = latent.astype(BF16)
    senders_out[...] = latent
    pre = mm(latent, weight(stack, GS)) + recv_pre[...]
    value, slope = silu_parts(pre)
    slope_out[...] = slope.astype(BF16)
    sums = mm(recv_rows[...], value.astype(BF16))
    part_out[...] = sums
    even = even_on("lat")
    near_out[...] = jnp.where(even, sums[half:], sums[:half]).astype(BF16)
    far_out[...] = jnp.where(even, sums[:half], sums[half:]).astype(BF16)


def node_kernel(part, near, far, mesh_near, mesh_far, mesh_in, stack, mesh_out, slope_out):
    node_count = mesh_in.shape[0]
    rim = node_count // 2
    even = even_on("lat")
    left = jnp.where(even, far[...], near[...]).astype(F32)
    right = jnp.where(even, near[...], far[...]).astype(F32)
    total = part[...] + jnp.concatenate([left, right], axis=0)
    mesh_left = jnp.where(even, mesh_far[...], mesh_near[...])[rim:]
    mesh_right = jnp.where(even, mesh_near[...], mesh_far[...])[:rim]
    cycle = jnp.concatenate([mesh_left, mesh_in[...], mesh_right], axis=0)
    value, slope = silu_parts(mm(total.astype(BF16), weight(stack, GN)))
    mesh_out[...] = (cycle.astype(F32) + value).astype(BF16)
    slope_out[...] = slope


def process_own_kernel(own_hits, to_hits, own, stack, pre_out):
    rim = own.shape[0] // 4
    home = own[rim : own.shape[0] - rim]
    table = jnp.concatenate(halves(mm(own[...], weight(stack, MS))), axis=0)
    recv_table = jnp.concatenate(halves(mm(home, weight(stack, MR))), axis=0)
    pre_out[...] = mm(own_hits[...], table) + mm(to_hits[...], recv_table)


def process_kernel(
    own_pre, outer_hits, to_hits, from_rows, to_rows, near, own, far, d_out, stack,
    mesh_out, sums_out, recv_out, near_out, far_out,
):
    cycle = own.shape[0]
    node_count = cycle // 2
    rim = node_count // 2
    home = own[rim : rim + node_count]
    block = jnp.concatenate([near[...], far[...]], axis=0)
    table = jnp.concatenate(halves(mm(block, weight(stack, MS))), axis=0)
    pre = own_pre[...] + mm(outer_hits[...], table)
    value, slope = silu_parts(pre)
    gate = mm(mm(to_rows[...], value.astype(BF16)).astype(BF16), weight(stack, MN))
    gate_value, gate_slope = silu_parts(gate)
    mesh_out[...] = (home.astype(F32) + gate_value).astype(BF16)
    gate_two = (d_out[...].astype(F32) * gate_slope).astype(BF16)
    back = jnp.concatenate(halves(mm_nt(gate_two, weight(stack, MN))), axis=0)
    edge_slope = (mm(to_hits[...], back) * slope).astype(BF16)
    sums = mm(from_rows[...], edge_slope)
    recv_out[...] = mm(to_rows[...], edge_slope).astype(BF16)
    sums_out[...] = sums
    near_out[...] = sums[:cycle].astype(BF16)
    far_out[...] = sums[2 * cycle :].astype(BF16)


def block_of(x, dom_shift, lat_shift, doms, lats):
    cols = x.shape[1] // (doms * lats)
    dom = lax.rem(lax.axis_index("dom") + dom_shift, doms)
    index = dom * lats + lax.rem(lax.axis_index("lat") + lat_shift, lats)
    pick = x[:, :cols]
    for i in range(1, doms * lats):
        pick = jnp.where(index == i, x[:, i * cols : (i + 1) * cols], pick)
    return pick


def home_kernel(recv_sum, d_out, stack, senders, home_out, turned_out):
    home_out[...] = mm_nt(recv_sum[...], weight(stack, MR)) + d_out[...].astype(F32)
    turned_out[...] = senders[...].T


def cotangent_kernel(sums, near, far, home, part_out, near_out, far_out):
    cycle = near.shape[0]
    half = cycle // 2
    rim = half // 2
    total = sums[cycle : 2 * cycle] + near[...].astype(F32) + far[...].astype(F32)
    part_out[...] = total
    even = even_on("lat")
    near_out[:half] = jnp.where(even, total[half:], total[:half]).astype(BF16)
    near_out[half:] = jnp.where(even, home[rim:], home[:rim]).astype(BF16)
    far_out[:half] = jnp.where(even, total[:half], total[half:]).astype(BF16)
    far_out[half:] = jnp.where(even, home[:rim], home[rim:]).astype(BF16)


def gradient_block(recv_hits, back, edge_slope, senders, dom_shift, lat_shift, doms, lats):
    place = (dom_shift, lat_shift, doms, lats)
    slope = mm(recv_hits[...], block_of(back, *place))
    slope = slope * block_of(edge_slope, *place).astype(F32)
    return mm(senders[...], slope.astype(BF16))


def encode_grad_kernel(
    recv_hits, part, near, far, home, node_slope, stack, senders, edge_slope,
    sends, back_out, total_out,
):
    half = part.shape[0] // 2
    even = even_on("lat")
    left = jnp.where(even, far[...], near[...]).astype(F32)
    right = jnp.where(even, near[...], far[...]).astype(F32)
    total = part[...] + jnp.concatenate([left[:half], right[:half]], axis=0)
    total = total.astype(BF16)
    rest = jnp.concatenate([left[half:], home[...], right[half:]], axis=0)
    cot = rest + mm_nt(total, weight(stack, MS))
    gate_one = (cot * node_slope[...]).astype(BF16)
    back = jnp.concatenate(halves(mm_nt(gate_one, weight(stack, GN))), axis=0)
    back_out[...] = back
    lats = sends.shape[0] + 1
    doms = sends.shape[1] + 1
    for i in range(1, lats):
        for j in range(1, doms):
            block = gradient_block(recv_hits, back, edge_slope, senders, j, i, doms, lats)
            sends[i - 1, j - 1] = block.astype(BF16)
    for j in range(doms):
        total_out[j] = block_of(total, j, 0, doms, lats)


def kept_blocks_kernel(recv_hits, back, edge_slope, senders, after, kept):
    doms = kept.shape[0] + 1
    lats = back.shape[1] // kept.shape[2] // doms
    for j in range(1, doms):
        kept[j - 1] = gradient_block(recv_hits, back, edge_slope, senders, j, 0, doms, lats)


def rows_at(ref, place, partner):
    bands = lax.axis_size("band")
    rows = ref.shape[-2] // bands
    at = pl.multiple_of(lax.bitwise_xor(lax.axis_index("band"), partner) * rows, rows)
    return ref[(*place, pl.ds(at, rows))]


def add_kernel(kept, total, *refs):
    *came, first_out, second_out = refs
    bands = lax.axis_size("band")
    half = bands // 2
    rows = kept.shape[1] // bands
    for j in range(kept.shape[0]):
        for k in range(bands):
            block = rows_at(kept, (j,), k)
            for part in came:
                block = block + rows_at(part, (j,), k).astype(F32)
            out = first_out if k >= half else second_out
            at = (k % half) * rows
            out[j, at : at + rows] = block.astype(BF16)
        first_out[j, half * rows :] = total[j + 1]


def other_lats_kernel(recv_hits, back, edge_slope, senders, after, sends):
    lats = sends.shape[0] + 1
    doms = back.shape[1] // sends.shape[2] // lats
    for i in range(1, lats):
        block = gradient_block(recv_hits, back, edge_slope, senders, 0, i, doms, lats)
        sends[i - 1] = block.astype(BF16)


def own_block_kernel(recv_hits, back, edge_slope, senders, *refs):
    *came, out = refs
    lats = len(came) + 1
    doms = back.shape[1] // out.shape[1] // lats
    block = gradient_block(recv_hits, back, edge_slope, senders, 0, 0, doms, lats)
    for part in came:
        block = block + part[...].astype(F32)
    out[...] = block


def first_kernel(kept, total, nodes, *refs):
    doms = total.shape[0]
    came, (*sends_out, sums) = refs[: 2 * (doms - 1)], refs[2 * (doms - 1) :]
    came, came_nodes = came[: doms - 1], came[doms - 1 :]
    half = len(sends_out)
    rows = sends_out[0].shape[1]
    second = mm_tn(nodes[...], total[0])
    for part, part_nodes in zip(came, came_nodes):
        second = second + mm_tn(part_nodes[...], part[half * rows :])
    sums[...] = second
    for i, out in enumerate(sends_out):
        block = rows_at(kept, (), half + i)
        for part in came:
            block = block + part[i * rows : (i + 1) * rows].astype(F32)
        out[0] = block.astype(BF16)
        out[1] = rows_at(sums, (), half + i).astype(BF16)


def second_kernel(kept, sums, *refs):
    half = lax.axis_size("band") // 2
    came, outs = refs[:-half], refs[-half:]
    rows = outs[0].shape[1]
    for i, out in enumerate(outs):
        block = rows_at(kept, (), i)
        for part in came:
            block = block + part[i * rows : (i + 1) * rows].astype(F32)
        out[0] = block.astype(out.dtype)
        out[1] = rows_at(sums, (), i).astype(out.dtype)


def over_band_kernel(*refs):
    *came, own, first_out, second_out = refs
    for k, out in enumerate((first_out, second_out)):
        total = own[k]
        for part in came:
            total = total + part[k].astype(F32)
        out[...] = total


def call(kernel, outs, *args, scalars=(), scratch=()):
    in_specs = [
        pl.BlockSpec(memory_space=pltpu.SMEM if i in scalars else pltpu.VMEM)
        for i in range(len(args))
    ]
    return pl.pallas_call(
        kernel,
        out_shape=[jax.ShapeDtypeStruct(shape, dtype) for shape, dtype in outs],
        in_specs=in_specs,
        out_specs=[pl.BlockSpec(memory_space=pltpu.VMEM)] * len(outs),
        scratch_shapes=scratch,
        compiler_params=pltpu.CompilerParams(vmem_limit_bytes=16 << 20),
    )(*args)


def ring_pairings(count):
    far = [(i, (i + 1 if i % 2 else i - 1) % count) for i in range(count)]
    return [(i, i ^ 1) for i in range(count)], far


def line_pairings(bands, doms, lats):
    far = []
    for band in range(bands):
        other = band + 1 if band % 2 else band - 1
        for dom in range(doms):
            for lat in range(lats):
                here = (band * doms + dom) * lats + lat
                if 0 <= other < bands:
                    there = (other * doms + dom) * lats + lat
                else:
                    there = (band * doms + dom) * lats + (lat ^ 1)
                far.append((here, there))
    return [(i, i ^ 1) for i in range(bands)], far


def shifted(x, axis, shift):
    count = lax.axis_size(axis)
    return lax.ppermute(x, axis, [(i, (i + shift) % count) for i in range(count)])


def over_band(x, partner):
    count = lax.axis_size("band")
    return lax.ppermute(x, "band", [(b, b ^ partner) for b in range(count)])


def on_device(
    grid_in, w_grid, w_gs, w_gr, w_gn, w_ms, w_mr, w_mn, mesh_in, d_out,
    g2m_send, g2m_recv, g2m_count, mesh_send, mesh_recv, mesh_count,
):
    latent = w_grid.shape[1]
    variables = w_grid.shape[0]
    node_count = mesh_in.shape[0]
    cycle = 2 * node_count
    bands = lax.axis_size("band")
    sectors = lax.axis_size(("dom", "lat"))
    edges = g2m_send.shape[2]
    around = ("dom", "lat")
    whole = ("band", "dom", "lat")
    band_near, band_far = line_pairings(bands, lax.axis_size("dom"), lax.axis_size("lat"))
    ring_near, ring_far = ring_pairings(sectors)

    grid = jnp.transpose(grid_in, (0, 2, 1))
    pitch = -(-grid.shape[2] // LANES) * LANES
    band_rows = grid.shape[0]
    width = band_rows * pitch
    raw_near = lax.ppermute(grid, "band", band_near)
    raw_far = lax.ppermute(grid, whole, band_far)
    mesh_edges = mesh_send.shape[2]
    stack = jnp.concatenate([w_gs, w_gr, w_gn, w_ms, w_mr, w_mn, w_grid], axis=0)
    indices = jnp.concatenate([g2m_send, g2m_recv, mesh_send, mesh_recv], axis=2)
    (
        rows, recv_hits, recv_rows, own_hits, outer_hits, to_hits, from_rows, to_rows, *halo_hits
    ) = call(
        index_kernel,
        [
            ((edges, variables), BF16),
            ((edges, 2 * cycle), BF16),
            ((cycle, edges), BF16),
            ((mesh_edges, 2 * cycle), BF16),
            ((mesh_edges, 4 * cycle), BF16),
            ((mesh_edges, 2 * node_count), BF16),
            ((3 * cycle, mesh_edges), BF16),
            ((node_count, mesh_edges), BF16),
            ((edges, width), BF16),
            ((edges, width), BF16),
        ],
        g2m_count, mesh_count, indices, grid,
        scalars=(0, 1),
        scratch=[pltpu.VMEM((variables, width), BF16)],
    )
    late_mesh, rows = lax.optimization_barrier((mesh_in, rows))
    mesh_near = lax.ppermute(late_mesh, around, ring_near)
    mesh_far = lax.ppermute(late_mesh, around, ring_far)
    (recv_pre,) = call(
        receiver_kernel,
        [((edges, latent), F32)],
        mesh_near, mesh_far, mesh_in, recv_hits, stack,
    )
    near_hits, far_hits = halo_hits
    (rows,) = call(
        gather_kernel,
        [((edges, variables), BF16)],
        raw_far, far_hits, rows,
        scratch=[pltpu.VMEM((variables, width), BF16)],
    )
    senders, edge_slope, part, to_near, to_far = call(
        encode_kernel,
        [
            ((edges, latent), BF16),
            ((edges, latent), BF16),
            ((cycle, latent), F32),
            ((node_count, latent), BF16),
            ((node_count, latent), BF16),
        ],
        raw_near, near_hits, recv_rows, rows, recv_pre, stack,
        scratch=[pltpu.VMEM((variables, width), BF16)],
    )
    from_far = lax.ppermute(to_far, around, ring_far)
    from_near = lax.ppermute(to_near, around, ring_near)
    mesh_one, node_slope = call(
        node_kernel,
        [((cycle, latent), BF16), ((cycle, latent), F32)],
        part, from_near, from_far, mesh_near, mesh_far, mesh_in, stack,
    )
    one_near = lax.ppermute(mesh_one, "band", band_near)
    one_far = lax.ppermute(mesh_one, whole, band_far)
    doms = lax.axis_size("dom")
    lats = lax.axis_size("lat")
    dom_nodes = [shifted(mesh_one, "dom", i + 1) for i in range(doms - 1)]
    (own_pre,) = call(
        process_own_kernel, [((mesh_edges, latent), F32)], own_hits, to_hits, mesh_one, stack
    )
    mesh_out, sums, recv_sum, to_near, to_far = call(
        process_kernel,
        [
            ((node_count, latent), BF16),
            ((3 * cycle, latent), F32),
            ((node_count, latent), BF16),
            ((cycle, latent), BF16),
            ((cycle, latent), BF16),
        ],
        own_pre, outer_hits, to_hits, from_rows, to_rows, one_near, mesh_one, one_far, d_out,
        stack,
    )
    from_near = lax.ppermute(to_near, "band", band_near)
    from_far = lax.ppermute(to_far, whole, band_far)
    from_near, *dom_nodes = lax.optimization_barrier((from_near, *dom_nodes))
    home, senders = call(
        home_kernel,
        [((node_count, latent), F32), ((latent, edges), BF16)],
        recv_sum, d_out, stack, senders,
    )
    message = (node_count + node_count // 2, latent)
    part, to_near, to_far = call(
        cotangent_kernel,
        [((cycle, latent), F32), (message, BF16), (message, BF16)],
        sums, from_near, from_far, home,
    )
    from_far = lax.ppermute(to_far, around, ring_far)
    from_near = lax.ppermute(to_near, around, ring_near)

    cols = latent // sectors
    rows = latent // bands
    sends, back, total = call(
        encode_grad_kernel,
        [
            ((lats - 1, doms - 1, latent, cols), BF16),
            ((2 * cycle, latent), BF16),
            ((doms, cycle, cols), BF16),
        ],
        recv_hits, part, from_near, from_far, home, node_slope, stack, senders, edge_slope,
    )
    edge = (recv_hits, back, edge_slope, senders)
    came = [shifted(sends[i], "lat", i + 1) for i in range(lats - 1)]
    block = (latent, cols)
    (kept,) = call(kept_blocks_kernel, [((doms - 1,) + block, F32)], *edge, sends)
    (own_sends,) = call(other_lats_kernel, [((lats - 1,) + block, BF16)], *edge, sends)
    own_came = [shifted(own_sends[i], "lat", i + 1) for i in range(lats - 1)]
    kept, own_sends = lax.optimization_barrier((kept, own_sends))
    half = bands // 2
    first, second = call(
        add_kernel,
        [
            ((doms - 1, half * rows + cycle, cols), BF16),
            ((doms - 1, half * rows, cols), BF16),
        ],
        kept, total, *came,
    )
    first = [shifted(first[i], "dom", i + 1) for i in range(doms - 1)]
    second = [shifted(second[i], "dom", i + 1) for i in range(doms - 1)]
    (kept,) = call(own_block_kernel, [(block, F32)], *edge, *own_came)
    pair = (2, rows, cols)
    *far_sends, sums = call(
        first_kernel,
        [(pair, BF16)] * half + [(block, F32)],
        kept, total, mesh_one, *first, *dom_nodes,
    )
    came = [over_band(x, half + i) for i, x in reversed(list(enumerate(far_sends)))]
    own, *near_sends = call(
        second_kernel,
        [(pair, F32)] + [(pair, BF16)] * (half - 1),
        kept, sums, *second,
    )
    came += [over_band(x, i + 1) for i, x in reversed(list(enumerate(near_sends)))]
    tile = ((rows, cols), F32)
    grad_gs, grad_ms = call(over_band_kernel, [tile, tile], *came, own)
    return mesh_out, grad_gs, grad_ms


def solution(mesh):
    flat = P(("groups", "band", "dom", "lat"), None)
    grid = P(("groups", "band"), ("dom", "lat"), None)
    count = P(("groups", "band"), ("dom", "lat"))
    placed = (grid,) + (P(),) * 7 + (flat, flat) + (grid, grid, count) * 2
    return jax.shard_map(
        on_device,
        mesh=mesh,
        in_specs=placed,
        out_specs=(flat, count, count),
        check_vma=False,
    )
```

```python
import jax
import jax.numpy as jnp
from jax import lax
from jax.experimental import pallas as pl
from jax.experimental.pallas import tpu as pltpu
from jax.sharding import PartitionSpec as P

F32 = jnp.float32
BF16 = jnp.bfloat16
LANES = 128
GS, GR, GN, MS, MR, MN = range(6)


def mm(a, b):
    return jnp.dot(a, b, preferred_element_type=F32)


def mm_nt(a, b):
    return lax.dot_general(a, b, (((1,), (1,)), ((), ())), preferred_element_type=F32)


def mm_tn(a, b):
    return lax.dot_general(a, b, (((0,), (0,)), ((), ())), preferred_element_type=F32)


def halves(x):
    high = x.astype(BF16)
    return high, (x - high.astype(F32)).astype(BF16)


def silu_parts(x):
    g = 0.5 * jnp.tanh(0.5 * x) + 0.5
    value = x * g
    return value, g + value * (1.0 - g)


def ones_at(mask):
    return jnp.where(mask, 1.0, 0.0).astype(BF16)


def columns(row):
    count = row.shape[1]
    parts = [
        jnp.broadcast_to(row[:, i : i + LANES], (LANES, LANES)).T
        for i in range(0, count, LANES)
    ]
    return parts[0] if len(parts) == 1 else jnp.concatenate(parts, axis=0)


def hits_from(cols, width, period, start=0):
    parts = []
    for i in range(0, width, LANES):
        size = min(LANES, width - i)
        lane = lax.broadcasted_iota(jnp.int32, (cols.shape[0], size), 1) + i
        if period < width:
            lane = lax.rem(lane, period)
        parts.append(ones_at(cols[:, :size] == lane + start))
    return parts[0] if len(parts) == 1 else jnp.concatenate(parts, axis=1)


def hits_to(row, count):
    return ones_at(lax.broadcasted_iota(jnp.int32, (count, row.shape[1]), 0) == row)


def live_only(row, count, first=0):
    slot = lax.broadcasted_iota(jnp.int32, row.shape, 1) + first
    return jnp.where(slot < count, row, -1)


def weight(stack, index):
    latent = stack.shape[1]
    return stack[index * latent : (index + 1) * latent]


def even_on(axis):
    return lax.rem(lax.axis_index(axis), 2) == 0


def spread(index, blocks, cols, pitch):
    extra = jnp.zeros_like(index)
    for block in range(1, blocks):
        extra = extra + jnp.where(index >= block * cols, pitch - cols, 0)
    return index + extra


def fill(wide, blocks, pitch, first):
    cols = blocks.shape[2]
    for k in range(blocks.shape[0]):
        at = first + k * pitch
        wide[:, at : at + cols] = blocks[k]
        if cols < pitch:
            wide[:, at + cols : at + pitch] = jnp.zeros(
                (wide.shape[0], pitch - cols), wide.dtype
            )


def index_kernel(
    count, mesh_count, indices, grid,
    own_out, recv_hits, recv_rows, own_hits, outer_hits, to_hits, from_rows, to_rows, near_hits, far_hits, wide,
):
    edges = recv_hits.shape[0]
    mesh_edges = to_hits.shape[0]
    send, recv, mesh_send, mesh_recv = (
        indices[0, :, first : first + size]
        for first, size in (
            (0, edges),
            (edges, edges),
            (2 * edges, mesh_edges),
            (2 * edges + mesh_edges, mesh_edges),
        )
    )
    band_rows, _, cols = grid.shape
    pitch = wide.shape[1] // band_rows
    width = band_rows * pitch
    cycle = recv_rows.shape[0]
    node_count = to_rows.shape[0]
    even_band = even_on("band")
    fill(wide, grid, pitch, 0)
    near_base = jnp.where(even_band, 2 * width, 0)
    far_base = jnp.where(even_band, 0, 2 * width)
    block = 256
    for first in range(0, edges, block):
        part_of = slice(first, first + block)
        index = columns(spread(send[:, part_of], 3 * band_rows, cols, pitch))
        own_hit = hits_from(index, width, width, width)
        own_out[part_of] = mm_nt(own_hit, wide[...]).astype(BF16)
        near_hits[part_of] = hits_from(index, width, width, near_base)
        far_hits[part_of] = hits_from(index, width, width, far_base)
        target = live_only(recv[:, part_of], count[0, 0], first)
        recv_hits[part_of] = hits_from(columns(target), 2 * cycle, cycle)
        recv_rows[:, part_of] = hits_to(target, cycle)
    raw = mesh_send
    inner = (raw >= cycle) & (raw < 2 * cycle)
    above_near = jnp.where(raw < cycle, raw + cycle, raw - 2 * cycle)
    below_near = jnp.where(raw < cycle, raw, raw - cycle)
    outer = jnp.where(inner, -1, jnp.where(even_band, above_near, below_near))
    target = live_only(mesh_recv, mesh_count[0, 0])
    own_hits[...] = hits_from(columns(jnp.where(inner, raw - cycle, -1)), 2 * cycle, cycle)
    outer_hits[...] = hits_from(columns(outer), 4 * cycle, 2 * cycle)
    to_hits[...] = hits_from(columns(target), 2 * node_count, node_count)
    source = jnp.where(inner, raw, jnp.where(outer < cycle, outer, outer + cycle))
    from_rows[...] = hits_to(source, 3 * cycle)
    to_rows[...] = hits_to(target, node_count)


def receiver_kernel(near, far, mesh_in, recv_hits, stack, pre_out):
    node_count = mesh_in.shape[0]
    rim = node_count // 2
    even = even_on("lat")
    left = jnp.where(even, far[...], near[...])[rim:]
    right = jnp.where(even, near[...], far[...])[:rim]
    cycle = jnp.concatenate([left, mesh_in[...], right], axis=0)
    table = jnp.concatenate(halves(mm(cycle, weight(stack, GR))), axis=0)
    pre_out[...] = mm(recv_hits[...], table)


def gather_kernel(halo, hits, rows, rows_out, wide):
    fill(wide, halo, wide.shape[1] // halo.shape[0], 0)
    rows_out[...] = rows[...] + mm_nt(hits[...], wide[...]).astype(BF16)


def encode_kernel(
    near, near_hits, recv_rows, rows, recv_pre, stack,
    senders_out, slope_out, part_out, near_out, far_out, wide,
):
    half = recv_rows.shape[0] // 2
    fill(wide, near, wide.shape[1] // near.shape[0], 0)
    block = rows.shape[0] // 2
    sums = None
    for first in range(0, rows.shape[0], block):
        part_of = slice(first, first + block)
        raw = rows[part_of] + mm_nt(near_hits[part_of], wide[...]).astype(BF16)
        latent, _ = silu_parts(mm(raw, stack[stack.shape[0] - raw.shape[1] :]))
        latent = latent.astype(BF16)
        senders_out[part_of] = latent
        pre = mm(latent, weight(stack, GS)) + recv_pre[part_of]
        value, slope = silu_parts(pre)
        slope_out[part_of] = slope.astype(BF16)
        part = mm(recv_rows[:, part_of], value.astype(BF16))
        sums = part if sums is None else sums + part
    part_out[...] = sums
    even = even_on("lat")
    near_out[...] = jnp.where(even, sums[half:], sums[:half]).astype(BF16)
    far_out[...] = jnp.where(even, sums[:half], sums[half:]).astype(BF16)


def node_kernel(part, near, far, mesh_near, mesh_far, mesh_in, stack, mesh_out, slope_out):
    node_count = mesh_in.shape[0]
    rim = node_count // 2
    even = even_on("lat")
    left = jnp.where(even, far[...], near[...]).astype(F32)
    right = jnp.where(even, near[...], far[...]).astype(F32)
    total = part[...] + jnp.concatenate([left, right], axis=0)
    mesh_left = jnp.where(even, mesh_far[...], mesh_near[...])[rim:]
    mesh_right = jnp.where(even, mesh_near[...], mesh_far[...])[:rim]
    cycle = jnp.concatenate([mesh_left, mesh_in[...], mesh_right], axis=0)
    value, slope = silu_parts(mm(total.astype(BF16), weight(stack, GN)))
    mesh_out[...] = (cycle.astype(F32) + value).astype(BF16)
    slope_out[...] = slope


def process_own_kernel(own_hits, to_hits, own, stack, pre_out):
    rim = own.shape[0] // 4
    home = own[rim : own.shape[0] - rim]
    table = jnp.concatenate(halves(mm(own[...], weight(stack, MS))), axis=0)
    recv_table = jnp.concatenate(halves(mm(home, weight(stack, MR))), axis=0)
    pre_out[...] = mm(own_hits[...], table) + mm(to_hits[...], recv_table)


def process_kernel(
    own_pre, outer_hits, to_hits, from_rows, to_rows, near, own, far, d_out, stack,
    mesh_out, sums_out, recv_out, near_out, far_out,
):
    cycle = own.shape[0]
    node_count = cycle // 2
    rim = node_count // 2
    home = own[rim : rim + node_count]
    block = jnp.concatenate([near[...], far[...]], axis=0)
    table = jnp.concatenate(halves(mm(block, weight(stack, MS))), axis=0)
    pre = own_pre[...] + mm(outer_hits[...], table)
    value, slope = silu_parts(pre)
    gate = mm(mm(to_rows[...], value.astype(BF16)).astype(BF16), weight(stack, MN))
    gate_value, gate_slope = silu_parts(gate)
    mesh_out[...] = (home.astype(F32) + gate_value).astype(BF16)
    gate_two = (d_out[...].astype(F32) * gate_slope).astype(BF16)
    back = jnp.concatenate(halves(mm_nt(gate_two, weight(stack, MN))), axis=0)
    edge_slope = (mm(to_hits[...], back) * slope).astype(BF16)
    sums = mm(from_rows[...], edge_slope)
    recv_out[...] = mm(to_rows[...], edge_slope).astype(BF16)
    sums_out[...] = sums
    near_out[...] = sums[:cycle].astype(BF16)
    far_out[...] = sums[2 * cycle :].astype(BF16)


def block_of(x, dom_shift, lat_shift, doms, lats):
    cols = x.shape[1] // (doms * lats)
    dom = lax.rem(lax.axis_index("dom") + dom_shift, doms)
    index = dom * lats + lax.rem(lax.axis_index("lat") + lat_shift, lats)
    pick = x[:, :cols]
    for i in range(1, doms * lats):
        pick = jnp.where(index == i, x[:, i * cols : (i + 1) * cols], pick)
    return pick


def home_kernel(recv_sum, d_out, stack, senders, home_out, turned_out):
    home_out[...] = mm_nt(recv_sum[...], weight(stack, MR)) + d_out[...].astype(F32)
    turned_out[...] = senders[...].T


def cotangent_kernel(sums, near, far, home, part_out, near_out, far_out):
    cycle = near.shape[0]
    half = cycle // 2
    rim = half // 2
    total = sums[cycle : 2 * cycle] + near[...].astype(F32) + far[...].astype(F32)
    part_out[...] = total
    even = even_on("lat")
    near_out[:half] = jnp.where(even, total[half:], total[:half]).astype(BF16)
    near_out[half:] = jnp.where(even, home[rim:], home[:rim]).astype(BF16)
    far_out[:half] = jnp.where(even, total[:half], total[half:]).astype(BF16)
    far_out[half:] = jnp.where(even, home[:rim], home[rim:]).astype(BF16)


def gradient_block(recv_hits, back, edge_slope, senders, dom_shift, lat_shift, doms, lats):
    place = (dom_shift, lat_shift, doms, lats)
    slope = mm(recv_hits[...], block_of(back, *place))
    slope = slope * block_of(edge_slope, *place).astype(F32)
    return mm(senders[...], slope.astype(BF16))


def encode_grad_kernel(
    recv_hits, part, near, far, home, node_slope, stack, senders, edge_slope,
    sends, back_out, total_out,
):
    half = part.shape[0] // 2
    even = even_on("lat")
    left = jnp.where(even, far[...], near[...]).astype(F32)
    right = jnp.where(even, near[...], far[...]).astype(F32)
    total = part[...] + jnp.concatenate([left[:half], right[:half]], axis=0)
    total = total.astype(BF16)
    rest = jnp.concatenate([left[half:], home[...], right[half:]], axis=0)
    cot = rest + mm_nt(total, weight(stack, MS))
    gate_one = (cot * node_slope[...]).astype(BF16)
    back = jnp.concatenate(halves(mm_nt(gate_one, weight(stack, GN))), axis=0)
    back_out[...] = back
    lats = sends.shape[0] + 1
    doms = sends.shape[1] + 1
    for i in range(1, lats):
        for j in range(1, doms):
            block = gradient_block(recv_hits, back, edge_slope, senders, j, i, doms, lats)
            sends[i - 1, j - 1] = block.astype(BF16)
    for j in range(doms):
        total_out[j] = block_of(total, j, 0, doms, lats)


def kept_blocks_kernel(recv_hits, back, edge_slope, senders, after, kept):
    doms = kept.shape[0] + 1
    lats = back.shape[1] // kept.shape[2] // doms
    for j in range(1, doms):
        kept[j - 1] = gradient_block(recv_hits, back, edge_slope, senders, j, 0, doms, lats)


def rows_at(ref, place, partner):
    bands = lax.axis_size("band")
    rows = ref.shape[-2] // bands
    at = pl.multiple_of(lax.bitwise_xor(lax.axis_index("band"), partner) * rows, rows)
    return ref[(*place, pl.ds(at, rows))]


def add_kernel(kept, total, *refs):
    *came, first_out, second_out = refs
    bands = lax.axis_size("band")
    rows = kept.shape[1] // bands
    near = second_out.shape[1] // rows
    for j in range(kept.shape[0]):
        for k in range(bands):
            block = rows_at(kept, (j,), k)
            for part in came:
                block = block + rows_at(part, (j,), k).astype(F32)
            out, at = (first_out, k - near) if k >= near else (second_out, k)
            at = at * rows
            out[j, at : at + rows] = block.astype(BF16)
        first_out[j, (bands - near) * rows :] = total[j + 1]


def other_lats_kernel(recv_hits, back, edge_slope, senders, after, sends):
    lats = sends.shape[0] + 1
    doms = back.shape[1] // sends.shape[2] // lats
    for i in range(1, lats):
        block = gradient_block(recv_hits, back, edge_slope, senders, 0, i, doms, lats)
        sends[i - 1] = block.astype(BF16)


def own_block_kernel(recv_hits, back, edge_slope, senders, *refs):
    *came, out = refs
    lats = len(came) + 1
    doms = back.shape[1] // out.shape[1] // lats
    block = gradient_block(recv_hits, back, edge_slope, senders, 0, 0, doms, lats)
    for part in came:
        block = block + part[...].astype(F32)
    out[...] = block


def first_kernel(kept, total, nodes, *refs):
    doms = total.shape[0]
    came, (*sends_out, sums) = refs[: 2 * (doms - 1)], refs[2 * (doms - 1) :]
    came, came_nodes = came[: doms - 1], came[doms - 1 :]
    far = len(sends_out)
    near = lax.axis_size("band") - far
    rows = sends_out[0].shape[1]
    second = mm_tn(nodes[...], total[0])
    for part, part_nodes in zip(came, came_nodes):
        second = second + mm_tn(part_nodes[...], part[far * rows :])
    sums[...] = second
    for i, out in enumerate(sends_out):
        block = rows_at(kept, (), near + i)
        for part in came:
            block = block + part[i * rows : (i + 1) * rows].astype(F32)
        out[0] = block.astype(BF16)
        out[1] = rows_at(sums, (), near + i).astype(BF16)


def second_kernel(kept, sums, *refs):
    doms = lax.axis_size("dom")
    came, outs = refs[: doms - 1], refs[doms - 1 :]
    rows = outs[0].shape[1]
    for i, out in enumerate(outs):
        block = rows_at(kept, (), i)
        for part in came:
            block = block + part[i * rows : (i + 1) * rows].astype(F32)
        out[0] = block.astype(out.dtype)
        out[1] = rows_at(sums, (), i).astype(out.dtype)


def over_band_kernel(*refs):
    *came, own, first_out, second_out = refs
    for k, out in enumerate((first_out, second_out)):
        total = own[k]
        for part in came:
            total = total + part[k].astype(F32)
        out[...] = total


def call(kernel, outs, *args, scalars=(), scratch=()):
    in_specs = [
        pl.BlockSpec(memory_space=pltpu.SMEM if i in scalars else pltpu.VMEM)
        for i in range(len(args))
    ]
    return pl.pallas_call(
        kernel,
        out_shape=[jax.ShapeDtypeStruct(shape, dtype) for shape, dtype in outs],
        in_specs=in_specs,
        out_specs=[pl.BlockSpec(memory_space=pltpu.VMEM)] * len(outs),
        scratch_shapes=scratch,
        compiler_params=pltpu.CompilerParams(vmem_limit_bytes=16 << 20),
    )(*args)


def ring_pairings(count):
    far = [(i, (i + 1 if i % 2 else i - 1) % count) for i in range(count)]
    return [(i, i ^ 1) for i in range(count)], far


def line_pairings(bands, doms, lats):
    far = []
    for band in range(bands):
        other = band + 1 if band % 2 else band - 1
        for dom in range(doms):
            for lat in range(lats):
                here = (band * doms + dom) * lats + lat
                if 0 <= other < bands:
                    there = (other * doms + dom) * lats + lat
                else:
                    there = (band * doms + dom) * lats + (lat ^ 1)
                far.append((here, there))
    return [(i, i ^ 1) for i in range(bands)], far


def shifted(x, axis, shift):
    count = lax.axis_size(axis)
    return lax.ppermute(x, axis, [(i, (i + shift) % count) for i in range(count)])


def over_band(x, partner):
    count = lax.axis_size("band")
    return lax.ppermute(x, "band", [(b, b ^ partner) for b in range(count)])


def on_device(
    grid_in, w_grid, w_gs, w_gr, w_gn, w_ms, w_mr, w_mn, mesh_in, d_out,
    g2m_send, g2m_recv, g2m_count, mesh_send, mesh_recv, mesh_count,
):
    latent = w_grid.shape[1]
    variables = w_grid.shape[0]
    node_count = mesh_in.shape[0]
    cycle = 2 * node_count
    bands = lax.axis_size("band")
    sectors = lax.axis_size(("dom", "lat"))
    edges = g2m_send.shape[2]
    around = ("dom", "lat")
    whole = ("band", "dom", "lat")
    band_near, band_far = line_pairings(bands, lax.axis_size("dom"), lax.axis_size("lat"))
    ring_near, ring_far = ring_pairings(sectors)

    grid = jnp.transpose(grid_in, (0, 2, 1))
    pitch = -(-grid.shape[2] // LANES) * LANES
    band_rows = grid.shape[0]
    width = band_rows * pitch
    raw_near = lax.ppermute(grid, "band", band_near)
    raw_far = lax.ppermute(grid, whole, band_far)
    mesh_edges = mesh_send.shape[2]
    stack = jnp.concatenate([w_gs, w_gr, w_gn, w_ms, w_mr, w_mn, w_grid], axis=0)
    indices = jnp.concatenate([g2m_send, g2m_recv, mesh_send, mesh_recv], axis=2)
    (
        rows, recv_hits, recv_rows, own_hits, outer_hits, to_hits, from_rows, to_rows, *halo_hits
    ) = call(
        index_kernel,
        [
            ((edges, variables), BF16),
            ((edges, 2 * cycle), BF16),
            ((cycle, edges), BF16),
            ((mesh_edges, 2 * cycle), BF16),
            ((mesh_edges, 4 * cycle), BF16),
            ((mesh_edges, 2 * node_count), BF16),
            ((3 * cycle, mesh_edges), BF16),
            ((node_count, mesh_edges), BF16),
            ((edges, width), BF16),
            ((edges, width), BF16),
        ],
        g2m_count, mesh_count, indices, grid,
        scalars=(0, 1),
        scratch=[pltpu.VMEM((variables, width), BF16)],
    )
    late_mesh, rows = lax.optimization_barrier((mesh_in, rows))
    mesh_near = lax.ppermute(late_mesh, around, ring_near)
    mesh_far = lax.ppermute(late_mesh, around, ring_far)
    (recv_pre,) = call(
        receiver_kernel,
        [((edges, latent), F32)],
        mesh_near, mesh_far, mesh_in, recv_hits, stack,
    )
    near_hits, far_hits = halo_hits
    (rows,) = call(
        gather_kernel,
        [((edges, variables), BF16)],
        raw_far, far_hits, rows,
        scratch=[pltpu.VMEM((variables, width), BF16)],
    )
    senders, edge_slope, part, to_near, to_far = call(
        encode_kernel,
        [
            ((edges, latent), BF16),
            ((edges, latent), BF16),
            ((cycle, latent), F32),
            ((node_count, latent), BF16),
            ((node_count, latent), BF16),
        ],
        raw_near, near_hits, recv_rows, rows, recv_pre, stack,
        scratch=[pltpu.VMEM((variables, width), BF16)],
    )
    from_far = lax.ppermute(to_far, around, ring_far)
    from_near = lax.ppermute(to_near, around, ring_near)
    mesh_one, node_slope = call(
        node_kernel,
        [((cycle, latent), BF16), ((cycle, latent), F32)],
        part, from_near, from_far, mesh_near, mesh_far, mesh_in, stack,
    )
    one_near = lax.ppermute(mesh_one, "band", band_near)
    one_far = lax.ppermute(mesh_one, whole, band_far)
    doms = lax.axis_size("dom")
    lats = lax.axis_size("lat")
    dom_nodes = [shifted(mesh_one, "dom", i + 1) for i in range(doms - 1)]
    (own_pre,) = call(
        process_own_kernel, [((mesh_edges, latent), F32)], own_hits, to_hits, mesh_one, stack
    )
    mesh_out, sums, recv_sum, to_near, to_far = call(
        process_kernel,
        [
            ((node_count, latent), BF16),
            ((3 * cycle, latent), F32),
            ((node_count, latent), BF16),
            ((cycle, latent), BF16),
            ((cycle, latent), BF16),
        ],
        own_pre, outer_hits, to_hits, from_rows, to_rows, one_near, mesh_one, one_far, d_out,
        stack,
    )
    from_near = lax.ppermute(to_near, "band", band_near)
    from_far = lax.ppermute(to_far, whole, band_far)
    from_near, *dom_nodes = lax.optimization_barrier((from_near, *dom_nodes))
    home, senders = call(
        home_kernel,
        [((node_count, latent), F32), ((latent, edges), BF16)],
        recv_sum, d_out, stack, senders,
    )
    message = (node_count + node_count // 2, latent)
    part, to_near, to_far = call(
        cotangent_kernel,
        [((cycle, latent), F32), (message, BF16), (message, BF16)],
        sums, from_near, from_far, home,
    )
    from_far = lax.ppermute(to_far, around, ring_far)
    from_near = lax.ppermute(to_near, around, ring_near)

    cols = latent // sectors
    rows = latent // bands
    sends, back, total = call(
        encode_grad_kernel,
        [
            ((lats - 1, doms - 1, latent, cols), BF16),
            ((2 * cycle, latent), BF16),
            ((doms, cycle, cols), BF16),
        ],
        recv_hits, part, from_near, from_far, home, node_slope, stack, senders, edge_slope,
    )
    edge = (recv_hits, back, edge_slope, senders)
    came = [shifted(sends[i], "lat", i + 1) for i in range(lats - 1)]
    block = (latent, cols)
    (kept,) = call(kept_blocks_kernel, [((doms - 1,) + block, F32)], *edge, sends)
    (own_sends,) = call(other_lats_kernel, [((lats - 1,) + block, BF16)], *edge, sends)
    own_came = [shifted(own_sends[i], "lat", i + 1) for i in range(lats - 1)]
    kept, own_sends = lax.optimization_barrier((kept, own_sends))
    far = bands // 2
    first, second = call(
        add_kernel,
        [
            ((doms - 1, far * rows + cycle, cols), BF16),
            ((doms - 1, (bands - far) * rows, cols), BF16),
        ],
        kept, total, *came,
    )
    first = [shifted(first[i], "dom", i + 1) for i in range(doms - 1)]
    second = [shifted(second[i], "dom", i + 1) for i in range(doms - 1)]
    (kept,) = call(own_block_kernel, [(block, F32)], *edge, *own_came)
    pair = (2, rows, cols)
    *far_sends, sums = call(
        first_kernel,
        [(pair, BF16)] * far + [(block, F32)],
        kept, total, mesh_one, *first, *dom_nodes,
    )
    came = [over_band(x, bands - far + i) for i, x in reversed(list(enumerate(far_sends)))]
    own, *near_sends = call(
        second_kernel,
        [(pair, F32)] + [(pair, BF16)] * (bands - far - 1),
        kept, sums, *second,
    )
    came += [over_band(x, i + 1) for i, x in reversed(list(enumerate(near_sends)))]
    tile = ((rows, cols), F32)
    grad_gs, grad_ms = call(over_band_kernel, [tile, tile], *came, own)
    return mesh_out, grad_gs, grad_ms


def solution(mesh):
    flat = P(("groups", "band", "dom", "lat"), None)
    grid = P(("groups", "band"), ("dom", "lat"), None)
    count = P(("groups", "band"), ("dom", "lat"))
    placed = (grid,) + (P(),) * 7 + (flat, flat) + (grid, grid, count) * 2
    return jax.shard_map(
        on_device,
        mesh=mesh,
        in_specs=placed,
        out_specs=(flat, count, count),
        check_vma=False,
    )
```

```python
import jax
import jax.numpy as jnp
from jax import lax
from jax.experimental import pallas as pl
from jax.experimental.pallas import tpu as pltpu
from jax.sharding import PartitionSpec as P

F32 = jnp.float32
BF16 = jnp.bfloat16
LANES = 128
GS, GR, GN, MS, MR, MN = range(6)


def mm(a, b):
    return jnp.dot(a, b, preferred_element_type=F32)


def mm_nt(a, b):
    return lax.dot_general(a, b, (((1,), (1,)), ((), ())), preferred_element_type=F32)


def mm_tn(a, b):
    return lax.dot_general(a, b, (((0,), (0,)), ((), ())), preferred_element_type=F32)


def halves(x):
    high = x.astype(BF16)
    return high, (x - high.astype(F32)).astype(BF16)


def silu_parts(x):
    g = 0.5 * jnp.tanh(0.5 * x) + 0.5
    value = x * g
    return value, g + value * (1.0 - g)


def ones_at(mask):
    return jnp.where(mask, 1.0, 0.0).astype(BF16)


def columns(row):
    count = row.shape[1]
    parts = [
        jnp.broadcast_to(row[:, i : i + LANES], (LANES, LANES)).T
        for i in range(0, count, LANES)
    ]
    return parts[0] if len(parts) == 1 else jnp.concatenate(parts, axis=0)


def hits_from(cols, width, period, start=0):
    parts = []
    for i in range(0, width, LANES):
        size = min(LANES, width - i)
        lane = lax.broadcasted_iota(jnp.int32, (cols.shape[0], size), 1) + i
        if period < width:
            lane = lax.rem(lane, period)
        parts.append(ones_at(cols[:, :size] == lane + start))
    return parts[0] if len(parts) == 1 else jnp.concatenate(parts, axis=1)


def hits_to(row, count):
    return ones_at(lax.broadcasted_iota(jnp.int32, (count, row.shape[1]), 0) == row)


def live_only(row, count, first=0):
    slot = lax.broadcasted_iota(jnp.int32, row.shape, 1) + first
    return jnp.where(slot < count, row, -1)


def weight(stack, index):
    latent = stack.shape[1]
    return stack[index * latent : (index + 1) * latent]


def even_on(axis):
    return lax.rem(lax.axis_index(axis), 2) == 0


def spread(index, blocks, cols, pitch):
    extra = jnp.zeros_like(index)
    for block in range(1, blocks):
        extra = extra + jnp.where(index >= block * cols, pitch - cols, 0)
    return index + extra


def fill(wide, blocks, pitch, first):
    cols = blocks.shape[2]
    for k in range(blocks.shape[0]):
        at = first + k * pitch
        wide[:, at : at + cols] = blocks[k]
        if cols < pitch:
            wide[:, at + cols : at + pitch] = jnp.zeros(
                (wide.shape[0], pitch - cols), wide.dtype
            )


def index_kernel(
    count, mesh_count, indices, grid,
    own_out, recv_hits, recv_rows, own_hits, outer_hits, to_hits, from_rows, to_rows, near_hits, far_hits, wide,
):
    edges = recv_hits.shape[0]
    mesh_edges = to_hits.shape[0]
    send, recv, mesh_send, mesh_recv = (
        indices[0, :, first : first + size]
        for first, size in (
            (0, edges),
            (edges, edges),
            (2 * edges, mesh_edges),
            (2 * edges + mesh_edges, mesh_edges),
        )
    )
    band_rows, _, cols = grid.shape
    pitch = wide.shape[1] // band_rows
    width = band_rows * pitch
    cycle = recv_rows.shape[0]
    node_count = to_rows.shape[0]
    even_band = even_on("band")
    fill(wide, grid, pitch, 0)
    near_base = jnp.where(even_band, 2 * width, 0)
    far_base = jnp.where(even_band, 0, 2 * width)
    block = 256
    for first in range(0, edges, block):
        part_of = slice(first, first + block)
        index = columns(spread(send[:, part_of], 3 * band_rows, cols, pitch))
        own_hit = hits_from(index, width, width, width)
        own_out[part_of] = mm_nt(own_hit, wide[...]).astype(BF16)
        near_hits[part_of] = hits_from(index, width, width, near_base)
        far_hits[part_of] = hits_from(index, width, width, far_base)
        target = live_only(recv[:, part_of], count[0, 0], first)
        recv_hits[part_of] = hits_from(columns(target), 2 * cycle, cycle)
        recv_rows[:, part_of] = hits_to(target, cycle)
    raw = mesh_send
    inner = (raw >= cycle) & (raw < 2 * cycle)
    above_near = jnp.where(raw < cycle, raw + cycle, raw - 2 * cycle)
    below_near = jnp.where(raw < cycle, raw, raw - cycle)
    outer = jnp.where(inner, -1, jnp.where(even_band, above_near, below_near))
    target = live_only(mesh_recv, mesh_count[0, 0])
    own_hits[...] = hits_from(columns(jnp.where(inner, raw - cycle, -1)), 2 * cycle, cycle)
    outer_hits[...] = hits_from(columns(outer), 4 * cycle, 2 * cycle)
    to_hits[...] = hits_from(columns(target), 2 * node_count, node_count)
    source = jnp.where(inner, raw, jnp.where(outer < cycle, outer, outer + cycle))
    from_rows[...] = hits_to(source, 3 * cycle)
    to_rows[...] = hits_to(target, node_count)


def receiver_kernel(near, far, mesh_in, recv_hits, stack, pre_out):
    node_count = mesh_in.shape[0]
    rim = node_count // 2
    even = even_on("lat")
    left = jnp.where(even, far[...], near[...])[rim:]
    right = jnp.where(even, near[...], far[...])[:rim]
    cycle = jnp.concatenate([left, mesh_in[...], right], axis=0)
    table = jnp.concatenate(halves(mm(cycle, weight(stack, GR))), axis=0)
    pre_out[...] = mm(recv_hits[...], table)


def gather_kernel(halo, hits, rows, rows_out, wide):
    fill(wide, halo, wide.shape[1] // halo.shape[0], 0)
    rows_out[...] = rows[...] + mm_nt(hits[...], wide[...]).astype(BF16)


def encode_kernel(
    near, near_hits, recv_rows, rows, recv_pre, stack,
    senders_out, slope_out, part_out, near_out, far_out, wide,
):
    half = recv_rows.shape[0] // 2
    fill(wide, near, wide.shape[1] // near.shape[0], 0)
    block = rows.shape[0] // 2
    sums = None
    for first in range(0, rows.shape[0], block):
        part_of = slice(first, first + block)
        raw = rows[part_of] + mm_nt(near_hits[part_of], wide[...]).astype(BF16)
        latent, _ = silu_parts(mm(raw, stack[stack.shape[0] - raw.shape[1] :]))
        latent = latent.astype(BF16)
        senders_out[part_of] = latent
        pre = mm(latent, weight(stack, GS)) + recv_pre[part_of]
        value, slope = silu_parts(pre)
        slope_out[part_of] = slope.astype(BF16)
        part = mm(recv_rows[:, part_of], value.astype(BF16))
        sums = part if sums is None else sums + part
    part_out[...] = sums
    even = even_on("lat")
    near_out[...] = jnp.where(even, sums[half:], sums[:half]).astype(BF16)
    far_out[...] = jnp.where(even, sums[:half], sums[half:]).astype(BF16)


def node_kernel(part, near, far, mesh_near, mesh_far, mesh_in, stack, mesh_out, slope_out):
    node_count = mesh_in.shape[0]
    rim = node_count // 2
    even = even_on("lat")
    left = jnp.where(even, far[...], near[...]).astype(F32)
    right = jnp.where(even, near[...], far[...]).astype(F32)
    total = part[...] + jnp.concatenate([left, right], axis=0)
    mesh_left = jnp.where(even, mesh_far[...], mesh_near[...])[rim:]
    mesh_right = jnp.where(even, mesh_near[...], mesh_far[...])[:rim]
    cycle = jnp.concatenate([mesh_left, mesh_in[...], mesh_right], axis=0)
    value, slope = silu_parts(mm(total.astype(BF16), weight(stack, GN)))
    mesh_out[...] = (cycle.astype(F32) + value).astype(BF16)
    slope_out[...] = slope


def process_own_kernel(own_hits, to_hits, own, stack, pre_out):
    rim = own.shape[0] // 4
    home = own[rim : own.shape[0] - rim]
    table = jnp.concatenate(halves(mm(own[...], weight(stack, MS))), axis=0)
    recv_table = jnp.concatenate(halves(mm(home, weight(stack, MR))), axis=0)
    pre_out[...] = mm(own_hits[...], table) + mm(to_hits[...], recv_table)


def process_kernel(
    own_pre, outer_hits, to_hits, from_rows, to_rows, near, own, far, d_out, stack,
    mesh_out, sums_out, recv_out, near_out, far_out,
):
    cycle = own.shape[0]
    node_count = cycle // 2
    rim = node_count // 2
    home = own[rim : rim + node_count]
    block = jnp.concatenate([near[...], far[...]], axis=0)
    table = jnp.concatenate(halves(mm(block, weight(stack, MS))), axis=0)
    halves_of = [slice(i, i + own_pre.shape[0] // 2) for i in (0, own_pre.shape[0] // 2)]
    slopes = []
    total = None
    for part_of in halves_of:
        pre = own_pre[part_of] + mm(outer_hits[part_of], table)
        value, slope = silu_parts(pre)
        slopes.append(slope)
        part = mm(to_rows[:, part_of], value.astype(BF16))
        total = part if total is None else total + part
    gate = mm(total.astype(BF16), weight(stack, MN))
    gate_value, gate_slope = silu_parts(gate)
    mesh_out[...] = (home.astype(F32) + gate_value).astype(BF16)
    gate_two = (d_out[...].astype(F32) * gate_slope).astype(BF16)
    back = jnp.concatenate(halves(mm_nt(gate_two, weight(stack, MN))), axis=0)
    sums = received = None
    for part_of, slope in zip(halves_of, slopes):
        edge_slope = (mm(to_hits[part_of], back) * slope).astype(BF16)
        part = mm(from_rows[:, part_of], edge_slope)
        sums = part if sums is None else sums + part
        part = mm(to_rows[:, part_of], edge_slope)
        received = part if received is None else received + part
    recv_out[...] = received.astype(BF16)
    sums_out[...] = sums
    near_out[...] = sums[:cycle].astype(BF16)
    far_out[...] = sums[2 * cycle :].astype(BF16)


def block_of(x, dom_shift, lat_shift, doms, lats):
    cols = x.shape[1] // (doms * lats)
    dom = lax.rem(lax.axis_index("dom") + dom_shift, doms)
    index = dom * lats + lax.rem(lax.axis_index("lat") + lat_shift, lats)
    pick = x[:, :cols]
    for i in range(1, doms * lats):
        pick = jnp.where(index == i, x[:, i * cols : (i + 1) * cols], pick)
    return pick


def home_kernel(recv_sum, d_out, stack, senders, home_out, turned_out):
    home_out[...] = mm_nt(recv_sum[...], weight(stack, MR)) + d_out[...].astype(F32)
    turned_out[...] = senders[...].T


def cotangent_kernel(sums, near, far, home, part_out, near_out, far_out):
    cycle = near.shape[0]
    half = cycle // 2
    rim = half // 2
    total = sums[cycle : 2 * cycle] + near[...].astype(F32) + far[...].astype(F32)
    part_out[...] = total
    even = even_on("lat")
    near_out[:half] = jnp.where(even, total[half:], total[:half]).astype(BF16)
    near_out[half:] = jnp.where(even, home[rim:], home[:rim]).astype(BF16)
    far_out[:half] = jnp.where(even, total[:half], total[half:]).astype(BF16)
    far_out[half:] = jnp.where(even, home[:rim], home[rim:]).astype(BF16)


def gradient_block(recv_hits, back, edge_slope, senders, shifts, doms, lats):
    edges = recv_hits.shape[0]
    back = [block_of(back, *shift, doms, lats) for shift in shifts]
    back = back[0] if len(back) == 1 else jnp.concatenate(back, axis=1)
    total = None
    for first in range(0, edges, edges // 2):
        part_of = slice(first, first + edges // 2)
        weights = [block_of(edge_slope[part_of], *shift, doms, lats) for shift in shifts]
        weights = weights[0] if len(weights) == 1 else jnp.concatenate(weights, axis=1)
        slope = mm(recv_hits[part_of], back) * weights.astype(F32)
        part = mm(senders[:, part_of], slope.astype(BF16))
        total = part if total is None else total + part
    return total


def encode_grad_kernel(
    recv_hits, part, near, far, home, node_slope, stack, senders, edge_slope,
    sends, back_out, total_out,
):
    half = part.shape[0] // 2
    even = even_on("lat")
    left = jnp.where(even, far[...], near[...]).astype(F32)
    right = jnp.where(even, near[...], far[...]).astype(F32)
    total = part[...] + jnp.concatenate([left[:half], right[:half]], axis=0)
    total = total.astype(BF16)
    rest = jnp.concatenate([left[half:], home[...], right[half:]], axis=0)
    cot = rest + mm_nt(total, weight(stack, MS))
    gate_one = (cot * node_slope[...]).astype(BF16)
    back = jnp.concatenate(halves(mm_nt(gate_one, weight(stack, GN))), axis=0)
    back_out[...] = back
    lats = sends.shape[0] + 1
    doms = sends.shape[1] + 1
    for i in range(1, lats):
        for j in range(1, doms):
            block = gradient_block(
                recv_hits, back, edge_slope, senders, [(j, i)], doms, lats
            )
            sends[i - 1, j - 1] = block.astype(BF16)
    for j in range(doms):
        total_out[j] = block_of(total, j, 0, doms, lats)


def middle_blocks_kernel(recv_hits, back, edge_slope, senders, after, kept, sends):
    doms = kept.shape[0] + 1
    lats = sends.shape[0] + 1
    cols = kept.shape[2]
    shifts = [(j, 0) for j in range(1, doms)] + [(0, i) for i in range(1, lats)]
    blocks = gradient_block(recv_hits, back[...], edge_slope, senders, shifts, doms, lats)
    for k in range(len(shifts)):
        block = blocks[:, k * cols : (k + 1) * cols]
        if k < doms - 1:
            kept[k] = block
        else:
            sends[k - doms + 1] = block.astype(BF16)


def rows_at(ref, place, partner):
    bands = lax.axis_size("band")
    rows = ref.shape[-2] // bands
    at = pl.multiple_of(lax.bitwise_xor(lax.axis_index("band"), partner) * rows, rows)
    return ref[(*place, pl.ds(at, rows))]


def add_kernel(kept, total, *refs):
    *came, first_out, second_out = refs
    bands = lax.axis_size("band")
    rows = kept.shape[1] // bands
    near = second_out.shape[1] // rows
    for j in range(kept.shape[0]):
        for k in range(bands):
            block = rows_at(kept, (j,), k)
            for part in came:
                block = block + rows_at(part, (j,), k).astype(F32)
            out, at = (first_out, k - near) if k >= near else (second_out, k)
            at = at * rows
            out[j, at : at + rows] = block.astype(BF16)
        first_out[j, (bands - near) * rows :] = total[j + 1]


def own_block_kernel(recv_hits, back, edge_slope, senders, *refs):
    *came, out = refs
    lats = len(came) + 1
    doms = back.shape[1] // out.shape[1] // lats
    block = gradient_block(
        recv_hits, back[...], edge_slope, senders, [(0, 0)], doms, lats
    )
    for part in came:
        block = block + part[...].astype(F32)
    out[...] = block


def first_kernel(kept, total, nodes, *refs):
    doms = total.shape[0]
    came, (*sends_out, sums) = refs[: 2 * (doms - 1)], refs[2 * (doms - 1) :]
    came, came_nodes = came[: doms - 1], came[doms - 1 :]
    far = len(sends_out)
    near = lax.axis_size("band") - far
    rows = sends_out[0].shape[1]
    second = mm_tn(nodes[...], total[0])
    for part, part_nodes in zip(came, came_nodes):
        second = second + mm_tn(part_nodes[...], part[far * rows :])
    sums[...] = second
    for i, out in enumerate(sends_out):
        block = rows_at(kept, (), near + i)
        for part in came:
            block = block + part[i * rows : (i + 1) * rows].astype(F32)
        out[0] = block.astype(BF16)
        out[1] = rows_at(sums, (), near + i).astype(BF16)


def second_kernel(kept, sums, *refs):
    doms = lax.axis_size("dom")
    came, outs = refs[: doms - 1], refs[doms - 1 :]
    rows = outs[0].shape[1]
    for i, out in enumerate(outs):
        block = rows_at(kept, (), i)
        for part in came:
            block = block + part[i * rows : (i + 1) * rows].astype(F32)
        out[0] = block.astype(out.dtype)
        out[1] = rows_at(sums, (), i).astype(out.dtype)


def over_band_kernel(*refs):
    *came, own, first_out, second_out = refs
    for k, out in enumerate((first_out, second_out)):
        total = own[k]
        for part in came:
            total = total + part[k].astype(F32)
        out[...] = total


def call(kernel, outs, *args, scalars=(), scratch=()):
    in_specs = [
        pl.BlockSpec(memory_space=pltpu.SMEM if i in scalars else pltpu.VMEM)
        for i in range(len(args))
    ]
    return pl.pallas_call(
        kernel,
        out_shape=[jax.ShapeDtypeStruct(shape, dtype) for shape, dtype in outs],
        in_specs=in_specs,
        out_specs=[pl.BlockSpec(memory_space=pltpu.VMEM)] * len(outs),
        scratch_shapes=scratch,
        compiler_params=pltpu.CompilerParams(vmem_limit_bytes=16 << 20),
    )(*args)


def ring_pairings(count):
    far = [(i, (i + 1 if i % 2 else i - 1) % count) for i in range(count)]
    return [(i, i ^ 1) for i in range(count)], far


def line_pairings(bands, doms, lats):
    far = []
    for band in range(bands):
        other = band + 1 if band % 2 else band - 1
        for dom in range(doms):
            for lat in range(lats):
                here = (band * doms + dom) * lats + lat
                if 0 <= other < bands:
                    there = (other * doms + dom) * lats + lat
                else:
                    there = (band * doms + dom) * lats + (lat ^ 1)
                far.append((here, there))
    return [(i, i ^ 1) for i in range(bands)], far


def shifted(x, axis, shift):
    count = lax.axis_size(axis)
    return lax.ppermute(x, axis, [(i, (i + shift) % count) for i in range(count)])


def over_band(x, partner):
    count = lax.axis_size("band")
    return lax.ppermute(x, "band", [(b, b ^ partner) for b in range(count)])


def on_device(
    grid_in, w_grid, w_gs, w_gr, w_gn, w_ms, w_mr, w_mn, mesh_in, d_out,
    g2m_send, g2m_recv, g2m_count, mesh_send, mesh_recv, mesh_count,
):
    latent = w_grid.shape[1]
    variables = w_grid.shape[0]
    node_count = mesh_in.shape[0]
    cycle = 2 * node_count
    bands = lax.axis_size("band")
    sectors = lax.axis_size(("dom", "lat"))
    edges = g2m_send.shape[2]
    around = ("dom", "lat")
    whole = ("band", "dom", "lat")
    band_near, band_far = line_pairings(bands, lax.axis_size("dom"), lax.axis_size("lat"))
    ring_near, ring_far = ring_pairings(sectors)

    grid = jnp.transpose(grid_in, (0, 2, 1))
    pitch = -(-grid.shape[2] // LANES) * LANES
    band_rows = grid.shape[0]
    width = band_rows * pitch
    raw_near = lax.ppermute(grid, "band", band_near)
    raw_far = lax.ppermute(grid, whole, band_far)
    mesh_edges = mesh_send.shape[2]
    stack = jnp.concatenate([w_gs, w_gr, w_gn, w_ms, w_mr, w_mn, w_grid], axis=0)
    indices = jnp.concatenate([g2m_send, g2m_recv, mesh_send, mesh_recv], axis=2)
    (
        rows, recv_hits, recv_rows, own_hits, outer_hits, to_hits, from_rows, to_rows, *halo_hits
    ) = call(
        index_kernel,
        [
            ((edges, variables), BF16),
            ((edges, 2 * cycle), BF16),
            ((cycle, edges), BF16),
            ((mesh_edges, 2 * cycle), BF16),
            ((mesh_edges, 4 * cycle), BF16),
            ((mesh_edges, 2 * node_count), BF16),
            ((3 * cycle, mesh_edges), BF16),
            ((node_count, mesh_edges), BF16),
            ((edges, width), BF16),
            ((edges, width), BF16),
        ],
        g2m_count, mesh_count, indices, grid,
        scalars=(0, 1),
        scratch=[pltpu.VMEM((variables, width), BF16)],
    )
    late_mesh, rows = lax.optimization_barrier((mesh_in, rows))
    mesh_near = lax.ppermute(late_mesh, around, ring_near)
    mesh_far = lax.ppermute(late_mesh, around, ring_far)
    (recv_pre,) = call(
        receiver_kernel,
        [((edges, latent), F32)],
        mesh_near, mesh_far, mesh_in, recv_hits, stack,
    )
    near_hits, far_hits = halo_hits
    (rows,) = call(
        gather_kernel,
        [((edges, variables), BF16)],
        raw_far, far_hits, rows,
        scratch=[pltpu.VMEM((variables, width), BF16)],
    )
    senders, edge_slope, part, to_near, to_far = call(
        encode_kernel,
        [
            ((edges, latent), BF16),
            ((edges, latent), BF16),
            ((cycle, latent), F32),
            ((node_count, latent), BF16),
            ((node_count, latent), BF16),
        ],
        raw_near, near_hits, recv_rows, rows, recv_pre, stack,
        scratch=[pltpu.VMEM((variables, width), BF16)],
    )
    from_far = lax.ppermute(to_far, around, ring_far)
    from_near = lax.ppermute(to_near, around, ring_near)
    mesh_one, node_slope = call(
        node_kernel,
        [((cycle, latent), BF16), ((cycle, latent), F32)],
        part, from_near, from_far, mesh_near, mesh_far, mesh_in, stack,
    )
    one_near = lax.ppermute(mesh_one, "band", band_near)
    one_far = lax.ppermute(mesh_one, whole, band_far)
    doms = lax.axis_size("dom")
    lats = lax.axis_size("lat")
    dom_nodes = [shifted(mesh_one, "dom", i + 1) for i in range(doms - 1)]
    (own_pre,) = call(
        process_own_kernel, [((mesh_edges, latent), F32)], own_hits, to_hits, mesh_one, stack
    )
    mesh_out, sums, recv_sum, to_near, to_far = call(
        process_kernel,
        [
            ((node_count, latent), BF16),
            ((3 * cycle, latent), F32),
            ((node_count, latent), BF16),
            ((cycle, latent), BF16),
            ((cycle, latent), BF16),
        ],
        own_pre, outer_hits, to_hits, from_rows, to_rows, one_near, mesh_one, one_far, d_out,
        stack,
    )
    from_near = lax.ppermute(to_near, "band", band_near)
    from_far = lax.ppermute(to_far, whole, band_far)
    from_near, *dom_nodes = lax.optimization_barrier((from_near, *dom_nodes))
    home, senders = call(
        home_kernel,
        [((node_count, latent), F32), ((latent, edges), BF16)],
        recv_sum, d_out, stack, senders,
    )
    message = (node_count + node_count // 2, latent)
    part, to_near, to_far = call(
        cotangent_kernel,
        [((cycle, latent), F32), (message, BF16), (message, BF16)],
        sums, from_near, from_far, home,
    )
    from_far = lax.ppermute(to_far, around, ring_far)
    from_near = lax.ppermute(to_near, around, ring_near)

    cols = latent // sectors
    rows = latent // bands
    sends, back, total = call(
        encode_grad_kernel,
        [
            ((lats - 1, doms - 1, latent, cols), BF16),
            ((2 * cycle, latent), BF16),
            ((doms, cycle, cols), BF16),
        ],
        recv_hits, part, from_near, from_far, home, node_slope, stack, senders, edge_slope,
    )
    edge = (recv_hits, back, edge_slope, senders)
    came = [shifted(sends[i], "lat", i + 1) for i in range(lats - 1)]
    block = (latent, cols)
    kept, own_sends = call(
        middle_blocks_kernel,
        [((doms - 1,) + block, F32), ((lats - 1,) + block, BF16)],
        *edge, sends,
    )
    own_came = [shifted(own_sends[i], "lat", i + 1) for i in range(lats - 1)]
    far = bands // 2
    first, second = call(
        add_kernel,
        [
            ((doms - 1, far * rows + cycle, cols), BF16),
            ((doms - 1, (bands - far) * rows, cols), BF16),
        ],
        kept, total, *came,
    )
    first = [shifted(first[i], "dom", i + 1) for i in range(doms - 1)]
    second = [shifted(second[i], "dom", i + 1) for i in range(doms - 1)]
    (kept,) = call(own_block_kernel, [(block, F32)], *edge, *own_came)
    pair = (2, rows, cols)
    *far_sends, sums = call(
        first_kernel,
        [(pair, BF16)] * far + [(block, F32)],
        kept, total, mesh_one, *first, *dom_nodes,
    )
    came = [over_band(x, bands - far + i) for i, x in reversed(list(enumerate(far_sends)))]
    own, *near_sends = call(
        second_kernel,
        [(pair, F32)] + [(pair, BF16)] * (bands - far - 1),
        kept, sums, *second,
    )
    came += [over_band(x, i + 1) for i, x in reversed(list(enumerate(near_sends)))]
    tile = ((rows, cols), F32)
    grad_gs, grad_ms = call(over_band_kernel, [tile, tile], *came, own)
    return mesh_out, grad_gs, grad_ms


def solution(mesh):
    flat = P(("groups", "band", "dom", "lat"), None)
    grid = P(("groups", "band"), ("dom", "lat"), None)
    count = P(("groups", "band"), ("dom", "lat"))
    placed = (grid,) + (P(),) * 7 + (flat, flat) + (grid, grid, count) * 2
    return jax.shard_map(
        on_device,
        mesh=mesh,
        in_specs=placed,
        out_specs=(flat, count, count),
        check_vma=False,
    )
```

```python
import jax
import jax.numpy as jnp
from jax import lax
from jax.experimental import pallas as pl
from jax.experimental.pallas import tpu as pltpu
from jax.sharding import PartitionSpec as P

F32 = jnp.float32
BF16 = jnp.bfloat16
LANES = 128
GS, GR, GN, MS, MR, MN = range(6)


def mm(a, b):
    return jnp.dot(a, b, preferred_element_type=F32)


def mm_nt(a, b):
    return lax.dot_general(a, b, (((1,), (1,)), ((), ())), preferred_element_type=F32)


def mm_tn(a, b):
    return lax.dot_general(a, b, (((0,), (0,)), ((), ())), preferred_element_type=F32)


def halves(x):
    high = x.astype(BF16)
    return high, (x - high.astype(F32)).astype(BF16)


def silu_parts(x):
    g = 0.5 * jnp.tanh(0.5 * x) + 0.5
    value = x * g
    return value, g + value * (1.0 - g)


def ones_at(mask):
    return jnp.where(mask, 1.0, 0.0).astype(BF16)


def columns(row):
    count = row.shape[1]
    parts = [
        jnp.broadcast_to(row[:, i : i + LANES], (LANES, LANES)).T
        for i in range(0, count, LANES)
    ]
    return parts[0] if len(parts) == 1 else jnp.concatenate(parts, axis=0)


def hits_from(cols, width, period, start=0):
    parts = []
    for i in range(0, width, LANES):
        size = min(LANES, width - i)
        lane = lax.broadcasted_iota(jnp.int32, (cols.shape[0], size), 1) + i
        if period < width:
            lane = lax.rem(lane, period)
        parts.append(ones_at(cols[:, :size] == lane + start))
    return parts[0] if len(parts) == 1 else jnp.concatenate(parts, axis=1)


def hits_to(row, count):
    return ones_at(lax.broadcasted_iota(jnp.int32, (count, row.shape[1]), 0) == row)


def live_only(row, count, first=0):
    slot = lax.broadcasted_iota(jnp.int32, row.shape, 1) + first
    return jnp.where(slot < count, row, -1)


def weight(stack, index):
    latent = stack.shape[1]
    return stack[index * latent : (index + 1) * latent]


def even_on(axis):
    return lax.rem(lax.axis_index(axis), 2) == 0


def spread(index, blocks, cols, pitch):
    extra = jnp.zeros_like(index)
    for block in range(1, blocks):
        extra = extra + jnp.where(index >= block * cols, pitch - cols, 0)
    return index + extra


def fill(wide, blocks, pitch, first):
    cols = blocks.shape[2]
    for k in range(blocks.shape[0]):
        at = first + k * pitch
        wide[:, at : at + cols] = blocks[k]
        if cols < pitch:
            wide[:, at + cols : at + pitch] = jnp.zeros(
                (wide.shape[0], pitch - cols), wide.dtype
            )


def index_kernel(
    count, mesh_count, indices, grid,
    own_out, recv_hits, recv_rows, own_hits, outer_hits, to_hits, from_rows, to_rows, near_hits, far_hits, wide,
):
    edges = recv_hits.shape[0]
    mesh_edges = to_hits.shape[0]
    send, recv, mesh_send, mesh_recv = (
        indices[0, :, first : first + size]
        for first, size in (
            (0, edges),
            (edges, edges),
            (2 * edges, mesh_edges),
            (2 * edges + mesh_edges, mesh_edges),
        )
    )
    band_rows, _, cols = grid.shape
    pitch = wide.shape[1] // band_rows
    width = band_rows * pitch
    cycle = recv_rows.shape[0]
    node_count = to_rows.shape[0]
    even_band = even_on("band")
    fill(wide, grid, pitch, 0)
    near_base = jnp.where(even_band, 2 * width, 0)
    far_base = jnp.where(even_band, 0, 2 * width)
    block = 256
    for first in range(0, edges, block):
        part_of = slice(first, first + block)
        index = columns(spread(send[:, part_of], 3 * band_rows, cols, pitch))
        own_hit = hits_from(index, width, width, width)
        own_out[part_of] = mm_nt(own_hit, wide[...]).astype(BF16)
        near_hits[part_of] = hits_from(index, width, width, near_base)
        far_hits[part_of] = hits_from(index, width, width, far_base)
        target = live_only(recv[:, part_of], count[0, 0], first)
        recv_hits[part_of] = hits_from(columns(target), 2 * cycle, cycle)
        recv_rows[:, part_of] = hits_to(target, cycle)
    raw = mesh_send
    inner = (raw >= cycle) & (raw < 2 * cycle)
    above_near = jnp.where(raw < cycle, raw + cycle, raw - 2 * cycle)
    below_near = jnp.where(raw < cycle, raw, raw - cycle)
    outer = jnp.where(inner, -1, jnp.where(even_band, above_near, below_near))
    target = live_only(mesh_recv, mesh_count[0, 0])
    own_hits[...] = hits_from(columns(jnp.where(inner, raw - cycle, -1)), 2 * cycle, cycle)
    outer_hits[...] = hits_from(columns(outer), 4 * cycle, 2 * cycle)
    to_hits[...] = hits_from(columns(target), 2 * node_count, node_count)
    source = jnp.where(inner, raw, jnp.where(outer < cycle, outer, outer + cycle))
    from_rows[...] = hits_to(source, 3 * cycle)
    to_rows[...] = hits_to(target, node_count)


def receiver_kernel(near, far, mesh_in, recv_hits, stack, pre_out):
    node_count = mesh_in.shape[0]
    rim = node_count // 2
    even = even_on("lat")
    left = jnp.where(even, far[...], near[...])[rim:]
    right = jnp.where(even, near[...], far[...])[:rim]
    cycle = jnp.concatenate([left, mesh_in[...], right], axis=0)
    table = jnp.concatenate(halves(mm(cycle, weight(stack, GR))), axis=0)
    pre_out[...] = mm(recv_hits[...], table)


def gather_kernel(halo, hits, rows, rows_out, wide):
    fill(wide, halo, wide.shape[1] // halo.shape[0], 0)
    rows_out[...] = rows[...] + mm_nt(hits[...], wide[...]).astype(BF16)


def encode_kernel(
    near, near_hits, recv_rows, rows, recv_pre, stack,
    senders_out, slope_out, part_out, near_out, far_out, wide,
):
    half = recv_rows.shape[0] // 2
    fill(wide, near, wide.shape[1] // near.shape[0], 0)
    block = rows.shape[0] // 4
    sums = None
    for first in range(0, rows.shape[0], block):
        part_of = slice(first, first + block)
        raw = rows[part_of] + mm_nt(near_hits[part_of], wide[...]).astype(BF16)
        latent, _ = silu_parts(mm(raw, stack[stack.shape[0] - raw.shape[1] :]))
        latent = latent.astype(BF16)
        senders_out[part_of] = latent
        pre = mm(latent, weight(stack, GS)) + recv_pre[part_of]
        value, slope = silu_parts(pre)
        slope_out[part_of] = slope.astype(BF16)
        part = mm(recv_rows[:, part_of], value.astype(BF16))
        sums = part if sums is None else sums + part
    part_out[...] = sums
    even = even_on("lat")
    near_out[...] = jnp.where(even, sums[half:], sums[:half]).astype(BF16)
    far_out[...] = jnp.where(even, sums[:half], sums[half:]).astype(BF16)


def node_kernel(part, near, far, mesh_near, mesh_far, mesh_in, stack, mesh_out, slope_out):
    node_count = mesh_in.shape[0]
    rim = node_count // 2
    even = even_on("lat")
    left = jnp.where(even, far[...], near[...]).astype(F32)
    right = jnp.where(even, near[...], far[...]).astype(F32)
    total = part[...] + jnp.concatenate([left, right], axis=0)
    mesh_left = jnp.where(even, mesh_far[...], mesh_near[...])[rim:]
    mesh_right = jnp.where(even, mesh_near[...], mesh_far[...])[:rim]
    cycle = jnp.concatenate([mesh_left, mesh_in[...], mesh_right], axis=0)
    value, slope = silu_parts(mm(total.astype(BF16), weight(stack, GN)))
    mesh_out[...] = (cycle.astype(F32) + value).astype(BF16)
    slope_out[...] = slope


def process_own_kernel(own_hits, to_hits, own, stack, pre_out):
    rim = own.shape[0] // 4
    home = own[rim : own.shape[0] - rim]
    table = jnp.concatenate(halves(mm(own[...], weight(stack, MS))), axis=0)
    recv_table = jnp.concatenate(halves(mm(home, weight(stack, MR))), axis=0)
    pre_out[...] = mm(own_hits[...], table) + mm(to_hits[...], recv_table)


def process_kernel(
    own_pre, outer_hits, to_hits, from_rows, to_rows, far, own, near, d_out, stack,
    mesh_out, sums_out, recv_out, near_out, far_out,
):
    cycle = own.shape[0]
    node_count = cycle // 2
    rim = node_count // 2
    home = own[rim : rim + node_count]
    block = jnp.concatenate([near[...], far[...]], axis=0)
    table = jnp.concatenate(halves(mm(block, weight(stack, MS))), axis=0)
    pre = own_pre[...] + mm(outer_hits[...], table)
    value, slope = silu_parts(pre)
    gate = mm(mm(to_rows[...], value.astype(BF16)).astype(BF16), weight(stack, MN))
    gate_value, gate_slope = silu_parts(gate)
    mesh_out[...] = (home.astype(F32) + gate_value).astype(BF16)
    gate_two = (d_out[...].astype(F32) * gate_slope).astype(BF16)
    back = jnp.concatenate(halves(mm_nt(gate_two, weight(stack, MN))), axis=0)
    edge_slope = (mm(to_hits[...], back) * slope).astype(BF16)
    sums = mm(from_rows[...], edge_slope)
    recv_out[...] = mm(to_rows[...], edge_slope).astype(BF16)
    sums_out[...] = sums
    near_out[...] = sums[:cycle].astype(BF16)
    far_out[...] = sums[2 * cycle :].astype(BF16)


def block_of(x, dom_shift, lat_shift, doms, lats):
    cols = x.shape[1] // (doms * lats)
    dom = lax.rem(lax.axis_index("dom") + dom_shift, doms)
    index = dom * lats + lax.rem(lax.axis_index("lat") + lat_shift, lats)
    pick = x[:, :cols]
    for i in range(1, doms * lats):
        pick = jnp.where(index == i, x[:, i * cols : (i + 1) * cols], pick)
    return pick


def home_kernel(recv_sum, d_out, stack, senders, home_out, turned_out):
    home_out[...] = mm_nt(recv_sum[...], weight(stack, MR)) + d_out[...].astype(F32)
    turned_out[...] = senders[...].T


def cotangent_kernel(sums, near, far, home, part_out, near_out, far_out):
    cycle = near.shape[0]
    half = cycle // 2
    rim = half // 2
    total = sums[cycle : 2 * cycle] + near[...].astype(F32) + far[...].astype(F32)
    part_out[...] = total
    even = even_on("lat")
    near_out[:half] = jnp.where(even, total[half:], total[:half]).astype(BF16)
    near_out[half:] = jnp.where(even, home[rim:], home[:rim]).astype(BF16)
    far_out[:half] = jnp.where(even, total[:half], total[half:]).astype(BF16)
    far_out[half:] = jnp.where(even, home[:rim], home[rim:]).astype(BF16)


def gradient_block(recv_hits, back, edge_slope, senders, shifts, doms, lats):
    edges = recv_hits.shape[0]
    back = [block_of(back, *shift, doms, lats) for shift in shifts]
    back = back[0] if len(back) == 1 else jnp.concatenate(back, axis=1)
    total = None
    for first in range(0, edges, edges // 2):
        part_of = slice(first, first + edges // 2)
        weights = [block_of(edge_slope[part_of], *shift, doms, lats) for shift in shifts]
        weights = weights[0] if len(weights) == 1 else jnp.concatenate(weights, axis=1)
        slope = mm(recv_hits[part_of], back) * weights.astype(F32)
        part = mm(senders[:, part_of], slope.astype(BF16))
        total = part if total is None else total + part
    return total


def encode_grad_kernel(
    recv_hits, part, near, far, home, node_slope, stack, senders, edge_slope,
    sends, back_out, total_out,
):
    half = part.shape[0] // 2
    even = even_on("lat")
    left = jnp.where(even, far[...], near[...]).astype(F32)
    right = jnp.where(even, near[...], far[...]).astype(F32)
    total = part[...] + jnp.concatenate([left[:half], right[:half]], axis=0)
    total = total.astype(BF16)
    rest = jnp.concatenate([left[half:], home[...], right[half:]], axis=0)
    cot = rest + mm_nt(total, weight(stack, MS))
    gate_one = (cot * node_slope[...]).astype(BF16)
    back = jnp.concatenate(halves(mm_nt(gate_one, weight(stack, GN))), axis=0)
    back_out[...] = back
    lats = sends.shape[0] + 1
    doms = sends.shape[1] + 1
    for i in range(1, lats):
        for j in range(1, doms):
            block = gradient_block(
                recv_hits, back, edge_slope, senders, [(j, i)], doms, lats
            )
            sends[i - 1, j - 1] = block.astype(BF16)
    for j in range(doms):
        total_out[j] = block_of(total, j, 0, doms, lats)


def middle_blocks_kernel(recv_hits, back, edge_slope, senders, after, kept, sends):
    doms = kept.shape[0] + 1
    lats = sends.shape[0] + 1
    cols = kept.shape[2]
    shifts = [(j, 0) for j in range(1, doms)] + [(0, i) for i in range(1, lats)]
    blocks = gradient_block(recv_hits, back[...], edge_slope, senders, shifts, doms, lats)
    for k in range(len(shifts)):
        block = blocks[:, k * cols : (k + 1) * cols]
        if k < doms - 1:
            kept[k] = block
        else:
            sends[k - doms + 1] = block.astype(BF16)


def rows_at(ref, place, partner):
    bands = lax.axis_size("band")
    rows = ref.shape[-2] // bands
    at = pl.multiple_of(lax.bitwise_xor(lax.axis_index("band"), partner) * rows, rows)
    return ref[(*place, pl.ds(at, rows))]


def add_kernel(kept, total, *refs):
    *came, first_out, second_out = refs
    bands = lax.axis_size("band")
    rows = kept.shape[1] // bands
    near = second_out.shape[1] // rows
    for j in range(kept.shape[0]):
        for k in range(bands):
            block = rows_at(kept, (j,), k)
            for part in came:
                block = block + rows_at(part, (j,), k).astype(F32)
            out, at = (first_out, k - near) if k >= near else (second_out, k)
            at = at * rows
            out[j, at : at + rows] = block.astype(BF16)
        first_out[j, (bands - near) * rows :] = total[j + 1]


def own_block_kernel(recv_hits, back, edge_slope, senders, *refs):
    *came, out = refs
    lats = len(came) + 1
    doms = back.shape[1] // out.shape[1] // lats
    block = gradient_block(
        recv_hits, back[...], edge_slope, senders, [(0, 0)], doms, lats
    )
    for part in came:
        block = block + part[...].astype(F32)
    out[...] = block


def first_kernel(kept, total, nodes, *refs):
    doms = total.shape[0]
    came, (*sends_out, sums) = refs[: 2 * (doms - 1)], refs[2 * (doms - 1) :]
    came, came_nodes = came[: doms - 1], came[doms - 1 :]
    far = len(sends_out)
    near = lax.axis_size("band") - far
    rows = sends_out[0].shape[1]
    second = mm_tn(nodes[...], total[0])
    for part, part_nodes in zip(came, came_nodes):
        second = second + mm_tn(part_nodes[...], part[far * rows :])
    sums[...] = second
    for i, out in enumerate(sends_out):
        block = rows_at(kept, (), near + i)
        for part in came:
            block = block + part[i * rows : (i + 1) * rows].astype(F32)
        out[0] = block.astype(BF16)
        out[1] = rows_at(sums, (), near + i).astype(BF16)


def second_kernel(kept, sums, *refs):
    doms = lax.axis_size("dom")
    came, outs = refs[: doms - 1], refs[doms - 1 :]
    rows = outs[0].shape[1]
    for i, out in enumerate(outs):
        block = rows_at(kept, (), i)
        for part in came:
            block = block + part[i * rows : (i + 1) * rows].astype(F32)
        out[0] = block.astype(out.dtype)
        out[1] = rows_at(sums, (), i).astype(out.dtype)


def over_band_kernel(*refs):
    *came, own, first_out, second_out = refs
    for k, out in enumerate((first_out, second_out)):
        total = own[k]
        for part in came:
            total = total + part[k].astype(F32)
        out[...] = total


def call(kernel, outs, *args, scalars=(), scratch=()):
    in_specs = [
        pl.BlockSpec(memory_space=pltpu.SMEM if i in scalars else pltpu.VMEM)
        for i in range(len(args))
    ]
    return pl.pallas_call(
        kernel,
        out_shape=[jax.ShapeDtypeStruct(shape, dtype) for shape, dtype in outs],
        in_specs=in_specs,
        out_specs=[pl.BlockSpec(memory_space=pltpu.VMEM)] * len(outs),
        scratch_shapes=scratch,
        compiler_params=pltpu.CompilerParams(vmem_limit_bytes=16 << 20),
    )(*args)


def ring_pairings(count):
    far = [(i, (i + 1 if i % 2 else i - 1) % count) for i in range(count)]
    return [(i, i ^ 1) for i in range(count)], far


def line_pairings(bands, doms, lats):
    far = []
    for band in range(bands):
        other = band + 1 if band % 2 else band - 1
        for dom in range(doms):
            for lat in range(lats):
                here = (band * doms + dom) * lats + lat
                if 0 <= other < bands:
                    there = (other * doms + dom) * lats + lat
                else:
                    there = (band * doms + dom) * lats + (lat ^ 1)
                far.append((here, there))
    return [(i, i ^ 1) for i in range(bands)], far


def shifted(x, axis, shift):
    count = lax.axis_size(axis)
    return lax.ppermute(x, axis, [(i, (i + shift) % count) for i in range(count)])


def over_band(x, partner):
    count = lax.axis_size("band")
    return lax.ppermute(x, "band", [(b, b ^ partner) for b in range(count)])


def on_device(
    grid_in, w_grid, w_gs, w_gr, w_gn, w_ms, w_mr, w_mn, mesh_in, d_out,
    g2m_send, g2m_recv, g2m_count, mesh_send, mesh_recv, mesh_count,
):
    latent = w_grid.shape[1]
    variables = w_grid.shape[0]
    node_count = mesh_in.shape[0]
    cycle = 2 * node_count
    bands = lax.axis_size("band")
    sectors = lax.axis_size(("dom", "lat"))
    edges = g2m_send.shape[2]
    around = ("dom", "lat")
    whole = ("band", "dom", "lat")
    band_near, band_far = line_pairings(bands, lax.axis_size("dom"), lax.axis_size("lat"))
    ring_near, ring_far = ring_pairings(sectors)

    grid = jnp.transpose(grid_in, (0, 2, 1))
    pitch = -(-grid.shape[2] // LANES) * LANES
    band_rows = grid.shape[0]
    width = band_rows * pitch
    raw_near = lax.ppermute(grid, "band", band_near)
    raw_far = lax.ppermute(grid, whole, band_far)
    mesh_edges = mesh_send.shape[2]
    stack = jnp.concatenate([w_gs, w_gr, w_gn, w_ms, w_mr, w_mn, w_grid], axis=0)
    indices = jnp.concatenate([g2m_send, g2m_recv, mesh_send, mesh_recv], axis=2)
    (
        rows, recv_hits, recv_rows, own_hits, outer_hits, to_hits, from_rows, to_rows, *halo_hits
    ) = call(
        index_kernel,
        [
            ((edges, variables), BF16),
            ((edges, 2 * cycle), BF16),
            ((cycle, edges), BF16),
            ((mesh_edges, 2 * cycle), BF16),
            ((mesh_edges, 4 * cycle), BF16),
            ((mesh_edges, 2 * node_count), BF16),
            ((3 * cycle, mesh_edges), BF16),
            ((node_count, mesh_edges), BF16),
            ((edges, width), BF16),
            ((edges, width), BF16),
        ],
        g2m_count, mesh_count, indices, grid,
        scalars=(0, 1),
        scratch=[pltpu.VMEM((variables, width), BF16)],
    )
    late_mesh, rows = lax.optimization_barrier((mesh_in, rows))
    mesh_near = lax.ppermute(late_mesh, around, ring_near)
    mesh_far = lax.ppermute(late_mesh, around, ring_far)
    (recv_pre,) = call(
        receiver_kernel,
        [((edges, latent), F32)],
        mesh_near, mesh_far, mesh_in, recv_hits, stack,
    )
    near_hits, far_hits = halo_hits
    (rows,) = call(
        gather_kernel,
        [((edges, variables), BF16)],
        raw_far, far_hits, rows,
        scratch=[pltpu.VMEM((variables, width), BF16)],
    )
    senders, edge_slope, part, to_near, to_far = call(
        encode_kernel,
        [
            ((edges, latent), BF16),
            ((edges, latent), BF16),
            ((cycle, latent), F32),
            ((node_count, latent), BF16),
            ((node_count, latent), BF16),
        ],
        raw_near, near_hits, recv_rows, rows, recv_pre, stack,
        scratch=[pltpu.VMEM((variables, width), BF16)],
    )
    from_far = lax.ppermute(to_far, around, ring_far)
    from_near = lax.ppermute(to_near, around, ring_near)
    mesh_one, node_slope = call(
        node_kernel,
        [((cycle, latent), BF16), ((cycle, latent), F32)],
        part, from_near, from_far, mesh_near, mesh_far, mesh_in, stack,
    )
    one_near = lax.ppermute(mesh_one, "band", band_near)
    one_far = lax.ppermute(mesh_one, whole, band_far)
    doms = lax.axis_size("dom")
    lats = lax.axis_size("lat")
    dom_nodes = [shifted(mesh_one, "dom", i + 1) for i in range(doms - 1)]
    (own_pre,) = call(
        process_own_kernel, [((mesh_edges, latent), F32)], own_hits, to_hits, mesh_one, stack
    )
    mesh_out, sums, recv_sum, to_near, to_far = call(
        process_kernel,
        [
            ((node_count, latent), BF16),
            ((3 * cycle, latent), F32),
            ((node_count, latent), BF16),
            ((cycle, latent), BF16),
            ((cycle, latent), BF16),
        ],
        own_pre, outer_hits, to_hits, from_rows, to_rows, one_far, mesh_one, one_near, d_out,
        stack,
    )
    from_near = lax.ppermute(to_near, "band", band_near)
    from_far = lax.ppermute(to_far, whole, band_far)
    from_near, *dom_nodes = lax.optimization_barrier((from_near, *dom_nodes))
    home, senders = call(
        home_kernel,
        [((node_count, latent), F32), ((latent, edges), BF16)],
        recv_sum, d_out, stack, senders,
    )
    message = (node_count + node_count // 2, latent)
    part, to_near, to_far = call(
        cotangent_kernel,
        [((cycle, latent), F32), (message, BF16), (message, BF16)],
        sums, from_near, from_far, home,
    )
    from_far = lax.ppermute(to_far, around, ring_far)
    from_near = lax.ppermute(to_near, around, ring_near)

    cols = latent // sectors
    rows = latent // bands
    sends, back, total = call(
        encode_grad_kernel,
        [
            ((lats - 1, doms - 1, latent, cols), BF16),
            ((2 * cycle, latent), BF16),
            ((doms, cycle, cols), BF16),
        ],
        recv_hits, part, from_near, from_far, home, node_slope, stack, senders, edge_slope,
    )
    edge = (recv_hits, back, edge_slope, senders)
    came = [shifted(sends[i], "lat", i + 1) for i in range(lats - 1)]
    block = (latent, cols)
    kept, own_sends = call(
        middle_blocks_kernel,
        [((doms - 1,) + block, F32), ((lats - 1,) + block, BF16)],
        *edge, sends,
    )
    own_came = [shifted(own_sends[i], "lat", i + 1) for i in range(lats - 1)]
    far = bands // 2
    first, second = call(
        add_kernel,
        [
            ((doms - 1, far * rows + cycle, cols), BF16),
            ((doms - 1, (bands - far) * rows, cols), BF16),
        ],
        kept, total, *came,
    )
    first = [shifted(first[i], "dom", i + 1) for i in range(doms - 1)]
    second = [shifted(second[i], "dom", i + 1) for i in range(doms - 1)]
    (kept,) = call(own_block_kernel, [(block, F32)], *edge, *own_came)
    pair = (2, rows, cols)
    *far_sends, sums = call(
        first_kernel,
        [(pair, BF16)] * far + [(block, F32)],
        kept, total, mesh_one, *first, *dom_nodes,
    )
    came = [over_band(x, bands - far + i) for i, x in reversed(list(enumerate(far_sends)))]
    own, *near_sends = call(
        second_kernel,
        [(pair, F32)] + [(pair, BF16)] * (bands - far - 1),
        kept, sums, *second,
    )
    came += [over_band(x, i + 1) for i, x in reversed(list(enumerate(near_sends)))]
    tile = ((rows, cols), F32)
    grad_gs, grad_ms = call(over_band_kernel, [tile, tile], *came, own)
    return mesh_out, grad_gs, grad_ms


def solution(mesh):
    flat = P(("groups", "band", "dom", "lat"), None)
    grid = P(("groups", "band"), ("dom", "lat"), None)
    count = P(("groups", "band"), ("dom", "lat"))
    placed = (grid,) + (P(),) * 7 + (flat, flat) + (grid, grid, count) * 2
    return jax.shard_map(
        on_device,
        mesh=mesh,
        in_specs=placed,
        out_specs=(flat, count, count),
        check_vma=False,
    )
```

```python
import jax
import jax.numpy as jnp
from jax import lax
from jax.experimental import pallas as pl
from jax.experimental.pallas import tpu as pltpu
from jax.sharding import PartitionSpec as P

F32 = jnp.float32
BF16 = jnp.bfloat16
LANES = 128
GS, GR, GN, MS, MR, MN = range(6)


def mm(a, b):
    return jnp.dot(a, b, preferred_element_type=F32)


def mm_nt(a, b):
    return lax.dot_general(a, b, (((1,), (1,)), ((), ())), preferred_element_type=F32)


def mm_tn(a, b):
    return lax.dot_general(a, b, (((0,), (0,)), ((), ())), preferred_element_type=F32)


def halves(x):
    high = x.astype(BF16)
    return high, (x - high.astype(F32)).astype(BF16)


def silu_parts(x):
    g = 0.5 * jnp.tanh(0.5 * x) + 0.5
    value = x * g
    return value, g + value * (1.0 - g)


def ones_at(mask):
    return jnp.where(mask, 1.0, 0.0).astype(BF16)


def columns(row):
    count = row.shape[1]
    parts = [
        jnp.broadcast_to(row[:, i : i + LANES], (LANES, LANES)).T
        for i in range(0, count, LANES)
    ]
    return parts[0] if len(parts) == 1 else jnp.concatenate(parts, axis=0)


def hits_from(cols, width, period, start=0):
    parts = []
    for i in range(0, width, LANES):
        size = min(LANES, width - i)
        lane = lax.broadcasted_iota(jnp.int32, (cols.shape[0], size), 1) + i
        if period < width:
            lane = lax.rem(lane, period)
        parts.append(ones_at(cols[:, :size] == lane + start))
    return parts[0] if len(parts) == 1 else jnp.concatenate(parts, axis=1)


def hits_to(row, count):
    return ones_at(lax.broadcasted_iota(jnp.int32, (count, row.shape[1]), 0) == row)


def live_only(row, count, first=0):
    slot = lax.broadcasted_iota(jnp.int32, row.shape, 1) + first
    return jnp.where(slot < count, row, -1)


def weight(stack, index):
    latent = stack.shape[1]
    return stack[index * latent : (index + 1) * latent]


def even_on(axis):
    return lax.rem(lax.axis_index(axis), 2) == 0


def spread(index, blocks, cols, pitch):
    extra = jnp.zeros_like(index)
    for block in range(1, blocks):
        extra = extra + jnp.where(index >= block * cols, pitch - cols, 0)
    return index + extra


def fill(wide, blocks, pitch, first):
    cols = blocks.shape[2]
    for k in range(blocks.shape[0]):
        at = first + k * pitch
        wide[:, at : at + cols] = blocks[k]
        if cols < pitch:
            wide[:, at + cols : at + pitch] = jnp.zeros(
                (wide.shape[0], pitch - cols), wide.dtype
            )


def index_kernel(
    count, mesh_count, indices, grid,
    own_out, recv_hits, recv_rows, own_hits, outer_hits, to_hits, from_rows, to_rows, near_hits, far_hits, wide,
):
    edges = recv_hits.shape[0]
    mesh_edges = to_hits.shape[0]
    send, recv, mesh_send, mesh_recv = (
        indices[0, :, first : first + size]
        for first, size in (
            (0, edges),
            (edges, edges),
            (2 * edges, mesh_edges),
            (2 * edges + mesh_edges, mesh_edges),
        )
    )
    band_rows, _, cols = grid.shape
    pitch = wide.shape[1] // band_rows
    width = band_rows * pitch
    cycle = recv_rows.shape[0]
    node_count = to_rows.shape[0]
    even_band = even_on("band")
    fill(wide, grid, pitch, 0)
    near_base = jnp.where(even_band, 2 * width, 0)
    far_base = jnp.where(even_band, 0, 2 * width)
    block = 256
    for first in range(0, edges, block):
        part_of = slice(first, first + block)
        index = columns(spread(send[:, part_of], 3 * band_rows, cols, pitch))
        own_hit = hits_from(index, width, width, width)
        own_out[part_of] = mm_nt(own_hit, wide[...]).astype(BF16)
        near_hits[part_of] = hits_from(index, width, width, near_base)
        far_hits[part_of] = hits_from(index, width, width, far_base)
        target = live_only(recv[:, part_of], count[0, 0], first)
        recv_hits[part_of] = hits_from(columns(target), 2 * cycle, cycle)
        recv_rows[:, part_of] = hits_to(target, cycle)
    raw = mesh_send
    inner = (raw >= cycle) & (raw < 2 * cycle)
    above_near = jnp.where(raw < cycle, raw + cycle, raw - 2 * cycle)
    below_near = jnp.where(raw < cycle, raw, raw - cycle)
    outer = jnp.where(inner, -1, jnp.where(even_band, above_near, below_near))
    target = live_only(mesh_recv, mesh_count[0, 0])
    own_hits[...] = hits_from(columns(jnp.where(inner, raw - cycle, -1)), 2 * cycle, cycle)
    outer_hits[...] = hits_from(columns(outer), 4 * cycle, 2 * cycle)
    to_hits[...] = hits_from(columns(target), 2 * node_count, node_count)
    source = jnp.where(inner, raw, jnp.where(outer < cycle, outer, outer + cycle))
    from_rows[...] = hits_to(source, 3 * cycle)
    to_rows[...] = hits_to(target, node_count)


def receiver_kernel(near, far, mesh_in, recv_hits, stack, pre_out):
    node_count = mesh_in.shape[0]
    rim = node_count // 2
    even = even_on("lat")
    left = jnp.where(even, far[...], near[...])[rim:]
    right = jnp.where(even, near[...], far[...])[:rim]
    cycle = jnp.concatenate([left, mesh_in[...], right], axis=0)
    table = jnp.concatenate(halves(mm(cycle, weight(stack, GR))), axis=0)
    pre_out[...] = mm(recv_hits[...], table)


def gather_kernel(halo, hits, rows, rows_out, wide):
    fill(wide, halo, wide.shape[1] // halo.shape[0], 0)
    rows_out[...] = rows[...] + mm_nt(hits[...], wide[...]).astype(BF16)


def encode_kernel(
    near, near_hits, recv_rows, rows, recv_pre, stack,
    senders_out, slope_out, part_out, near_out, far_out, wide,
):
    half = recv_rows.shape[0] // 2
    fill(wide, near, wide.shape[1] // near.shape[0], 0)
    block = rows.shape[0] // 2
    sums = None
    for first in range(0, rows.shape[0], block):
        part_of = slice(first, first + block)
        raw = rows[part_of] + mm_nt(near_hits[part_of], wide[...]).astype(BF16)
        latent, _ = silu_parts(mm(raw, stack[stack.shape[0] - raw.shape[1] :]))
        latent = latent.astype(BF16)
        senders_out[part_of] = latent
        pre = mm(latent, weight(stack, GS)) + recv_pre[part_of]
        value, slope = silu_parts(pre)
        slope_out[part_of] = slope.astype(BF16)
        part = mm(recv_rows[:, part_of], value.astype(BF16))
        sums = part if sums is None else sums + part
    part_out[...] = sums
    even = even_on("lat")
    near_out[...] = jnp.where(even, sums[half:], sums[:half]).astype(BF16)
    far_out[...] = jnp.where(even, sums[:half], sums[half:]).astype(BF16)


def node_kernel(part, near, far, mesh_near, mesh_far, mesh_in, stack, mesh_out, slope_out):
    node_count = mesh_in.shape[0]
    rim = node_count // 2
    even = even_on("lat")
    left = jnp.where(even, far[...], near[...]).astype(F32)
    right = jnp.where(even, near[...], far[...]).astype(F32)
    total = part[...] + jnp.concatenate([left, right], axis=0)
    mesh_left = jnp.where(even, mesh_far[...], mesh_near[...])[rim:]
    mesh_right = jnp.where(even, mesh_near[...], mesh_far[...])[:rim]
    cycle = jnp.concatenate([mesh_left, mesh_in[...], mesh_right], axis=0)
    value, slope = silu_parts(mm(total.astype(BF16), weight(stack, GN)))
    mesh_out[...] = (cycle.astype(F32) + value).astype(BF16)
    slope_out[...] = slope


def process_own_kernel(own_hits, to_hits, own, stack, pre_out):
    rim = own.shape[0] // 4
    home = own[rim : own.shape[0] - rim]
    table = jnp.concatenate(halves(mm(own[...], weight(stack, MS))), axis=0)
    recv_table = jnp.concatenate(halves(mm(home, weight(stack, MR))), axis=0)
    pre_out[...] = mm(own_hits[...], table) + mm(to_hits[...], recv_table)


def process_kernel(
    own_pre, outer_hits, to_hits, from_rows, to_rows, far, own, near, d_out, stack,
    mesh_out, sums_out, recv_out, near_out, far_out,
):
    cycle = own.shape[0]
    node_count = cycle // 2
    rim = node_count // 2
    home = own[rim : rim + node_count]
    block = jnp.concatenate([near[...], far[...]], axis=0)
    table = jnp.concatenate(halves(mm(block, weight(stack, MS))), axis=0)
    pre = own_pre[...] + mm(outer_hits[...], table)
    value, slope = silu_parts(pre)
    gate = mm(mm(to_rows[...], value.astype(BF16)).astype(BF16), weight(stack, MN))
    gate_value, gate_slope = silu_parts(gate)
    mesh_out[...] = (home.astype(F32) + gate_value).astype(BF16)
    gate_two = (d_out[...].astype(F32) * gate_slope).astype(BF16)
    back = jnp.concatenate(halves(mm_nt(gate_two, weight(stack, MN))), axis=0)
    edge_slope = (mm(to_hits[...], back) * slope).astype(BF16)
    sums = mm(from_rows[...], edge_slope)
    recv_out[...] = mm(to_rows[...], edge_slope).astype(BF16)
    sums_out[...] = sums
    near_out[...] = sums[:cycle].astype(BF16)
    far_out[...] = sums[2 * cycle :].astype(BF16)


def block_of(x, dom_shift, lat_shift, doms, lats):
    cols = x.shape[1] // (doms * lats)
    dom = lax.rem(lax.axis_index("dom") + dom_shift, doms)
    index = dom * lats + lax.rem(lax.axis_index("lat") + lat_shift, lats)
    pick = x[:, :cols]
    for i in range(1, doms * lats):
        pick = jnp.where(index == i, x[:, i * cols : (i + 1) * cols], pick)
    return pick


def home_kernel(recv_sum, d_out, stack, senders, home_out, turned_out):
    home_out[...] = mm_nt(recv_sum[...], weight(stack, MR)) + d_out[...].astype(F32)
    turned_out[...] = senders[...].T


def cotangent_kernel(sums, near, far, home, part_out, near_out, far_out):
    cycle = near.shape[0]
    half = cycle // 2
    rim = half // 2
    total = sums[cycle : 2 * cycle] + near[...].astype(F32) + far[...].astype(F32)
    part_out[...] = total
    even = even_on("lat")
    near_out[:half] = jnp.where(even, total[half:], total[:half]).astype(BF16)
    near_out[half:] = jnp.where(even, home[rim:], home[:rim]).astype(BF16)
    far_out[:half] = jnp.where(even, total[:half], total[half:]).astype(BF16)
    far_out[half:] = jnp.where(even, home[:rim], home[rim:]).astype(BF16)


def gradient_block(recv_hits, back, edge_slope, senders, shifts, doms, lats):
    edges = recv_hits.shape[0]
    back = [block_of(back, *shift, doms, lats) for shift in shifts]
    back = back[0] if len(back) == 1 else jnp.concatenate(back, axis=1)
    total = None
    for first in range(0, edges, edges // 2):
        part_of = slice(first, first + edges // 2)
        weights = [block_of(edge_slope[part_of], *shift, doms, lats) for shift in shifts]
        weights = weights[0] if len(weights) == 1 else jnp.concatenate(weights, axis=1)
        slope = mm(recv_hits[part_of], back) * weights.astype(F32)
        part = mm(senders[:, part_of], slope.astype(BF16))
        total = part if total is None else total + part
    return total


def encode_grad_kernel(
    recv_hits, part, near, far, home, node_slope, stack, senders, edge_slope,
    sends, back_out, total_out,
):
    half = part.shape[0] // 2
    even = even_on("lat")
    left = jnp.where(even, far[...], near[...]).astype(F32)
    right = jnp.where(even, near[...], far[...]).astype(F32)
    total = part[...] + jnp.concatenate([left[:half], right[:half]], axis=0)
    total = total.astype(BF16)
    rest = jnp.concatenate([left[half:], home[...], right[half:]], axis=0)
    cot = rest + mm_nt(total, weight(stack, MS))
    gate_one = (cot * node_slope[...]).astype(BF16)
    back = jnp.concatenate(halves(mm_nt(gate_one, weight(stack, GN))), axis=0)
    back_out[...] = back
    lats = sends.shape[0] + 1
    doms = sends.shape[1] + 1
    for i in range(1, lats):
        for j in range(1, doms):
            block = gradient_block(
                recv_hits, back, edge_slope, senders, [(j, i)], doms, lats
            )
            sends[i - 1, j - 1] = block.astype(BF16)
    for j in range(doms):
        total_out[j] = block_of(total, j, 0, doms, lats)


def middle_blocks_kernel(recv_hits, back, edge_slope, senders, after, kept, sends):
    doms = kept.shape[0] + 1
    lats = sends.shape[0] + 1
    cols = kept.shape[2]
    shifts = [(j, 0) for j in range(1, doms)] + [(0, i) for i in range(1, lats)]
    blocks = gradient_block(recv_hits, back[...], edge_slope, senders, shifts, doms, lats)
    for k in range(len(shifts)):
        block = blocks[:, k * cols : (k + 1) * cols]
        if k < doms - 1:
            kept[k] = block
        else:
            sends[k - doms + 1] = block.astype(BF16)


def rows_at(ref, place, partner):
    bands = lax.axis_size("band")
    rows = ref.shape[-2] // bands
    at = pl.multiple_of(lax.bitwise_xor(lax.axis_index("band"), partner) * rows, rows)
    return ref[(*place, pl.ds(at, rows))]


def add_kernel(kept, total, *refs):
    *came, first_out, second_out = refs
    bands = lax.axis_size("band")
    rows = kept.shape[1] // bands
    near = second_out.shape[1] // rows
    for j in range(kept.shape[0]):
        for k in range(bands):
            block = rows_at(kept, (j,), k)
            for part in came:
                block = block + rows_at(part, (j,), k).astype(F32)
            out, at = (first_out, k - near) if k >= near else (second_out, k)
            at = at * rows
            out[j, at : at + rows] = block.astype(BF16)
        first_out[j, (bands - near) * rows :] = total[j + 1]


def own_block_kernel(recv_hits, back, edge_slope, senders, *refs):
    *came, out = refs
    lats = len(came) + 1
    doms = back.shape[1] // out.shape[1] // lats
    block = gradient_block(
        recv_hits, back[...], edge_slope, senders, [(0, 0)], doms, lats
    )
    for part in came:
        block = block + part[...].astype(F32)
    out[...] = block


def first_kernel(kept, total, nodes, *refs):
    doms = total.shape[0]
    came, (*sends_out, sums) = refs[: 2 * (doms - 1)], refs[2 * (doms - 1) :]
    came, came_nodes = came[: doms - 1], came[doms - 1 :]
    far = len(sends_out)
    near = lax.axis_size("band") - far
    rows = sends_out[0].shape[1]
    second = mm_tn(nodes[...], total[0])
    for part, part_nodes in zip(came, came_nodes):
        second = second + mm_tn(part_nodes[...], part[far * rows :])
    sums[...] = second
    for i, out in enumerate(sends_out):
        block = rows_at(kept, (), near + i)
        for part in came:
            block = block + part[i * rows : (i + 1) * rows].astype(F32)
        out[0] = block.astype(BF16)
        out[1] = rows_at(sums, (), near + i).astype(BF16)


def second_kernel(kept, sums, *refs):
    doms = lax.axis_size("dom")
    came, outs = refs[: doms - 1], refs[doms - 1 :]
    rows = outs[0].shape[1]
    for i, out in enumerate(outs):
        block = rows_at(kept, (), i)
        for part in came:
            block = block + part[i * rows : (i + 1) * rows].astype(F32)
        out[0] = block.astype(out.dtype)
        out[1] = rows_at(sums, (), i).astype(out.dtype)


def over_band_kernel(*refs):
    *came, own, first_out, second_out = refs
    for k, out in enumerate((first_out, second_out)):
        total = own[k]
        for part in came:
            total = total + part[k].astype(F32)
        out[...] = total


def call(kernel, outs, *args, scalars=(), scratch=()):
    in_specs = [
        pl.BlockSpec(memory_space=pltpu.SMEM if i in scalars else pltpu.VMEM)
        for i in range(len(args))
    ]
    return pl.pallas_call(
        kernel,
        out_shape=[jax.ShapeDtypeStruct(shape, dtype) for shape, dtype in outs],
        in_specs=in_specs,
        out_specs=[pl.BlockSpec(memory_space=pltpu.VMEM)] * len(outs),
        scratch_shapes=scratch,
        compiler_params=pltpu.CompilerParams(vmem_limit_bytes=16 << 20),
    )(*args)


def ring_pairings(count):
    far = [(i, (i + 1 if i % 2 else i - 1) % count) for i in range(count)]
    return [(i, i ^ 1) for i in range(count)], far


def line_pairings(bands, doms, lats):
    far = []
    for band in range(bands):
        other = band + 1 if band % 2 else band - 1
        for dom in range(doms):
            for lat in range(lats):
                here = (band * doms + dom) * lats + lat
                if 0 <= other < bands:
                    there = (other * doms + dom) * lats + lat
                else:
                    there = (band * doms + dom) * lats + (lat ^ 1)
                far.append((here, there))
    return [(i, i ^ 1) for i in range(bands)], far


def shifted(x, axis, shift):
    count = lax.axis_size(axis)
    return lax.ppermute(x, axis, [(i, (i + shift) % count) for i in range(count)])


def over_band(x, partner):
    count = lax.axis_size("band")
    return lax.ppermute(x, "band", [(b, b ^ partner) for b in range(count)])


def on_device(
    grid_in, w_grid, w_gs, w_gr, w_gn, w_ms, w_mr, w_mn, mesh_in, d_out,
    g2m_send, g2m_recv, g2m_count, mesh_send, mesh_recv, mesh_count,
):
    latent = w_grid.shape[1]
    variables = w_grid.shape[0]
    node_count = mesh_in.shape[0]
    cycle = 2 * node_count
    bands = lax.axis_size("band")
    sectors = lax.axis_size(("dom", "lat"))
    edges = g2m_send.shape[2]
    around = ("dom", "lat")
    whole = ("band", "dom", "lat")
    band_near, band_far = line_pairings(bands, lax.axis_size("dom"), lax.axis_size("lat"))
    ring_near, ring_far = ring_pairings(sectors)

    grid = jnp.transpose(grid_in, (0, 2, 1))
    pitch = -(-grid.shape[2] // LANES) * LANES
    band_rows = grid.shape[0]
    width = band_rows * pitch
    raw_near = lax.ppermute(grid, "band", band_near)
    raw_far = lax.ppermute(grid, whole, band_far)
    mesh_edges = mesh_send.shape[2]
    stack = jnp.concatenate([w_gs, w_gr, w_gn, w_ms, w_mr, w_mn, w_grid], axis=0)
    indices = jnp.concatenate([g2m_send, g2m_recv, mesh_send, mesh_recv], axis=2)
    (
        rows, recv_hits, recv_rows, own_hits, outer_hits, to_hits, from_rows, to_rows, *halo_hits
    ) = call(
        index_kernel,
        [
            ((edges, variables), BF16),
            ((edges, 2 * cycle), BF16),
            ((cycle, edges), BF16),
            ((mesh_edges, 2 * cycle), BF16),
            ((mesh_edges, 4 * cycle), BF16),
            ((mesh_edges, 2 * node_count), BF16),
            ((3 * cycle, mesh_edges), BF16),
            ((node_count, mesh_edges), BF16),
            ((edges, width), BF16),
            ((edges, width), BF16),
        ],
        g2m_count, mesh_count, indices, grid,
        scalars=(0, 1),
        scratch=[pltpu.VMEM((variables, width), BF16)],
    )
    late_mesh, rows = lax.optimization_barrier((mesh_in, rows))
    mesh_near = lax.ppermute(late_mesh, around, ring_near)
    mesh_far = lax.ppermute(late_mesh, around, ring_far)
    (recv_pre,) = call(
        receiver_kernel,
        [((edges, latent), F32)],
        mesh_near, mesh_far, mesh_in, recv_hits, stack,
    )
    near_hits, far_hits = halo_hits
    (rows,) = call(
        gather_kernel,
        [((edges, variables), BF16)],
        raw_far, far_hits, rows,
        scratch=[pltpu.VMEM((variables, width), BF16)],
    )
    senders, edge_slope, part, to_near, to_far = call(
        encode_kernel,
        [
            ((edges, latent), BF16),
            ((edges, latent), BF16),
            ((cycle, latent), F32),
            ((node_count, latent), BF16),
            ((node_count, latent), BF16),
        ],
        raw_near, near_hits, recv_rows, rows, recv_pre, stack,
        scratch=[pltpu.VMEM((variables, width), BF16)],
    )
    from_far = lax.ppermute(to_far, around, ring_far)
    from_near = lax.ppermute(to_near, around, ring_near)
    mesh_one, node_slope = call(
        node_kernel,
        [((cycle, latent), BF16), ((cycle, latent), F32)],
        part, from_near, from_far, mesh_near, mesh_far, mesh_in, stack,
    )
    one_near = lax.ppermute(mesh_one, "band", band_near)
    one_far = lax.ppermute(mesh_one, whole, band_far)
    doms = lax.axis_size("dom")
    lats = lax.axis_size("lat")
    dom_nodes = [shifted(mesh_one, "dom", i + 1) for i in range(doms - 1)]
    (own_pre,) = call(
        process_own_kernel, [((mesh_edges, latent), F32)], own_hits, to_hits, mesh_one, stack
    )
    mesh_out, sums, recv_sum, to_near, to_far = call(
        process_kernel,
        [
            ((node_count, latent), BF16),
            ((3 * cycle, latent), F32),
            ((node_count, latent), BF16),
            ((cycle, latent), BF16),
            ((cycle, latent), BF16),
        ],
        own_pre, outer_hits, to_hits, from_rows, to_rows, one_far, mesh_one, one_near, d_out,
        stack,
    )
    from_near = lax.ppermute(to_near, "band", band_near)
    from_far = lax.ppermute(to_far, whole, band_far)
    home, senders = call(
        home_kernel,
        [((node_count, latent), F32), ((latent, edges), BF16)],
        recv_sum, d_out, stack, senders,
    )
    message = (node_count + node_count // 2, latent)
    part, to_near, to_far = call(
        cotangent_kernel,
        [((cycle, latent), F32), (message, BF16), (message, BF16)],
        sums, from_near, from_far, home,
    )
    from_far = lax.ppermute(to_far, around, ring_far)
    from_near = lax.ppermute(to_near, around, ring_near)

    from_near, *dom_nodes = lax.optimization_barrier((from_near, *dom_nodes))
    cols = latent // sectors
    rows = latent // bands
    sends, back, total = call(
        encode_grad_kernel,
        [
            ((lats - 1, doms - 1, latent, cols), BF16),
            ((2 * cycle, latent), BF16),
            ((doms, cycle, cols), BF16),
        ],
        recv_hits, part, from_near, from_far, home, node_slope, stack, senders, edge_slope,
    )
    edge = (recv_hits, back, edge_slope, senders)
    came = [shifted(sends[i], "lat", i + 1) for i in range(lats - 1)]
    block = (latent, cols)
    kept, own_sends = call(
        middle_blocks_kernel,
        [((doms - 1,) + block, F32), ((lats - 1,) + block, BF16)],
        *edge, sends,
    )
    own_came = [shifted(own_sends[i], "lat", i + 1) for i in range(lats - 1)]
    far = bands // 2
    first, second = call(
        add_kernel,
        [
            ((doms - 1, far * rows + cycle, cols), BF16),
            ((doms - 1, (bands - far) * rows, cols), BF16),
        ],
        kept, total, *came,
    )
    first = [shifted(first[i], "dom", i + 1) for i in range(doms - 1)]
    second = [shifted(second[i], "dom", i + 1) for i in range(doms - 1)]
    (kept,) = call(own_block_kernel, [(block, F32)], *edge, *own_came)
    pair = (2, rows, cols)
    *far_sends, sums = call(
        first_kernel,
        [(pair, BF16)] * far + [(block, F32)],
        kept, total, mesh_one, *first, *dom_nodes,
    )
    came = [over_band(x, bands - far + i) for i, x in reversed(list(enumerate(far_sends)))]
    own, *near_sends = call(
        second_kernel,
        [(pair, F32)] + [(pair, BF16)] * (bands - far - 1),
        kept, sums, *second,
    )
    came += [over_band(x, i + 1) for i, x in reversed(list(enumerate(near_sends)))]
    tile = ((rows, cols), F32)
    grad_gs, grad_ms = call(over_band_kernel, [tile, tile], *came, own)
    return mesh_out, grad_gs, grad_ms


def solution(mesh):
    flat = P(("groups", "band", "dom", "lat"), None)
    grid = P(("groups", "band"), ("dom", "lat"), None)
    count = P(("groups", "band"), ("dom", "lat"))
    placed = (grid,) + (P(),) * 7 + (flat, flat) + (grid, grid, count) * 2
    return jax.shard_map(
        on_device,
        mesh=mesh,
        in_specs=placed,
        out_specs=(flat, count, count),
        check_vma=False,
    )
```

```python
import jax
import jax.numpy as jnp
from jax import lax
from jax.experimental import pallas as pl
from jax.experimental.pallas import tpu as pltpu
from jax.sharding import PartitionSpec as P

F32 = jnp.float32
BF16 = jnp.bfloat16
LANES = 128
GS, GR, GN, MS, MR, MN = range(6)


def mm(a, b):
    return jnp.dot(a, b, preferred_element_type=F32)


def mm_nt(a, b):
    return lax.dot_general(a, b, (((1,), (1,)), ((), ())), preferred_element_type=F32)


def mm_tn(a, b):
    return lax.dot_general(a, b, (((0,), (0,)), ((), ())), preferred_element_type=F32)


def halves(x):
    high = x.astype(BF16)
    return high, (x - high.astype(F32)).astype(BF16)


def silu_parts(x):
    g = 0.5 * jnp.tanh(0.5 * x) + 0.5
    value = x * g
    return value, g + value * (1.0 - g)


def ones_at(mask):
    return jnp.where(mask, 1.0, 0.0).astype(BF16)


def columns(row):
    count = row.shape[1]
    parts = [
        jnp.broadcast_to(row[:, i : i + LANES], (LANES, LANES)).T
        for i in range(0, count, LANES)
    ]
    return parts[0] if len(parts) == 1 else jnp.concatenate(parts, axis=0)


def hits_from(cols, width, period, start=0):
    parts = []
    for i in range(0, width, LANES):
        size = min(LANES, width - i)
        lane = lax.broadcasted_iota(jnp.int32, (cols.shape[0], size), 1) + i
        if period < width:
            lane = lax.rem(lane, period)
        parts.append(ones_at(cols[:, :size] == lane + start))
    return parts[0] if len(parts) == 1 else jnp.concatenate(parts, axis=1)


def hits_to(row, count):
    return ones_at(lax.broadcasted_iota(jnp.int32, (count, row.shape[1]), 0) == row)


def live_only(row, count, first=0):
    slot = lax.broadcasted_iota(jnp.int32, row.shape, 1) + first
    return jnp.where(slot < count, row, -1)


def weight(stack, index):
    latent = stack.shape[1]
    return stack[index * latent : (index + 1) * latent]


def even_on(axis):
    return lax.rem(lax.axis_index(axis), 2) == 0


def spread(index, blocks, cols, pitch):
    extra = jnp.zeros_like(index)
    for block in range(1, blocks):
        extra = extra + jnp.where(index >= block * cols, pitch - cols, 0)
    return index + extra


def fill(wide, blocks, pitch, first):
    cols = blocks.shape[2]
    for k in range(blocks.shape[0]):
        at = first + k * pitch
        wide[:, at : at + cols] = blocks[k]
        if cols < pitch:
            wide[:, at + cols : at + pitch] = jnp.zeros(
                (wide.shape[0], pitch - cols), wide.dtype
            )


def index_kernel(
    count, mesh_count, indices, grid,
    own_out, recv_hits, recv_rows, own_hits, outer_hits, to_hits, from_rows, to_rows, near_hits, far_hits, wide,
):
    edges = recv_hits.shape[0]
    mesh_edges = to_hits.shape[0]
    send, recv, mesh_send, mesh_recv = (
        indices[0, :, first : first + size]
        for first, size in (
            (0, edges),
            (edges, edges),
            (2 * edges, mesh_edges),
            (2 * edges + mesh_edges, mesh_edges),
        )
    )
    band_rows, _, cols = grid.shape
    pitch = wide.shape[1] // band_rows
    width = band_rows * pitch
    cycle = recv_rows.shape[0]
    node_count = to_rows.shape[0]
    even_band = even_on("band")
    fill(wide, grid, pitch, 0)
    near_base = jnp.where(even_band, 2 * width, 0)
    far_base = jnp.where(even_band, 0, 2 * width)
    block = 256
    for first in range(0, edges, block):
        part_of = slice(first, first + block)
        index = columns(spread(send[:, part_of], 3 * band_rows, cols, pitch))
        own_hit = hits_from(index, width, width, width)
        own_out[part_of] = mm_nt(own_hit, wide[...]).astype(BF16)
        near_hits[part_of] = hits_from(index, width, width, near_base)
        far_hits[part_of] = hits_from(index, width, width, far_base)
        target = live_only(recv[:, part_of], count[0, 0], first)
        recv_hits[part_of] = hits_from(columns(target), 2 * cycle, cycle)
        recv_rows[:, part_of] = hits_to(target, cycle)
    raw = mesh_send
    inner = (raw >= cycle) & (raw < 2 * cycle)
    above_near = jnp.where(raw < cycle, raw + cycle, raw - 2 * cycle)
    below_near = jnp.where(raw < cycle, raw, raw - cycle)
    outer = jnp.where(inner, -1, jnp.where(even_band, above_near, below_near))
    target = live_only(mesh_recv, mesh_count[0, 0])
    own_hits[...] = hits_from(columns(jnp.where(inner, raw - cycle, -1)), 2 * cycle, cycle)
    outer_hits[...] = hits_from(columns(outer), 4 * cycle, 2 * cycle)
    to_hits[...] = hits_from(columns(target), 2 * node_count, node_count)
    source = jnp.where(inner, raw, jnp.where(outer < cycle, outer, outer + cycle))
    from_rows[...] = hits_to(source, 3 * cycle)
    to_rows[...] = hits_to(target, node_count)


def receiver_kernel(near, far, mesh_in, recv_hits, stack, pre_out):
    node_count = mesh_in.shape[0]
    rim = node_count // 2
    even = even_on("lat")
    left = jnp.where(even, far[...], near[...])[rim:]
    right = jnp.where(even, near[...], far[...])[:rim]
    cycle = jnp.concatenate([left, mesh_in[...], right], axis=0)
    table = jnp.concatenate(halves(mm(cycle, weight(stack, GR))), axis=0)
    pre_out[...] = mm(recv_hits[...], table)


def live_blocks(count, edges, work, rest):
    work(slice(0, edges // 2))
    for first in (edges // 2, 3 * edges // 4):
        part_of = slice(first, first + edges // 4)
        pl.when(count[0, 0] > first)(lambda part_of=part_of: work(part_of))
        pl.when(count[0, 0] <= first)(lambda part_of=part_of: rest(part_of))


def gather_kernel(count, halo, hits, rows, rows_out, wide):
    fill(wide, halo, wide.shape[1] // halo.shape[0], 0)

    def work(part_of):
        gathered = mm_nt(hits[part_of], wide[...]).astype(BF16)
        rows_out[part_of] = rows[part_of] + gathered

    def rest(part_of):
        rows_out[part_of] = jnp.zeros_like(rows_out[part_of])

    live_blocks(count, rows.shape[0], work, rest)


def encode_kernel(
    count, near, near_hits, recv_rows, rows, recv_pre, stack,
    senders_out, slope_out, part_out, near_out, far_out, wide,
):
    half = recv_rows.shape[0] // 2
    fill(wide, near, wide.shape[1] // near.shape[0], 0)
    part_out[...] = jnp.zeros_like(part_out)

    def work(part_of):
        raw = rows[part_of] + mm_nt(near_hits[part_of], wide[...]).astype(BF16)
        latent, _ = silu_parts(mm(raw, stack[stack.shape[0] - raw.shape[1] :]))
        latent = latent.astype(BF16)
        senders_out[part_of] = latent
        pre = mm(latent, weight(stack, GS)) + recv_pre[part_of]
        value, slope = silu_parts(pre)
        slope_out[part_of] = slope.astype(BF16)
        part_out[...] += mm(recv_rows[:, part_of], value.astype(BF16))

    def rest(part_of):
        senders_out[part_of] = jnp.zeros_like(senders_out[part_of])
        slope_out[part_of] = jnp.zeros_like(slope_out[part_of])

    live_blocks(count, rows.shape[0], work, rest)
    sums = part_out[...]
    even = even_on("lat")
    near_out[...] = jnp.where(even, sums[half:], sums[:half]).astype(BF16)
    far_out[...] = jnp.where(even, sums[:half], sums[half:]).astype(BF16)


def node_kernel(part, near, far, mesh_near, mesh_far, mesh_in, stack, mesh_out, slope_out):
    node_count = mesh_in.shape[0]
    rim = node_count // 2
    even = even_on("lat")
    left = jnp.where(even, far[...], near[...]).astype(F32)
    right = jnp.where(even, near[...], far[...]).astype(F32)
    total = part[...] + jnp.concatenate([left, right], axis=0)
    mesh_left = jnp.where(even, mesh_far[...], mesh_near[...])[rim:]
    mesh_right = jnp.where(even, mesh_near[...], mesh_far[...])[:rim]
    cycle = jnp.concatenate([mesh_left, mesh_in[...], mesh_right], axis=0)
    value, slope = silu_parts(mm(total.astype(BF16), weight(stack, GN)))
    mesh_out[...] = (cycle.astype(F32) + value).astype(BF16)
    slope_out[...] = slope


def process_own_kernel(own_hits, to_hits, own, stack, pre_out):
    rim = own.shape[0] // 4
    home = own[rim : own.shape[0] - rim]
    table = jnp.concatenate(halves(mm(own[...], weight(stack, MS))), axis=0)
    recv_table = jnp.concatenate(halves(mm(home, weight(stack, MR))), axis=0)
    pre_out[...] = mm(own_hits[...], table) + mm(to_hits[...], recv_table)


def process_kernel(
    own_pre, outer_hits, to_hits, from_rows, to_rows, far, own, near, d_out, stack,
    mesh_out, sums_out, recv_out, near_out, far_out,
):
    cycle = own.shape[0]
    node_count = cycle // 2
    rim = node_count // 2
    home = own[rim : rim + node_count]
    block = jnp.concatenate([near[...], far[...]], axis=0)
    table = jnp.concatenate(halves(mm(block, weight(stack, MS))), axis=0)
    pre = own_pre[...] + mm(outer_hits[...], table)
    value, slope = silu_parts(pre)
    gate = mm(mm(to_rows[...], value.astype(BF16)).astype(BF16), weight(stack, MN))
    gate_value, gate_slope = silu_parts(gate)
    mesh_out[...] = (home.astype(F32) + gate_value).astype(BF16)
    gate_two = (d_out[...].astype(F32) * gate_slope).astype(BF16)
    back = jnp.concatenate(halves(mm_nt(gate_two, weight(stack, MN))), axis=0)
    edge_slope = (mm(to_hits[...], back) * slope).astype(BF16)
    sums = mm(from_rows[...], edge_slope)
    recv_out[...] = mm(to_rows[...], edge_slope).astype(BF16)
    sums_out[...] = sums
    near_out[...] = sums[:cycle].astype(BF16)
    far_out[...] = sums[2 * cycle :].astype(BF16)


def block_of(x, dom_shift, lat_shift, doms, lats):
    cols = x.shape[1] // (doms * lats)
    dom = lax.rem(lax.axis_index("dom") + dom_shift, doms)
    index = dom * lats + lax.rem(lax.axis_index("lat") + lat_shift, lats)
    pick = x[:, :cols]
    for i in range(1, doms * lats):
        pick = jnp.where(index == i, x[:, i * cols : (i + 1) * cols], pick)
    return pick


def home_kernel(recv_sum, d_out, stack, senders, home_out, turned_out):
    home_out[...] = mm_nt(recv_sum[...], weight(stack, MR)) + d_out[...].astype(F32)
    turned_out[...] = senders[...].T


def cotangent_kernel(sums, near, far, home, part_out, near_out, far_out):
    cycle = near.shape[0]
    half = cycle // 2
    rim = half // 2
    total = sums[cycle : 2 * cycle] + near[...].astype(F32) + far[...].astype(F32)
    part_out[...] = total
    even = even_on("lat")
    near_out[:half] = jnp.where(even, total[half:], total[:half]).astype(BF16)
    near_out[half:] = jnp.where(even, home[rim:], home[:rim]).astype(BF16)
    far_out[:half] = jnp.where(even, total[:half], total[half:]).astype(BF16)
    far_out[half:] = jnp.where(even, home[:rim], home[rim:]).astype(BF16)


def gradient_block(recv_hits, back, edge_slope, senders, shifts, doms, lats):
    edges = recv_hits.shape[0]
    back = [block_of(back, *shift, doms, lats) for shift in shifts]
    back = back[0] if len(back) == 1 else jnp.concatenate(back, axis=1)
    total = None
    for first in range(0, edges, edges // 2):
        part_of = slice(first, first + edges // 2)
        weights = [block_of(edge_slope[part_of], *shift, doms, lats) for shift in shifts]
        weights = weights[0] if len(weights) == 1 else jnp.concatenate(weights, axis=1)
        slope = mm(recv_hits[part_of], back) * weights.astype(F32)
        part = mm(senders[:, part_of], slope.astype(BF16))
        total = part if total is None else total + part
    return total


def encode_grad_kernel(
    recv_hits, part, near, far, home, node_slope, stack, senders, edge_slope,
    sends, back_out, total_out,
):
    half = part.shape[0] // 2
    even = even_on("lat")
    left = jnp.where(even, far[...], near[...]).astype(F32)
    right = jnp.where(even, near[...], far[...]).astype(F32)
    total = part[...] + jnp.concatenate([left[:half], right[:half]], axis=0)
    total = total.astype(BF16)
    rest = jnp.concatenate([left[half:], home[...], right[half:]], axis=0)
    cot = rest + mm_nt(total, weight(stack, MS))
    gate_one = (cot * node_slope[...]).astype(BF16)
    back = jnp.concatenate(halves(mm_nt(gate_one, weight(stack, GN))), axis=0)
    back_out[...] = back
    lats = sends.shape[0] + 1
    doms = sends.shape[1] + 1
    for i in range(1, lats):
        for j in range(1, doms):
            block = gradient_block(
                recv_hits, back, edge_slope, senders, [(j, i)], doms, lats
            )
            sends[i - 1, j - 1] = block.astype(BF16)
    for j in range(doms):
        total_out[j] = block_of(total, j, 0, doms, lats)


def middle_blocks_kernel(recv_hits, back, edge_slope, senders, after, kept, sends):
    doms = kept.shape[0] + 1
    lats = sends.shape[0] + 1
    cols = kept.shape[2]
    shifts = [(j, 0) for j in range(1, doms)] + [(0, i) for i in range(1, lats)]
    blocks = gradient_block(recv_hits, back[...], edge_slope, senders, shifts, doms, lats)
    for k in range(len(shifts)):
        block = blocks[:, k * cols : (k + 1) * cols]
        if k < doms - 1:
            kept[k] = block
        else:
            sends[k - doms + 1] = block.astype(BF16)


def rows_at(ref, place, partner):
    bands = lax.axis_size("band")
    rows = ref.shape[-2] // bands
    at = pl.multiple_of(lax.bitwise_xor(lax.axis_index("band"), partner) * rows, rows)
    return ref[(*place, pl.ds(at, rows))]


def add_kernel(kept, total, *refs):
    *came, first_out, second_out = refs
    bands = lax.axis_size("band")
    rows = kept.shape[1] // bands
    near = second_out.shape[1] // rows
    for j in range(kept.shape[0]):
        for k in range(bands):
            block = rows_at(kept, (j,), k)
            for part in came:
                block = block + rows_at(part, (j,), k).astype(F32)
            out, at = (first_out, k - near) if k >= near else (second_out, k)
            at = at * rows
            out[j, at : at + rows] = block.astype(BF16)
        first_out[j, (bands - near) * rows :] = total[j + 1]


def own_block_kernel(recv_hits, back, edge_slope, senders, *refs):
    *came, out = refs
    lats = len(came) + 1
    doms = back.shape[1] // out.shape[1] // lats
    block = gradient_block(
        recv_hits, back[...], edge_slope, senders, [(0, 0)], doms, lats
    )
    for part in came:
        block = block + part[...].astype(F32)
    out[...] = block


def first_kernel(kept, total, nodes, *refs):
    doms = total.shape[0]
    came, (*sends_out, sums) = refs[: 2 * (doms - 1)], refs[2 * (doms - 1) :]
    came, came_nodes = came[: doms - 1], came[doms - 1 :]
    far = len(sends_out)
    near = lax.axis_size("band") - far
    rows = sends_out[0].shape[1]
    second = mm_tn(nodes[...], total[0])
    for part, part_nodes in zip(came, came_nodes):
        second = second + mm_tn(part_nodes[...], part[far * rows :])
    sums[...] = second
    for i, out in enumerate(sends_out):
        block = rows_at(kept, (), near + i)
        for part in came:
            block = block + part[i * rows : (i + 1) * rows].astype(F32)
        out[0] = block.astype(BF16)
        out[1] = rows_at(sums, (), near + i).astype(BF16)


def second_kernel(kept, sums, *refs):
    doms = lax.axis_size("dom")
    came, outs = refs[: doms - 1], refs[doms - 1 :]
    rows = outs[0].shape[1]
    for i, out in enumerate(outs):
        block = rows_at(kept, (), i)
        for part in came:
            block = block + part[i * rows : (i + 1) * rows].astype(F32)
        out[0] = block.astype(out.dtype)
        out[1] = rows_at(sums, (), i).astype(out.dtype)


def over_band_kernel(*refs):
    *came, own, first_out, second_out = refs
    for k, out in enumerate((first_out, second_out)):
        total = own[k]
        for part in came:
            total = total + part[k].astype(F32)
        out[...] = total


def call(kernel, outs, *args, scalars=(), scratch=()):
    in_specs = [
        pl.BlockSpec(memory_space=pltpu.SMEM if i in scalars else pltpu.VMEM)
        for i in range(len(args))
    ]
    return pl.pallas_call(
        kernel,
        out_shape=[jax.ShapeDtypeStruct(shape, dtype) for shape, dtype in outs],
        in_specs=in_specs,
        out_specs=[pl.BlockSpec(memory_space=pltpu.VMEM)] * len(outs),
        scratch_shapes=scratch,
        compiler_params=pltpu.CompilerParams(vmem_limit_bytes=16 << 20),
    )(*args)


def ring_pairings(count):
    far = [(i, (i + 1 if i % 2 else i - 1) % count) for i in range(count)]
    return [(i, i ^ 1) for i in range(count)], far


def line_pairings(bands, doms, lats):
    far = []
    for band in range(bands):
        other = band + 1 if band % 2 else band - 1
        for dom in range(doms):
            for lat in range(lats):
                here = (band * doms + dom) * lats + lat
                if 0 <= other < bands:
                    there = (other * doms + dom) * lats + lat
                else:
                    there = (band * doms + dom) * lats + (lat ^ 1)
                far.append((here, there))
    return [(i, i ^ 1) for i in range(bands)], far


def shifted(x, axis, shift):
    count = lax.axis_size(axis)
    return lax.ppermute(x, axis, [(i, (i + shift) % count) for i in range(count)])


def over_band(x, partner):
    count = lax.axis_size("band")
    return lax.ppermute(x, "band", [(b, b ^ partner) for b in range(count)])


def on_device(
    grid_in, w_grid, w_gs, w_gr, w_gn, w_ms, w_mr, w_mn, mesh_in, d_out,
    g2m_send, g2m_recv, g2m_count, mesh_send, mesh_recv, mesh_count,
):
    latent = w_grid.shape[1]
    variables = w_grid.shape[0]
    node_count = mesh_in.shape[0]
    cycle = 2 * node_count
    bands = lax.axis_size("band")
    sectors = lax.axis_size(("dom", "lat"))
    edges = g2m_send.shape[2]
    around = ("dom", "lat")
    whole = ("band", "dom", "lat")
    band_near, band_far = line_pairings(bands, lax.axis_size("dom"), lax.axis_size("lat"))
    ring_near, ring_far = ring_pairings(sectors)

    grid = jnp.transpose(grid_in, (0, 2, 1))
    pitch = -(-grid.shape[2] // LANES) * LANES
    band_rows = grid.shape[0]
    width = band_rows * pitch
    raw_near = lax.ppermute(grid, "band", band_near)
    raw_far = lax.ppermute(grid, whole, band_far)
    mesh_edges = mesh_send.shape[2]
    stack = jnp.concatenate([w_gs, w_gr, w_gn, w_ms, w_mr, w_mn, w_grid], axis=0)
    indices = jnp.concatenate([g2m_send, g2m_recv, mesh_send, mesh_recv], axis=2)
    (
        rows, recv_hits, recv_rows, own_hits, outer_hits, to_hits, from_rows, to_rows, *halo_hits
    ) = call(
        index_kernel,
        [
            ((edges, variables), BF16),
            ((edges, 2 * cycle), BF16),
            ((cycle, edges), BF16),
            ((mesh_edges, 2 * cycle), BF16),
            ((mesh_edges, 4 * cycle), BF16),
            ((mesh_edges, 2 * node_count), BF16),
            ((3 * cycle, mesh_edges), BF16),
            ((node_count, mesh_edges), BF16),
            ((edges, width), BF16),
            ((edges, width), BF16),
        ],
        g2m_count, mesh_count, indices, grid,
        scalars=(0, 1),
        scratch=[pltpu.VMEM((variables, width), BF16)],
    )
    late_mesh, rows = lax.optimization_barrier((mesh_in, rows))
    mesh_near = lax.ppermute(late_mesh, around, ring_near)
    mesh_far = lax.ppermute(late_mesh, around, ring_far)
    (recv_pre,) = call(
        receiver_kernel,
        [((edges, latent), F32)],
        mesh_near, mesh_far, mesh_in, recv_hits, stack,
    )
    near_hits, far_hits = halo_hits
    (rows,) = call(
        gather_kernel,
        [((edges, variables), BF16)],
        g2m_count, raw_far, far_hits, rows,
        scalars=(0,),
        scratch=[pltpu.VMEM((variables, width), BF16)],
    )
    senders, edge_slope, part, to_near, to_far = call(
        encode_kernel,
        [
            ((edges, latent), BF16),
            ((edges, latent), BF16),
            ((cycle, latent), F32),
            ((node_count, latent), BF16),
            ((node_count, latent), BF16),
        ],
        g2m_count, raw_near, near_hits, recv_rows, rows, recv_pre, stack,
        scalars=(0,),
        scratch=[pltpu.VMEM((variables, width), BF16)],
    )
    from_far = lax.ppermute(to_far, around, ring_far)
    from_near = lax.ppermute(to_near, around, ring_near)
    mesh_one, node_slope = call(
        node_kernel,
        [((cycle, latent), BF16), ((cycle, latent), F32)],
        part, from_near, from_far, mesh_near, mesh_far, mesh_in, stack,
    )
    one_near = lax.ppermute(mesh_one, "band", band_near)
    one_far = lax.ppermute(mesh_one, whole, band_far)
    doms = lax.axis_size("dom")
    lats = lax.axis_size("lat")
    dom_nodes = [shifted(mesh_one, "dom", i + 1) for i in range(doms - 1)]
    (own_pre,) = call(
        process_own_kernel, [((mesh_edges, latent), F32)], own_hits, to_hits, mesh_one, stack
    )
    mesh_out, sums, recv_sum, to_near, to_far = call(
        process_kernel,
        [
            ((node_count, latent), BF16),
            ((3 * cycle, latent), F32),
            ((node_count, latent), BF16),
            ((cycle, latent), BF16),
            ((cycle, latent), BF16),
        ],
        own_pre, outer_hits, to_hits, from_rows, to_rows, one_far, mesh_one, one_near, d_out,
        stack,
    )
    from_near = lax.ppermute(to_near, "band", band_near)
    from_far = lax.ppermute(to_far, whole, band_far)
    home, senders = call(
        home_kernel,
        [((node_count, latent), F32), ((latent, edges), BF16)],
        recv_sum, d_out, stack, senders,
    )
    message = (node_count + node_count // 2, latent)
    part, to_near, to_far = call(
        cotangent_kernel,
        [((cycle, latent), F32), (message, BF16), (message, BF16)],
        sums, from_near, from_far, home,
    )
    from_far = lax.ppermute(to_far, around, ring_far)
    from_near = lax.ppermute(to_near, around, ring_near)

    from_near, *dom_nodes = lax.optimization_barrier((from_near, *dom_nodes))
    cols = latent // sectors
    rows = latent // bands
    sends, back, total = call(
        encode_grad_kernel,
        [
            ((lats - 1, doms - 1, latent, cols), BF16),
            ((2 * cycle, latent), BF16),
            ((doms, cycle, cols), BF16),
        ],
        recv_hits, part, from_near, from_far, home, node_slope, stack, senders, edge_slope,
    )
    edge = (recv_hits, back, edge_slope, senders)
    came = [shifted(sends[i], "lat", i + 1) for i in range(lats - 1)]
    block = (latent, cols)
    kept, own_sends = call(
        middle_blocks_kernel,
        [((doms - 1,) + block, F32), ((lats - 1,) + block, BF16)],
        *edge, sends,
    )
    own_came = [shifted(own_sends[i], "lat", i + 1) for i in range(lats - 1)]
    far = bands // 2
    first, second = call(
        add_kernel,
        [
            ((doms - 1, far * rows + cycle, cols), BF16),
            ((doms - 1, (bands - far) * rows, cols), BF16),
        ],
        kept, total, *came,
    )
    first = [shifted(first[i], "dom", i + 1) for i in range(doms - 1)]
    second = [shifted(second[i], "dom", i + 1) for i in range(doms - 1)]
    (kept,) = call(own_block_kernel, [(block, F32)], *edge, *own_came)
    pair = (2, rows, cols)
    *far_sends, sums = call(
        first_kernel,
        [(pair, BF16)] * far + [(block, F32)],
        kept, total, mesh_one, *first, *dom_nodes,
    )
    came = [over_band(x, bands - far + i) for i, x in reversed(list(enumerate(far_sends)))]
    own, *near_sends = call(
        second_kernel,
        [(pair, F32)] + [(pair, BF16)] * (bands - far - 1),
        kept, sums, *second,
    )
    came += [over_band(x, i + 1) for i, x in reversed(list(enumerate(near_sends)))]
    tile = ((rows, cols), F32)
    grad_gs, grad_ms = call(over_band_kernel, [tile, tile], *came, own)
    return mesh_out, grad_gs, grad_ms


def solution(mesh):
    flat = P(("groups", "band", "dom", "lat"), None)
    grid = P(("groups", "band"), ("dom", "lat"), None)
    count = P(("groups", "band"), ("dom", "lat"))
    placed = (grid,) + (P(),) * 7 + (flat, flat) + (grid, grid, count) * 2
    return jax.shard_map(
        on_device,
        mesh=mesh,
        in_specs=placed,
        out_specs=(flat, count, count),
        check_vma=False,
    )
```

```python
import jax
import jax.numpy as jnp
from jax import lax
from jax.experimental import pallas as pl
from jax.experimental.pallas import tpu as pltpu
from jax.sharding import PartitionSpec as P

F32 = jnp.float32
BF16 = jnp.bfloat16
LANES = 128
GS, GR, GN, MS, MR, MN = range(6)


def mm(a, b):
    return jnp.dot(a, b, preferred_element_type=F32)


def mm_nt(a, b):
    return lax.dot_general(a, b, (((1,), (1,)), ((), ())), preferred_element_type=F32)


def mm_tn(a, b):
    return lax.dot_general(a, b, (((0,), (0,)), ((), ())), preferred_element_type=F32)


def halves(x):
    high = x.astype(BF16)
    return high, (x - high.astype(F32)).astype(BF16)


def silu_parts(x):
    g = 0.5 * jnp.tanh(0.5 * x) + 0.5
    value = x * g
    return value, g + value * (1.0 - g)


def ones_at(mask):
    return jnp.where(mask, 1.0, 0.0).astype(BF16)


def columns(row):
    count = row.shape[1]
    parts = [
        jnp.broadcast_to(row[:, i : i + LANES], (LANES, LANES)).T
        for i in range(0, count, LANES)
    ]
    return parts[0] if len(parts) == 1 else jnp.concatenate(parts, axis=0)


def hits_from(cols, width, period, start=0):
    parts = []
    for i in range(0, width, LANES):
        size = min(LANES, width - i)
        lane = lax.broadcasted_iota(jnp.int32, (cols.shape[0], size), 1) + i
        if period < width:
            lane = lax.rem(lane, period)
        parts.append(ones_at(cols[:, :size] == lane + start))
    return parts[0] if len(parts) == 1 else jnp.concatenate(parts, axis=1)


def hits_to(row, count):
    return ones_at(lax.broadcasted_iota(jnp.int32, (count, row.shape[1]), 0) == row)


def live_only(row, count, first=0):
    slot = lax.broadcasted_iota(jnp.int32, row.shape, 1) + first
    return jnp.where(slot < count, row, -1)


def weight(stack, index):
    latent = stack.shape[1]
    return stack[index * latent : (index + 1) * latent]


def even_on(axis):
    return lax.rem(lax.axis_index(axis), 2) == 0


def spread(index, blocks, cols, pitch):
    extra = jnp.zeros_like(index)
    for block in range(1, blocks):
        extra = extra + jnp.where(index >= block * cols, pitch - cols, 0)
    return index + extra


def fill(wide, blocks, pitch, first):
    cols = blocks.shape[2]
    for k in range(blocks.shape[0]):
        at = first + k * pitch
        wide[:, at : at + cols] = blocks[k]
        if cols < pitch:
            wide[:, at + cols : at + pitch] = jnp.zeros(
                (wide.shape[0], pitch - cols), wide.dtype
            )


def index_kernel(
    count, mesh_count, indices, grid,
    own_out, recv_hits, recv_rows, own_hits, outer_hits, to_hits, from_rows, to_rows, near_hits, far_hits, wide,
):
    edges = recv_hits.shape[0]
    mesh_edges = to_hits.shape[0]
    send, recv, mesh_send, mesh_recv = (
        indices[0, :, first : first + size]
        for first, size in (
            (0, edges),
            (edges, edges),
            (2 * edges, mesh_edges),
            (2 * edges + mesh_edges, mesh_edges),
        )
    )
    band_rows, _, cols = grid.shape
    pitch = wide.shape[1] // band_rows
    width = band_rows * pitch
    cycle = recv_rows.shape[0]
    node_count = to_rows.shape[0]
    even_band = even_on("band")
    fill(wide, grid, pitch, 0)
    near_base = jnp.where(even_band, 2 * width, 0)
    far_base = jnp.where(even_band, 0, 2 * width)
    block = 256
    for first in range(0, edges, block):
        part_of = slice(first, first + block)
        index = columns(spread(send[:, part_of], 3 * band_rows, cols, pitch))
        own_hit = hits_from(index, width, width, width)
        own_out[part_of] = mm_nt(own_hit, wide[...]).astype(BF16)
        near_hits[part_of] = hits_from(index, width, width, near_base)
        far_hits[part_of] = hits_from(index, width, width, far_base)
        target = live_only(recv[:, part_of], count[0, 0], first)
        recv_hits[part_of] = hits_from(columns(target), 2 * cycle, cycle)
        recv_rows[:, part_of] = hits_to(target, cycle)
    raw = mesh_send
    inner = (raw >= cycle) & (raw < 2 * cycle)
    above_near = jnp.where(raw < cycle, raw + cycle, raw - 2 * cycle)
    below_near = jnp.where(raw < cycle, raw, raw - cycle)
    outer = jnp.where(inner, -1, jnp.where(even_band, above_near, below_near))
    target = live_only(mesh_recv, mesh_count[0, 0])
    own_hits[...] = hits_from(columns(jnp.where(inner, raw - cycle, -1)), 2 * cycle, cycle)
    outer_hits[...] = hits_from(columns(outer), 4 * cycle, 2 * cycle)
    to_hits[...] = hits_from(columns(target), 2 * node_count, node_count)
    source = jnp.where(inner, raw, jnp.where(outer < cycle, outer, outer + cycle))
    from_rows[...] = hits_to(source, 3 * cycle)
    to_rows[...] = hits_to(target, node_count)


def receiver_kernel(near, far, mesh_in, recv_hits, stack, pre_out):
    node_count = mesh_in.shape[0]
    rim = node_count // 2
    even = even_on("lat")
    left = jnp.where(even, far[...], near[...])[rim:]
    right = jnp.where(even, near[...], far[...])[:rim]
    cycle = jnp.concatenate([left, mesh_in[...], right], axis=0)
    table = jnp.concatenate(halves(mm(cycle, weight(stack, GR))), axis=0)
    pre_out[...] = mm(recv_hits[...], table)


def live_slots(count, edges, work, rest):
    lower = 0
    for size in (edges // 2, 3 * edges // 4, edges):

        def case(size=size):
            work([slice(0, size // 2), slice(size // 2, size)])
            if size < edges:
                rest(slice(size, edges))

        live = count[0, 0]
        pl.when((live > lower) & (live <= size) if size < edges else live > lower)(case)
        lower = size


def gather_kernel(count, halo, hits, rows, rows_out, wide):
    fill(wide, halo, wide.shape[1] // halo.shape[0], 0)

    def work(parts):
        part_of = slice(0, parts[-1].stop)
        gathered = mm_nt(hits[part_of], wide[...]).astype(BF16)
        rows_out[part_of] = rows[part_of] + gathered

    def rest(part_of):
        rows_out[part_of] = jnp.zeros_like(rows_out[part_of])

    live_slots(count, rows.shape[0], work, rest)


def encode_kernel(
    count, near, near_hits, recv_rows, rows, recv_pre, stack,
    senders_out, slope_out, part_out, near_out, far_out, wide,
):
    half = recv_rows.shape[0] // 2
    fill(wide, near, wide.shape[1] // near.shape[0], 0)

    def work(parts):
        sums = None
        for part_of in parts:
            raw = rows[part_of] + mm_nt(near_hits[part_of], wide[...]).astype(BF16)
            latent, _ = silu_parts(mm(raw, stack[stack.shape[0] - raw.shape[1] :]))
            latent = latent.astype(BF16)
            senders_out[part_of] = latent
            pre = mm(latent, weight(stack, GS)) + recv_pre[part_of]
            value, slope = silu_parts(pre)
            slope_out[part_of] = slope.astype(BF16)
            part = mm(recv_rows[:, part_of], value.astype(BF16))
            sums = part if sums is None else sums + part
        part_out[...] = sums
        even = even_on("lat")
        near_out[...] = jnp.where(even, sums[half:], sums[:half]).astype(BF16)
        far_out[...] = jnp.where(even, sums[:half], sums[half:]).astype(BF16)

    def rest(part_of):
        senders_out[part_of] = jnp.zeros_like(senders_out[part_of])
        slope_out[part_of] = jnp.zeros_like(slope_out[part_of])

    live_slots(count, rows.shape[0], work, rest)


def node_kernel(part, near, far, mesh_near, mesh_far, mesh_in, stack, mesh_out, slope_out):
    node_count = mesh_in.shape[0]
    rim = node_count // 2
    even = even_on("lat")
    left = jnp.where(even, far[...], near[...]).astype(F32)
    right = jnp.where(even, near[...], far[...]).astype(F32)
    total = part[...] + jnp.concatenate([left, right], axis=0)
    mesh_left = jnp.where(even, mesh_far[...], mesh_near[...])[rim:]
    mesh_right = jnp.where(even, mesh_near[...], mesh_far[...])[:rim]
    cycle = jnp.concatenate([mesh_left, mesh_in[...], mesh_right], axis=0)
    value, slope = silu_parts(mm(total.astype(BF16), weight(stack, GN)))
    mesh_out[...] = (cycle.astype(F32) + value).astype(BF16)
    slope_out[...] = slope


def process_own_kernel(own_hits, to_hits, own, stack, pre_out):
    rim = own.shape[0] // 4
    home = own[rim : own.shape[0] - rim]
    table = jnp.concatenate(halves(mm(own[...], weight(stack, MS))), axis=0)
    recv_table = jnp.concatenate(halves(mm(home, weight(stack, MR))), axis=0)
    pre_out[...] = mm(own_hits[...], table) + mm(to_hits[...], recv_table)


def process_kernel(
    own_pre, outer_hits, to_hits, from_rows, to_rows, far, own, near, d_out, stack,
    mesh_out, sums_out, recv_out, near_out, far_out,
):
    cycle = own.shape[0]
    node_count = cycle // 2
    rim = node_count // 2
    home = own[rim : rim + node_count]
    block = jnp.concatenate([near[...], far[...]], axis=0)
    table = jnp.concatenate(halves(mm(block, weight(stack, MS))), axis=0)
    pre = own_pre[...] + mm(outer_hits[...], table)
    value, slope = silu_parts(pre)
    gate = mm(mm(to_rows[...], value.astype(BF16)).astype(BF16), weight(stack, MN))
    gate_value, gate_slope = silu_parts(gate)
    mesh_out[...] = (home.astype(F32) + gate_value).astype(BF16)
    gate_two = (d_out[...].astype(F32) * gate_slope).astype(BF16)
    back = jnp.concatenate(halves(mm_nt(gate_two, weight(stack, MN))), axis=0)
    edge_slope = (mm(to_hits[...], back) * slope).astype(BF16)
    sums = mm(from_rows[...], edge_slope)
    recv_out[...] = mm(to_rows[...], edge_slope).astype(BF16)
    sums_out[...] = sums
    near_out[...] = sums[:cycle].astype(BF16)
    far_out[...] = sums[2 * cycle :].astype(BF16)


def block_of(x, dom_shift, lat_shift, doms, lats):
    cols = x.shape[1] // (doms * lats)
    dom = lax.rem(lax.axis_index("dom") + dom_shift, doms)
    index = dom * lats + lax.rem(lax.axis_index("lat") + lat_shift, lats)
    pick = x[:, :cols]
    for i in range(1, doms * lats):
        pick = jnp.where(index == i, x[:, i * cols : (i + 1) * cols], pick)
    return pick


def home_kernel(recv_sum, d_out, stack, senders, home_out, turned_out):
    home_out[...] = mm_nt(recv_sum[...], weight(stack, MR)) + d_out[...].astype(F32)
    turned_out[...] = senders[...].T


def cotangent_kernel(sums, near, far, home, part_out, near_out, far_out):
    cycle = near.shape[0]
    half = cycle // 2
    rim = half // 2
    total = sums[cycle : 2 * cycle] + near[...].astype(F32) + far[...].astype(F32)
    part_out[...] = total
    even = even_on("lat")
    near_out[:half] = jnp.where(even, total[half:], total[:half]).astype(BF16)
    near_out[half:] = jnp.where(even, home[rim:], home[:rim]).astype(BF16)
    far_out[:half] = jnp.where(even, total[:half], total[half:]).astype(BF16)
    far_out[half:] = jnp.where(even, home[:rim], home[rim:]).astype(BF16)


def gradient_block(recv_hits, back, edge_slope, senders, shifts, doms, lats):
    edges = recv_hits.shape[0]
    back = [block_of(back, *shift, doms, lats) for shift in shifts]
    back = back[0] if len(back) == 1 else jnp.concatenate(back, axis=1)
    total = None
    for first in range(0, edges, edges // 2):
        part_of = slice(first, first + edges // 2)
        weights = [block_of(edge_slope[part_of], *shift, doms, lats) for shift in shifts]
        weights = weights[0] if len(weights) == 1 else jnp.concatenate(weights, axis=1)
        slope = mm(recv_hits[part_of], back) * weights.astype(F32)
        part = mm(senders[:, part_of], slope.astype(BF16))
        total = part if total is None else total + part
    return total


def encode_grad_kernel(
    recv_hits, part, near, far, home, node_slope, stack, senders, edge_slope,
    sends, back_out, total_out,
):
    half = part.shape[0] // 2
    even = even_on("lat")
    left = jnp.where(even, far[...], near[...]).astype(F32)
    right = jnp.where(even, near[...], far[...]).astype(F32)
    total = part[...] + jnp.concatenate([left[:half], right[:half]], axis=0)
    total = total.astype(BF16)
    rest = jnp.concatenate([left[half:], home[...], right[half:]], axis=0)
    cot = rest + mm_nt(total, weight(stack, MS))
    gate_one = (cot * node_slope[...]).astype(BF16)
    back = jnp.concatenate(halves(mm_nt(gate_one, weight(stack, GN))), axis=0)
    back_out[...] = back
    lats = sends.shape[0] + 1
    doms = sends.shape[1] + 1
    for i in range(1, lats):
        for j in range(1, doms):
            block = gradient_block(
                recv_hits, back, edge_slope, senders, [(j, i)], doms, lats
            )
            sends[i - 1, j - 1] = block.astype(BF16)
    for j in range(doms):
        total_out[j] = block_of(total, j, 0, doms, lats)


def middle_blocks_kernel(recv_hits, back, edge_slope, senders, after, kept, sends):
    doms = kept.shape[0] + 1
    lats = sends.shape[0] + 1
    cols = kept.shape[2]
    shifts = [(j, 0) for j in range(1, doms)] + [(0, i) for i in range(1, lats)]
    blocks = gradient_block(recv_hits, back[...], edge_slope, senders, shifts, doms, lats)
    for k in range(len(shifts)):
        block = blocks[:, k * cols : (k + 1) * cols]
        if k < doms - 1:
            kept[k] = block
        else:
            sends[k - doms + 1] = block.astype(BF16)


def rows_at(ref, place, partner):
    bands = lax.axis_size("band")
    rows = ref.shape[-2] // bands
    at = pl.multiple_of(lax.bitwise_xor(lax.axis_index("band"), partner) * rows, rows)
    return ref[(*place, pl.ds(at, rows))]


def add_kernel(kept, total, *refs):
    *came, first_out, second_out = refs
    bands = lax.axis_size("band")
    rows = kept.shape[1] // bands
    near = second_out.shape[1] // rows
    for j in range(kept.shape[0]):
        for k in range(bands):
            block = rows_at(kept, (j,), k)
            for part in came:
                block = block + rows_at(part, (j,), k).astype(F32)
            out, at = (first_out, k - near) if k >= near else (second_out, k)
            at = at * rows
            out[j, at : at + rows] = block.astype(BF16)
        first_out[j, (bands - near) * rows :] = total[j + 1]


def own_block_kernel(recv_hits, back, edge_slope, senders, *refs):
    *came, out = refs
    lats = len(came) + 1
    doms = back.shape[1] // out.shape[1] // lats
    block = gradient_block(
        recv_hits, back[...], edge_slope, senders, [(0, 0)], doms, lats
    )
    for part in came:
        block = block + part[...].astype(F32)
    out[...] = block


def first_kernel(kept, total, nodes, *refs):
    doms = total.shape[0]
    came, (*sends_out, sums) = refs[: 2 * (doms - 1)], refs[2 * (doms - 1) :]
    came, came_nodes = came[: doms - 1], came[doms - 1 :]
    far = len(sends_out)
    near = lax.axis_size("band") - far
    rows = sends_out[0].shape[1]
    second = mm_tn(nodes[...], total[0])
    for part, part_nodes in zip(came, came_nodes):
        second = second + mm_tn(part_nodes[...], part[far * rows :])
    sums[...] = second
    for i, out in enumerate(sends_out):
        block = rows_at(kept, (), near + i)
        for part in came:
            block = block + part[i * rows : (i + 1) * rows].astype(F32)
        out[0] = block.astype(BF16)
        out[1] = rows_at(sums, (), near + i).astype(BF16)


def second_kernel(kept, sums, *refs):
    doms = lax.axis_size("dom")
    came, outs = refs[: doms - 1], refs[doms - 1 :]
    rows = outs[0].shape[1]
    for i, out in enumerate(outs):
        block = rows_at(kept, (), i)
        for part in came:
            block = block + part[i * rows : (i + 1) * rows].astype(F32)
        out[0] = block.astype(out.dtype)
        out[1] = rows_at(sums, (), i).astype(out.dtype)


def over_band_kernel(*refs):
    *came, own, first_out, second_out = refs
    for k, out in enumerate((first_out, second_out)):
        total = own[k]
        for part in came:
            total = total + part[k].astype(F32)
        out[...] = total


def call(kernel, outs, *args, scalars=(), scratch=()):
    in_specs = [
        pl.BlockSpec(memory_space=pltpu.SMEM if i in scalars else pltpu.VMEM)
        for i in range(len(args))
    ]
    return pl.pallas_call(
        kernel,
        out_shape=[jax.ShapeDtypeStruct(shape, dtype) for shape, dtype in outs],
        in_specs=in_specs,
        out_specs=[pl.BlockSpec(memory_space=pltpu.VMEM)] * len(outs),
        scratch_shapes=scratch,
        compiler_params=pltpu.CompilerParams(vmem_limit_bytes=16 << 20),
    )(*args)


def ring_pairings(count):
    far = [(i, (i + 1 if i % 2 else i - 1) % count) for i in range(count)]
    return [(i, i ^ 1) for i in range(count)], far


def line_pairings(bands, doms, lats):
    far = []
    for band in range(bands):
        other = band + 1 if band % 2 else band - 1
        for dom in range(doms):
            for lat in range(lats):
                here = (band * doms + dom) * lats + lat
                if 0 <= other < bands:
                    there = (other * doms + dom) * lats + lat
                else:
                    there = (band * doms + dom) * lats + (lat ^ 1)
                far.append((here, there))
    return [(i, i ^ 1) for i in range(bands)], far


def shifted(x, axis, shift):
    count = lax.axis_size(axis)
    return lax.ppermute(x, axis, [(i, (i + shift) % count) for i in range(count)])


def over_band(x, partner):
    count = lax.axis_size("band")
    return lax.ppermute(x, "band", [(b, b ^ partner) for b in range(count)])


def on_device(
    grid_in, w_grid, w_gs, w_gr, w_gn, w_ms, w_mr, w_mn, mesh_in, d_out,
    g2m_send, g2m_recv, g2m_count, mesh_send, mesh_recv, mesh_count,
):
    latent = w_grid.shape[1]
    variables = w_grid.shape[0]
    node_count = mesh_in.shape[0]
    cycle = 2 * node_count
    bands = lax.axis_size("band")
    sectors = lax.axis_size(("dom", "lat"))
    edges = g2m_send.shape[2]
    around = ("dom", "lat")
    whole = ("band", "dom", "lat")
    band_near, band_far = line_pairings(bands, lax.axis_size("dom"), lax.axis_size("lat"))
    ring_near, ring_far = ring_pairings(sectors)

    grid = jnp.transpose(grid_in, (0, 2, 1))
    pitch = -(-grid.shape[2] // LANES) * LANES
    band_rows = grid.shape[0]
    width = band_rows * pitch
    raw_near = lax.ppermute(grid, "band", band_near)
    raw_far = lax.ppermute(grid, whole, band_far)
    mesh_edges = mesh_send.shape[2]
    stack = jnp.concatenate([w_gs, w_gr, w_gn, w_ms, w_mr, w_mn, w_grid], axis=0)
    indices = jnp.concatenate([g2m_send, g2m_recv, mesh_send, mesh_recv], axis=2)
    (
        rows, recv_hits, recv_rows, own_hits, outer_hits, to_hits, from_rows, to_rows, *halo_hits
    ) = call(
        index_kernel,
        [
            ((edges, variables), BF16),
            ((edges, 2 * cycle), BF16),
            ((cycle, edges), BF16),
            ((mesh_edges, 2 * cycle), BF16),
            ((mesh_edges, 4 * cycle), BF16),
            ((mesh_edges, 2 * node_count), BF16),
            ((3 * cycle, mesh_edges), BF16),
            ((node_count, mesh_edges), BF16),
            ((edges, width), BF16),
            ((edges, width), BF16),
        ],
        g2m_count, mesh_count, indices, grid,
        scalars=(0, 1),
        scratch=[pltpu.VMEM((variables, width), BF16)],
    )
    late_mesh, rows = lax.optimization_barrier((mesh_in, rows))
    mesh_near = lax.ppermute(late_mesh, around, ring_near)
    mesh_far = lax.ppermute(late_mesh, around, ring_far)
    (recv_pre,) = call(
        receiver_kernel,
        [((edges, latent), F32)],
        mesh_near, mesh_far, mesh_in, recv_hits, stack,
    )
    near_hits, far_hits = halo_hits
    (rows,) = call(
        gather_kernel,
        [((edges, variables), BF16)],
        g2m_count, raw_far, far_hits, rows,
        scalars=(0,),
        scratch=[pltpu.VMEM((variables, width), BF16)],
    )
    senders, edge_slope, part, to_near, to_far = call(
        encode_kernel,
        [
            ((edges, latent), BF16),
            ((edges, latent), BF16),
            ((cycle, latent), F32),
            ((node_count, latent), BF16),
            ((node_count, latent), BF16),
        ],
        g2m_count, raw_near, near_hits, recv_rows, rows, recv_pre, stack,
        scalars=(0,),
        scratch=[pltpu.VMEM((variables, width), BF16)],
    )
    from_far = lax.ppermute(to_far, around, ring_far)
    from_near = lax.ppermute(to_near, around, ring_near)
    mesh_one, node_slope = call(
        node_kernel,
        [((cycle, latent), BF16), ((cycle, latent), F32)],
        part, from_near, from_far, mesh_near, mesh_far, mesh_in, stack,
    )
    one_near = lax.ppermute(mesh_one, "band", band_near)
    one_far = lax.ppermute(mesh_one, whole, band_far)
    doms = lax.axis_size("dom")
    lats = lax.axis_size("lat")
    dom_nodes = [shifted(mesh_one, "dom", i + 1) for i in range(doms - 1)]
    (own_pre,) = call(
        process_own_kernel, [((mesh_edges, latent), F32)], own_hits, to_hits, mesh_one, stack
    )
    mesh_out, sums, recv_sum, to_near, to_far = call(
        process_kernel,
        [
            ((node_count, latent), BF16),
            ((3 * cycle, latent), F32),
            ((node_count, latent), BF16),
            ((cycle, latent), BF16),
            ((cycle, latent), BF16),
        ],
        own_pre, outer_hits, to_hits, from_rows, to_rows, one_far, mesh_one, one_near, d_out,
        stack,
    )
    from_near = lax.ppermute(to_near, "band", band_near)
    from_far = lax.ppermute(to_far, whole, band_far)
    home, senders = call(
        home_kernel,
        [((node_count, latent), F32), ((latent, edges), BF16)],
        recv_sum, d_out, stack, senders,
    )
    message = (node_count + node_count // 2, latent)
    part, to_near, to_far = call(
        cotangent_kernel,
        [((cycle, latent), F32), (message, BF16), (message, BF16)],
        sums, from_near, from_far, home,
    )
    from_far = lax.ppermute(to_far, around, ring_far)
    from_near = lax.ppermute(to_near, around, ring_near)

    from_near, *dom_nodes = lax.optimization_barrier((from_near, *dom_nodes))
    cols = latent // sectors
    rows = latent // bands
    sends, back, total = call(
        encode_grad_kernel,
        [
            ((lats - 1, doms - 1, latent, cols), BF16),
            ((2 * cycle, latent), BF16),
            ((doms, cycle, cols), BF16),
        ],
        recv_hits, part, from_near, from_far, home, node_slope, stack, senders, edge_slope,
    )
    edge = (recv_hits, back, edge_slope, senders)
    came = [shifted(sends[i], "lat", i + 1) for i in range(lats - 1)]
    block = (latent, cols)
    kept, own_sends = call(
        middle_blocks_kernel,
        [((doms - 1,) + block, F32), ((lats - 1,) + block, BF16)],
        *edge, sends,
    )
    own_came = [shifted(own_sends[i], "lat", i + 1) for i in range(lats - 1)]
    far = bands // 2
    first, second = call(
        add_kernel,
        [
            ((doms - 1, far * rows + cycle, cols), BF16),
            ((doms - 1, (bands - far) * rows, cols), BF16),
        ],
        kept, total, *came,
    )
    first = [shifted(first[i], "dom", i + 1) for i in range(doms - 1)]
    second = [shifted(second[i], "dom", i + 1) for i in range(doms - 1)]
    (kept,) = call(own_block_kernel, [(block, F32)], *edge, *own_came)
    pair = (2, rows, cols)
    *far_sends, sums = call(
        first_kernel,
        [(pair, BF16)] * far + [(block, F32)],
        kept, total, mesh_one, *first, *dom_nodes,
    )
    came = [over_band(x, bands - far + i) for i, x in reversed(list(enumerate(far_sends)))]
    own, *near_sends = call(
        second_kernel,
        [(pair, F32)] + [(pair, BF16)] * (bands - far - 1),
        kept, sums, *second,
    )
    came += [over_band(x, i + 1) for i, x in reversed(list(enumerate(near_sends)))]
    tile = ((rows, cols), F32)
    grad_gs, grad_ms = call(over_band_kernel, [tile, tile], *came, own)
    return mesh_out, grad_gs, grad_ms


def solution(mesh):
    flat = P(("groups", "band", "dom", "lat"), None)
    grid = P(("groups", "band"), ("dom", "lat"), None)
    count = P(("groups", "band"), ("dom", "lat"))
    placed = (grid,) + (P(),) * 7 + (flat, flat) + (grid, grid, count) * 2
    return jax.shard_map(
        on_device,
        mesh=mesh,
        in_specs=placed,
        out_specs=(flat, count, count),
        check_vma=False,
    )
```

```python
import jax
import jax.numpy as jnp
from jax import lax
from jax.experimental import pallas as pl
from jax.experimental.pallas import tpu as pltpu
from jax.sharding import PartitionSpec as P

F32 = jnp.float32
BF16 = jnp.bfloat16
LANES = 128
GS, GR, GN, MS, MR, MN = range(6)


def mm(a, b):
    return jnp.dot(a, b, preferred_element_type=F32)


def mm_nt(a, b):
    return lax.dot_general(a, b, (((1,), (1,)), ((), ())), preferred_element_type=F32)


def mm_tn(a, b):
    return lax.dot_general(a, b, (((0,), (0,)), ((), ())), preferred_element_type=F32)


def halves(x):
    high = x.astype(BF16)
    return high, (x - high.astype(F32)).astype(BF16)


def silu_parts(x):
    g = 0.5 * jnp.tanh(0.5 * x) + 0.5
    value = x * g
    return value, g + value * (1.0 - g)


def ones_at(mask):
    return jnp.where(mask, 1.0, 0.0).astype(BF16)


def columns(row):
    count = row.shape[1]
    parts = [
        jnp.broadcast_to(row[:, i : i + LANES], (LANES, LANES)).T
        for i in range(0, count, LANES)
    ]
    return parts[0] if len(parts) == 1 else jnp.concatenate(parts, axis=0)


def hits_from(cols, width, period, start=0):
    parts = []
    for i in range(0, width, LANES):
        size = min(LANES, width - i)
        lane = lax.broadcasted_iota(jnp.int32, (cols.shape[0], size), 1) + i
        if period < width:
            lane = lax.rem(lane, period)
        parts.append(ones_at(cols[:, :size] == lane + start))
    return parts[0] if len(parts) == 1 else jnp.concatenate(parts, axis=1)


def hits_to(row, count):
    return ones_at(lax.broadcasted_iota(jnp.int32, (count, row.shape[1]), 0) == row)


def live_only(row, count, first=0):
    slot = lax.broadcasted_iota(jnp.int32, row.shape, 1) + first
    return jnp.where(slot < count, row, -1)


def weight(stack, index):
    latent = stack.shape[1]
    return stack[index * latent : (index + 1) * latent]


def even_on(axis):
    return lax.rem(lax.axis_index(axis), 2) == 0


def spread(index, blocks, cols, pitch):
    extra = jnp.zeros_like(index)
    for block in range(1, blocks):
        extra = extra + jnp.where(index >= block * cols, pitch - cols, 0)
    return index + extra


def fill(wide, blocks, pitch, first):
    cols = blocks.shape[2]
    for k in range(blocks.shape[0]):
        at = first + k * pitch
        wide[:, at : at + cols] = blocks[k]
        if cols < pitch:
            wide[:, at + cols : at + pitch] = jnp.zeros(
                (wide.shape[0], pitch - cols), wide.dtype
            )


def index_kernel(
    count, mesh_count, indices, grid,
    own_out, recv_hits, recv_rows, own_hits, outer_hits, to_hits, from_rows, to_rows, near_hits, far_hits, wide,
):
    edges = recv_hits.shape[0]
    mesh_edges = to_hits.shape[0]
    send, recv, mesh_send, mesh_recv = (
        indices[0, :, first : first + size]
        for first, size in (
            (0, edges),
            (edges, edges),
            (2 * edges, mesh_edges),
            (2 * edges + mesh_edges, mesh_edges),
        )
    )
    band_rows, _, cols = grid.shape
    pitch = wide.shape[1] // band_rows
    width = band_rows * pitch
    cycle = recv_rows.shape[0]
    node_count = to_rows.shape[0]
    even_band = even_on("band")
    fill(wide, grid, pitch, 0)
    near_base = jnp.where(even_band, 2 * width, 0)
    far_base = jnp.where(even_band, 0, 2 * width)
    block = 256
    for first in range(0, edges, block):
        part_of = slice(first, first + block)
        index = columns(spread(send[:, part_of], 3 * band_rows, cols, pitch))
        own_hit = hits_from(index, width, width, width)
        own_out[part_of] = mm_nt(own_hit, wide[...]).astype(BF16)
        near_hits[part_of] = hits_from(index, width, width, near_base)
        far_hits[part_of] = hits_from(index, width, width, far_base)
        target = live_only(recv[:, part_of], count[0, 0], first)
        recv_hits[part_of] = hits_from(columns(target), 2 * cycle, cycle)
        recv_rows[:, part_of] = hits_to(target, cycle)
    raw = mesh_send
    inner = (raw >= cycle) & (raw < 2 * cycle)
    above_near = jnp.where(raw < cycle, raw + cycle, raw - 2 * cycle)
    below_near = jnp.where(raw < cycle, raw, raw - cycle)
    outer = jnp.where(inner, -1, jnp.where(even_band, above_near, below_near))
    target = live_only(mesh_recv, mesh_count[0, 0])
    own_hits[...] = hits_from(columns(jnp.where(inner, raw - cycle, -1)), 2 * cycle, cycle)
    outer_hits[...] = hits_from(columns(outer), 4 * cycle, 2 * cycle)
    to_hits[...] = hits_from(columns(target), 2 * node_count, node_count)
    source = jnp.where(inner, raw, jnp.where(outer < cycle, outer, outer + cycle))
    from_rows[...] = hits_to(source, 3 * cycle)
    to_rows[...] = hits_to(target, node_count)


def receiver_kernel(near, far, mesh_in, recv_hits, stack, pre_out):
    node_count = mesh_in.shape[0]
    rim = node_count // 2
    even = even_on("lat")
    left = jnp.where(even, far[...], near[...])[rim:]
    right = jnp.where(even, near[...], far[...])[:rim]
    cycle = jnp.concatenate([left, mesh_in[...], right], axis=0)
    table = jnp.concatenate(halves(mm(cycle, weight(stack, GR))), axis=0)
    pre_out[...] = mm(recv_hits[...], table)


def live_slots(count, edges, work, rest):
    lower = 0
    for size in range(edges // 2, edges + 1, edges // 8):

        def case(size=size):
            middle = -(-size // 2 // LANES) * LANES
            work([slice(0, middle), slice(middle, size)])
            if size < edges:
                rest(slice(size, edges))

        live = count[0, 0]
        pl.when((live > lower) & (live <= size) if size < edges else live > lower)(case)
        lower = size


def gather_kernel(count, halo, hits, rows, rows_out, wide):
    def work(parts):
        fill(wide, halo, wide.shape[1] // halo.shape[0], 0)
        part_of = slice(0, parts[-1].stop)
        gathered = mm_nt(hits[part_of], wide[...]).astype(BF16)
        rows_out[part_of] = rows[part_of] + gathered

    def rest(part_of):
        rows_out[part_of] = jnp.zeros_like(rows_out[part_of])

    live_slots(count, rows.shape[0], work, rest)


def encode_kernel(
    count, near, near_hits, recv_rows, rows, recv_pre, stack,
    senders_out, slope_out, part_out, near_out, far_out, wide,
):
    half = recv_rows.shape[0] // 2

    def work(parts):
        fill(wide, near, wide.shape[1] // near.shape[0], 0)
        sums = None
        for part_of in parts:
            raw = rows[part_of] + mm_nt(near_hits[part_of], wide[...]).astype(BF16)
            latent, _ = silu_parts(mm(raw, stack[stack.shape[0] - raw.shape[1] :]))
            latent = latent.astype(BF16)
            senders_out[part_of] = latent
            pre = mm(latent, weight(stack, GS)) + recv_pre[part_of]
            value, slope = silu_parts(pre)
            slope_out[part_of] = slope.astype(BF16)
            part = mm(recv_rows[:, part_of], value.astype(BF16))
            sums = part if sums is None else sums + part
        part_out[...] = sums
        even = even_on("lat")
        near_out[...] = jnp.where(even, sums[half:], sums[:half]).astype(BF16)
        far_out[...] = jnp.where(even, sums[:half], sums[half:]).astype(BF16)

    def rest(part_of):
        senders_out[part_of] = jnp.zeros_like(senders_out[part_of])
        slope_out[part_of] = jnp.zeros_like(slope_out[part_of])

    live_slots(count, rows.shape[0], work, rest)


def node_kernel(part, near, far, mesh_near, mesh_far, mesh_in, stack, mesh_out, slope_out):
    node_count = mesh_in.shape[0]
    rim = node_count // 2
    even = even_on("lat")
    left = jnp.where(even, far[...], near[...]).astype(F32)
    right = jnp.where(even, near[...], far[...]).astype(F32)
    total = part[...] + jnp.concatenate([left, right], axis=0)
    mesh_left = jnp.where(even, mesh_far[...], mesh_near[...])[rim:]
    mesh_right = jnp.where(even, mesh_near[...], mesh_far[...])[:rim]
    cycle = jnp.concatenate([mesh_left, mesh_in[...], mesh_right], axis=0)
    value, slope = silu_parts(mm(total.astype(BF16), weight(stack, GN)))
    mesh_out[...] = (cycle.astype(F32) + value).astype(BF16)
    slope_out[...] = slope


def process_own_kernel(own_hits, to_hits, own, stack, pre_out):
    rim = own.shape[0] // 4
    home = own[rim : own.shape[0] - rim]
    table = jnp.concatenate(halves(mm(own[...], weight(stack, MS))), axis=0)
    recv_table = jnp.concatenate(halves(mm(home, weight(stack, MR))), axis=0)
    pre_out[...] = mm(own_hits[...], table) + mm(to_hits[...], recv_table)


def process_kernel(
    own_pre, outer_hits, to_hits, from_rows, to_rows, far, own, near, d_out, stack,
    mesh_out, sums_out, recv_out, near_out, far_out,
):
    cycle = own.shape[0]
    node_count = cycle // 2
    rim = node_count // 2
    home = own[rim : rim + node_count]
    block = jnp.concatenate([near[...], far[...]], axis=0)
    table = jnp.concatenate(halves(mm(block, weight(stack, MS))), axis=0)
    pre = own_pre[...] + mm(outer_hits[...], table)
    value, slope = silu_parts(pre)
    gate = mm(mm(to_rows[...], value.astype(BF16)).astype(BF16), weight(stack, MN))
    gate_value, gate_slope = silu_parts(gate)
    mesh_out[...] = (home.astype(F32) + gate_value).astype(BF16)
    gate_two = (d_out[...].astype(F32) * gate_slope).astype(BF16)
    back = jnp.concatenate(halves(mm_nt(gate_two, weight(stack, MN))), axis=0)
    edge_slope = (mm(to_hits[...], back) * slope).astype(BF16)
    sums = mm(from_rows[...], edge_slope)
    recv_out[...] = mm(to_rows[...], edge_slope).astype(BF16)
    sums_out[...] = sums
    near_out[...] = sums[:cycle].astype(BF16)
    far_out[...] = sums[2 * cycle :].astype(BF16)


def block_of(x, dom_shift, lat_shift, doms, lats):
    cols = x.shape[1] // (doms * lats)
    dom = lax.rem(lax.axis_index("dom") + dom_shift, doms)
    index = dom * lats + lax.rem(lax.axis_index("lat") + lat_shift, lats)
    pick = x[:, :cols]
    for i in range(1, doms * lats):
        pick = jnp.where(index == i, x[:, i * cols : (i + 1) * cols], pick)
    return pick


def home_kernel(recv_sum, d_out, stack, senders, home_out, turned_out):
    home_out[...] = mm_nt(recv_sum[...], weight(stack, MR)) + d_out[...].astype(F32)
    turned_out[...] = senders[...].T


def cotangent_kernel(sums, near, far, home, part_out, near_out, far_out):
    cycle = near.shape[0]
    half = cycle // 2
    rim = half // 2
    total = sums[cycle : 2 * cycle] + near[...].astype(F32) + far[...].astype(F32)
    part_out[...] = total
    even = even_on("lat")
    near_out[:half] = jnp.where(even, total[half:], total[:half]).astype(BF16)
    near_out[half:] = jnp.where(even, home[rim:], home[:rim]).astype(BF16)
    far_out[:half] = jnp.where(even, total[:half], total[half:]).astype(BF16)
    far_out[half:] = jnp.where(even, home[:rim], home[rim:]).astype(BF16)


def gradient_block(recv_hits, back, edge_slope, senders, shifts, doms, lats):
    edges = recv_hits.shape[0]
    back = [block_of(back, *shift, doms, lats) for shift in shifts]
    back = back[0] if len(back) == 1 else jnp.concatenate(back, axis=1)
    total = None
    for first in range(0, edges, edges // 2):
        part_of = slice(first, first + edges // 2)
        weights = [block_of(edge_slope[part_of], *shift, doms, lats) for shift in shifts]
        weights = weights[0] if len(weights) == 1 else jnp.concatenate(weights, axis=1)
        slope = mm(recv_hits[part_of], back) * weights.astype(F32)
        part = mm(senders[:, part_of], slope.astype(BF16))
        total = part if total is None else total + part
    return total


def encode_grad_kernel(
    recv_hits, part, near, far, home, node_slope, stack, senders, edge_slope,
    sends, back_out, total_out,
):
    half = part.shape[0] // 2
    even = even_on("lat")
    left = jnp.where(even, far[...], near[...]).astype(F32)
    right = jnp.where(even, near[...], far[...]).astype(F32)
    total = part[...] + jnp.concatenate([left[:half], right[:half]], axis=0)
    total = total.astype(BF16)
    rest = jnp.concatenate([left[half:], home[...], right[half:]], axis=0)
    cot = rest + mm_nt(total, weight(stack, MS))
    gate_one = (cot * node_slope[...]).astype(BF16)
    back = jnp.concatenate(halves(mm_nt(gate_one, weight(stack, GN))), axis=0)
    back_out[...] = back
    lats = sends.shape[0] + 1
    doms = sends.shape[1] + 1
    for i in range(1, lats):
        for j in range(1, doms):
            block = gradient_block(
                recv_hits, back, edge_slope, senders, [(j, i)], doms, lats
            )
            sends[i - 1, j - 1] = block.astype(BF16)
    for j in range(doms):
        total_out[j] = block_of(total, j, 0, doms, lats)


def middle_blocks_kernel(recv_hits, back, edge_slope, senders, after, kept, sends):
    doms = kept.shape[0] + 1
    lats = sends.shape[0] + 1
    cols = kept.shape[2]
    shifts = [(j, 0) for j in range(1, doms)] + [(0, i) for i in range(1, lats)]
    blocks = gradient_block(recv_hits, back[...], edge_slope, senders, shifts, doms, lats)
    for k in range(len(shifts)):
        block = blocks[:, k * cols : (k + 1) * cols]
        if k < doms - 1:
            kept[k] = block
        else:
            sends[k - doms + 1] = block.astype(BF16)


def rows_at(ref, place, partner):
    bands = lax.axis_size("band")
    rows = ref.shape[-2] // bands
    at = pl.multiple_of(lax.bitwise_xor(lax.axis_index("band"), partner) * rows, rows)
    return ref[(*place, pl.ds(at, rows))]


def add_kernel(kept, total, *refs):
    *came, first_out, second_out = refs
    bands = lax.axis_size("band")
    rows = kept.shape[1] // bands
    near = second_out.shape[1] // rows
    for j in range(kept.shape[0]):
        for k in range(bands):
            block = rows_at(kept, (j,), k)
            for part in came:
                block = block + rows_at(part, (j,), k).astype(F32)
            out, at = (first_out, k - near) if k >= near else (second_out, k)
            at = at * rows
            out[j, at : at + rows] = block.astype(BF16)
        first_out[j, (bands - near) * rows :] = total[j + 1]


def own_block_kernel(recv_hits, back, edge_slope, senders, *refs):
    *came, out = refs
    lats = len(came) + 1
    doms = back.shape[1] // out.shape[1] // lats
    block = gradient_block(
        recv_hits, back[...], edge_slope, senders, [(0, 0)], doms, lats
    )
    for part in came:
        block = block + part[...].astype(F32)
    out[...] = block


def first_kernel(kept, total, nodes, *refs):
    doms = total.shape[0]
    came, (*sends_out, sums) = refs[: 2 * (doms - 1)], refs[2 * (doms - 1) :]
    came, came_nodes = came[: doms - 1], came[doms - 1 :]
    far = len(sends_out)
    near = lax.axis_size("band") - far
    rows = sends_out[0].shape[1]
    second = mm_tn(nodes[...], total[0])
    for part, part_nodes in zip(came, came_nodes):
        second = second + mm_tn(part_nodes[...], part[far * rows :])
    sums[...] = second
    for i, out in enumerate(sends_out):
        block = rows_at(kept, (), near + i)
        for part in came:
            block = block + part[i * rows : (i + 1) * rows].astype(F32)
        out[0] = block.astype(BF16)
        out[1] = rows_at(sums, (), near + i).astype(BF16)


def second_kernel(kept, sums, *refs):
    doms = lax.axis_size("dom")
    came, outs = refs[: doms - 1], refs[doms - 1 :]
    rows = outs[0].shape[1]
    for i, out in enumerate(outs):
        block = rows_at(kept, (), i)
        for part in came:
            block = block + part[i * rows : (i + 1) * rows].astype(F32)
        out[0] = block.astype(out.dtype)
        out[1] = rows_at(sums, (), i).astype(out.dtype)


def over_band_kernel(*refs):
    *came, own, first_out, second_out = refs
    for k, out in enumerate((first_out, second_out)):
        total = own[k]
        for part in came:
            total = total + part[k].astype(F32)
        out[...] = total


def call(kernel, outs, *args, scalars=(), scratch=()):
    in_specs = [
        pl.BlockSpec(memory_space=pltpu.SMEM if i in scalars else pltpu.VMEM)
        for i in range(len(args))
    ]
    return pl.pallas_call(
        kernel,
        out_shape=[jax.ShapeDtypeStruct(shape, dtype) for shape, dtype in outs],
        in_specs=in_specs,
        out_specs=[pl.BlockSpec(memory_space=pltpu.VMEM)] * len(outs),
        scratch_shapes=scratch,
        compiler_params=pltpu.CompilerParams(vmem_limit_bytes=16 << 20),
    )(*args)


def ring_pairings(count):
    far = [(i, (i + 1 if i % 2 else i - 1) % count) for i in range(count)]
    return [(i, i ^ 1) for i in range(count)], far


def line_pairings(bands, doms, lats):
    far = []
    for band in range(bands):
        other = band + 1 if band % 2 else band - 1
        for dom in range(doms):
            for lat in range(lats):
                here = (band * doms + dom) * lats + lat
                if 0 <= other < bands:
                    there = (other * doms + dom) * lats + lat
                else:
                    there = (band * doms + dom) * lats + (lat ^ 1)
                far.append((here, there))
    return [(i, i ^ 1) for i in range(bands)], far


def shifted(x, axis, shift):
    count = lax.axis_size(axis)
    return lax.ppermute(x, axis, [(i, (i + shift) % count) for i in range(count)])


def over_band(x, partner):
    count = lax.axis_size("band")
    return lax.ppermute(x, "band", [(b, b ^ partner) for b in range(count)])


def on_device(
    grid_in, w_grid, w_gs, w_gr, w_gn, w_ms, w_mr, w_mn, mesh_in, d_out,
    g2m_send, g2m_recv, g2m_count, mesh_send, mesh_recv, mesh_count,
):
    latent = w_grid.shape[1]
    variables = w_grid.shape[0]
    node_count = mesh_in.shape[0]
    cycle = 2 * node_count
    bands = lax.axis_size("band")
    sectors = lax.axis_size(("dom", "lat"))
    edges = g2m_send.shape[2]
    around = ("dom", "lat")
    whole = ("band", "dom", "lat")
    band_near, band_far = line_pairings(bands, lax.axis_size("dom"), lax.axis_size("lat"))
    ring_near, ring_far = ring_pairings(sectors)

    grid = jnp.transpose(grid_in, (0, 2, 1))
    pitch = -(-grid.shape[2] // LANES) * LANES
    band_rows = grid.shape[0]
    width = band_rows * pitch
    raw_near = lax.ppermute(grid, "band", band_near)
    raw_far = lax.ppermute(grid, whole, band_far)
    mesh_edges = mesh_send.shape[2]
    stack = jnp.concatenate([w_gs, w_gr, w_gn, w_ms, w_mr, w_mn, w_grid], axis=0)
    indices = jnp.concatenate([g2m_send, g2m_recv, mesh_send, mesh_recv], axis=2)
    (
        rows, recv_hits, recv_rows, own_hits, outer_hits, to_hits, from_rows, to_rows, *halo_hits
    ) = call(
        index_kernel,
        [
            ((edges, variables), BF16),
            ((edges, 2 * cycle), BF16),
            ((cycle, edges), BF16),
            ((mesh_edges, 2 * cycle), BF16),
            ((mesh_edges, 4 * cycle), BF16),
            ((mesh_edges, 2 * node_count), BF16),
            ((3 * cycle, mesh_edges), BF16),
            ((node_count, mesh_edges), BF16),
            ((edges, width), BF16),
            ((edges, width), BF16),
        ],
        g2m_count, mesh_count, indices, grid,
        scalars=(0, 1),
        scratch=[pltpu.VMEM((variables, width), BF16)],
    )
    late_mesh, rows = lax.optimization_barrier((mesh_in, rows))
    mesh_near = lax.ppermute(late_mesh, around, ring_near)
    mesh_far = lax.ppermute(late_mesh, around, ring_far)
    (recv_pre,) = call(
        receiver_kernel,
        [((edges, latent), F32)],
        mesh_near, mesh_far, mesh_in, recv_hits, stack,
    )
    near_hits, far_hits = halo_hits
    (rows,) = call(
        gather_kernel,
        [((edges, variables), BF16)],
        g2m_count, raw_far, far_hits, rows,
        scalars=(0,),
        scratch=[pltpu.VMEM((variables, width), BF16)],
    )
    senders, edge_slope, part, to_near, to_far = call(
        encode_kernel,
        [
            ((edges, latent), BF16),
            ((edges, latent), BF16),
            ((cycle, latent), F32),
            ((node_count, latent), BF16),
            ((node_count, latent), BF16),
        ],
        g2m_count, raw_near, near_hits, recv_rows, rows, recv_pre, stack,
        scalars=(0,),
        scratch=[pltpu.VMEM((variables, width), BF16)],
    )
    from_far = lax.ppermute(to_far, around, ring_far)
    from_near = lax.ppermute(to_near, around, ring_near)
    mesh_one, node_slope = call(
        node_kernel,
        [((cycle, latent), BF16), ((cycle, latent), F32)],
        part, from_near, from_far, mesh_near, mesh_far, mesh_in, stack,
    )
    one_near = lax.ppermute(mesh_one, "band", band_near)
    one_far = lax.ppermute(mesh_one, whole, band_far)
    doms = lax.axis_size("dom")
    lats = lax.axis_size("lat")
    dom_nodes = [shifted(mesh_one, "dom", i + 1) for i in range(doms - 1)]
    (own_pre,) = call(
        process_own_kernel, [((mesh_edges, latent), F32)], own_hits, to_hits, mesh_one, stack
    )
    mesh_out, sums, recv_sum, to_near, to_far = call(
        process_kernel,
        [
            ((node_count, latent), BF16),
            ((3 * cycle, latent), F32),
            ((node_count, latent), BF16),
            ((cycle, latent), BF16),
            ((cycle, latent), BF16),
        ],
        own_pre, outer_hits, to_hits, from_rows, to_rows, one_far, mesh_one, one_near, d_out,
        stack,
    )
    from_near = lax.ppermute(to_near, "band", band_near)
    from_far = lax.ppermute(to_far, whole, band_far)
    home, senders = call(
        home_kernel,
        [((node_count, latent), F32), ((latent, edges), BF16)],
        recv_sum, d_out, stack, senders,
    )
    message = (node_count + node_count // 2, latent)
    part, to_near, to_far = call(
        cotangent_kernel,
        [((cycle, latent), F32), (message, BF16), (message, BF16)],
        sums, from_near, from_far, home,
    )
    from_far = lax.ppermute(to_far, around, ring_far)
    from_near = lax.ppermute(to_near, around, ring_near)

    from_near, *dom_nodes = lax.optimization_barrier((from_near, *dom_nodes))
    cols = latent // sectors
    rows = latent // bands
    sends, back, total = call(
        encode_grad_kernel,
        [
            ((lats - 1, doms - 1, latent, cols), BF16),
            ((2 * cycle, latent), BF16),
            ((doms, cycle, cols), BF16),
        ],
        recv_hits, part, from_near, from_far, home, node_slope, stack, senders, edge_slope,
    )
    edge = (recv_hits, back, edge_slope, senders)
    came = [shifted(sends[i], "lat", i + 1) for i in range(lats - 1)]
    block = (latent, cols)
    kept, own_sends = call(
        middle_blocks_kernel,
        [((doms - 1,) + block, F32), ((lats - 1,) + block, BF16)],
        *edge, sends,
    )
    own_came = [shifted(own_sends[i], "lat", i + 1) for i in range(lats - 1)]
    far = bands // 2
    first, second = call(
        add_kernel,
        [
            ((doms - 1, far * rows + cycle, cols), BF16),
            ((doms - 1, (bands - far) * rows, cols), BF16),
        ],
        kept, total, *came,
    )
    first = [shifted(first[i], "dom", i + 1) for i in range(doms - 1)]
    second = [shifted(second[i], "dom", i + 1) for i in range(doms - 1)]
    (kept,) = call(own_block_kernel, [(block, F32)], *edge, *own_came)
    pair = (2, rows, cols)
    *far_sends, sums = call(
        first_kernel,
        [(pair, BF16)] * far + [(block, F32)],
        kept, total, mesh_one, *first, *dom_nodes,
    )
    came = [over_band(x, bands - far + i) for i, x in reversed(list(enumerate(far_sends)))]
    own, *near_sends = call(
        second_kernel,
        [(pair, F32)] + [(pair, BF16)] * (bands - far - 1),
        kept, sums, *second,
    )
    came += [over_band(x, i + 1) for i, x in reversed(list(enumerate(near_sends)))]
    tile = ((rows, cols), F32)
    grad_gs, grad_ms = call(over_band_kernel, [tile, tile], *came, own)
    return mesh_out, grad_gs, grad_ms


def solution(mesh):
    flat = P(("groups", "band", "dom", "lat"), None)
    grid = P(("groups", "band"), ("dom", "lat"), None)
    count = P(("groups", "band"), ("dom", "lat"))
    placed = (grid,) + (P(),) * 7 + (flat, flat) + (grid, grid, count) * 2
    return jax.shard_map(
        on_device,
        mesh=mesh,
        in_specs=placed,
        out_specs=(flat, count, count),
        check_vma=False,
    )
```

```python
import jax
import jax.numpy as jnp
from jax import lax
from jax.experimental import pallas as pl
from jax.experimental.pallas import tpu as pltpu
from jax.sharding import PartitionSpec as P

F32 = jnp.float32
BF16 = jnp.bfloat16
LANES = 128
GS, GR, GN, MS, MR, MN = range(6)


def mm(a, b):
    return jnp.dot(a, b, preferred_element_type=F32)


def mm_nt(a, b):
    return lax.dot_general(a, b, (((1,), (1,)), ((), ())), preferred_element_type=F32)


def mm_tn(a, b):
    return lax.dot_general(a, b, (((0,), (0,)), ((), ())), preferred_element_type=F32)


def halves(x):
    high = x.astype(BF16)
    return high, (x - high.astype(F32)).astype(BF16)


def silu_parts(x):
    g = 0.5 * jnp.tanh(0.5 * x) + 0.5
    value = x * g
    return value, g + value * (1.0 - g)


def ones_at(mask):
    return jnp.where(mask, 1.0, 0.0).astype(BF16)


def columns(row):
    count = row.shape[1]
    parts = [
        jnp.broadcast_to(row[:, i : i + LANES], (LANES, LANES)).T
        for i in range(0, count, LANES)
    ]
    return parts[0] if len(parts) == 1 else jnp.concatenate(parts, axis=0)


def hits_from(cols, width, period, start=0):
    parts = []
    for i in range(0, width, LANES):
        size = min(LANES, width - i)
        lane = lax.broadcasted_iota(jnp.int32, (cols.shape[0], size), 1) + i
        if period < width:
            lane = lax.rem(lane, period)
        parts.append(ones_at(cols[:, :size] == lane + start))
    return parts[0] if len(parts) == 1 else jnp.concatenate(parts, axis=1)


def hits_to(row, count):
    return ones_at(lax.broadcasted_iota(jnp.int32, (count, row.shape[1]), 0) == row)


def live_only(row, count, first=0):
    slot = lax.broadcasted_iota(jnp.int32, row.shape, 1) + first
    return jnp.where(slot < count, row, -1)


def weight(stack, index):
    latent = stack.shape[1]
    return stack[index * latent : (index + 1) * latent]


def even_on(axis):
    return lax.rem(lax.axis_index(axis), 2) == 0


def spread(index, blocks, cols, pitch):
    extra = jnp.zeros_like(index)
    for block in range(1, blocks):
        extra = extra + jnp.where(index >= block * cols, pitch - cols, 0)
    return index + extra


def fill(wide, blocks, pitch, first):
    cols = blocks.shape[2]
    for k in range(blocks.shape[0]):
        at = first + k * pitch
        wide[:, at : at + cols] = blocks[k]
        if cols < pitch:
            wide[:, at + cols : at + pitch] = jnp.zeros(
                (wide.shape[0], pitch - cols), wide.dtype
            )


def index_kernel(
    count, mesh_count, indices, grid,
    own_out, recv_hits, recv_rows, own_hits, outer_hits, to_hits, from_rows, to_rows, near_hits, far_hits, wide,
):
    edges = recv_hits.shape[0]
    mesh_edges = to_hits.shape[0]
    send, recv, mesh_send, mesh_recv = (
        indices[0, :, first : first + size]
        for first, size in (
            (0, edges),
            (edges, edges),
            (2 * edges, mesh_edges),
            (2 * edges + mesh_edges, mesh_edges),
        )
    )
    band_rows, _, cols = grid.shape
    pitch = wide.shape[1] // band_rows
    width = band_rows * pitch
    cycle = recv_rows.shape[0]
    node_count = to_rows.shape[0]
    even_band = even_on("band")
    fill(wide, grid, pitch, 0)
    near_base = jnp.where(even_band, 2 * width, 0)
    far_base = jnp.where(even_band, 0, 2 * width)
    block = 256
    for first in range(0, edges, block):
        part_of = slice(first, first + block)
        index = columns(spread(send[:, part_of], 3 * band_rows, cols, pitch))
        own_hit = hits_from(index, width, width, width)
        own_out[part_of] = mm_nt(own_hit, wide[...]).astype(BF16)
        near_hits[part_of] = hits_from(index, width, width, near_base)
        far_hits[part_of] = hits_from(index, width, width, far_base)
        target = live_only(recv[:, part_of], count[0, 0], first)
        recv_hits[part_of] = hits_from(columns(target), 2 * cycle, cycle)
        recv_rows[:, part_of] = hits_to(target, cycle)
    raw = mesh_send
    inner = (raw >= cycle) & (raw < 2 * cycle)
    above_near = jnp.where(raw < cycle, raw + cycle, raw - 2 * cycle)
    below_near = jnp.where(raw < cycle, raw, raw - cycle)
    outer = jnp.where(inner, -1, jnp.where(even_band, above_near, below_near))
    target = live_only(mesh_recv, mesh_count[0, 0])
    own_hits[...] = hits_from(columns(jnp.where(inner, raw - cycle, -1)), 2 * cycle, cycle)
    outer_hits[...] = hits_from(columns(outer), 4 * cycle, 2 * cycle)
    to_hits[...] = hits_from(columns(target), 2 * node_count, node_count)
    source = jnp.where(inner, raw, jnp.where(outer < cycle, outer, outer + cycle))
    from_rows[...] = hits_to(source, 3 * cycle)
    to_rows[...] = hits_to(target, node_count)


def receiver_kernel(near, far, mesh_in, recv_hits, stack, pre_out):
    node_count = mesh_in.shape[0]
    rim = node_count // 2
    even = even_on("lat")
    left = jnp.where(even, far[...], near[...])[rim:]
    right = jnp.where(even, near[...], far[...])[:rim]
    cycle = jnp.concatenate([left, mesh_in[...], right], axis=0)
    table = jnp.concatenate(halves(mm(cycle, weight(stack, GR))), axis=0)
    pre_out[...] = mm(recv_hits[...], table)


def live_sizes(count, edges, steps, case):
    lower = 0
    for step in steps:
        size = edges * step // 8
        live = count[0, 0]
        fits = (live > lower) & (live <= size) if size < edges else live > lower
        pl.when(fits)(lambda size=size: case(size))
        lower = size


def in_two(size):
    middle = -(-size // 2 // LANES) * LANES
    return [slice(0, middle), slice(middle, size)]


def live_slots(count, edges, work, rest):
    def case(size):
        work(in_two(size))
        if size < edges:
            rest(slice(size, edges))

    live_sizes(count, edges, (4, 5, 6, 7, 8), case)


def gather_kernel(count, halo, hits, rows, rows_out, wide):
    def work(parts):
        fill(wide, halo, wide.shape[1] // halo.shape[0], 0)
        part_of = slice(0, parts[-1].stop)
        gathered = mm_nt(hits[part_of], wide[...]).astype(BF16)
        rows_out[part_of] = rows[part_of] + gathered

    def rest(part_of):
        rows_out[part_of] = jnp.zeros_like(rows_out[part_of])

    live_slots(count, rows.shape[0], work, rest)


def encode_kernel(
    count, near, near_hits, recv_rows, rows, recv_pre, stack,
    senders_out, slope_out, part_out, near_out, far_out, wide,
):
    half = recv_rows.shape[0] // 2

    def work(parts):
        fill(wide, near, wide.shape[1] // near.shape[0], 0)
        sums = None
        for part_of in parts:
            raw = rows[part_of] + mm_nt(near_hits[part_of], wide[...]).astype(BF16)
            latent, _ = silu_parts(mm(raw, stack[stack.shape[0] - raw.shape[1] :]))
            latent = latent.astype(BF16)
            senders_out[part_of] = latent
            pre = mm(latent, weight(stack, GS)) + recv_pre[part_of]
            value, slope = silu_parts(pre)
            slope_out[part_of] = slope.astype(BF16)
            part = mm(recv_rows[:, part_of], value.astype(BF16))
            sums = part if sums is None else sums + part
        part_out[...] = sums
        even = even_on("lat")
        near_out[...] = jnp.where(even, sums[half:], sums[:half]).astype(BF16)
        far_out[...] = jnp.where(even, sums[:half], sums[half:]).astype(BF16)

    def rest(part_of):
        senders_out[part_of] = jnp.zeros_like(senders_out[part_of])
        slope_out[part_of] = jnp.zeros_like(slope_out[part_of])

    live_slots(count, rows.shape[0], work, rest)


def node_kernel(part, near, far, mesh_near, mesh_far, mesh_in, stack, mesh_out, slope_out):
    node_count = mesh_in.shape[0]
    rim = node_count // 2
    even = even_on("lat")
    left = jnp.where(even, far[...], near[...]).astype(F32)
    right = jnp.where(even, near[...], far[...]).astype(F32)
    total = part[...] + jnp.concatenate([left, right], axis=0)
    mesh_left = jnp.where(even, mesh_far[...], mesh_near[...])[rim:]
    mesh_right = jnp.where(even, mesh_near[...], mesh_far[...])[:rim]
    cycle = jnp.concatenate([mesh_left, mesh_in[...], mesh_right], axis=0)
    value, slope = silu_parts(mm(total.astype(BF16), weight(stack, GN)))
    mesh_out[...] = (cycle.astype(F32) + value).astype(BF16)
    slope_out[...] = slope


def process_own_kernel(own_hits, to_hits, own, stack, pre_out):
    rim = own.shape[0] // 4
    home = own[rim : own.shape[0] - rim]
    table = jnp.concatenate(halves(mm(own[...], weight(stack, MS))), axis=0)
    recv_table = jnp.concatenate(halves(mm(home, weight(stack, MR))), axis=0)
    pre_out[...] = mm(own_hits[...], table) + mm(to_hits[...], recv_table)


def process_kernel(
    count, own_pre, outer_hits, to_hits, from_rows, to_rows, far, own, near, d_out, stack,
    mesh_out, sums_out, recv_out, near_out, far_out,
):
    cycle = own.shape[0]
    node_count = cycle // 2
    rim = node_count // 2

    def case(size):
        live = slice(0, size)
        home = own[rim : rim + node_count]
        block = jnp.concatenate([near[...], far[...]], axis=0)
        table = jnp.concatenate(halves(mm(block, weight(stack, MS))), axis=0)
        pre = own_pre[live] + mm(outer_hits[live], table)
        value, slope = silu_parts(pre)
        total = mm(to_rows[:, live], value.astype(BF16))
        gate = mm(total.astype(BF16), weight(stack, MN))
        gate_value, gate_slope = silu_parts(gate)
        mesh_out[...] = (home.astype(F32) + gate_value).astype(BF16)
        gate_two = (d_out[...].astype(F32) * gate_slope).astype(BF16)
        back = jnp.concatenate(halves(mm_nt(gate_two, weight(stack, MN))), axis=0)
        edge_slope = (mm(to_hits[live], back) * slope).astype(BF16)
        sums = mm(from_rows[:, live], edge_slope)
        recv_out[...] = mm(to_rows[:, live], edge_slope).astype(BF16)
        sums_out[...] = sums
        near_out[...] = sums[:cycle].astype(BF16)
        far_out[...] = sums[2 * cycle :].astype(BF16)

    live_sizes(count, own_pre.shape[0], (2, 4, 6, 8), case)


def block_of(x, dom_shift, lat_shift, doms, lats):
    cols = x.shape[1] // (doms * lats)
    dom = lax.rem(lax.axis_index("dom") + dom_shift, doms)
    index = dom * lats + lax.rem(lax.axis_index("lat") + lat_shift, lats)
    pick = x[:, :cols]
    for i in range(1, doms * lats):
        pick = jnp.where(index == i, x[:, i * cols : (i + 1) * cols], pick)
    return pick


def home_kernel(recv_sum, d_out, stack, senders, home_out, turned_out):
    home_out[...] = mm_nt(recv_sum[...], weight(stack, MR)) + d_out[...].astype(F32)
    turned_out[...] = senders[...].T


def cotangent_kernel(sums, near, far, home, part_out, near_out, far_out):
    cycle = near.shape[0]
    half = cycle // 2
    rim = half // 2
    total = sums[cycle : 2 * cycle] + near[...].astype(F32) + far[...].astype(F32)
    part_out[...] = total
    even = even_on("lat")
    near_out[:half] = jnp.where(even, total[half:], total[:half]).astype(BF16)
    near_out[half:] = jnp.where(even, home[rim:], home[:rim]).astype(BF16)
    far_out[:half] = jnp.where(even, total[:half], total[half:]).astype(BF16)
    far_out[half:] = jnp.where(even, home[:rim], home[rim:]).astype(BF16)


def gradient_block(recv_hits, back, edge_slope, senders, shifts, doms, lats, size=None):
    back = [block_of(back, *shift, doms, lats) for shift in shifts]
    back = back[0] if len(back) == 1 else jnp.concatenate(back, axis=1)
    total = None
    for part_of in in_two(size or recv_hits.shape[0]):
        weights = [block_of(edge_slope[part_of], *shift, doms, lats) for shift in shifts]
        weights = weights[0] if len(weights) == 1 else jnp.concatenate(weights, axis=1)
        slope = mm(recv_hits[part_of], back) * weights.astype(F32)
        part = mm(senders[:, part_of], slope.astype(BF16))
        total = part if total is None else total + part
    return total


def encode_grad_kernel(
    count, recv_hits, part, near, far, home, node_slope, stack, senders, edge_slope,
    sends, back_out, total_out,
):
    half = part.shape[0] // 2
    even = even_on("lat")
    left = jnp.where(even, far[...], near[...]).astype(F32)
    right = jnp.where(even, near[...], far[...]).astype(F32)
    total = part[...] + jnp.concatenate([left[:half], right[:half]], axis=0)
    total = total.astype(BF16)
    rest = jnp.concatenate([left[half:], home[...], right[half:]], axis=0)
    cot = rest + mm_nt(total, weight(stack, MS))
    gate_one = (cot * node_slope[...]).astype(BF16)
    back = jnp.concatenate(halves(mm_nt(gate_one, weight(stack, GN))), axis=0)
    back_out[...] = back
    lats = sends.shape[0] + 1
    doms = sends.shape[1] + 1

    def case(size):
        for i in range(1, lats):
            for j in range(1, doms):
                block = gradient_block(
                    recv_hits, back, edge_slope, senders, [(j, i)], doms, lats, size
                )
                sends[i - 1, j - 1] = block.astype(BF16)

    live_sizes(count, recv_hits.shape[0], (4, 5, 6, 7, 8), case)
    for j in range(doms):
        total_out[j] = block_of(total, j, 0, doms, lats)


def middle_blocks_kernel(recv_hits, back, edge_slope, senders, after, kept, sends):
    doms = kept.shape[0] + 1
    lats = sends.shape[0] + 1
    cols = kept.shape[2]
    shifts = [(j, 0) for j in range(1, doms)] + [(0, i) for i in range(1, lats)]
    blocks = gradient_block(recv_hits, back[...], edge_slope, senders, shifts, doms, lats)
    for k in range(len(shifts)):
        block = blocks[:, k * cols : (k + 1) * cols]
        if k < doms - 1:
            kept[k] = block
        else:
            sends[k - doms + 1] = block.astype(BF16)


def rows_at(ref, place, partner):
    bands = lax.axis_size("band")
    rows = ref.shape[-2] // bands
    at = pl.multiple_of(lax.bitwise_xor(lax.axis_index("band"), partner) * rows, rows)
    return ref[(*place, pl.ds(at, rows))]


def add_kernel(kept, total, *refs):
    *came, first_out, second_out = refs
    bands = lax.axis_size("band")
    rows = kept.shape[1] // bands
    near = second_out.shape[1] // rows
    for j in range(kept.shape[0]):
        for k in range(bands):
            block = rows_at(kept, (j,), k)
            for part in came:
                block = block + rows_at(part, (j,), k).astype(F32)
            out, at = (first_out, k - near) if k >= near else (second_out, k)
            at = at * rows
            out[j, at : at + rows] = block.astype(BF16)
        first_out[j, (bands - near) * rows :] = total[j + 1]


def own_block_kernel(recv_hits, back, edge_slope, senders, *refs):
    *came, out = refs
    lats = len(came) + 1
    doms = back.shape[1] // out.shape[1] // lats
    block = gradient_block(
        recv_hits, back[...], edge_slope, senders, [(0, 0)], doms, lats
    )
    for part in came:
        block = block + part[...].astype(F32)
    out[...] = block


def first_kernel(kept, total, nodes, *refs):
    doms = total.shape[0]
    came, (*sends_out, sums) = refs[: 2 * (doms - 1)], refs[2 * (doms - 1) :]
    came, came_nodes = came[: doms - 1], came[doms - 1 :]
    far = len(sends_out)
    near = lax.axis_size("band") - far
    rows = sends_out[0].shape[1]
    second = mm_tn(nodes[...], total[0])
    for part, part_nodes in zip(came, came_nodes):
        second = second + mm_tn(part_nodes[...], part[far * rows :])
    sums[...] = second
    for i, out in enumerate(sends_out):
        block = rows_at(kept, (), near + i)
        for part in came:
            block = block + part[i * rows : (i + 1) * rows].astype(F32)
        out[0] = block.astype(BF16)
        out[1] = rows_at(sums, (), near + i).astype(BF16)


def second_kernel(kept, sums, *refs):
    doms = lax.axis_size("dom")
    came, outs = refs[: doms - 1], refs[doms - 1 :]
    rows = outs[0].shape[1]
    for i, out in enumerate(outs):
        block = rows_at(kept, (), i)
        for part in came:
            block = block + part[i * rows : (i + 1) * rows].astype(F32)
        out[0] = block.astype(out.dtype)
        out[1] = rows_at(sums, (), i).astype(out.dtype)


def over_band_kernel(*refs):
    *came, own, first_out, second_out = refs
    for k, out in enumerate((first_out, second_out)):
        total = own[k]
        for part in came:
            total = total + part[k].astype(F32)
        out[...] = total


def call(kernel, outs, *args, scalars=(), scratch=()):
    in_specs = [
        pl.BlockSpec(memory_space=pltpu.SMEM if i in scalars else pltpu.VMEM)
        for i in range(len(args))
    ]
    return pl.pallas_call(
        kernel,
        out_shape=[jax.ShapeDtypeStruct(shape, dtype) for shape, dtype in outs],
        in_specs=in_specs,
        out_specs=[pl.BlockSpec(memory_space=pltpu.VMEM)] * len(outs),
        scratch_shapes=scratch,
        compiler_params=pltpu.CompilerParams(vmem_limit_bytes=16 << 20),
    )(*args)


def ring_pairings(count):
    far = [(i, (i + 1 if i % 2 else i - 1) % count) for i in range(count)]
    return [(i, i ^ 1) for i in range(count)], far


def line_pairings(bands, doms, lats):
    far = []
    for band in range(bands):
        other = band + 1 if band % 2 else band - 1
        for dom in range(doms):
            for lat in range(lats):
                here = (band * doms + dom) * lats + lat
                if 0 <= other < bands:
                    there = (other * doms + dom) * lats + lat
                else:
                    there = (band * doms + dom) * lats + (lat ^ 1)
                far.append((here, there))
    return [(i, i ^ 1) for i in range(bands)], far


def shifted(x, axis, shift):
    count = lax.axis_size(axis)
    return lax.ppermute(x, axis, [(i, (i + shift) % count) for i in range(count)])


def over_band(x, partner):
    count = lax.axis_size("band")
    return lax.ppermute(x, "band", [(b, b ^ partner) for b in range(count)])


def on_device(
    grid_in, w_grid, w_gs, w_gr, w_gn, w_ms, w_mr, w_mn, mesh_in, d_out,
    g2m_send, g2m_recv, g2m_count, mesh_send, mesh_recv, mesh_count,
):
    latent = w_grid.shape[1]
    variables = w_grid.shape[0]
    node_count = mesh_in.shape[0]
    cycle = 2 * node_count
    bands = lax.axis_size("band")
    sectors = lax.axis_size(("dom", "lat"))
    edges = g2m_send.shape[2]
    around = ("dom", "lat")
    whole = ("band", "dom", "lat")
    band_near, band_far = line_pairings(bands, lax.axis_size("dom"), lax.axis_size("lat"))
    ring_near, ring_far = ring_pairings(sectors)

    grid = jnp.transpose(grid_in, (0, 2, 1))
    pitch = -(-grid.shape[2] // LANES) * LANES
    band_rows = grid.shape[0]
    width = band_rows * pitch
    raw_near = lax.ppermute(grid, "band", band_near)
    raw_far = lax.ppermute(grid, whole, band_far)
    mesh_edges = mesh_send.shape[2]
    stack = jnp.concatenate([w_gs, w_gr, w_gn, w_ms, w_mr, w_mn, w_grid], axis=0)
    indices = jnp.concatenate([g2m_send, g2m_recv, mesh_send, mesh_recv], axis=2)
    (
        rows, recv_hits, recv_rows, own_hits, outer_hits, to_hits, from_rows, to_rows, *halo_hits
    ) = call(
        index_kernel,
        [
            ((edges, variables), BF16),
            ((edges, 2 * cycle), BF16),
            ((cycle, edges), BF16),
            ((mesh_edges, 2 * cycle), BF16),
            ((mesh_edges, 4 * cycle), BF16),
            ((mesh_edges, 2 * node_count), BF16),
            ((3 * cycle, mesh_edges), BF16),
            ((node_count, mesh_edges), BF16),
            ((edges, width), BF16),
            ((edges, width), BF16),
        ],
        g2m_count, mesh_count, indices, grid,
        scalars=(0, 1),
        scratch=[pltpu.VMEM((variables, width), BF16)],
    )
    late_mesh, rows = lax.optimization_barrier((mesh_in, rows))
    mesh_near = lax.ppermute(late_mesh, around, ring_near)
    mesh_far = lax.ppermute(late_mesh, around, ring_far)
    (recv_pre,) = call(
        receiver_kernel,
        [((edges, latent), F32)],
        mesh_near, mesh_far, mesh_in, recv_hits, stack,
    )
    near_hits, far_hits = halo_hits
    (rows,) = call(
        gather_kernel,
        [((edges, variables), BF16)],
        g2m_count, raw_far, far_hits, rows,
        scalars=(0,),
        scratch=[pltpu.VMEM((variables, width), BF16)],
    )
    senders, edge_slope, part, to_near, to_far = call(
        encode_kernel,
        [
            ((edges, latent), BF16),
            ((edges, latent), BF16),
            ((cycle, latent), F32),
            ((node_count, latent), BF16),
            ((node_count, latent), BF16),
        ],
        g2m_count, raw_near, near_hits, recv_rows, rows, recv_pre, stack,
        scalars=(0,),
        scratch=[pltpu.VMEM((variables, width), BF16)],
    )
    from_far = lax.ppermute(to_far, around, ring_far)
    from_near = lax.ppermute(to_near, around, ring_near)
    mesh_one, node_slope = call(
        node_kernel,
        [((cycle, latent), BF16), ((cycle, latent), F32)],
        part, from_near, from_far, mesh_near, mesh_far, mesh_in, stack,
    )
    one_near = lax.ppermute(mesh_one, "band", band_near)
    one_far = lax.ppermute(mesh_one, whole, band_far)
    doms = lax.axis_size("dom")
    lats = lax.axis_size("lat")
    dom_nodes = [shifted(mesh_one, "dom", i + 1) for i in range(doms - 1)]
    (own_pre,) = call(
        process_own_kernel, [((mesh_edges, latent), F32)], own_hits, to_hits, mesh_one, stack
    )
    mesh_out, sums, recv_sum, to_near, to_far = call(
        process_kernel,
        [
            ((node_count, latent), BF16),
            ((3 * cycle, latent), F32),
            ((node_count, latent), BF16),
            ((cycle, latent), BF16),
            ((cycle, latent), BF16),
        ],
        mesh_count, own_pre, outer_hits, to_hits, from_rows, to_rows, one_far, mesh_one,
        one_near, d_out, stack,
        scalars=(0,),
    )
    from_near = lax.ppermute(to_near, "band", band_near)
    from_far = lax.ppermute(to_far, whole, band_far)
    home, senders = call(
        home_kernel,
        [((node_count, latent), F32), ((latent, edges), BF16)],
        recv_sum, d_out, stack, senders,
    )
    message = (node_count + node_count // 2, latent)
    part, to_near, to_far = call(
        cotangent_kernel,
        [((cycle, latent), F32), (message, BF16), (message, BF16)],
        sums, from_near, from_far, home,
    )
    from_far = lax.ppermute(to_far, around, ring_far)
    from_near = lax.ppermute(to_near, around, ring_near)

    from_near, *dom_nodes = lax.optimization_barrier((from_near, *dom_nodes))
    cols = latent // sectors
    rows = latent // bands
    sends, back, total = call(
        encode_grad_kernel,
        [
            ((lats - 1, doms - 1, latent, cols), BF16),
            ((2 * cycle, latent), BF16),
            ((doms, cycle, cols), BF16),
        ],
        g2m_count, recv_hits, part, from_near, from_far, home, node_slope, stack, senders,
        edge_slope,
        scalars=(0,),
    )
    edge = (recv_hits, back, edge_slope, senders)
    came = [shifted(sends[i], "lat", i + 1) for i in range(lats - 1)]
    block = (latent, cols)
    kept, own_sends = call(
        middle_blocks_kernel,
        [((doms - 1,) + block, F32), ((lats - 1,) + block, BF16)],
        *edge, sends,
    )
    own_came = [shifted(own_sends[i], "lat", i + 1) for i in range(lats - 1)]
    far = bands // 2
    first, second = call(
        add_kernel,
        [
            ((doms - 1, far * rows + cycle, cols), BF16),
            ((doms - 1, (bands - far) * rows, cols), BF16),
        ],
        kept, total, *came,
    )
    first = [shifted(first[i], "dom", i + 1) for i in range(doms - 1)]
    second = [shifted(second[i], "dom", i + 1) for i in range(doms - 1)]
    (kept,) = call(own_block_kernel, [(block, F32)], *edge, *own_came)
    pair = (2, rows, cols)
    *far_sends, sums = call(
        first_kernel,
        [(pair, BF16)] * far + [(block, F32)],
        kept, total, mesh_one, *first, *dom_nodes,
    )
    came = [over_band(x, bands - far + i) for i, x in reversed(list(enumerate(far_sends)))]
    own, *near_sends = call(
        second_kernel,
        [(pair, F32)] + [(pair, BF16)] * (bands - far - 1),
        kept, sums, *second,
    )
    came += [over_band(x, i + 1) for i, x in reversed(list(enumerate(near_sends)))]
    tile = ((rows, cols), F32)
    grad_gs, grad_ms = call(over_band_kernel, [tile, tile], *came, own)
    return mesh_out, grad_gs, grad_ms


def solution(mesh):
    flat = P(("groups", "band", "dom", "lat"), None)
    grid = P(("groups", "band"), ("dom", "lat"), None)
    count = P(("groups", "band"), ("dom", "lat"))
    placed = (grid,) + (P(),) * 7 + (flat, flat) + (grid, grid, count) * 2
    return jax.shard_map(
        on_device,
        mesh=mesh,
        in_specs=placed,
        out_specs=(flat, count, count),
        check_vma=False,
    )
```

```python
import jax
import jax.numpy as jnp
from jax import lax
from jax.experimental import pallas as pl
from jax.experimental.pallas import tpu as pltpu
from jax.sharding import PartitionSpec as P

F32 = jnp.float32
BF16 = jnp.bfloat16
LANES = 128
GS, GR, GN, MS, MR, MN = range(6)


def mm(a, b):
    return jnp.dot(a, b, preferred_element_type=F32)


def mm_nt(a, b):
    return lax.dot_general(a, b, (((1,), (1,)), ((), ())), preferred_element_type=F32)


def mm_tn(a, b):
    return lax.dot_general(a, b, (((0,), (0,)), ((), ())), preferred_element_type=F32)


def halves(x):
    high = x.astype(BF16)
    return high, (x - high.astype(F32)).astype(BF16)


def silu_parts(x):
    g = 0.5 * jnp.tanh(0.5 * x) + 0.5
    value = x * g
    return value, g + value * (1.0 - g)


def ones_at(mask):
    return jnp.where(mask, 1.0, 0.0).astype(BF16)


def columns(row):
    count = row.shape[1]
    parts = [
        jnp.broadcast_to(row[:, i : i + LANES], (LANES, LANES)).T
        for i in range(0, count, LANES)
    ]
    return parts[0] if len(parts) == 1 else jnp.concatenate(parts, axis=0)


def hits_from(cols, width, period, start=0):
    parts = []
    for i in range(0, width, LANES):
        size = min(LANES, width - i)
        lane = lax.broadcasted_iota(jnp.int32, (cols.shape[0], size), 1) + i
        if period < width:
            lane = lax.rem(lane, period)
        parts.append(ones_at(cols[:, :size] == lane + start))
    return parts[0] if len(parts) == 1 else jnp.concatenate(parts, axis=1)


def hits_to(row, count):
    return ones_at(lax.broadcasted_iota(jnp.int32, (count, row.shape[1]), 0) == row)


def live_only(row, count, first=0):
    slot = lax.broadcasted_iota(jnp.int32, row.shape, 1) + first
    return jnp.where(slot < count, row, -1)


def weight(stack, index):
    latent = stack.shape[1]
    return stack[index * latent : (index + 1) * latent]


def even_on(axis):
    return lax.rem(lax.axis_index(axis), 2) == 0


def spread(index, blocks, cols, pitch):
    extra = jnp.zeros_like(index)
    for block in range(1, blocks):
        extra = extra + jnp.where(index >= block * cols, pitch - cols, 0)
    return index + extra


def fill(wide, blocks, pitch, first):
    cols = blocks.shape[2]
    for k in range(blocks.shape[0]):
        at = first + k * pitch
        wide[:, at : at + cols] = blocks[k]
        if cols < pitch:
            wide[:, at + cols : at + pitch] = jnp.zeros(
                (wide.shape[0], pitch - cols), wide.dtype
            )


def index_kernel(
    count, mesh_count, indices, grid,
    own_out, recv_hits, recv_rows, own_hits, outer_hits, to_hits, from_rows, to_rows, near_hits, far_hits, wide,
):
    edges = recv_hits.shape[0]
    mesh_edges = to_hits.shape[0]
    send, recv, mesh_send, mesh_recv = (
        indices[0, :, first : first + size]
        for first, size in (
            (0, edges),
            (edges, edges),
            (2 * edges, mesh_edges),
            (2 * edges + mesh_edges, mesh_edges),
        )
    )
    band_rows, _, cols = grid.shape
    pitch = wide.shape[1] // band_rows
    width = band_rows * pitch
    cycle = recv_rows.shape[0]
    node_count = to_rows.shape[0]
    even_band = even_on("band")
    fill(wide, grid, pitch, 0)
    near_base = jnp.where(even_band, 2 * width, 0)
    far_base = jnp.where(even_band, 0, 2 * width)
    block = 256
    for first in range(0, edges, block):
        part_of = slice(first, first + block)
        index = columns(spread(send[:, part_of], 3 * band_rows, cols, pitch))
        own_hit = hits_from(index, width, width, width)
        own_out[part_of] = mm_nt(own_hit, wide[...]).astype(BF16)
        near_hits[part_of] = hits_from(index, width, width, near_base)
        far_hits[part_of] = hits_from(index, width, width, far_base)
        target = live_only(recv[:, part_of], count[0, 0], first)
        recv_hits[part_of] = hits_from(columns(target), 2 * cycle, cycle)
        recv_rows[:, part_of] = hits_to(target, cycle)
    raw = mesh_send
    inner = (raw >= cycle) & (raw < 2 * cycle)
    above_near = jnp.where(raw < cycle, raw + cycle, raw - 2 * cycle)
    below_near = jnp.where(raw < cycle, raw, raw - cycle)
    outer = jnp.where(inner, -1, jnp.where(even_band, above_near, below_near))
    target = live_only(mesh_recv, mesh_count[0, 0])
    own_hits[...] = hits_from(columns(jnp.where(inner, raw - cycle, -1)), 2 * cycle, cycle)
    outer_hits[...] = hits_from(columns(outer), 4 * cycle, 2 * cycle)
    to_hits[...] = hits_from(columns(target), 2 * node_count, node_count)
    source = jnp.where(inner, raw, jnp.where(outer < cycle, outer, outer + cycle))
    from_rows[...] = hits_to(source, 3 * cycle)
    to_rows[...] = hits_to(target, node_count)


def receiver_kernel(near, far, mesh_in, recv_hits, stack, pre_out):
    node_count = mesh_in.shape[0]
    rim = node_count // 2
    even = even_on("lat")
    left = jnp.where(even, far[...], near[...])[rim:]
    right = jnp.where(even, near[...], far[...])[:rim]
    cycle = jnp.concatenate([left, mesh_in[...], right], axis=0)
    table = jnp.concatenate(halves(mm(cycle, weight(stack, GR))), axis=0)
    pre_out[...] = mm(recv_hits[...], table)


def live_slots(count, edges, work, rest):
    lower = 0
    for size in range(edges // 2, edges + 1, edges // 8):

        def case(size=size):
            middle = -(-size // 2 // LANES) * LANES
            work([slice(0, middle), slice(middle, size)])
            if size < edges:
                rest(slice(size, edges))

        live = count[0, 0]
        pl.when((live > lower) & (live <= size) if size < edges else live > lower)(case)
        lower = size


def gather_kernel(count, halo, hits, rows, rows_out, wide):
    def work(parts):
        fill(wide, halo, wide.shape[1] // halo.shape[0], 0)
        part_of = slice(0, parts[-1].stop)
        gathered = mm_nt(hits[part_of], wide[...]).astype(BF16)
        rows_out[part_of] = rows[part_of] + gathered

    def rest(part_of):
        rows_out[part_of] = jnp.zeros_like(rows_out[part_of])

    live_slots(count, rows.shape[0], work, rest)


def encode_kernel(
    count, near, near_hits, recv_rows, rows, recv_pre, stack,
    senders_out, slope_out, part_out, near_out, far_out, wide,
):
    half = recv_rows.shape[0] // 2

    def work(parts):
        fill(wide, near, wide.shape[1] // near.shape[0], 0)
        sums = None
        for part_of in parts:
            raw = rows[part_of] + mm_nt(near_hits[part_of], wide[...]).astype(BF16)
            latent, _ = silu_parts(mm(raw, stack[stack.shape[0] - raw.shape[1] :]))
            latent = latent.astype(BF16)
            senders_out[part_of] = latent
            pre = mm(latent, weight(stack, GS)) + recv_pre[part_of]
            value, slope = silu_parts(pre)
            slope_out[part_of] = slope.astype(BF16)
            part = mm(recv_rows[:, part_of], value.astype(BF16))
            sums = part if sums is None else sums + part
        part_out[...] = sums
        even = even_on("lat")
        near_out[...] = jnp.where(even, sums[half:], sums[:half]).astype(BF16)
        far_out[...] = jnp.where(even, sums[:half], sums[half:]).astype(BF16)

    def rest(part_of):
        senders_out[part_of] = jnp.zeros_like(senders_out[part_of])
        slope_out[part_of] = jnp.zeros_like(slope_out[part_of])

    live_slots(count, rows.shape[0], work, rest)


def node_kernel(part, near, far, mesh_near, mesh_far, mesh_in, stack, mesh_out, slope_out):
    node_count = mesh_in.shape[0]
    rim = node_count // 2
    even = even_on("lat")
    left = jnp.where(even, far[...], near[...]).astype(F32)
    right = jnp.where(even, near[...], far[...]).astype(F32)
    total = part[...] + jnp.concatenate([left, right], axis=0)
    mesh_left = jnp.where(even, mesh_far[...], mesh_near[...])[rim:]
    mesh_right = jnp.where(even, mesh_near[...], mesh_far[...])[:rim]
    cycle = jnp.concatenate([mesh_left, mesh_in[...], mesh_right], axis=0)
    value, slope = silu_parts(mm(total.astype(BF16), weight(stack, GN)))
    mesh_out[...] = (cycle.astype(F32) + value).astype(BF16)
    slope_out[...] = slope


def process_own_kernel(own_hits, to_hits, own, stack, pre_out):
    rim = own.shape[0] // 4
    home = own[rim : own.shape[0] - rim]
    table = jnp.concatenate(halves(mm(own[...], weight(stack, MS))), axis=0)
    recv_table = jnp.concatenate(halves(mm(home, weight(stack, MR))), axis=0)
    pre_out[...] = mm(own_hits[...], table) + mm(to_hits[...], recv_table)


def process_kernel(
    own_pre, outer_hits, to_hits, from_rows, to_rows, far, own, near, d_out, stack,
    mesh_out, sums_out, recv_out, near_out, far_out,
):
    cycle = own.shape[0]
    node_count = cycle // 2
    rim = node_count // 2
    home = own[rim : rim + node_count]
    block = jnp.concatenate([near[...], far[...]], axis=0)
    table = jnp.concatenate(halves(mm(block, weight(stack, MS))), axis=0)
    pre = own_pre[...] + mm(outer_hits[...], table)
    value, slope = silu_parts(pre)
    gate = mm(mm(to_rows[...], value.astype(BF16)).astype(BF16), weight(stack, MN))
    gate_value, gate_slope = silu_parts(gate)
    mesh_out[...] = (home.astype(F32) + gate_value).astype(BF16)
    gate_two = (d_out[...].astype(F32) * gate_slope).astype(BF16)
    back = jnp.concatenate(halves(mm_nt(gate_two, weight(stack, MN))), axis=0)
    edge_slope = (mm(to_hits[...], back) * slope).astype(BF16)
    sums = mm(from_rows[...], edge_slope)
    recv_out[...] = mm(to_rows[...], edge_slope).astype(BF16)
    sums_out[...] = sums
    near_out[...] = sums[:cycle].astype(BF16)
    far_out[...] = sums[2 * cycle :].astype(BF16)


def block_of(x, dom_shift, lat_shift, doms, lats):
    cols = x.shape[1] // (doms * lats)
    dom = lax.rem(lax.axis_index("dom") + dom_shift, doms)
    index = dom * lats + lax.rem(lax.axis_index("lat") + lat_shift, lats)
    pick = x[:, :cols]
    for i in range(1, doms * lats):
        pick = jnp.where(index == i, x[:, i * cols : (i + 1) * cols], pick)
    return pick


def home_kernel(recv_sum, d_out, stack, senders, home_out, turned_out):
    home_out[...] = mm_nt(recv_sum[...], weight(stack, MR)) + d_out[...].astype(F32)
    turned_out[...] = senders[...].T


def cotangent_kernel(sums, near, far, home, part_out, near_out, far_out):
    cycle = near.shape[0]
    half = cycle // 2
    rim = half // 2
    total = sums[cycle : 2 * cycle] + near[...].astype(F32) + far[...].astype(F32)
    part_out[...] = total
    even = even_on("lat")
    near_out[:half] = jnp.where(even, total[half:], total[:half]).astype(BF16)
    near_out[half:] = jnp.where(even, home[rim:], home[:rim]).astype(BF16)
    far_out[:half] = jnp.where(even, total[:half], total[half:]).astype(BF16)
    far_out[half:] = jnp.where(even, home[:rim], home[rim:]).astype(BF16)


def gradient_block(recv_hits, back, edge_slope, senders, shifts, doms, lats):
    edges = recv_hits.shape[0]
    back = [block_of(back, *shift, doms, lats) for shift in shifts]
    back = back[0] if len(back) == 1 else jnp.concatenate(back, axis=1)
    total = None
    for first in range(0, edges, edges // 2):
        part_of = slice(first, first + edges // 2)
        weights = [block_of(edge_slope[part_of], *shift, doms, lats) for shift in shifts]
        weights = weights[0] if len(weights) == 1 else jnp.concatenate(weights, axis=1)
        slope = mm(recv_hits[part_of], back) * weights.astype(F32)
        part = mm(senders[:, part_of], slope.astype(BF16))
        total = part if total is None else total + part
    return total


def encode_grad_kernel(
    recv_hits, part, near, far, home, node_slope, stack, senders, edge_slope,
    sends, back_out, total_out,
):
    half = part.shape[0] // 2
    even = even_on("lat")
    left = jnp.where(even, far[...], near[...]).astype(F32)
    right = jnp.where(even, near[...], far[...]).astype(F32)
    total = part[...] + jnp.concatenate([left[:half], right[:half]], axis=0)
    total = total.astype(BF16)
    rest = jnp.concatenate([left[half:], home[...], right[half:]], axis=0)
    cot = rest + mm_nt(total, weight(stack, MS))
    gate_one = (cot * node_slope[...]).astype(BF16)
    back = jnp.concatenate(halves(mm_nt(gate_one, weight(stack, GN))), axis=0)
    back_out[...] = back
    lats = sends.shape[0] + 1
    doms = sends.shape[1] + 1
    for i in range(1, lats):
        for j in range(1, doms):
            block = gradient_block(
                recv_hits, back, edge_slope, senders, [(j, i)], doms, lats
            )
            sends[i - 1, j - 1] = block.astype(BF16)
    for j in range(doms):
        total_out[j] = block_of(total, j, 0, doms, lats)


def middle_blocks_kernel(recv_hits, back, edge_slope, senders, after, kept, sends):
    doms = kept.shape[0] + 1
    lats = sends.shape[0] + 1
    cols = kept.shape[2]
    shifts = [(j, 0) for j in range(1, doms)] + [(0, i) for i in range(1, lats)]
    blocks = gradient_block(recv_hits, back[...], edge_slope, senders, shifts, doms, lats)
    for k in range(len(shifts)):
        block = blocks[:, k * cols : (k + 1) * cols]
        if k < doms - 1:
            kept[k] = block
        else:
            sends[k - doms + 1] = block.astype(BF16)


def rows_at(ref, place, partner):
    bands = lax.axis_size("band")
    rows = ref.shape[-2] // bands
    at = pl.multiple_of(lax.bitwise_xor(lax.axis_index("band"), partner) * rows, rows)
    return ref[(*place, pl.ds(at, rows))]


def add_kernel(kept, total, *refs):
    *came, first_out, second_out = refs
    bands = lax.axis_size("band")
    rows = kept.shape[1] // bands
    near = second_out.shape[1] // rows
    for j in range(kept.shape[0]):
        for k in range(bands):
            block = rows_at(kept, (j,), k)
            for part in came:
                block = block + rows_at(part, (j,), k).astype(F32)
            out, at = (first_out, k - near) if k >= near else (second_out, k)
            at = at * rows
            out[j, at : at + rows] = block.astype(BF16)
        first_out[j, (bands - near) * rows :] = total[j + 1]


def own_block_kernel(recv_hits, back, edge_slope, senders, total, nodes, *refs):
    *came, out, sums_out = refs
    lats = len(came) + 1
    doms = back.shape[1] // out.shape[1] // lats
    block = gradient_block(
        recv_hits, back[...], edge_slope, senders, [(0, 0)], doms, lats
    )
    for part in came:
        block = block + part[...].astype(F32)
    out[...] = block
    sums_out[...] = mm_tn(nodes[...], total[0])


def first_kernel(kept, own_sums, *refs):
    doms = lax.axis_size("dom")
    came, (*sends_out, sums) = refs[: 2 * (doms - 1)], refs[2 * (doms - 1) :]
    came, came_nodes = came[: doms - 1], came[doms - 1 :]
    far = len(sends_out)
    near = lax.axis_size("band") - far
    rows = sends_out[0].shape[1]
    second = own_sums[...]
    for part, part_nodes in zip(came, came_nodes):
        second = second + mm_tn(part_nodes[...], part[far * rows :])
    sums[...] = second
    for i, out in enumerate(sends_out):
        block = rows_at(kept, (), near + i)
        for part in came:
            block = block + part[i * rows : (i + 1) * rows].astype(F32)
        out[0] = block.astype(BF16)
        out[1] = rows_at(sums, (), near + i).astype(BF16)


def second_kernel(kept, sums, *refs):
    doms = lax.axis_size("dom")
    came, outs = refs[: doms - 1], refs[doms - 1 :]
    rows = outs[0].shape[1]
    for i, out in enumerate(outs):
        block = rows_at(kept, (), i)
        for part in came:
            block = block + part[i * rows : (i + 1) * rows].astype(F32)
        out[0] = block.astype(out.dtype)
        out[1] = rows_at(sums, (), i).astype(out.dtype)


def over_band_kernel(*refs):
    *came, own, first_out, second_out = refs
    for k, out in enumerate((first_out, second_out)):
        total = own[k]
        for part in came:
            total = total + part[k].astype(F32)
        out[...] = total


def call(kernel, outs, *args, scalars=(), scratch=()):
    in_specs = [
        pl.BlockSpec(memory_space=pltpu.SMEM if i in scalars else pltpu.VMEM)
        for i in range(len(args))
    ]
    return pl.pallas_call(
        kernel,
        out_shape=[jax.ShapeDtypeStruct(shape, dtype) for shape, dtype in outs],
        in_specs=in_specs,
        out_specs=[pl.BlockSpec(memory_space=pltpu.VMEM)] * len(outs),
        scratch_shapes=scratch,
        compiler_params=pltpu.CompilerParams(vmem_limit_bytes=16 << 20),
    )(*args)


def ring_pairings(count):
    far = [(i, (i + 1 if i % 2 else i - 1) % count) for i in range(count)]
    return [(i, i ^ 1) for i in range(count)], far


def line_pairings(bands, doms, lats):
    far = []
    for band in range(bands):
        other = band + 1 if band % 2 else band - 1
        for dom in range(doms):
            for lat in range(lats):
                here = (band * doms + dom) * lats + lat
                if 0 <= other < bands:
                    there = (other * doms + dom) * lats + lat
                else:
                    there = (band * doms + dom) * lats + (lat ^ 1)
                far.append((here, there))
    return [(i, i ^ 1) for i in range(bands)], far


def shifted(x, axis, shift):
    count = lax.axis_size(axis)
    return lax.ppermute(x, axis, [(i, (i + shift) % count) for i in range(count)])


def over_band(x, partner):
    count = lax.axis_size("band")
    return lax.ppermute(x, "band", [(b, b ^ partner) for b in range(count)])


def on_device(
    grid_in, w_grid, w_gs, w_gr, w_gn, w_ms, w_mr, w_mn, mesh_in, d_out,
    g2m_send, g2m_recv, g2m_count, mesh_send, mesh_recv, mesh_count,
):
    latent = w_grid.shape[1]
    variables = w_grid.shape[0]
    node_count = mesh_in.shape[0]
    cycle = 2 * node_count
    bands = lax.axis_size("band")
    sectors = lax.axis_size(("dom", "lat"))
    edges = g2m_send.shape[2]
    around = ("dom", "lat")
    whole = ("band", "dom", "lat")
    band_near, band_far = line_pairings(bands, lax.axis_size("dom"), lax.axis_size("lat"))
    ring_near, ring_far = ring_pairings(sectors)

    grid = jnp.transpose(grid_in, (0, 2, 1))
    pitch = -(-grid.shape[2] // LANES) * LANES
    band_rows = grid.shape[0]
    width = band_rows * pitch
    raw_near = lax.ppermute(grid, "band", band_near)
    raw_far = lax.ppermute(grid, whole, band_far)
    mesh_edges = mesh_send.shape[2]
    stack = jnp.concatenate([w_gs, w_gr, w_gn, w_ms, w_mr, w_mn, w_grid], axis=0)
    indices = jnp.concatenate([g2m_send, g2m_recv, mesh_send, mesh_recv], axis=2)
    (
        rows, recv_hits, recv_rows, own_hits, outer_hits, to_hits, from_rows, to_rows, *halo_hits
    ) = call(
        index_kernel,
        [
            ((edges, variables), BF16),
            ((edges, 2 * cycle), BF16),
            ((cycle, edges), BF16),
            ((mesh_edges, 2 * cycle), BF16),
            ((mesh_edges, 4 * cycle), BF16),
            ((mesh_edges, 2 * node_count), BF16),
            ((3 * cycle, mesh_edges), BF16),
            ((node_count, mesh_edges), BF16),
            ((edges, width), BF16),
            ((edges, width), BF16),
        ],
        g2m_count, mesh_count, indices, grid,
        scalars=(0, 1),
        scratch=[pltpu.VMEM((variables, width), BF16)],
    )
    late_mesh, rows = lax.optimization_barrier((mesh_in, rows))
    mesh_near = lax.ppermute(late_mesh, around, ring_near)
    mesh_far = lax.ppermute(late_mesh, around, ring_far)
    (recv_pre,) = call(
        receiver_kernel,
        [((edges, latent), F32)],
        mesh_near, mesh_far, mesh_in, recv_hits, stack,
    )
    near_hits, far_hits = halo_hits
    (rows,) = call(
        gather_kernel,
        [((edges, variables), BF16)],
        g2m_count, raw_far, far_hits, rows,
        scalars=(0,),
        scratch=[pltpu.VMEM((variables, width), BF16)],
    )
    senders, edge_slope, part, to_near, to_far = call(
        encode_kernel,
        [
            ((edges, latent), BF16),
            ((edges, latent), BF16),
            ((cycle, latent), F32),
            ((node_count, latent), BF16),
            ((node_count, latent), BF16),
        ],
        g2m_count, raw_near, near_hits, recv_rows, rows, recv_pre, stack,
        scalars=(0,),
        scratch=[pltpu.VMEM((variables, width), BF16)],
    )
    from_far = lax.ppermute(to_far, around, ring_far)
    from_near = lax.ppermute(to_near, around, ring_near)
    mesh_one, node_slope = call(
        node_kernel,
        [((cycle, latent), BF16), ((cycle, latent), F32)],
        part, from_near, from_far, mesh_near, mesh_far, mesh_in, stack,
    )
    one_near = lax.ppermute(mesh_one, "band", band_near)
    one_far = lax.ppermute(mesh_one, whole, band_far)
    doms = lax.axis_size("dom")
    lats = lax.axis_size("lat")
    dom_nodes = [shifted(mesh_one, "dom", i + 1) for i in range(doms - 1)]
    (own_pre,) = call(
        process_own_kernel, [((mesh_edges, latent), F32)], own_hits, to_hits, mesh_one, stack
    )
    mesh_out, sums, recv_sum, to_near, to_far = call(
        process_kernel,
        [
            ((node_count, latent), BF16),
            ((3 * cycle, latent), F32),
            ((node_count, latent), BF16),
            ((cycle, latent), BF16),
            ((cycle, latent), BF16),
        ],
        own_pre, outer_hits, to_hits, from_rows, to_rows, one_far, mesh_one, one_near, d_out,
        stack,
    )
    from_near = lax.ppermute(to_near, "band", band_near)
    from_far = lax.ppermute(to_far, whole, band_far)
    home, senders = call(
        home_kernel,
        [((node_count, latent), F32), ((latent, edges), BF16)],
        recv_sum, d_out, stack, senders,
    )
    message = (node_count + node_count // 2, latent)
    part, to_near, to_far = call(
        cotangent_kernel,
        [((cycle, latent), F32), (message, BF16), (message, BF16)],
        sums, from_near, from_far, home,
    )
    from_far = lax.ppermute(to_far, around, ring_far)
    from_near = lax.ppermute(to_near, around, ring_near)

    from_near, *dom_nodes = lax.optimization_barrier((from_near, *dom_nodes))
    cols = latent // sectors
    rows = latent // bands
    sends, back, total = call(
        encode_grad_kernel,
        [
            ((lats - 1, doms - 1, latent, cols), BF16),
            ((2 * cycle, latent), BF16),
            ((doms, cycle, cols), BF16),
        ],
        recv_hits, part, from_near, from_far, home, node_slope, stack, senders, edge_slope,
    )
    edge = (recv_hits, back, edge_slope, senders)
    came = [shifted(sends[i], "lat", i + 1) for i in range(lats - 1)]
    block = (latent, cols)
    kept, own_sends = call(
        middle_blocks_kernel,
        [((doms - 1,) + block, F32), ((lats - 1,) + block, BF16)],
        *edge, sends,
    )
    own_came = [shifted(own_sends[i], "lat", i + 1) for i in range(lats - 1)]
    far = bands // 2
    first, second = call(
        add_kernel,
        [
            ((doms - 1, far * rows + cycle, cols), BF16),
            ((doms - 1, (bands - far) * rows, cols), BF16),
        ],
        kept, total, *came,
    )
    first = [shifted(first[i], "dom", i + 1) for i in range(doms - 1)]
    second = [shifted(second[i], "dom", i + 1) for i in range(doms - 1)]
    kept, own_sums = call(
        own_block_kernel, [(block, F32)] * 2, *edge, total, mesh_one, *own_came
    )
    pair = (2, rows, cols)
    *far_sends, sums = call(
        first_kernel,
        [(pair, BF16)] * far + [(block, F32)],
        kept, own_sums, *first, *dom_nodes,
    )
    came = [over_band(x, bands - far + i) for i, x in reversed(list(enumerate(far_sends)))]
    own, *near_sends = call(
        second_kernel,
        [(pair, F32)] + [(pair, BF16)] * (bands - far - 1),
        kept, sums, *second,
    )
    came += [over_band(x, i + 1) for i, x in reversed(list(enumerate(near_sends)))]
    tile = ((rows, cols), F32)
    grad_gs, grad_ms = call(over_band_kernel, [tile, tile], *came, own)
    return mesh_out, grad_gs, grad_ms


def solution(mesh):
    flat = P(("groups", "band", "dom", "lat"), None)
    grid = P(("groups", "band"), ("dom", "lat"), None)
    count = P(("groups", "band"), ("dom", "lat"))
    placed = (grid,) + (P(),) * 7 + (flat, flat) + (grid, grid, count) * 2
    return jax.shard_map(
        on_device,
        mesh=mesh,
        in_specs=placed,
        out_specs=(flat, count, count),
        check_vma=False,
    )
```
